32 devices in a mesh: rows: 8 (over z, x), seq: 4 (over y, core).
Axes of the slice: x: 2, y: 2, z: 4, core: 2. Of those that a mesh axis runs over, the one named last changes fastest.
Arguments:
- frames_in: bfloat16 [16, 4096, 512], P('rows', 'seq'), may hold values from -6 to 6
- lengths: int32 [16, 4], P('rows'), may hold values from 1 to 2048, 4096 in all within a row
- bw_ids: int32 [16, 4], P('rows'), may hold values from 0 to 3
- owner_list: int32 [137], replicated, may hold values from 0 to 7, as said below
- master: float32 [216, 32, 512], P('rows')
- moment1: float32 [216, 32, 512], P('rows')
- moment2: float32 [216, 32, 512], P('rows'), as said below
- wave_grad: bfloat16 [16, 1310720], P('rows', 'seq'), may hold values from -6 to 6
Outputs:
- waveform: float32 [16, 1310720], P('rows', 'seq')
- input_grad: float32 [16, 4096, 512], P('rows', 'seq')
- new_master: float32 [216, 32, 512], P('rows')
- new_moment1: float32 [216, 32, 512], P('rows')
- new_moment2: float32 [216, 32, 512], P('rows')
The draws below stay inside these ranges and needn't reach their ends.
Inputs may be any that keep to these rules, and one draw needn't show every extreme that they name: `owner_list`: no index along rows owns more than 27 buckets, and some index owns exactly 27. `moment2`: every entry is positive.
All inputs are finite; a program needn't handle non-finite values.
Results may differ from the reference program's by a relative error of at most 0.012.
The reference program's roundings to bfloat16 on the way count: a program that leaves them out, or rounds other values in their place, can miss the bound.
Values may be sent and summed in bfloat16 or wider, within the bound.
No kernel may reach another device: no remote copies, remote signals or barrier semaphores. Data moves between devices by JAX's collectives and lax.ppermute only.
A program may use at most 192 MiB of HBM per device.

```python
import math
import jax
import jax.numpy as jnp
import numpy as np
from jax import lax

D = 512
FF = 1536
NFFT = 1280
HOP = 320
NBW = 4
KW = 7
UTT = 4
BR = 32
STEP_COUNT = 6
BINS = 641
NOUT = 1282
LAPS = 4
FRAMES = 4096
ROWS = 16
SAMPLES = 1310720
MOST = 2048
VROWS = 20
IN_ROWS = 3
HEAD_ROWS = 3
PR = 4380
NB = 137
SLOTS = 27
SLOTS_ALL = 216


def owner_table(key):
    base_key = jax.random.fold_in(key, 101)
    first_key, second_key, third_key = jax.random.split(base_key, 3)
    owner_count = SLOTS_ALL // SLOTS
    chosen = jax.random.randint(first_key, (), 0, owner_count)
    tokens = jnp.arange(SLOTS_ALL, dtype=jnp.int32) // SLOTS
    shuffled = tokens[jax.random.permutation(second_key, SLOTS_ALL)]
    ranked = jnp.argsort((shuffled != chosen).astype(jnp.int32), stable=True)
    picked = shuffled[ranked][:NB]
    return picked[jax.random.permutation(third_key, NB)].astype(jnp.int32)


def slot_grid(key):
    owner_list = owner_table(key)
    bucket_index = jnp.arange(NB, dtype=jnp.int32)
    same_owner = owner_list[None, :] == owner_list[:, None]
    before = bucket_index[None, :] < bucket_index[:, None]
    slot_rank = jnp.sum((same_owner & before).astype(jnp.int32), axis=1)
    bucket_place = owner_list * SLOTS + slot_rank
    targets = jnp.arange(SLOTS_ALL, dtype=jnp.int32)
    slot_match = bucket_place[None, :] == targets[:, None]
    found_bucket = jnp.sum(slot_match.astype(jnp.int32) * bucket_index[None, :], axis=1)
    source = jnp.where(jnp.any(slot_match, axis=1), found_bucket, NB)
    table_rows = source[:, None, None] * BR + jnp.arange(BR, dtype=jnp.int32)[None, :, None]
    columns = jnp.arange(D, dtype=jnp.int32)[None, None, :]
    return (table_rows + 0 * columns, columns + 0 * table_rows)


def grad_level(table_rows):
    level = jnp.where(table_rows < FF, 0.12, 0.2)
    level = jnp.where(table_rows >= 2 * FF, 0.5, level)
    level = jnp.where(table_rows >= 2 * FF + NOUT, 0.25, level)
    level = jnp.where(table_rows >= 2 * FF + NOUT + VROWS, 0.12, level)
    level = jnp.where(table_rows >= 2 * FF + NOUT + VROWS + IN_ROWS, 0.5, level)
    level = jnp.where(table_rows >= PR, 0.1, level)
    return level.astype(jnp.float32) * math.sqrt(ROWS * FRAMES)


def signed_noise(noise_key, shape):
    return jnp.clip(jax.random.normal(noise_key, shape, jnp.float32), -4.0, 4.0)


def draw_owner_list(key, part):
    return owner_table(key)


def draw_master(key, part):
    table_rows, columns = slot_grid(key)
    noise_key, spread_key = jax.random.split(jax.random.fold_in(key, 202))
    noise = signed_noise(noise_key, table_rows.shape)
    spread = jax.random.uniform(spread_key, table_rows.shape, jnp.float32, 0.0, 1.0)
    gain_like = 0.5 + spread
    values = noise * D ** (-0.5)
    values = jnp.where(table_rows >= FF, noise * FF ** (-0.5), values)
    values = jnp.where(table_rows >= 2 * FF, noise * 0.5 * D ** (-0.5), values)
    vec_row = table_rows - (2 * FF + NOUT)
    vec_value = noise * 0.4
    vec_value = jnp.where(vec_row == KW, noise * 0.3, vec_value)
    vec_value = jnp.where((vec_row > KW) & (vec_row <= KW + NBW), gain_like, vec_value)
    vec_value = jnp.where((vec_row > KW + NBW) & (vec_row <= KW + 2 * NBW), noise * 0.3, vec_value)
    vec_value = jnp.where(vec_row == KW + 2 * NBW + 1, noise * 0.2, vec_value)
    vec_value = jnp.where(vec_row == KW + 2 * NBW + 2, gain_like, vec_value)
    vec_value = jnp.where(vec_row == KW + 2 * NBW + 3, gain_like, vec_value)
    vec_value = jnp.where(vec_row == KW + 2 * NBW + 4, noise * 0.3, vec_value)
    values = jnp.where(table_rows >= 2 * FF + NOUT, vec_value, values)
    bias_start = 2 * FF + NOUT + VROWS
    values = jnp.where(table_rows >= bias_start, noise * 0.3, values)
    head_start = bias_start + IN_ROWS
    head_entry = (table_rows - head_start) * D + columns
    head_value = jnp.where(head_entry < BINS, 2.5 + spread, math.pi * (2.0 * spread - 1.0))
    values = jnp.where(table_rows >= head_start, head_value, values)
    values = jnp.where(table_rows >= PR, noise * 0.1, values)
    return values.astype(jnp.float32)


def draw_moment1(key, part):
    table_rows, columns = slot_grid(key)
    noise = signed_noise(jax.random.fold_in(key, 303), table_rows.shape)
    return (noise * 0.25 * grad_level(table_rows)).astype(jnp.float32)


def draw_moment2(key, part):
    table_rows, columns = slot_grid(key)
    first_key, second_key = jax.random.split(jax.random.fold_in(key, 404))
    factor_one = jax.random.uniform(first_key, table_rows.shape, jnp.float32, 1.0, 4.0)
    factor_two = jnp.exp(jax.random.uniform(second_key, table_rows.shape, jnp.float32, -0.6931472, 0.6931472))
    level = grad_level(table_rows)
    return (0.111 * level * level * factor_one * factor_two).astype(jnp.float32)


def touch_ends(entries, own_key, smallest, top_value):
    shape = entries.shape
    index_at = [jax.random.randint(jax.random.fold_in(own_key, axis), (), 0, shape[axis]) for axis in range(len(shape))]
    entries = entries.at[tuple(index_at)].set(smallest)
    longest = shape.index(max(shape))
    index_at[longest] = (index_at[longest] + 1) % shape[longest]
    return entries.at[tuple(index_at)].set(top_value)


def levels(key, dims, cuts, least, top_value):
    def one(axis_at, shards_of):
        draws = jax.random.uniform(jax.random.fold_in(jax.random.fold_in(key, 6), axis_at), (shards_of,), jnp.float32, least / len(cuts), top_value / len(cuts))
        return jnp.repeat(jnp.exp(draws), dims[axis_at] // shards_of).reshape((-1,) + (1,) * (len(dims) - axis_at - 1))

    level = one(*cuts[0])
    for cut in cuts[1:]:
        level = level * one(*cut)
    return level


def profile(number_of, total, bound, skew):
    weights = [(1 << 20) // math.isqrt(grade ** skew) + 1 for grade in range(2, number_of + 1)]
    rest, given = total - bound - (number_of - 1), [1] * (number_of - 1)
    while rest > 0:
        movable = [i for i in range(number_of - 1) if given[i] < bound]
        whole, remaining = sum([weights[i] for i in movable]), rest
        for i in movable:
            addition = min(bound - given[i], max(1, remaining * weights[i] // whole), rest)
            given[i] = given[i] + addition
            rest = rest - addition
    return np.array([bound] + given)


def ragged(key, number_of, total, limit, slope):
    if number_of == 2:
        one = jax.random.randint(key, (), max(1, total - limit), min(limit, total - 1) + 1)
        return jnp.stack([one, total - one])
    sizes = jnp.asarray(profile(number_of, total, limit, slope), jnp.int32)
    pairs = (number_of - 1) // 2
    source_of, sink = sizes[1:1 + 2 * pairs:2], sizes[2:2 + 2 * pairs:2]
    slack = jnp.minimum(source_of - 1, limit - sink)
    shifted = jax.random.randint(jax.random.fold_in(key, 1), (pairs,), 0, 1 << 20) % (slack + 1)
    sizes = sizes.at[1:1 + 2 * pairs:2].set(source_of - shifted).at[2:2 + 2 * pairs:2].set(sink + shifted)
    return sizes[jax.random.permutation(jax.random.fold_in(key, 2), number_of)]


def bell_draw(key, shape, scale, most, shards=(), kind=jnp.bfloat16):
    factor_of = levels(key, shape, shards, -0.22, 0.18) if shards else 1.0
    drawn = jax.random.normal(key, shape, jnp.float32) * scale * factor_of
    return jnp.minimum(jnp.maximum(drawn, -most), most).astype(kind)


def setup_inputs(seed: int = 0) -> dict:
    streams_of = jax.random.split(jax.random.key(seed), 9)
    frames_in = bell_draw(streams_of[0], (ROWS, FRAMES, D), 1.0, 6.0, ((0, 8), (1, 4)))
    lengths = jax.vmap(lambda own: ragged(own, UTT, FRAMES, MOST, 2))(jax.random.split(streams_of[1], ROWS)).reshape((ROWS, UTT)).astype(jnp.int32)
    bw_ids = touch_ends(jax.random.randint(streams_of[2], (ROWS, UTT), 0, NBW), jax.random.fold_in(streams_of[2], 1), 0, NBW - 1).astype(jnp.int32)
    owner_list = draw_owner_list(jax.random.fold_in(streams_of[8], 71), 0)
    master = draw_master(jax.random.fold_in(streams_of[8], 71), 0)
    moment1 = draw_moment1(jax.random.fold_in(streams_of[8], 71), 0)
    moment2 = draw_moment2(jax.random.fold_in(streams_of[8], 71), 0)
    wave_grad = bell_draw(streams_of[7], (ROWS, SAMPLES), 1.0, 6.0, ((0, 8), (1, 4)))
    return {"frames_in": frames_in, "lengths": lengths, "bw_ids": bw_ids, "owner_list": owner_list, "master": master, "moment1": moment1, "moment2": moment2, "wave_grad": wave_grad}


@jax.custom_vjp
def low(v):
    return lax.optimization_barrier(v.astype(jnp.bfloat16)).astype(jnp.float32)

@jax.custom_vjp
def low_back(v):
    return v

def low_keep(v):
    return (low(v), None)

def low_pass(kept, grad):
    return (grad,)

def back_keep(v):
    return (v, None)

def back_low(kept, grad):
    return (low(grad),)
low.defvjp(low_keep, low_pass)
low_back.defvjp(back_keep, back_low)
NORM_EPS = 1e-06
ENV_FLOOR = 0.5
BETA_ONE = 0.8
BETA_TWO = 0.9
LEARN_RATE = 0.04
WEIGHT_DECAY = 0.01
ADAM_EPS = 1e-08

def slot_source(owner_list):
    bucket_count = owner_list.shape[0]
    bucket_index = jnp.arange(bucket_count, dtype=jnp.int32)
    same_owner = owner_list[None, :] == owner_list[:, None]
    before = bucket_index[None, :] < bucket_index[:, None]
    slot_rank = lax.optimization_barrier(jnp.sum((same_owner & before).astype(jnp.int32), axis=1))
    bucket_place = (owner_list * SLOTS + slot_rank).astype(jnp.int32)
    targets = jnp.arange(SLOTS_ALL, dtype=jnp.int32)
    slot_match = bucket_place[None, :] == targets[:, None]
    found_bucket = lax.optimization_barrier(jnp.sum(slot_match.astype(jnp.int32) * bucket_index[None, :], axis=1))
    source = jnp.where(jnp.any(slot_match, axis=1), found_bucket, bucket_count).astype(jnp.int32)
    return (bucket_place, source)

def synthesis_table():
    bin_index = jnp.arange(BINS, dtype=jnp.int32)[:, None]
    tap_index = jnp.arange(NFFT, dtype=jnp.int32)[None, :]
    turns = bin_index * tap_index % NFFT
    angle = turns.astype(jnp.float32) * (2.0 * math.pi / NFFT)
    edge_bin = (bin_index == 0) | (bin_index == NFFT // 2)
    factor = jnp.where(edge_bin, 1.0, 2.0).astype(jnp.float32) / NFFT
    return jnp.concatenate([factor * jnp.cos(angle), -factor * jnp.sin(angle)], axis=0)

def hann_window():
    angle = jnp.arange(NFFT, dtype=jnp.int32).astype(jnp.float32) * (2.0 * math.pi / NFFT)
    return 0.5 - 0.5 * jnp.cos(angle)

def segment_of(lengths_row, frame_index):
    starts = jnp.cumsum(lengths_row) - lengths_row
    return lax.optimization_barrier(jnp.sum((starts[None, :] <= frame_index[:, None]).astype(jnp.int32), axis=1)) - 1

def layer_norm(values):
    row_mean = lax.optimization_barrier(jnp.mean(values, axis=-1, keepdims=True))
    centered = values - row_mean
    return centered * lax.rsqrt(lax.optimization_barrier(jnp.mean(centered * centered, axis=-1, keepdims=True)) + NORM_EPS)

def unpack(weight_table):
    w_in = weight_table[:FF]
    w_out = weight_table[FF:2 * FF]
    w_head = weight_table[2 * FF:2 * FF + NOUT]
    row_start = 2 * FF + NOUT
    channel_rows = weight_table[row_start:row_start + VROWS]
    row_start = row_start + VROWS
    bias_in = weight_table[row_start:row_start + IN_ROWS].reshape(-1)[:FF]
    row_start = row_start + IN_ROWS
    bias_head = weight_table[row_start:row_start + HEAD_ROWS].reshape(-1)[:NOUT]
    return (w_in, w_out, w_head, channel_rows, bias_in, bias_head)

def row_forward(weight_table, frames, lengths_row, ids_row, synthesis, window):
    w_in, w_out, w_head, channel_rows, bias_in, bias_head = unpack(weight_table)
    conv_weight = channel_rows[:KW]
    conv_bias = channel_rows[KW]
    ada_scale = channel_rows[KW + 1:KW + 1 + NBW]
    ada_shift = channel_rows[KW + 1 + NBW:KW + 1 + 2 * NBW]
    vec_base = KW + 1 + 2 * NBW
    bias_out = channel_rows[vec_base]
    layer_scale = channel_rows[vec_base + 1]
    norm_gain = channel_rows[vec_base + 2]
    norm_bias = channel_rows[vec_base + 3]
    rim_width = (KW - 1) // 2
    frame_index = jnp.arange(FRAMES + 2 * rim_width, dtype=jnp.int32) - rim_width
    inside = (frame_index >= 0) & (frame_index < FRAMES)
    segment = jnp.where(inside, segment_of(lengths_row, frame_index), -1)
    own_segment = segment[rim_width:rim_width + FRAMES]
    padded = jnp.pad(frames, ((rim_width, rim_width), (0, 0)))
    conv_out = jnp.zeros((FRAMES, D), jnp.float32) + conv_bias[None, :]
    for tap_index in range(KW):
        keep = (segment[tap_index:tap_index + FRAMES] == own_segment).astype(jnp.float32)
        conv_out = conv_out + keep[:, None] * padded[tap_index:tap_index + FRAMES] * conv_weight[tap_index][None, :]
    utt_pick = (own_segment[:, None] == jnp.arange(UTT, dtype=jnp.int32)[None, :]).astype(jnp.int32)
    frame_ids = lax.optimization_barrier(jnp.sum(utt_pick * ids_row[None, :], axis=1))
    bw_onehot = (frame_ids[:, None] == jnp.arange(NBW, dtype=jnp.int32)[None, :]).astype(jnp.float32)
    scale_rows = jnp.dot(bw_onehot, ada_scale, precision=lax.Precision.HIGHEST)
    shift_rows = jnp.dot(bw_onehot, ada_shift, precision=lax.Precision.HIGHEST)
    ada_out = low(layer_norm(conv_out) * scale_rows + shift_rows)
    hidden_pre = low_back(jnp.dot(ada_out, w_in.T, precision=lax.Precision.HIGHEST) + bias_in[None, :])
    activated = low(jax.nn.gelu(hidden_pre, approximate=False))
    branch = low_back(jnp.dot(activated, w_out, precision=lax.Precision.HIGHEST) + bias_out[None, :])
    residual = frames + layer_scale[None, :] * branch
    normed = low(layer_norm(residual) * norm_gain[None, :] + norm_bias[None, :])
    head_out = low_back(jnp.dot(normed, w_head.T, precision=lax.Precision.HIGHEST) + bias_head[None, :])
    magnitude = jnp.exp(head_out[:, :BINS])
    phase_angle = head_out[:, BINS:]
    spectrum = low(jnp.concatenate([magnitude * jnp.cos(phase_angle), magnitude * jnp.sin(phase_angle)], axis=1))
    signal = low_back(jnp.dot(spectrum, synthesis, precision=lax.Precision.HIGHEST))
    window_rows = window.reshape(LAPS, HOP)
    pieces = signal.reshape(FRAMES, LAPS, HOP) * window_rows[None, :, :]
    block_index = jnp.arange(FRAMES, dtype=jnp.int32)
    numerator = jnp.zeros((FRAMES, HOP), jnp.float32)
    envelope = jnp.zeros((FRAMES, HOP), jnp.float32)
    for lap_index in range(LAPS):
        source_segment = segment_of(lengths_row, block_index - lap_index)
        keep = (source_segment == own_segment).astype(jnp.float32)[:, None]
        moved = jnp.pad(pieces[:, lap_index], ((lap_index, 0), (0, 0)))[:FRAMES]
        numerator = numerator + keep * moved
        envelope = envelope + keep * (window_rows[lap_index] ** 2)[None, :]
    return (numerator / jnp.maximum(envelope, ENV_FLOOR)).reshape(-1)

def reference(frames_in, lengths, bw_ids, owner_list, master, moment1, moment2, wave_grad):
    bucket_place, source = slot_source(owner_list)
    buckets = jnp.take(master, bucket_place, axis=0)
    weight_table = low(buckets.reshape(NB * BR, D)[:PR])
    synthesis = low(synthesis_table())
    window = hann_window()

    def row_step(grand_total, row_items):
        frames, lengths_row, ids_row, cotangent = row_items

        def forward_only(table_value, frame_value):
            return row_forward(table_value, frame_value, lengths_row, ids_row, synthesis, window)
        wave_row, pullback = jax.vjp(forward_only, weight_table, frames.astype(jnp.float32))
        table_grad, frame_grad = pullback(cotangent.astype(jnp.float32))
        return (grand_total + table_grad, (wave_row, frame_grad))
    grand_total, (waveform, input_grad) = lax.scan(row_step, jnp.zeros((PR, D), jnp.float32), (frames_in, lengths, bw_ids, wave_grad))
    grad_full = jnp.concatenate([grand_total, jnp.zeros((NB * BR - PR, D), jnp.float32)], axis=0).reshape(NB, BR, D)
    grad_extended = jnp.concatenate([grad_full, jnp.zeros((1, BR, D), jnp.float32)], axis=0)
    reduced = jnp.take(grad_extended, source, axis=0)
    first_new = BETA_ONE * moment1 + (1.0 - BETA_ONE) * reduced
    second_new = BETA_TWO * moment2 + (1.0 - BETA_TWO) * reduced * reduced
    first_fix = 1.0 - BETA_ONE ** STEP_COUNT
    second_fix = 1.0 - BETA_TWO ** STEP_COUNT
    master_new = master - LEARN_RATE * (first_new / first_fix / (jnp.sqrt(second_new / second_fix) + ADAM_EPS) + WEIGHT_DECAY * master)
    return (waveform, input_grad, master_new, first_new, second_new)
```

```python
import functools
import math

import jax
import jax.numpy as jnp
import numpy as np
from jax import lax
from jax.experimental import pallas as pl
from jax.experimental.pallas import tpu as pltpu
from jax.sharding import PartitionSpec as P

FF = 1536
NFFT = 1280
HOP = 320
NBW = 4
KW = 7
UTT = 4
BR = 32
STEP_COUNT = 6
BINS = 641
NOUT = 1282
VROWS = 20
IN_ROWS = 3
HEAD_ROWS = 3
NB = 137

NORM_EPS = 1e-06
ENV_FLOOR = 0.5
BETA_ONE = 0.8
BETA_TWO = 0.9
LEARN_RATE = 0.04
WEIGHT_DECAY = 0.01
ADAM_EPS = 1e-08

LAPS = NFFT // HOP
RIM = (KW - 1) // 2
LAP_PAD = 384
BIN_PAD = 768
HALF = BR // 2
QUART = BR // 4
EDGE = 8
TILE = 256
CHUNK = 512
AXES = ("rows", "seq")

F32 = jnp.float32
BF16 = jnp.bfloat16
MIB = 1 << 20


def synthesis_table():
    k = np.arange(BINS)[:, None]
    n = np.arange(NFFT)[None, :]
    angle = (k * n % NFFT) * (2.0 * math.pi / NFFT)
    factor = np.where((k == 0) | (k == NFFT // 2), 1.0, 2.0) / NFFT
    out = np.zeros((2, BIN_PAD, LAPS, LAP_PAD), np.float32)
    out[0, :BINS, :, :HOP] = (factor * np.cos(angle)).reshape(BINS, LAPS, HOP)
    out[1, :BINS, :, :HOP] = (-factor * np.sin(angle)).reshape(BINS, LAPS, HOP)
    return out.reshape(2 * BIN_PAD, LAPS * LAP_PAD).astype(jnp.bfloat16)


def window_tables():
    window = 0.5 - 0.5 * np.cos(np.arange(NFFT) * (2.0 * math.pi / NFFT))
    rows = np.zeros((LAPS, LAP_PAD), np.float64)
    rows[:, :HOP] = window.reshape(LAPS, HOP)
    envelope = np.cumsum(rows**2, axis=0)
    return np.concatenate([rows, 1.0 / np.maximum(envelope, ENV_FLOOR)], axis=0).astype(np.float32)


def ring_of(count):
    if count != 8:
        return None
    return [0, 2, 4, 6, 7, 5, 3, 1]


def ring_step(ring, shift, seq_count):
    where = {r: i for i, r in enumerate(ring)}
    pairs = []
    for r in ring:
        target = ring[(where[r] + shift) % len(ring)]
        pairs += [(r * seq_count + s, target * seq_count + s) for s in range(seq_count)]
    return pairs


def seq_swap(value, bit):
    count = lax.axis_size("seq")
    return lax.ppermute(value, "seq", [(s, s ^ bit) for s in range(count)])


def rows_swap(value, bit):
    count = lax.axis_size("rows")
    return lax.ppermute(value, "rows", [(r, r ^ bit) for r in range(count)])


def shifted(value, distance):
    devices = range(lax.axis_size("seq"))
    return lax.ppermute(
        value, "seq", [(i - distance, i) for i in devices if i - distance in devices]
    )


def dot(a, b, dims):
    return lax.dot_general(a, b, (dims, ((), ())), preferred_element_type=F32)


NN = ((1,), (0,))
NT = ((1,), (1,))
TN = ((0,), (0,))


def frame_reach(meta, row, first, count, utts):
    index = first + lax.broadcasted_iota(jnp.int32, (count, 128), 0)
    start = jnp.zeros_like(index)
    end = jnp.zeros_like(index) + meta[row, 1]
    for u in range(1, utts):
        inside = index >= meta[row, u]
        start = jnp.where(inside, meta[row, u], start)
        end = jnp.where(inside, meta[row, u + 1], end)
    return index - start, end - 1 - index


def lanes(mask, count):
    return jnp.concatenate([mask] * count, axis=1)


def by_reach(reach, table, base, count):
    picked = jnp.broadcast_to(table[base + LAPS - 1 : base + LAPS], (reach.shape[0], LAP_PAD))
    for j in range(LAPS - 2, -1, -1):
        picked = jnp.where(lanes(reach == j, LAP_PAD // 128), table[base + j : base + j + 1], picked)
    return picked


def fold(values):
    rows, columns = values.shape
    return jnp.sum(values.reshape(rows // 8, 8, columns), axis=0)


def sincos(angle):
    turns = jnp.round(angle * (1.0 / math.pi))
    rest = angle - turns * 3.140625
    rest = rest - turns * 9.670257568359375e-4
    rest = rest - turns * 6.2771141529083251953e-7
    rest = rest - turns * 1.2154201256553420e-10
    half = turns * 0.5
    sign = 1.0 - 4.0 * (half - jnp.floor(half))
    sq = rest * rest
    sine = rest + rest * sq * (
        -1.6666667163e-01
        + sq * (8.3333337680e-03 + sq * (-1.9841270114e-04 + sq * (2.7557314297e-06 - sq * 2.5050759689e-08)))
    )
    cosine = 1.0 + sq * (
        -0.5
        + sq
        * (
            4.1666667908e-02
            + sq
            * (-1.3888889225e-03 + sq * (2.4801587642e-05 + sq * (-2.7557314297e-07 + sq * 2.0875723372e-09)))
        )
    )
    return sine * sign, cosine * sign


ANGLE_LIMIT = 8192.0


def pre_body(meta, wave_ref, synth_ref, win_ref, out_ref, scaled, *, tiles, utts):
    step = pl.program_id(0)
    row, first = step // tiles, (step % tiles) * TILE
    base = meta[row, 2 * utts + 1] + first
    reach, left = frame_reach(meta, row, base, TILE + EDGE, utts)
    wave = wave_ref[row, pl.ds(pl.multiple_of(first, TILE), TILE + 2 * EDGE), :].astype(F32)
    scaled[...] = wave[: TILE + EDGE] * by_reach(reach, win_ref, LAPS, LAP_PAD)
    parts = []
    for j in range(LAPS):
        part = scaled[j : j + TILE, :] * win_ref[j : j + 1, :]
        if j:
            part = jnp.where(lanes(left[:TILE] >= j, LAP_PAD // 128), part, 0.0)
        parts.append(part.astype(BF16))
    signal = jnp.concatenate(parts, axis=1)
    for c in range(0, 2 * BIN_PAD, 512):
        out_ref[:, c : c + 512] = dot(signal, synth_ref[c : c + 512, :], NT).astype(BF16)


def spectrum_cotangent(meta, wave, synth, win, rows, frames, utts):
    tiles = frames // TILE
    count = rows * frames
    return pl.pallas_call(
        functools.partial(pre_body, tiles=tiles, utts=utts),
        grid=(rows * tiles,),
        in_specs=[
            pl.BlockSpec(memory_space=pltpu.SMEM),
            pl.BlockSpec(memory_space=pltpu.VMEM),
            pl.BlockSpec(memory_space=pltpu.VMEM),
            pl.BlockSpec(memory_space=pltpu.VMEM),
        ],
        out_specs=pl.BlockSpec((TILE, 2 * BIN_PAD), lambda i: (i, 0)),
        out_shape=jax.ShapeDtypeStruct((count, 2 * BIN_PAD), BF16),
        scratch_shapes=[pltpu.VMEM((TILE + EDGE, LAP_PAD), F32)],
        compiler_params=pltpu.CompilerParams(vmem_limit_bytes=40 * MIB),
        cost_estimate=pl.CostEstimate(
            flops=2 * count * 1536 * 1536, bytes_accessed=count * 1536 * 2 + 8 * MIB, transcendentals=0
        ),
        name="spectrum_cotangent",
    )(meta, wave, synth, win)


def forward_body(
    meta,
    places,
    x_ref,
    cot_ref,
    *rest,
    parts,
    tiles,
    utts,
):
    sources = rest[:parts]
    (
        table,
        spec_ref,
        act_ref,
        der_ref,
        ada_ref,
        low_ref,
        resg_ref,
        xc_ref,
        rc_ref,
        send_ref,
        keep_ref,
        tail_ref,
        sums_ref,
        bsum_ref,
        xs,
        w_head,
        b_head,
        grad,
        hg,
        sem,
    ) = rest[parts:]
    step = pl.program_id(0)
    steps = pl.num_programs(0)
    core = meta[0, 2 * utts + 2]
    channels = x_ref.shape[2]

    @pl.when(step == 0)
    def _():
        def go(start):
            base = 0
            for index, ref in enumerate(sources):
                slots = ref.shape[0]
                side = core if index % 2 == 0 else 1 - core

                def one(s, carry, ref=ref, base=base, side=side):
                    bucket = places[0, base + s]

                    @pl.when(bucket < NB)
                    def _():
                        at = pl.multiple_of(bucket * BR + side * HALF, HALF)
                        copy = pltpu.make_async_copy(ref.at[s], table.at[pl.ds(at, HALF), :], sem)
                        if start:
                            copy.start()
                        else:
                            copy.wait()

                    return carry

                lax.fori_loop(0, slots, one, 0)
                if index % 2 == 1:
                    base = base + slots

        go(True)
        grad[...] = jnp.zeros_like(grad)
        sums_ref[...] = jnp.zeros_like(sums_ref)
        bsum_ref[...] = jnp.zeros_like(bsum_ref)
        go(False)
        head_at = 2 * FF
        w_head[0:640, :] = table[head_at : head_at + 640, :]
        edge = table[head_at + 640 : head_at + 640 + 656, :].astype(F32)
        inside = lax.broadcasted_iota(jnp.int32, (128, channels), 0)
        w_head[640:768, :] = jnp.where(inside < 1, edge[0:128], 0.0).astype(BF16)
        w_head[768:1408, :] = edge[1:641].astype(BF16)
        w_head[1408:1536, :] = jnp.where(inside < 1, edge[641:642], 0.0).astype(BF16)
        last = table[2 * FF + 1280 : 2 * FF + 1280 + BR, :].astype(F32)
        wide = jnp.concatenate([last[25:26], last[26:27], last[27:28]], axis=1)
        wide = jnp.broadcast_to(wide, (8, 3 * channels))
        column = lax.broadcasted_iota(jnp.int32, (8, BIN_PAD), 1)
        b_head[:, 0:BIN_PAD] = jnp.where(column < BINS, wide[:, 0:BIN_PAD], 0.0)
        moved = pltpu.roll(wide, 3 * channels - BINS, 1)
        b_head[:, BIN_PAD:] = jnp.where(column < BINS, moved[:, 0:BIN_PAD], 0.0)

    row, first = step // tiles, (step % tiles) * TILE
    base = meta[row, 2 * utts + 1] + first
    reach, left = frame_reach(meta, row, base, TILE, utts)
    last = table[2 * FF + 1280 : 2 * FF + 1280 + BR, :].astype(F32)
    vec = lambda v: last[2 + v : 3 + v]
    xs[...] = x_ref[row, pl.ds(pl.multiple_of(first, TILE), TILE + 2 * EDGE), :].astype(F32)
    conv = jnp.zeros((TILE, channels), F32) + vec(KW)
    for k in range(KW):
        offset = k - RIM
        moved = xs[EDGE + offset : EDGE + offset + TILE, :]
        if offset < 0:
            moved = jnp.where(lanes(reach >= -offset, channels // 128), moved, 0.0)
        elif offset > 0:
            moved = jnp.where(lanes(left >= offset, channels // 128), moved, 0.0)
        conv = conv + moved * vec(k)
    mean = jnp.mean(conv, axis=1, keepdims=True)
    conv = conv - mean
    rc = lax.rsqrt(jnp.mean(conv * conv, axis=1, keepdims=True) + NORM_EPS)
    xc = conv * rc
    xc_ref[...] = xc
    rc_ref[...] = jnp.broadcast_to(rc, (TILE, 128))
    index = base + lax.broadcasted_iota(jnp.int32, (TILE, 128), 0)

    def pick(offset):
        def of(u):
            wanted = meta[row, utts + 1 + u]
            value = vec(offset)
            for b in range(1, NBW):
                value = jnp.where(wanted == b, vec(offset + b), value)
            return value

        value = jnp.broadcast_to(of(0), (TILE, channels))
        for u in range(1, utts):
            value = jnp.where(lanes(index >= meta[row, u], channels // 128), of(u), value)
        return value

    ada = (xc * pick(KW + 1) + pick(KW + 1 + NBW)).astype(BF16)
    ada_ref[...] = ada
    for c in range(IN_ROWS):
        span = slice(c * CHUNK, (c + 1) * CHUNK)
        pre = dot(ada, table[span, :], NT) + last[2 + VROWS + c : 3 + VROWS + c]
        phi = 0.5 + 0.5 * lax.erf(pre * math.sqrt(0.5))
        act_ref[:, span] = (pre * phi).astype(BF16)
        bell = jnp.exp(-0.5 * pre * pre) * (1.0 / math.sqrt(2.0 * math.pi))
        der_ref[:, span] = (phi + pre * bell).astype(BF16)
    vec_at = KW + 1 + 2 * NBW
    branch = dot(act_ref[...], table[FF : 2 * FF, :], NN) + vec(vec_at)
    residual = xs[EDGE : EDGE + TILE, :] + vec(vec_at + 1) * branch
    residual = residual - jnp.mean(residual, axis=1, keepdims=True)
    rn = lax.rsqrt(jnp.mean(residual * residual, axis=1, keepdims=True) + NORM_EPS)
    xn = residual * rn
    normed = (xn * vec(vec_at + 2) + vec(vec_at + 3)).astype(BF16)
    def head(c, turn):
        logs = dot(normed, w_head[c : c + 256, :], NT) + b_head[0:1, c : c + 256]
        angle = (
            dot(normed, w_head[BIN_PAD + c : BIN_PAD + c + 256, :], NT)
            + b_head[0:1, BIN_PAD + c : BIN_PAD + c + 256]
        )
        size = jnp.exp(logs)
        sine, cosine = turn(angle)
        real, imag = size * cosine, size * sine
        spec_ref[:, c : c + 256] = real.astype(BF16)
        spec_ref[:, BIN_PAD + c : BIN_PAD + c + 256] = imag.astype(BF16)
        dre = cot_ref[:, c : c + 256].astype(F32)
        dim = cot_ref[:, BIN_PAD + c : BIN_PAD + c + 256].astype(F32)
        hg[:, c : c + 256] = (dre * real + dim * imag).astype(BF16)
        hg[:, BIN_PAD + c : BIN_PAD + c + 256] = (dim * real - dre * imag).astype(BF16)
        return jnp.max(jnp.abs(angle).reshape(TILE // 8, 8, 256), axis=0)

    widest = head(0, sincos)
    for c in range(256, BIN_PAD, 256):
        widest = jnp.maximum(widest, head(c, sincos))

    @pl.when(jnp.max(widest) > ANGLE_LIMIT)
    def _():
        for c in range(0, BIN_PAD, 256):
            head(c, lambda angle: (jnp.sin(angle), jnp.cos(angle)))

    bsum_ref[...] += fold(hg[...].astype(F32))
    grad[...] += dot(hg[...], normed, TN)
    ngrad = dot(hg[...], w_head[...], NN)
    e = ngrad * vec(vec_at + 2)
    resg = rn * (
        e - jnp.mean(e, axis=1, keepdims=True) - xn * jnp.mean(e * xn, axis=1, keepdims=True)
    )
    resg_ref[...] = resg
    low = (vec(vec_at + 1) * resg).astype(BF16)
    low_ref[...] = low
    sums_ref[0] += fold(low.astype(F32))
    sums_ref[1] += fold(resg * branch)
    sums_ref[2] += fold(ngrad * xn)
    sums_ref[3] += fold(ngrad)

    @pl.when(step == steps - 1)
    def _():
        grad[767:768, :] = grad[640:641, :]
        for b in range(40):
            at = b * BR if b < 20 else b * BR + 127
            low_half = grad[at : at + HALF, :].astype(BF16)
            high_half = grad[at + HALF : at + BR, :].astype(BF16)
            keep_ref[b] = jnp.where(core == 0, low_half, high_half)
            send_ref[b] = jnp.where(core == 0, high_half, low_half)
        tail_ref[...] = grad[1407:1415, :]


def forward(meta, places, xpad, cot, sources, rows, frames, utts):
    tiles = frames // TILE
    count = rows * frames
    channels = xpad.shape[2]
    wide = pl.BlockSpec((TILE, FF), lambda i: (i, 0))
    slim = pl.BlockSpec((TILE, channels), lambda i: (i, 0))
    whole = pl.BlockSpec(memory_space=pltpu.VMEM)
    smem = pl.BlockSpec(memory_space=pltpu.SMEM)
    shape = jax.ShapeDtypeStruct
    return pl.pallas_call(
        functools.partial(forward_body, parts=len(sources), tiles=tiles, utts=utts),
        grid=(rows * tiles,),
        in_specs=[smem, smem, whole, wide] + [pl.BlockSpec(memory_space=pl.ANY)] * len(sources),
        out_specs=[whole, wide, wide, wide, slim, slim, slim, slim]
        + [pl.BlockSpec((TILE, 128), lambda i: (i, 0))]
        + [whole] * 5,
        out_shape=[
            shape((NB * BR, channels), BF16),
            shape((count, FF), BF16),
            shape((count, FF), BF16),
            shape((count, FF), BF16),
            shape((count, channels), BF16),
            shape((count, channels), BF16),
            shape((count, channels), F32),
            shape((count, channels), F32),
            shape((count, 128), F32),
            shape((40, HALF, channels), BF16),
            shape((40, HALF, channels), BF16),
            shape((8, channels), F32),
            shape((4, 8, channels), F32),
            shape((8, 2 * BIN_PAD), F32),
        ],
        scratch_shapes=[
            pltpu.VMEM((TILE + 2 * EDGE, channels), F32),
            pltpu.VMEM((2 * BIN_PAD, channels), BF16),
            pltpu.VMEM((8, 2 * BIN_PAD), F32),
            pltpu.VMEM((2 * BIN_PAD, channels), F32),
            pltpu.VMEM((TILE, 2 * BIN_PAD), BF16),
            pltpu.SemaphoreType.DMA,
        ],
        compiler_params=pltpu.CompilerParams(vmem_limit_bytes=56 * MIB),
        cost_estimate=pl.CostEstimate(
            flops=10 * count * 1536 * 512, bytes_accessed=40 * MIB, transcendentals=count * 4096
        ),
        name="forward",
    )(meta, places, xpad, cot, *sources)


def mlp_body(meta, low_ref, act_ref, der_ref, ada_ref, wout_ref, pre_ref, send_ref, keep_ref, bsum_ref, gout, gin, *, utts):
    step = pl.program_id(0)
    core = meta[0, 2 * utts + 2]

    @pl.when(step == 0)
    def _():
        gout[...] = jnp.zeros_like(gout)
        gin[...] = jnp.zeros_like(gin)
        bsum_ref[...] = jnp.zeros_like(bsum_ref)

    low = low_ref[...]
    agrad = dot(low, wout_ref[...], NT)
    pre = (agrad * der_ref[...].astype(F32)).astype(BF16)
    pre_ref[...] = pre
    bsum_ref[...] += fold(pre.astype(F32))
    gout[...] += dot(act_ref[...], low, TN)
    gin[...] += dot(pre, ada_ref[...], TN)

    @pl.when(step == pl.num_programs(0) - 1)
    def _():
        buckets = CHUNK // BR
        for at, ref in ((0, gin), (buckets, gout)):
            for b in range(buckets):
                low_half = ref[b * BR : b * BR + HALF, :].astype(BF16)
                high_half = ref[b * BR + HALF : b * BR + BR, :].astype(BF16)
                keep_ref[at + b] = jnp.where(core == 0, low_half, high_half)
                send_ref[at + b] = jnp.where(core == 0, high_half, low_half)


def mlp_backward(chunk, meta, low, act, der, ada, table, utts):
    count, channels = low.shape
    tile = 512
    shape = jax.ShapeDtypeStruct
    slim = pl.BlockSpec((tile, channels), lambda i: (i, 0))
    part = pl.BlockSpec((tile, CHUNK), lambda i: (i, chunk))
    buckets = 2 * CHUNK // BR
    whole = pl.BlockSpec(memory_space=pltpu.VMEM)
    return pl.pallas_call(
        functools.partial(mlp_body, utts=utts),
        grid=(count // tile,),
        in_specs=[
            pl.BlockSpec(memory_space=pltpu.SMEM),
            slim,
            part,
            part,
            slim,
            pl.BlockSpec((CHUNK, channels), lambda i: (FF // CHUNK + chunk, 0)),
        ],
        out_specs=[pl.BlockSpec((tile, CHUNK), lambda i: (i, 0)), whole, whole, whole],
        out_shape=[
            shape((count, CHUNK), BF16),
            shape((buckets, HALF, channels), BF16),
            shape((buckets, HALF, channels), BF16),
            shape((8, CHUNK), F32),
        ],
        scratch_shapes=[pltpu.VMEM((CHUNK, channels), F32), pltpu.VMEM((CHUNK, channels), F32)],
        compiler_params=pltpu.CompilerParams(vmem_limit_bytes=40 * MIB),
        cost_estimate=pl.CostEstimate(
            flops=6 * count * CHUNK * 512, bytes_accessed=12 * MIB, transcendentals=0
        ),
        name=f"mlp_backward_{chunk}",
    )(meta, low, act, der, ada, table)


def conv_body(
    meta,
    x_ref,
    pre0,
    pre1,
    pre2,
    table,
    xc_ref,
    rc_ref,
    resg_ref,
    tail_ref,
    sums_ref,
    hsum_ref,
    bsum0,
    bsum1,
    bsum2,
    out_ref,
    edge_ref,
    vec_ref,
    xs,
    cg,
    part,
    *,
    tiles,
    utts,
):
    phase = pl.program_id(0)
    step = pl.program_id(1)
    steps = pl.num_programs(1)
    row, first = step // tiles, (step % tiles) * TILE
    channels = x_ref.shape[2]
    frames = tiles * TILE
    base = meta[row, 2 * utts + 1] + first
    last = table[2 * FF + 1280 : 2 * FF + 1280 + BR, :].astype(F32)
    vec = lambda v: last[2 + v : 3 + v]
    at = pl.multiple_of(first, TILE)
    reach, left = frame_reach(meta, row, base, TILE, utts)

    @pl.when((phase == 0) & (step == 0))
    def _():
        part[...] = jnp.zeros_like(part)
        cg[...] = jnp.zeros_like(cg)

    @pl.when(phase == 0)
    def _():
        agrad = dot(pre0[...], table[0:CHUNK, :], NN)
        agrad += dot(pre1[...], table[CHUNK : 2 * CHUNK, :], NN)
        agrad += dot(pre2[...], table[2 * CHUNK : 3 * CHUNK, :], NN)
        xc = xc_ref[...]
        rc = rc_ref[:, 0:1]
        index = base + lax.broadcasted_iota(jnp.int32, (TILE, 128), 0)
        scaled = agrad * xc
        scale = None
        for u in range(utts):
            low, high = meta[row, u], meta[row, u + 1]
            wanted = meta[row, utts + 1 + u]
            value = vec(KW + 1)
            for b in range(1, NBW):
                value = jnp.where(wanted == b, vec(KW + 1 + b), value)
            if u == 0:
                scale = jnp.broadcast_to(value, (TILE, channels))
            else:
                scale = jnp.where(lanes(index >= low, channels // 128), value, scale)

            @pl.when((low < base + TILE) & (high > base))
            def _(wanted=wanted, low=low, high=high):
                inside = lanes((index >= low) & (index < high), channels // 128)
                part[KW + 1 + wanted] += fold(jnp.where(inside, scaled, 0.0))
                part[KW + 1 + NBW + wanted] += fold(jnp.where(inside, agrad, 0.0))

        ec = agrad * scale
        cgrad = rc * (
            ec - jnp.mean(ec, axis=1, keepdims=True) - xc * jnp.mean(ec * xc, axis=1, keepdims=True)
        )
        cg[row, pl.ds(pl.multiple_of(first + EDGE, EDGE), TILE), :] = cgrad
        xs[...] = x_ref[row, pl.ds(at, TILE + 2 * EDGE), :].astype(F32)
        part[KW] += fold(cgrad)
        for k in range(KW):
            offset = k - RIM
            moved = xs[EDGE + offset : EDGE + offset + TILE, :] * cgrad
            if offset < 0:
                moved = jnp.where(lanes(reach >= -offset, channels // 128), moved, 0.0)
            elif offset > 0:
                moved = jnp.where(lanes(left >= offset, channels // 128), moved, 0.0)
            part[k] += fold(moved)

    @pl.when(phase == 1)
    def _():
        xs[...] = cg[row, pl.ds(at, TILE + 2 * EDGE), :]
        total = resg_ref[...]
        for k in range(KW):
            offset = RIM - k
            moved = xs[EDGE + offset : EDGE + offset + TILE, :]
            if offset < 0:
                moved = jnp.where(lanes(reach >= -offset, channels // 128), moved, 0.0)
            elif offset > 0:
                moved = jnp.where(lanes(left >= offset, channels // 128), moved, 0.0)
            total = total + moved * vec(k)
        out_ref[0] = total

    @pl.when((phase == 1) & (step == steps - 1))
    def _():
        for r in range(cg.shape[0]):
            edge_ref[r, 0] = cg[r, EDGE : 2 * EDGE, :]
            edge_ref[r, 1] = cg[r, frames : frames + EDGE, :]
        vec_ref[0:8, :] = jnp.zeros((8, channels), F32)
        vec_ref[0:2, :] = tail_ref[0:2, :]
        for v in range(VROWS):
            rows_of = part[v] if v < KW + 1 + 2 * NBW else sums_ref[v - (KW + 1 + 2 * NBW)]
            vec_ref[2 + v : 3 + v, :] = jnp.sum(rows_of, axis=0, keepdims=True)
        for c, ref in enumerate((bsum0, bsum1, bsum2)):
            vec_ref[2 + VROWS + c : 3 + VROWS + c, :] = jnp.sum(ref[...], axis=0, keepdims=True)
        flat = jnp.broadcast_to(
            jnp.sum(hsum_ref[...], axis=0, keepdims=True), (8, 2 * BIN_PAD)
        )
        column = lax.broadcasted_iota(jnp.int32, (8, 3 * channels), 1)
        moved = pltpu.roll(flat, 2 * BIN_PAD - (BIN_PAD - BINS), 1)
        joined = jnp.where(column < BINS, flat, moved)
        joined = jnp.where(column < NOUT, joined, 0.0)
        for c in range(HEAD_ROWS):
            at_row = 2 + VROWS + IN_ROWS + c
            vec_ref[at_row : at_row + 1, :] = joined[0:1, c * channels : (c + 1) * channels]
        vec_ref[28:32, :] = jnp.zeros((4, channels), F32)


def conv_backward(meta, xpad, pres, table, xc, rc, resg, tail, sums, hsum, bsums, rows, frames, utts):
    tiles = frames // TILE
    steps = rows * tiles
    count, channels = resg.shape
    shape = jax.ShapeDtypeStruct
    whole = pl.BlockSpec(memory_space=pltpu.VMEM)
    early = lambda p, i: (jnp.where(p == 0, i, steps - 1), 0)
    late = lambda p, i: (jnp.where(p == 0, 0, i), 0)
    late_out = lambda p, i: (jnp.where(p == 0, 0, i // tiles), jnp.where(p == 0, 0, i % tiles), 0)
    return pl.pallas_call(
        functools.partial(conv_body, tiles=tiles, utts=utts),
        grid=(2, steps),
        in_specs=[pl.BlockSpec(memory_space=pltpu.SMEM), whole]
        + [pl.BlockSpec((TILE, CHUNK), early)] * 3
        + [whole, pl.BlockSpec((TILE, channels), early), pl.BlockSpec((TILE, 128), early)]
        + [pl.BlockSpec((TILE, channels), late)]
        + [whole] * 6,
        out_specs=[pl.BlockSpec((1, TILE, channels), late_out), whole, whole],
        out_shape=[
            shape((rows, frames, channels), F32),
            shape((rows, 2, EDGE, channels), F32),
            shape((BR, channels), F32),
        ],
        scratch_shapes=[
            pltpu.VMEM((TILE + 2 * EDGE, channels), F32),
            pltpu.VMEM((rows, frames + 2 * EDGE, channels), F32),
            pltpu.VMEM((KW + 1 + 2 * NBW, 8, channels), F32),
        ],
        compiler_params=pltpu.CompilerParams(vmem_limit_bytes=56 * MIB),
        cost_estimate=pl.CostEstimate(
            flops=2 * count * 1536 * 512, bytes_accessed=24 * MIB, transcendentals=0
        ),
        name="conv_backward",
    )(meta, xpad, *pres, table, xc, rc, resg, tail, sums, hsum, *bsums)


def wave_body(meta, spec_ref, synth_ref, win_ref, out_ref, over_ref, held, *, tiles, utts):
    step = pl.program_id(0)
    row, first = step // tiles, (step % tiles) * TILE
    base = meta[row, 2 * utts + 1] + first
    reach, _ = frame_reach(meta, row, base, TILE + EDGE, utts)

    @pl.when(step % tiles == 0)
    def _():
        held[:, 0:EDGE, :] = jnp.zeros((LAPS, EDGE, LAP_PAD), F32)

    for j in range(LAPS):
        span = slice(j * LAP_PAD, (j + 1) * LAP_PAD)
        piece = dot(spec_ref[...], synth_ref[:, span], NN) * win_ref[j : j + 1, :]
        held[j, EDGE : EDGE + TILE, :] = piece
        held[j, EDGE + TILE :, :] = jnp.zeros((EDGE, LAP_PAD), F32)
    total = held[0, EDGE:, :]
    for j in range(1, LAPS):
        moved = held[j, EDGE - j : EDGE - j + TILE + EDGE, :]
        total = total + jnp.where(lanes(reach >= j, LAP_PAD // 128), moved, 0.0)
    out_ref[0] = total[:TILE] * by_reach(reach[:TILE], win_ref, LAPS, LAP_PAD)
    over_ref[row] = total[TILE:]
    held[:, 0:EDGE, :] = held[:, TILE : TILE + EDGE, :]


def wave_forward(meta, spec, synth, win, rows, frames, utts):
    tiles = frames // TILE
    count = rows * frames
    shape = jax.ShapeDtypeStruct
    whole = pl.BlockSpec(memory_space=pltpu.VMEM)
    return pl.pallas_call(
        functools.partial(wave_body, tiles=tiles, utts=utts),
        grid=(rows * tiles,),
        in_specs=[
            pl.BlockSpec(memory_space=pltpu.SMEM),
            pl.BlockSpec((TILE, 2 * BIN_PAD), lambda i: (i, 0)),
            whole,
            whole,
        ],
        out_specs=[
            pl.BlockSpec((1, TILE, LAP_PAD), lambda i: (i // tiles, i % tiles, 0)),
            whole,
        ],
        out_shape=[shape((rows, frames, LAP_PAD), F32), shape((rows, EDGE, LAP_PAD), F32)],
        scratch_shapes=[pltpu.VMEM((LAPS, TILE + 2 * EDGE, LAP_PAD), F32)],
        compiler_params=pltpu.CompilerParams(vmem_limit_bytes=40 * MIB),
        cost_estimate=pl.CostEstimate(
            flops=2 * count * 1536 * 1536, bytes_accessed=16 * MIB, transcendentals=0
        ),
        name="wave_forward",
    )(meta, spec, synth, win)


def slot_body(places, *refs, bounds):
    count = len(bounds)
    outs = refs[2 * count :]
    slots = outs[0].shape[0]
    for index, out in enumerate(outs):

        def one(s, carry, out=out, index=index):
            bucket = places[0, index * slots + s]
            for (start, stop), keep, came in zip(bounds, refs[:count], refs[count : 2 * count]):

                @pl.when((bucket >= start) & (bucket < stop))
                def _(keep=keep, came=came, start=start):
                    out[s] = (keep[bucket - start].astype(F32) + came[bucket - start].astype(F32)).astype(BF16)

            @pl.when(bucket >= NB - 1)
            def _():
                out[s] = jnp.zeros(out.shape[1:], BF16)

            return carry

        lax.fori_loop(0, slots, one, 0)


def to_slots(places, keeps, cames, bounds, owners, slots):
    channels = keeps[0].shape[2]
    whole = pl.BlockSpec(memory_space=pltpu.VMEM)
    return pl.pallas_call(
        functools.partial(slot_body, bounds=bounds),
        in_specs=[pl.BlockSpec(memory_space=pltpu.SMEM)] + [whole] * (2 * len(bounds)),
        out_specs=[whole] * owners,
        out_shape=[jax.ShapeDtypeStruct((slots, QUART, channels), BF16)] * owners,
        compiler_params=pltpu.CompilerParams(vmem_limit_bytes=40 * MIB),
        cost_estimate=pl.CostEstimate(flops=0, bytes_accessed=8 * MIB, transcendentals=0),
        name="to_slots",
    )(places, *keeps, *cames)


def adam_body(places, grad_ref, last_ref, master, first, second, out_master, out_first, out_second):
    bucket = places[0, pl.program_id(0)]
    grad = grad_ref[0].astype(F32)
    grad = jnp.where(bucket == NB - 1, last_ref[...], grad)
    grad = jnp.where(bucket < NB, grad, 0.0)
    old = master[0]
    one = BETA_ONE * first[0] + (1.0 - BETA_ONE) * grad
    two = BETA_TWO * second[0] + (1.0 - BETA_TWO) * grad * grad
    one_fix = 1.0 / (1.0 - BETA_ONE**STEP_COUNT)
    two_fix = 1.0 / (1.0 - BETA_TWO**STEP_COUNT)
    out_first[0] = one
    out_second[0] = two
    out_master[0] = old - LEARN_RATE * (
        one * one_fix / (jnp.sqrt(two * two_fix) + ADAM_EPS) + WEIGHT_DECAY * old
    )


def adam(places, grad, last, master, first, second):
    slots, depth, channels = master.shape
    block = pl.BlockSpec((1, depth, channels), lambda i: (i, 0, 0))
    return pl.pallas_call(
        adam_body,
        grid=(slots,),
        in_specs=[
            pl.BlockSpec(memory_space=pltpu.SMEM),
            block,
            pl.BlockSpec(memory_space=pltpu.VMEM),
            block,
            block,
            block,
        ],
        out_specs=[block] * 3,
        out_shape=[jax.ShapeDtypeStruct(master.shape, F32)] * 3,
        compiler_params=pltpu.CompilerParams(vmem_limit_bytes=40 * MIB),
        cost_estimate=pl.CostEstimate(flops=0, bytes_accessed=12 * MIB, transcendentals=0),
        name="adam",
    )(places, grad, last, master, first, second)


def local(frames_in, lengths, bw_ids, owner_list, master, moment1, moment2, wave_grad):
    rows, frames, channels = frames_in.shape
    slots = master.shape[0]
    utts = lengths.shape[1]
    owners = lax.axis_size("rows")
    seqs = lax.axis_size("seq")
    row_at = lax.axis_index("rows")
    seq_at = lax.axis_index("seq")
    core, plane = seq_at % 2, seq_at // 2
    ring = ring_of(owners)

    bucket_index = jnp.arange(NB, dtype=jnp.int32)
    same = owner_list[None, :] == owner_list[:, None]
    rank = jnp.sum((same & (bucket_index[None, :] < bucket_index[:, None])).astype(jnp.int32), axis=1)
    place = owner_list * slots + rank

    def held_by(owner_ids):
        targets = (owner_ids[:, None] * slots + jnp.arange(slots, dtype=jnp.int32)[None, :]).reshape(-1)
        match = place[None, :] == targets[:, None]
        return (NB + jnp.sum(match.astype(jnp.int32) * (bucket_index[None, :] - NB), axis=1))[None, :]

    mine = lax.dynamic_slice_in_dim(master, core * HALF, HALF, axis=1).astype(BF16)
    if ring:
        order = jnp.asarray(ring, jnp.int32)
        where = jnp.sum(jnp.where(order == row_at, jnp.arange(owners, dtype=jnp.int32), 0))
        offsets = [0]
        pieces = [mine]
        ahead = back = mine
        for hop in range(owners // 2):
            ahead = lax.ppermute(ahead, AXES, ring_step(ring, 1, seqs))
            pieces.append(ahead)
            offsets.append(-(hop + 1))
            if hop < owners // 2 - 1:
                back = lax.ppermute(back, AXES, ring_step(ring, -1, seqs))
                pieces.append(back)
                offsets.append(hop + 1)
        at = (where + jnp.asarray(offsets, jnp.int32)) % owners
        owner_ids = jnp.sum(
            jnp.where(at[:, None] == jnp.arange(owners, dtype=jnp.int32)[None, :], order[None, :], 0), axis=1
        )
    else:
        pieces = [lax.all_gather(mine, "rows", axis=0, tiled=True)]
        owner_ids = jnp.arange(owners, dtype=jnp.int32)
    sources = []
    for piece in pieces:
        sources += [piece, seq_swap(piece, 1)]
    places = held_by(owner_ids)

    starts = [jnp.zeros((rows, 1), jnp.int32)]
    for u in range(utts):
        starts.append(starts[-1] + lengths[:, u : u + 1])
    spot = jnp.broadcast_to(jnp.stack([seq_at * frames, core])[None, :], (rows, 2)).astype(jnp.int32)
    meta = jnp.concatenate(starts + [bw_ids, spot], axis=1)

    low = shifted(frames_in[:, frames - RIM :], 1)
    high = shifted(frames_in[:, :RIM], -1)
    gap = jnp.zeros((rows, EDGE - RIM, channels), BF16)
    xpad = jnp.concatenate([gap, low, frames_in, high, gap], axis=1)
    blocks = wave_grad.reshape(rows, frames, HOP)
    later = shifted(blocks[:, : LAPS - 1], -1)
    wave = jnp.concatenate(
        [blocks, later, jnp.zeros((rows, 2 * EDGE - LAPS + 1, HOP), BF16)], axis=1
    )
    wave = jnp.pad(wave, ((0, 0), (0, 0), (0, LAP_PAD - HOP)))
    synth = jnp.asarray(synthesis_table())
    win = jnp.asarray(window_tables())

    cot = spectrum_cotangent(meta, wave, synth, win, rows, frames, utts)
    (table, spec, act, der, ada, low_grad, resg, xc, rc, send, keep, tail, sums, hsum) = forward(
        meta, places, xpad, cot, sources, rows, frames, utts
    )

    def seq_sum(send, keep):
        both = (keep.astype(F32) + seq_swap(send, 1).astype(F32)).astype(BF16)
        stay = lax.dynamic_slice_in_dim(both, plane * QUART, QUART, axis=1)
        leave = lax.dynamic_slice_in_dim(both, (1 - plane) * QUART, QUART, axis=1)
        return stay, seq_swap(leave, 2)

    keeps, cames, bounds = [], [], []
    stay, came = seq_sum(send, keep)
    keeps.append(stay)
    cames.append(came)
    bounds.append((2 * FF // BR, NB - 1))
    pres, bsums = [], []
    per = CHUNK // BR
    for chunk in range(FF // CHUNK):
        pre, send, keep, bsum = mlp_backward(chunk, meta, low_grad, act, der, ada, table, utts)
        pres.append(pre)
        bsums.append(bsum)
        stay, came = seq_sum(send, keep)
        for at in (0, 1):
            keeps.append(stay[at * per : (at + 1) * per])
            cames.append(came[at * per : (at + 1) * per])
            begin = at * FF // BR + chunk * per
            bounds.append((begin, begin + per))
    if ring:
        chunks = to_slots(places, keeps, cames, tuple(bounds), owners, slots)
        by_offset = dict(zip(offsets, chunks))
        half = owners // 2
        plus = lambda a, b: (a.astype(F32) + b.astype(F32)).astype(BF16)
        up = by_offset[-half]
        for hop in range(half - 1, -1, -1):
            up = lax.ppermute(up, AXES, ring_step(ring, 1, seqs))
            if hop:
                up = plus(up, by_offset[hop])
        down = by_offset[-(half - 1)]
        for hop in range(half - 2, -1, -1):
            down = lax.ppermute(down, AXES, ring_step(ring, -1, seqs))
            if hop:
                down = plus(down, by_offset[-hop])
        total = (by_offset[0].astype(F32) + up.astype(F32) + down.astype(F32)).astype(BF16)
    else:
        [chunks] = to_slots(places, keeps, cames, tuple(bounds), 1, owners * slots)
        total = lax.psum_scatter(chunks, "rows", scatter_dimension=0, tiled=True)
    other = seq_swap(total, 2)
    pair = jnp.where(plane == 0, jnp.concatenate([total, other], axis=1), jnp.concatenate([other, total], axis=1))
    other = seq_swap(pair, 1)
    full = jnp.where(core == 0, jnp.concatenate([pair, other], axis=1), jnp.concatenate([other, pair], axis=1))

    input_grad, edges, last = conv_backward(
        meta, xpad, pres, table, xc, rc, resg, tail, sums, hsum, bsums, rows, frames, utts
    )
    if ring:
        for bit in (1, 2):
            last = last + seq_swap(last, bit)
        for bit in (1, 2, 4):
            last = last + rows_swap(last, bit)
    else:
        last = lax.psum(last, AXES)
    index = seq_at * frames + jnp.arange(frames, dtype=jnp.int32)
    seg = jnp.sum((meta[:, None, 1:utts] <= index[None, :, None]).astype(jnp.int32), axis=2)
    taps = table[2 * FF + NOUT : 2 * FF + NOUT + KW].astype(F32)
    from_low = shifted(edges[:, 1, EDGE - RIM :], 1)
    from_high = shifted(edges[:, 0, :RIM], -1)
    seg_at = lambda i: jnp.sum((meta[:, 1:utts] <= i).astype(jnp.int32), axis=1)
    begin = seq_at * frames
    low_fix, high_fix = [], []
    for i in range(RIM):
        fix = jnp.zeros((rows, channels), F32)
        for k in range(KW):
            source = i - k + RIM
            if source < 0:
                same_seg = (seg_at(begin + source) == seg_at(begin + i)).astype(F32)
                fix = fix + taps[k] * same_seg[:, None] * from_low[:, source + RIM]
        low_fix.append(fix)
        fix = jnp.zeros((rows, channels), F32)
        here = frames - RIM + i
        for k in range(KW):
            source = here - k + RIM
            if source >= frames:
                same_seg = (seg_at(begin + source) == seg_at(begin + here)).astype(F32)
                fix = fix + taps[k] * same_seg[:, None] * from_high[:, source - frames]
        high_fix.append(fix)
    input_grad = input_grad.at[:, :RIM].add(jnp.stack(low_fix, axis=1))
    input_grad = input_grad.at[:, frames - RIM :].add(jnp.stack(high_fix, axis=1))

    out, over = wave_forward(meta, spec, synth, win, rows, frames, utts)
    arrived = shifted(over, 1)
    first_reach = []
    for b in range(LAPS - 1):
        i = begin + b
        start = jnp.max(jnp.where(meta[:, :utts] <= i, meta[:, :utts], 0), axis=1)
        first_reach.append(i - start)
    reach = jnp.stack(first_reach, axis=1)
    scale = jnp.broadcast_to(win[2 * LAPS - 1], (rows, LAPS - 1, LAP_PAD))
    for j in range(LAPS - 1):
        scale = jnp.where((reach == j)[:, :, None], win[LAPS + j], scale)
    out = out.at[:, : LAPS - 1].add(arrived[:, : LAPS - 1] * scale)
    waveform = out[:, :, :HOP].reshape(rows, frames * HOP)

    held = held_by(row_at[None].astype(jnp.int32))
    new_master, new_first, new_second = adam(held, full, last, master, moment1, moment2)
    return waveform, input_grad, new_master, new_first, new_second


def solution(mesh):
    in_specs = (
        P("rows", "seq", None),
        P("rows", None),
        P("rows", None),
        P(),
        P("rows", None, None),
        P("rows", None, None),
        P("rows", None, None),
        P("rows", "seq"),
    )
    out_specs = (
        P("rows", "seq"),
        P("rows", "seq", None),
        P("rows", None, None),
        P("rows", None, None),
        P("rows", None, None),
    )
    return jax.shard_map(local, mesh=mesh, in_specs=in_specs, out_specs=out_specs, check_vma=False)
```

```python
import functools
import math

import jax
import jax.numpy as jnp
import numpy as np
from jax import lax
from jax.experimental import pallas as pl
from jax.experimental.pallas import tpu as pltpu
from jax.sharding import PartitionSpec as P

FF = 1536
NFFT = 1280
HOP = 320
NBW = 4
KW = 7
UTT = 4
BR = 32
STEP_COUNT = 6
BINS = 641
NOUT = 1282
VROWS = 20
IN_ROWS = 3
HEAD_ROWS = 3
NB = 137

NORM_EPS = 1e-06
ENV_FLOOR = 0.5
BETA_ONE = 0.8
BETA_TWO = 0.9
LEARN_RATE = 0.04
WEIGHT_DECAY = 0.01
ADAM_EPS = 1e-08

LAPS = NFFT // HOP
RIM = (KW - 1) // 2
LAP_PAD = 384
BIN_PAD = 768
HALF = BR // 2
QUART = BR // 4
EDGE = 16
TILE = 256
CHUNK = 512
LANE = 128
AXES = ("rows", "seq")

F32 = jnp.float32
BF16 = jnp.bfloat16
MIB = 1 << 20
VMEM_BYTES = 60 * MIB


def synthesis_table():
    k = np.arange(BINS)[:, None]
    n = np.arange(NFFT)[None, :]
    angle = (k * n % NFFT) * (2.0 * math.pi / NFFT)
    factor = np.where((k == 0) | (k == NFFT // 2), 1.0, 2.0) / NFFT
    out = np.zeros((2, BIN_PAD, LAPS, LAP_PAD), np.float32)
    out[0, :BINS, :, :HOP] = (factor * np.cos(angle)).reshape(BINS, LAPS, HOP)
    out[1, :BINS, :, :HOP] = (-factor * np.sin(angle)).reshape(BINS, LAPS, HOP)
    return out.reshape(2 * BIN_PAD, LAPS * LAP_PAD).astype(jnp.bfloat16)


def window_tables():
    window = 0.5 - 0.5 * np.cos(np.arange(NFFT) * (2.0 * math.pi / NFFT))
    rows = np.zeros((LAPS, LAP_PAD), np.float64)
    rows[:, :HOP] = window.reshape(LAPS, HOP)
    envelope = np.cumsum(rows**2, axis=0)
    return np.concatenate([rows, 1.0 / np.maximum(envelope, ENV_FLOOR)], axis=0).astype(np.float32)


def ring_of(count):
    if count != 8:
        return None
    return [0, 2, 4, 6, 7, 5, 3, 1]


def ring_step(ring, shift, seq_count):
    where = {r: i for i, r in enumerate(ring)}
    pairs = []
    for r in ring:
        target = ring[(where[r] + shift) % len(ring)]
        pairs += [(r * seq_count + s, target * seq_count + s) for s in range(seq_count)]
    return pairs


def seq_swap(value, bit):
    count = lax.axis_size("seq")
    return lax.ppermute(value, "seq", [(s, s ^ bit) for s in range(count)])


def rows_swap(value, bit):
    count = lax.axis_size("rows")
    return lax.ppermute(value, "rows", [(r, r ^ bit) for r in range(count)])


def shifted(value, distance):
    devices = range(lax.axis_size("seq"))
    return lax.ppermute(
        value, "seq", [(i - distance, i) for i in devices if i - distance in devices]
    )


def dot(a, b, dims):
    return lax.dot_general(a, b, (dims, ((), ())), preferred_element_type=F32)


NN = ((1,), (0,))
NT = ((1,), (1,))
TN = ((0,), (0,))


def frame_reach(meta, row, first, count, utts):
    index = first + lax.broadcasted_iota(jnp.int32, (count, 128), 0)
    start = jnp.zeros_like(index)
    end = jnp.zeros_like(index) + meta[row, 1]
    for u in range(1, utts):
        inside = index >= meta[row, u]
        start = jnp.where(inside, meta[row, u], start)
        end = jnp.where(inside, meta[row, u + 1], end)
    return index - start, end - 1 - index


def spans(count, size):
    return [(at, min(size, count - at)) for at in range(0, count, size)]


def over(table, base, reach, lane_tile, width=LANE):
    cut = slice(lane_tile * LANE, lane_tile * LANE + width)
    picked = jnp.broadcast_to(table[base + LAPS - 1 : base + LAPS, cut], (reach.shape[0], width))
    for j in range(LAPS - 2, -1, -1):
        picked = jnp.where(reach[:, :width] == j, table[base + j : base + j + 1, cut], picked)
    return picked


def keep_within(values, reach, left, offset):
    if offset < 0:
        return jnp.where(reach >= -offset, values, 0.0)
    if offset > 0:
        return jnp.where(left >= offset, values, 0.0)
    return values


def row_mean(values):
    return jnp.mean(values, axis=1, keepdims=True)


def fold(values):
    rows, columns = values.shape
    return jnp.sum(values.reshape(rows // 8, 8, columns), axis=0)


def sincos(angle):
    turns = jnp.round(angle * (1.0 / math.pi))
    rest = angle - turns * 3.140625
    rest = rest - turns * 9.670257568359375e-4
    rest = rest - turns * 6.2771141529083251953e-7
    rest = rest - turns * 1.2154201256553420e-10
    half = turns * 0.5
    sign = 1.0 - 4.0 * (half - jnp.floor(half))
    sq = rest * rest
    sine = rest + rest * sq * (
        -1.6666667163e-01
        + sq * (8.3333337680e-03 + sq * (-1.9841270114e-04 + sq * (2.7557314297e-06 - sq * 2.5050759689e-08)))
    )
    cosine = 1.0 + sq * (
        -0.5
        + sq
        * (
            4.1666667908e-02
            + sq
            * (-1.3888889225e-03 + sq * (2.4801587642e-05 + sq * (-2.7557314297e-07 + sq * 2.0875723372e-09)))
        )
    )
    return sine * sign, cosine * sign


ANGLE_LIMIT = 8192.0


def params():
    return pltpu.CompilerParams(vmem_limit_bytes=VMEM_BYTES)


def cost(flops, bytes_accessed, transcendentals=0):
    return pl.CostEstimate(
        flops=int(flops), bytes_accessed=int(bytes_accessed), transcendentals=int(transcendentals)
    )


WHOLE = pl.BlockSpec(memory_space=pltpu.VMEM)
SCALARS = pl.BlockSpec(memory_space=pltpu.SMEM)
ANYWHERE = pl.BlockSpec(memory_space=pl.ANY)
shape_of = jax.ShapeDtypeStruct


def pre_body(meta, wave_ref, halo_ref, synth_ref, win_ref, *rest, row, tiles, utts):
    out_ref, scaled, signal = rest[-3:]
    step = pl.program_id(0)
    first = pl.multiple_of(step * TILE, TILE)
    base = meta[row, 2 * utts + 1] + first
    reach, left = frame_reach(meta, row, base, TILE + EDGE, utts)

    @pl.when(step == 0)
    def _():
        scaled[...] = jnp.zeros_like(scaled)

    def scale(block, at, size):
        block = block.astype(F32)
        for c, width in ((0, LANE), (1, LANE), (2, HOP - 2 * LANE)):
            value = block[:, c * LANE : c * LANE + width]
            scaled[c, at : at + size, 0:width] = value * over(win_ref, LAPS, reach[at : at + size], c, width)

    for at, size in spans(TILE, 64):
        scale(wave_ref[row, pl.ds(pl.multiple_of(first + at, 64), size), :], at, size)

    @pl.when(step == tiles - 1)
    def _():
        scale(halo_ref[row], TILE, EDGE)

    @pl.when(step < tiles - 1)
    def _():
        scale(wave_ref[row, pl.ds(pl.multiple_of(first + TILE, TILE), EDGE), :], TILE, EDGE)

    for j in range(LAPS):
        for c in range(LAP_PAD // LANE):
            weight = win_ref[j : j + 1, c * LANE : (c + 1) * LANE]
            for at, size in spans(TILE, 64):
                part = scaled[c, at + j : at + j + size, :] * weight
                part = keep_within(part, None, left[at : at + size], j)
                column = j * LAP_PAD + c * LANE
                signal[at : at + size, column : column + LANE] = part.astype(BF16)
    for c in range(0, 2 * BIN_PAD, 512):
        out_ref[:, c : c + 512] = dot(signal[...], synth_ref[c : c + 512, :], NT).astype(BF16)


def spectrum_cotangent(row, before, meta, wave, halo, synth, win, utts):
    rows, frames, _ = wave.shape
    tiles = frames // TILE
    more = [] if before is None else [before]
    return pl.pallas_call(
        functools.partial(pre_body, row=row, tiles=tiles, utts=utts),
        grid=(tiles,),
        in_specs=[SCALARS, WHOLE, WHOLE, WHOLE, WHOLE] + [ANYWHERE] * len(more),
        out_specs=pl.BlockSpec((TILE, 2 * BIN_PAD), lambda i: (row * tiles + i, 0)),
        out_shape=shape_of((rows * frames, 2 * BIN_PAD), BF16),
        input_output_aliases={5: 0} if more else {},
        scratch_shapes=[
            pltpu.VMEM((LAP_PAD // LANE, TILE + EDGE, LANE), F32),
            pltpu.VMEM((TILE, LAPS * LAP_PAD), BF16),
        ],
        compiler_params=params(),
        cost_estimate=cost(2 * frames * 1536 * 1536, frames * 1536 * 2 + 8 * MIB),
        name=f"spectrum_cotangent_{row}",
    )(meta, wave, halo, synth, win, *more)


def fill_frames(xs, x_ref, low_ref, high_ref, row, tile, tiles, channels):
    first = pl.multiple_of(tile * TILE, TILE)

    def put(at, block):
        block = block.astype(F32)
        for c in range(channels // LANE):
            xs[c, at : at + block.shape[0], :] = block[:, c * LANE : (c + 1) * LANE]

    for at, size in spans(TILE, 64):
        put(EDGE + at, x_ref[row, pl.ds(pl.multiple_of(first + at, 64), size), :])

    @pl.when(tile == 0)
    def _():
        put(0, low_ref[row])

    @pl.when(tile > 0)
    def _():
        put(0, x_ref[row, pl.ds(pl.multiple_of(first - EDGE, EDGE), EDGE), :])

    @pl.when(tile == tiles - 1)
    def _():
        put(EDGE + TILE, high_ref[row])

    @pl.when(tile < tiles - 1)
    def _():
        put(EDGE + TILE, x_ref[row, pl.ds(pl.multiple_of(first + TILE, EDGE), EDGE), :])


def by_utterance(meta, row, utts, index, rows_of):
    value = jnp.broadcast_to(rows_of(0), (index.shape[0], LANE))
    for u in range(1, utts):
        value = jnp.where(index >= meta[row, u], rows_of(u), value)
    return value


def pick_rows(meta, row, utts, vec, out, channels):
    for u in range(utts):
        wanted = meta[row, utts + 1 + u]
        for at, offset in ((u, KW + 1), (utts + u, KW + 1 + NBW)):
            value = vec(offset)
            for b in range(1, NBW):
                value = jnp.where(wanted == b, vec(offset + b), value)
            out[at : at + 1, :] = value


def forward_body(meta, places, x_ref, low_ref, high_ref, cot_ref, *rest, parts, tiles, utts):
    sources = rest[:parts]
    (
        table,
        spec_ref,
        act_ref,
        der_ref,
        ada_ref,
        lowg_ref,
        resg_ref,
        xc_ref,
        rc_ref,
        send_ref,
        keep_ref,
        tail_ref,
        sums_ref,
        bsum_ref,
        xs,
        w_head,
        b_head,
        vecs,
        picks,
        grad,
        hg,
        wide,
        wide2,
        slim,
        xn_ref,
        normed,
        branch_ref,
        rn_ref,
        sem,
    ) = rest[parts:]
    step = pl.program_id(0)
    steps = pl.num_programs(0)
    core = meta[0, 2 * utts + 2]
    channels = x_ref.shape[2]
    lane_tiles = channels // LANE
    row, tile = step // tiles, step % tiles
    vec = lambda v: vecs[2 + v : 3 + v, :]
    vec_at = KW + 1 + 2 * NBW

    @pl.when(step == 0)
    def _():
        def go(start):
            base = 0
            for index, ref in enumerate(sources):
                slots = ref.shape[0]
                side = core if index % 2 == 0 else 1 - core

                def one(s, carry, ref=ref, base=base, side=side):
                    bucket = places[0, base + s]

                    @pl.when(bucket < NB)
                    def _():
                        at = pl.multiple_of(bucket * BR + side * HALF, HALF)
                        copy = pltpu.make_async_copy(ref.at[s], table.at[pl.ds(at, HALF), :], sem)
                        if start:
                            copy.start()
                        else:
                            copy.wait()

                    return carry

                lax.fori_loop(0, slots, one, 0)
                if index % 2 == 1:
                    base = base + slots

        go(True)
        grad[...] = jnp.zeros_like(grad)
        sums_ref[...] = jnp.zeros_like(sums_ref)
        bsum_ref[...] = jnp.zeros_like(bsum_ref)
        go(False)
        head_at = 2 * FF
        w_head[0:640, :] = table[head_at : head_at + 640, :]
        edge = table[head_at + 640 : head_at + 640 + 656, :].astype(F32)
        inside = lax.broadcasted_iota(jnp.int32, (128, channels), 0)
        w_head[640:768, :] = jnp.where(inside < 1, edge[0:128], 0.0).astype(BF16)
        w_head[768:1408, :] = edge[1:641].astype(BF16)
        w_head[1408:1536, :] = jnp.where(inside < 1, edge[641:642], 0.0).astype(BF16)
        last = table[2 * FF + 1280 : 2 * FF + 1280 + BR, :].astype(F32)
        vecs[...] = last
        line = jnp.concatenate([last[25:26], last[26:27], last[27:28]], axis=1)
        line = jnp.broadcast_to(line, (8, 3 * channels))
        column = lax.broadcasted_iota(jnp.int32, (8, BIN_PAD), 1)
        b_head[:, 0:BIN_PAD] = jnp.where(column < BINS, line[:, 0:BIN_PAD], 0.0)
        moved = pltpu.roll(line, 3 * channels - BINS, 1)
        b_head[:, BIN_PAD:] = jnp.where(column < BINS, moved[:, 0:BIN_PAD], 0.0)

    @pl.when(tile == 0)
    def _():
        pick_rows(meta, row, utts, vec, picks, channels)

    base = meta[row, 2 * utts + 1] + tile * TILE
    fill_frames(xs, x_ref, low_ref, high_ref, row, tile, tiles, channels)
    for at, size in spans(TILE, 32):
        reach, left = frame_reach(meta, row, base + at, size, utts)
        index = base + at + lax.broadcasted_iota(jnp.int32, (size, LANE), 0)
        conv = []
        for c in range(lane_tiles):
            cut = slice(c * LANE, (c + 1) * LANE)
            total = vecs[2 + KW : 3 + KW, cut]
            for k in range(KW):
                offset = k - RIM
                moved = xs[c, EDGE + offset + at : EDGE + offset + at + size, :]
                total = total + keep_within(moved, reach, left, offset) * vecs[2 + k : 3 + k, cut]
            conv.append(total)
        mean = jnp.sum(sum(conv), axis=1, keepdims=True) * (1.0 / channels)
        conv = [v - mean for v in conv]
        square = jnp.sum(sum([v * v for v in conv]), axis=1, keepdims=True) * (1.0 / channels)
        rc = jnp.broadcast_to(lax.rsqrt(square + NORM_EPS), (size, LANE))
        rc_ref[at : at + size, :] = rc
        for c in range(lane_tiles):
            cut = slice(c * LANE, (c + 1) * LANE)
            xc = conv[c] * rc
            xc_ref[at : at + size, cut] = xc
            scale = by_utterance(meta, row, utts, index, lambda u: picks[u : u + 1, cut])
            shift = by_utterance(meta, row, utts, index, lambda u: picks[utts + u : utts + u + 1, cut])
            ada_ref[at : at + size, cut] = (xc * scale + shift).astype(BF16)
    for c in range(IN_ROWS):
        pre_ref = (wide, wide2)[c % 2]
        pre_ref[...] = dot(ada_ref[...], table[c * CHUNK : (c + 1) * CHUNK, :], NT)
        for at, size in spans(TILE, 32):
            for d in range(0, CHUNK, 256):
                bias = vecs[2 + VROWS + c : 3 + VROWS + c, d : d + 256]
                pre = pre_ref[at : at + size, d : d + 256] + bias
                phi = 0.5 + 0.5 * lax.erf(pre * math.sqrt(0.5))
                bell = jnp.exp(-0.5 * pre * pre) * (1.0 / math.sqrt(2.0 * math.pi))
                cut = slice(c * CHUNK + d, c * CHUNK + d + 256)
                act_ref[at : at + size, cut] = (pre * phi).astype(BF16)
                der_ref[at : at + size, cut] = (phi + pre * bell).astype(BF16)
    slim[...] = dot(act_ref[...], table[FF : 2 * FF, :], NN)
    for at, size in spans(TILE, 16):
        span = slice(at, at + size)
        branch = slim[span, :] + vec(vec_at)
        branch_ref[span, :] = branch
        x = jnp.concatenate([xs[c, EDGE + at : EDGE + at + size, :] for c in range(lane_tiles)], axis=1)
        residual = x + vec(vec_at + 1) * branch
        residual = residual - row_mean(residual)
        rn = lax.rsqrt(row_mean(residual * residual) + NORM_EPS)
        rn_ref[span, :] = jnp.broadcast_to(rn, (size, LANE))
        xn = residual * rn
        xn_ref[span, :] = xn
        normed[span, :] = (xn * vec(vec_at + 2) + vec(vec_at + 3)).astype(BF16)

    def head(c, turn):
        logs_ref, angle_ref = wide, wide2
        half = slice((c // 256 % 2) * 256, (c // 256 % 2) * 256 + 256)
        logs_ref[:, half] = dot(normed[...], w_head[c : c + 256, :], NT)
        angle_ref[:, half] = dot(normed[...], w_head[BIN_PAD + c : BIN_PAD + c + 256, :], NT)
        widest = jnp.zeros((8, 256), F32)
        for at, size in spans(TILE, 16):
            span = slice(at, at + size)
            one, two = slice(c, c + 256), slice(BIN_PAD + c, BIN_PAD + c + 256)
            angle = angle_ref[span, half] + b_head[0:1, two]
            scale = jnp.exp(logs_ref[span, half] + b_head[0:1, one])
            sine, cosine = turn(angle)
            real, imag = scale * cosine, scale * sine
            spec_ref[span, one] = real.astype(BF16)
            spec_ref[span, two] = imag.astype(BF16)
            dre = cot_ref[span, one].astype(F32)
            dim = cot_ref[span, two].astype(F32)
            hg[span, one] = (dre * real + dim * imag).astype(BF16)
            hg[span, two] = (dim * real - dre * imag).astype(BF16)
            widest = jnp.maximum(widest, jnp.max(jnp.abs(angle).reshape(size // 8, 8, 256), axis=0))
        return widest

    widest = head(0, sincos)
    for c in range(256, BIN_PAD, 256):
        widest = jnp.maximum(widest, head(c, sincos))

    @pl.when(jnp.max(widest) > ANGLE_LIMIT)
    def _():
        for c in range(0, BIN_PAD, 256):
            head(c, lambda angle: (jnp.sin(angle), jnp.cos(angle)))

    slim[...] = dot(hg[...], w_head[...], NN)
    grad[...] += dot(hg[...], normed[...], TN)
    for c in range(0, 2 * BIN_PAD, 512):
        total = bsum_ref[:, c : c + 512]
        for at, size in spans(TILE, 32):
            total = total + fold(hg[at : at + size, c : c + 512].astype(F32))
        bsum_ref[:, c : c + 512] = total
    sums = [sums_ref[v] for v in range(4)]
    for at, size in spans(TILE, 16):
        span = slice(at, at + size)
        ngrad = slim[span, :]
        xn = xn_ref[span, :]
        e = ngrad * vec(vec_at + 2)
        resg = rn_ref[span, 0:1] * (e - row_mean(e) - xn * row_mean(e * xn))
        resg_ref[span, :] = resg
        low = (vec(vec_at + 1) * resg).astype(BF16)
        lowg_ref[span, :] = low
        sums[0] = sums[0] + fold(low.astype(F32))
        sums[1] = sums[1] + fold(resg * branch_ref[span, :])
        sums[2] = sums[2] + fold(ngrad * xn)
        sums[3] = sums[3] + fold(ngrad)
    for v in range(4):
        sums_ref[v] = sums[v]

    @pl.when(step == steps - 1)
    def _():
        grad[767:768, :] = grad[640:641, :]
        for b in range(40):
            at = b * BR if b < 20 else b * BR + 127
            low_half = grad[at : at + HALF, :].astype(BF16)
            high_half = grad[at + HALF : at + BR, :].astype(BF16)
            keep_ref[b] = jnp.where(core == 0, low_half, high_half)
            send_ref[b] = jnp.where(core == 0, high_half, low_half)
        tail_ref[...] = grad[1407:1415, :]


def forward(meta, places, x, low, high, cot, sources, utts):
    rows, frames, channels = x.shape
    tiles = frames // TILE
    count = rows * frames
    wide = pl.BlockSpec((TILE, FF), lambda i: (i, 0))
    slim = pl.BlockSpec((TILE, channels), lambda i: (i, 0))
    return pl.pallas_call(
        functools.partial(forward_body, parts=len(sources), tiles=tiles, utts=utts),
        grid=(rows * tiles,),
        in_specs=[SCALARS, SCALARS, WHOLE, WHOLE, WHOLE, wide] + [ANYWHERE] * len(sources),
        out_specs=[WHOLE, wide, wide, wide, slim, slim, slim, slim]
        + [pl.BlockSpec((TILE, LANE), lambda i: (i, 0))]
        + [WHOLE] * 5,
        out_shape=[
            shape_of((NB * BR, channels), BF16),
            shape_of((count, FF), BF16),
            shape_of((count, FF), BF16),
            shape_of((count, FF), BF16),
            shape_of((count, channels), BF16),
            shape_of((count, channels), BF16),
            shape_of((count, channels), F32),
            shape_of((count, channels), F32),
            shape_of((count, LANE), F32),
            shape_of((40, HALF, channels), BF16),
            shape_of((40, HALF, channels), BF16),
            shape_of((8, channels), F32),
            shape_of((4, 8, channels), F32),
            shape_of((8, 2 * BIN_PAD), F32),
        ],
        scratch_shapes=[
            pltpu.VMEM((channels // LANE, TILE + 2 * EDGE, LANE), F32),
            pltpu.VMEM((2 * BIN_PAD, channels), BF16),
            pltpu.VMEM((8, 2 * BIN_PAD), F32),
            pltpu.VMEM((BR, channels), F32),
            pltpu.VMEM((2 * utts, channels), F32),
            pltpu.VMEM((2 * BIN_PAD, channels), F32),
            pltpu.VMEM((TILE, 2 * BIN_PAD), BF16),
            pltpu.VMEM((TILE, CHUNK), F32),
            pltpu.VMEM((TILE, CHUNK), F32),
            pltpu.VMEM((TILE, channels), F32),
            pltpu.VMEM((TILE, channels), F32),
            pltpu.VMEM((TILE, channels), BF16),
            pltpu.VMEM((TILE, channels), F32),
            pltpu.VMEM((TILE, LANE), F32),
            pltpu.SemaphoreType.DMA,
        ],
        compiler_params=params(),
        cost_estimate=cost(10 * count * 1536 * 512, 40 * MIB, count * 4096),
        name="forward",
    )(meta, places, x, low, high, cot, *sources)


def mlp_body(meta, low_ref, act_ref, der_ref, ada_ref, wout_ref, *rest, utts):
    pre_ref, send_ref, keep_ref, bsum_ref, gout, gin, agrad = rest[-7:]
    step = pl.program_id(0)
    core = meta[0, 2 * utts + 2]
    tile = low_ref.shape[0]

    @pl.when(step == 0)
    def _():
        gout[...] = jnp.zeros_like(gout)
        gin[...] = jnp.zeros_like(gin)
        bsum_ref[...] = jnp.zeros_like(bsum_ref)

    agrad[...] = dot(low_ref[...], wout_ref[...], NT)
    gout[...] += dot(act_ref[...], low_ref[...], TN)
    total = bsum_ref[...]
    for at, size in spans(tile, 16):
        span = slice(at, at + size)
        pre = (agrad[span, :] * der_ref[span, :].astype(F32)).astype(BF16)
        pre_ref[span, :] = pre
        total = total + fold(pre.astype(F32))
    bsum_ref[...] = total
    gin[...] += dot(pre_ref[...], ada_ref[...], TN)

    @pl.when(step == pl.num_programs(0) - 1)
    def _():
        buckets = CHUNK // BR
        for at, ref in ((0, gin), (buckets, gout)):
            for b in range(buckets):
                low_half = ref[b * BR : b * BR + HALF, :].astype(BF16)
                high_half = ref[b * BR + HALF : b * BR + BR, :].astype(BF16)
                keep_ref[at + b] = jnp.where(core == 0, low_half, high_half)
                send_ref[at + b] = jnp.where(core == 0, high_half, low_half)


def mlp_backward(chunk, before, meta, low, act, der, ada, table, utts):
    count, channels = low.shape
    tile = 512
    slim = pl.BlockSpec((tile, channels), lambda i: (i, 0))
    part = pl.BlockSpec((tile, CHUNK), lambda i: (i, chunk))
    buckets = 2 * CHUNK // BR
    more = [] if before is None else [before]
    return pl.pallas_call(
        functools.partial(mlp_body, utts=utts),
        grid=(count // tile,),
        in_specs=[
            SCALARS,
            slim,
            part,
            part,
            slim,
            pl.BlockSpec((CHUNK, channels), lambda i: (FF // CHUNK + chunk, 0)),
        ]
        + [ANYWHERE] * len(more),
        out_specs=[part, WHOLE, WHOLE, WHOLE],
        out_shape=[
            shape_of((count, FF), BF16),
            shape_of((buckets, HALF, channels), BF16),
            shape_of((buckets, HALF, channels), BF16),
            shape_of((8, CHUNK), F32),
        ],
        input_output_aliases={6: 0} if more else {},
        scratch_shapes=[
            pltpu.VMEM((CHUNK, channels), F32),
            pltpu.VMEM((CHUNK, channels), F32),
            pltpu.VMEM((tile, CHUNK), F32),
        ],
        compiler_params=params(),
        cost_estimate=cost(6 * count * CHUNK * 512, 12 * MIB),
        name=f"mlp_backward_{chunk}",
    )(meta, low, act, der, ada, table, *more)


def norm_body(
    meta, x_ref, low_ref, high_ref, pre_ref, w_in, last_ref, xc_ref, rc_ref, *rest, row, tiles, utts, closing
):
    more = rest[: 7 if closing else 0]
    outs = rest[len(more) :]
    cg_ref, edge_ref, part_ref = outs[:3]
    xs, vecs, picks, agrad, cg, reaches = outs[-6:]
    tile = pl.program_id(0)
    channels = x_ref.shape[2]
    lane_tiles = channels // LANE
    base = meta[row, 2 * utts + 1] + tile * TILE
    vec = lambda v: vecs[2 + v : 3 + v, :]

    @pl.when(tile == 0)
    def _():
        vecs[...] = last_ref[...].astype(F32)
        part_ref[...] = more[0][...] if closing else jnp.zeros_like(part_ref)
        pick_rows(meta, row, utts, vec, picks, channels)

    agrad[...] = dot(pre_ref[...], w_in[...], NN)
    fill_frames(xs, x_ref, low_ref, high_ref, row, tile, tiles, channels)
    for at, size in spans(TILE, 32):
        span = slice(at, at + size)
        reach, left = frame_reach(meta, row, base + at, size, utts)
        reaches[0, span, :] = reach
        reaches[1, span, :] = left
        index = base + at + lax.broadcasted_iota(jnp.int32, (size, LANE), 0)
        ecs, xcs = [], []
        for c in range(lane_tiles):
            cut = slice(c * LANE, (c + 1) * LANE)
            scale = by_utterance(meta, row, utts, index, lambda u: picks[u : u + 1, cut])
            ecs.append(agrad[span, cut] * scale)
            xcs.append(xc_ref[span, cut])
        m_one = jnp.sum(sum(ecs), axis=1, keepdims=True) * (1.0 / channels)
        m_two = jnp.sum(sum([e * v for e, v in zip(ecs, xcs)]), axis=1, keepdims=True) * (1.0 / channels)
        rc = rc_ref[span, :]
        for c in range(lane_tiles):
            cut = slice(c * LANE, (c + 1) * LANE)
            value = rc * (ecs[c] - m_one - xcs[c] * m_two)
            cg[c, span, :] = value
            cg_ref[span, cut] = value
    for u in range(utts):
        begin, end = meta[row, u], meta[row, u + 1]

        @pl.when((begin < base + TILE) & (end > base))
        def _(u=u, begin=begin, end=end):
            wanted = meta[row, utts + 1 + u]
            for c in range(lane_tiles):
                cut = slice(c * LANE, (c + 1) * LANE)
                one = jnp.zeros((8, LANE), F32)
                two = jnp.zeros((8, LANE), F32)
                for at, size in spans(TILE, 64):
                    span = slice(at, at + size)
                    index = base + at + lax.broadcasted_iota(jnp.int32, (size, LANE), 0)
                    value = jnp.where((index >= begin) & (index < end), agrad[span, cut], 0.0)
                    one = one + fold(value * xc_ref[span, cut])
                    two = two + fold(value)
                part_ref[KW + 1 + wanted, :, cut] += one
                part_ref[KW + 1 + NBW + wanted, :, cut] += two

    for c in range(lane_tiles):
        cut = slice(c * LANE, (c + 1) * LANE)
        sums = [part_ref[k, :, cut] for k in range(KW + 1)]
        for at, size in spans(TILE, 32):
            span = slice(at, at + size)
            reach, left = reaches[0, span, :], reaches[1, span, :]
            value = cg[c, span, :]
            for k in range(KW):
                offset = k - RIM
                moved = xs[c, EDGE + offset + at : EDGE + offset + at + size, :] * value
                sums[k] = sums[k] + fold(keep_within(moved, reach, left, offset))
            sums[KW] = sums[KW] + fold(value)
        for k in range(KW + 1):
            part_ref[k, :, cut] = sums[k]

    @pl.when(tile == 0)
    def _():
        edge_ref[0] = cg_ref[0:8, :]

    @pl.when(tile == tiles - 1)
    def _():
        edge_ref[1] = cg_ref[TILE - 8 : TILE, :]

    if closing:
        _, tail_ref, sums_ref, hsum_ref, bsum0, bsum1, bsum2 = more
        vec_ref = outs[3]

        @pl.when(tile == tiles - 1)
        def _():
            vec_ref[0:8, :] = jnp.zeros((8, channels), F32)
            vec_ref[0:2, :] = tail_ref[0:2, :]
            for v in range(VROWS):
                at = v - (KW + 1 + 2 * NBW)
                rows_of = part_ref[v] if at < 0 else sums_ref[at]
                vec_ref[2 + v : 3 + v, :] = jnp.sum(rows_of, axis=0, keepdims=True)
            for c, ref in enumerate((bsum0, bsum1, bsum2)):
                vec_ref[2 + VROWS + c : 3 + VROWS + c, :] = jnp.sum(ref[...], axis=0, keepdims=True)
            flat = jnp.broadcast_to(jnp.sum(hsum_ref[...], axis=0, keepdims=True), (8, 2 * BIN_PAD))
            column = lax.broadcasted_iota(jnp.int32, (8, 3 * channels), 1)
            moved = pltpu.roll(flat, 2 * BIN_PAD - (BIN_PAD - BINS), 1)
            joined = jnp.where(column < BINS, flat, moved)
            joined = jnp.where(column < NOUT, joined, 0.0)
            for c in range(HEAD_ROWS):
                at = 2 + VROWS + IN_ROWS + c
                vec_ref[at : at + 1, :] = joined[0:1, c * channels : (c + 1) * channels]
            vec_ref[28:32, :] = jnp.zeros((4, channels), F32)


def norm_backward(row, closing, meta, x, low, high, pre, table, xc, rc, utts):
    rows, frames, channels = x.shape
    tiles = frames // TILE
    block = lambda width: pl.BlockSpec((TILE, width), lambda i: (row * tiles + i, 0))
    sums = KW + 1 + 2 * NBW
    out_specs = [pl.BlockSpec((TILE, channels), lambda i: (i, 0)), WHOLE, WHOLE]
    out_shape = [
        shape_of((frames, channels), F32),
        shape_of((2, 8, channels), F32),
        shape_of((sums, 8, channels), F32),
    ]
    if closing:
        out_specs.append(WHOLE)
        out_shape.append(shape_of((BR, channels), F32))
    return pl.pallas_call(
        functools.partial(norm_body, row=row, tiles=tiles, utts=utts, closing=bool(closing)),
        grid=(tiles,),
        in_specs=[SCALARS, WHOLE, WHOLE, WHOLE, block(FF)]
        + [
            pl.BlockSpec((FF, channels), lambda i: (0, 0)),
            pl.BlockSpec((BR, channels), lambda i: (NB - 1, 0)),
            block(channels),
            block(LANE),
        ]
        + [WHOLE] * len(closing),
        out_specs=out_specs,
        out_shape=out_shape,
        scratch_shapes=[
            pltpu.VMEM((channels // LANE, TILE + 2 * EDGE, LANE), F32),
            pltpu.VMEM((BR, channels), F32),
            pltpu.VMEM((2 * utts, channels), F32),
            pltpu.VMEM((TILE, channels), F32),
            pltpu.VMEM((channels // LANE, TILE, LANE), F32),
            pltpu.VMEM((2, TILE, LANE), jnp.int32),
        ],
        compiler_params=params(),
        cost_estimate=cost(2 * frames * 1536 * 512, 12 * MIB),
        name=f"norm_backward_{row}",
    )(meta, x, low, high, pre, table, table, xc, rc, *closing)


def conv_body(meta, cg_ref, before_ref, after_ref, low_ref, high_ref, resg_ref, last_ref, *rest, row, tiles, utts):
    out_ref, cs, vecs = rest[-3:]
    tile = pl.program_id(0)
    channels = cg_ref.shape[1]
    base = meta[row, 2 * utts + 1] + tile * TILE

    @pl.when(tile == 0)
    def _():
        vecs[...] = last_ref[...].astype(F32)

    for c in range(channels // LANE):
        cut = slice(c * LANE, (c + 1) * LANE)
        cs[c, 8 : 8 + TILE, :] = cg_ref[:, cut]
        cs[c, 0:8, :] = jnp.where(tile == 0, low_ref[row, :, cut], before_ref[:, cut])
        cs[c, 8 + TILE :, :] = jnp.where(tile == tiles - 1, high_ref[row, :, cut], after_ref[:, cut])
    for at, size in spans(TILE, 32):
        span = slice(at, at + size)
        reach, left = frame_reach(meta, row, base + at, size, utts)
        for c in range(channels // LANE):
            cut = slice(c * LANE, (c + 1) * LANE)
            total = resg_ref[span, cut]
            for k in range(KW):
                offset = RIM - k
                moved = cs[c, 8 + offset + at : 8 + offset + at + size, :]
                total = total + keep_within(moved, reach, left, offset) * vecs[2 + k : 3 + k, cut]
            out_ref[0, span, cut] = total


def conv_backward(row, before, meta, cg, low, high, resg, table, rows, utts):
    frames, channels = cg.shape
    tiles = frames // TILE
    per = TILE // 8
    more = [] if before is None else [before]
    return pl.pallas_call(
        functools.partial(conv_body, row=row, tiles=tiles, utts=utts),
        grid=(tiles,),
        in_specs=[
            SCALARS,
            pl.BlockSpec((TILE, channels), lambda i: (i, 0)),
            pl.BlockSpec((8, channels), lambda i: (jnp.maximum(i * per - 1, 0), 0)),
            pl.BlockSpec((8, channels), lambda i: (jnp.minimum((i + 1) * per, tiles * per - 1), 0)),
            WHOLE,
            WHOLE,
            pl.BlockSpec((TILE, channels), lambda i: (row * tiles + i, 0)),
            pl.BlockSpec((BR, channels), lambda i: (NB - 1, 0)),
        ]
        + [ANYWHERE] * len(more),
        out_specs=pl.BlockSpec((1, TILE, channels), lambda i: (row, i, 0)),
        out_shape=shape_of((rows, frames, channels), F32),
        input_output_aliases={8: 0} if more else {},
        scratch_shapes=[
            pltpu.VMEM((channels // LANE, TILE + 16, LANE), F32),
            pltpu.VMEM((BR, channels), F32),
        ],
        compiler_params=params(),
        cost_estimate=cost(16 * frames * 512, 6 * MIB),
        name=f"conv_backward_{row}",
    )(meta, cg, cg, cg, low, high, resg, table, *more)


def wave_body(meta, spec_ref, prev_ref, halo_ref, synth_ref, win_ref, *rest, row, tiles, utts):
    out_ref, spec, held = rest[-3:]
    tile = pl.program_id(0)
    base = meta[row, 2 * utts + 1] + tile * TILE
    spec[EDGE:, :] = spec_ref[...]
    spec[0:EDGE, :] = jnp.where(tile == 0, halo_ref[row], prev_ref[...])
    for j in range(LAPS):
        piece = dot(spec[...], synth_ref[:, j * LAP_PAD : (j + 1) * LAP_PAD], NN)
        for c in range(LAP_PAD // LANE):
            held[j, c] = piece[:, c * LANE : (c + 1) * LANE]
    for at, size in spans(TILE, 32):
        reach, _ = frame_reach(meta, row, base + at, size, utts)
        for c, width in ((0, LANE), (1, LANE), (2, HOP - 2 * LANE)):
            cut = slice(c * LANE, c * LANE + width)
            total = held[0, c, EDGE + at : EDGE + at + size, :] * win_ref[0:1, c * LANE : (c + 1) * LANE]
            for j in range(1, LAPS):
                moved = held[j, c, EDGE + at - j : EDGE + at - j + size, :]
                moved = moved * win_ref[j : j + 1, c * LANE : (c + 1) * LANE]
                total = total + jnp.where(reach >= j, moved, 0.0)
            out_ref[0, at : at + size, cut] = total[:, 0:width] * over(win_ref, LAPS, reach, c, width)


def wave_forward(row, before, meta, spec, halo, synth, win, rows, utts):
    frames = spec.shape[0] // rows
    tiles = frames // TILE
    per = TILE // EDGE
    more = [] if before is None else [before]
    return pl.pallas_call(
        functools.partial(wave_body, row=row, tiles=tiles, utts=utts),
        grid=(tiles,),
        in_specs=[
            SCALARS,
            pl.BlockSpec((TILE, 2 * BIN_PAD), lambda i: (row * tiles + i, 0)),
            pl.BlockSpec((EDGE, 2 * BIN_PAD), lambda i: (jnp.maximum((row * tiles + i) * per - 1, 0), 0)),
            WHOLE,
            WHOLE,
            WHOLE,
        ]
        + [ANYWHERE] * len(more),
        out_specs=pl.BlockSpec((1, TILE, HOP), lambda i: (row, i, 0)),
        out_shape=shape_of((rows, frames, HOP), F32),
        input_output_aliases={6: 0} if more else {},
        scratch_shapes=[
            pltpu.VMEM((TILE + EDGE, 2 * BIN_PAD), BF16),
            pltpu.VMEM((LAPS, LAP_PAD // LANE, TILE + EDGE, LANE), F32),
        ],
        compiler_params=params(),
        cost_estimate=cost(2 * frames * 1536 * 1536, 12 * MIB),
        name=f"wave_forward_{row}",
    )(meta, spec, spec, halo, synth, win, *more)


def slot_body(slot_of, *refs, bounds):
    count = len(bounds)
    out = refs[-1]
    for (start, stop), keep, came in zip(bounds, refs[:count], refs[count : 2 * count]):

        def one(b, carry, start=start, keep=keep, came=came):
            value = keep[b].astype(F32) + came[b].astype(F32)
            out[slot_of[0, start + b]] = value.astype(BF16)
            return carry

        lax.fori_loop(0, stop - start, one, 0)


def to_slots(slot_of, keeps, cames, bounds, total):
    channels = keeps[0].shape[2]
    return pl.pallas_call(
        functools.partial(slot_body, bounds=bounds),
        in_specs=[SCALARS] + [WHOLE] * (2 * len(bounds)),
        out_specs=WHOLE,
        out_shape=shape_of((total, QUART, channels), BF16),
        compiler_params=params(),
        cost_estimate=cost(0, 6 * MIB),
        name="to_slots",
    )(slot_of, *keeps, *cames)


def adam_body(places, spot, own, near, far, cross, last_ref, master, first, second, *outs, block):
    out_master, out_first, out_second = outs
    core, plane = spot[0], spot[1]
    one_fix = 1.0 / (1.0 - BETA_ONE**STEP_COUNT)
    two_fix = 1.0 / (1.0 - BETA_TWO**STEP_COUNT)
    for s in range(block):
        bucket = places[0, pl.program_id(0) * block + s]
        for ref, c, p in (
            (own, core, plane),
            (near, 1 - core, plane),
            (far, core, 1 - plane),
            (cross, 1 - core, 1 - plane),
        ):
            rows = pl.ds(pl.multiple_of(c * HALF + p * QUART, QUART), QUART)
            grad = ref[s].astype(F32)
            grad = jnp.where(bucket == NB - 1, last_ref[rows, :], grad)
            grad = jnp.where(bucket < NB, grad, 0.0)
            old = master[s, rows, :]
            one = BETA_ONE * first[s, rows, :] + (1.0 - BETA_ONE) * grad
            two = BETA_TWO * second[s, rows, :] + (1.0 - BETA_TWO) * grad * grad
            out_first[s, rows, :] = one
            out_second[s, rows, :] = two
            step = one * one_fix / (jnp.sqrt(two * two_fix) + ADAM_EPS)
            out_master[s, rows, :] = old - LEARN_RATE * (step + WEIGHT_DECAY * old)


def adam(places, spot, quarters, last, master, first, second):
    slots, depth, channels = master.shape
    block = max(b for b in range(1, 10) if slots % b == 0)
    full = pl.BlockSpec((block, depth, channels), lambda i: (i, 0, 0))
    part = pl.BlockSpec((block, QUART, channels), lambda i: (i, 0, 0))
    return pl.pallas_call(
        functools.partial(adam_body, block=block),
        grid=(slots // block,),
        in_specs=[SCALARS, SCALARS] + [part] * 4 + [WHOLE, full, full, full],
        out_specs=[full] * 3,
        out_shape=[shape_of(master.shape, F32)] * 3,
        compiler_params=params(),
        cost_estimate=cost(0, 12 * MIB),
        name="adam",
    )(places, spot, *quarters, last, master, first, second)


def tie(*values):
    return lax.optimization_barrier(values)


def plus(*values):
    return sum([v.astype(F32) for v in values]).astype(BF16)


def local(frames_in, lengths, bw_ids, owner_list, master, moment1, moment2, wave_grad):
    rows, frames, channels = frames_in.shape
    slots = master.shape[0]
    utts = lengths.shape[1]
    owners = lax.axis_size("rows")
    seqs = lax.axis_size("seq")
    row_at = lax.axis_index("rows")
    seq_at = lax.axis_index("seq")
    core, plane = seq_at % 2, seq_at // 2
    ring = ring_of(owners)
    half_ring = owners // 2

    mine = lax.dynamic_slice_in_dim(master, core * HALF, HALF, axis=1).astype(BF16)

    starts = [jnp.zeros((rows, 1), jnp.int32)]
    for u in range(utts):
        starts.append(starts[-1] + lengths[:, u : u + 1])
    spot = jnp.broadcast_to(jnp.stack([seq_at * frames, core])[None, :], (rows, 2)).astype(jnp.int32)
    meta = jnp.concatenate(starts + [bw_ids, spot], axis=1)
    blocks = wave_grad.reshape(rows, frames, HOP)
    synth = jnp.asarray(synthesis_table())
    win = jnp.asarray(window_tables())

    low = shifted(frames_in[:, frames - EDGE :], 1)
    high = shifted(frames_in[:, :EDGE], -1)
    later = shifted(blocks[:, :EDGE], -1)
    if ring:
        offsets = [0]
        sources = [mine, seq_swap(mine, 1)]
        ahead = back = mine
        cot = None
        for hop in range(half_ring):
            source = (ahead, back)
            ahead = lax.ppermute(ahead, AXES, ring_step(ring, 1, seqs))
            if hop < half_ring - 1:
                back = lax.ppermute(back, AXES, ring_step(ring, -1, seqs))
            if hop in (1, 2):
                feed = tie(blocks, *source)[0]
                cot = spectrum_cotangent(hop - 1, cot, meta, feed, later, synth, win, utts)
                ahead, back, cot = tie(ahead, back, cot)
            sources += [ahead, seq_swap(ahead, 1)]
            offsets.append(-(hop + 1))
            if hop < half_ring - 1:
                sources += [back, seq_swap(back, 1)]
                offsets.append(hop + 1)
        order = jnp.asarray(ring, jnp.int32)
        ids = jnp.arange(owners, dtype=jnp.int32)
        where = jnp.sum(jnp.where(order == row_at, ids, 0))
        at = (where + jnp.asarray(offsets, jnp.int32)) % owners
        owner_ids = jnp.sum(jnp.where(at[:, None] == ids[None, :], order[None, :], 0), axis=1)
    else:
        gathered = lax.all_gather(mine, "rows", axis=0, tiled=True)
        sources = [gathered, seq_swap(gathered, 1)]
        owner_ids = jnp.arange(owners, dtype=jnp.int32)
        cot = None
        for r in range(rows):
            cot = spectrum_cotangent(r, cot, meta, blocks, later, synth, win, utts)

    bucket_index = jnp.arange(NB, dtype=jnp.int32)
    same = owner_list[None, :] == owner_list[:, None]
    rank = jnp.sum((same & (bucket_index[None, :] < bucket_index[:, None])).astype(jnp.int32), axis=1)

    def held_by(ids):
        targets = (ids[:, None] * slots + jnp.arange(slots, dtype=jnp.int32)[None, :]).reshape(-1)
        match = (owner_list * slots + rank)[None, :] == targets[:, None]
        return (NB + jnp.sum(match.astype(jnp.int32) * (bucket_index[None, :] - NB), axis=1))[None, :]

    places = held_by(owner_ids)
    held = held_by(row_at[None].astype(jnp.int32))
    place_at = jnp.arange(owners, dtype=jnp.int32)
    rel = jnp.sum(jnp.where(owner_list[:, None] == owner_ids[None, :], place_at[None, :], 0), axis=1)
    slot_of = (rel * slots + rank)[None, :]
    places, held, slot_of, meta = tie(places, held, slot_of, meta)

    (table, spec, act, der, ada, low_grad, resg, xc, rc, send, keep, tail, sums, hsum) = forward(
        meta, places, frames_in, low, high, cot, sources, utts
    )
    halo = shifted(spec.reshape(rows, frames, 2 * BIN_PAD)[:, frames - EDGE :], 1)

    keeps, cames, bounds = [], [], []

    def split(keep, came):
        both = plus(keep, came)
        stay = lax.dynamic_slice_in_dim(both, plane * QUART, QUART, axis=1)
        leave = lax.dynamic_slice_in_dim(both, (1 - plane) * QUART, QUART, axis=1)
        return stay, leave

    def record(stay, came, begins, per):
        for at, begin in enumerate(begins):
            keeps.append(stay[at * per : (at + 1) * per])
            cames.append(came[at * per : (at + 1) * per])
            bounds.append((begin, begin + per))

    per = CHUNK // BR
    pre, bsums = None, []
    begins, count = (2 * FF // BR,), 40
    for chunk in range(FF // CHUNK):
        near = seq_swap(send, 1)
        pre, next_send, next_keep, bsum = mlp_backward(chunk, pre, meta, low_grad, act, der, ada, table, utts)
        near, pre, next_send, next_keep = tie(near, pre, next_send, next_keep)
        bsums.append(bsum)
        stay, leave = split(keep, near)
        record(stay, seq_swap(leave, 2), begins, count)
        send, keep = next_send, next_keep
        begins, count = (chunk * per, FF // BR + chunk * per), per

    near = seq_swap(send, 1)
    cg0, edge0, parts = norm_backward(0, (), meta, frames_in, low, high, pre, table, xc, rc, utts)
    near, cg0, edge0, parts, pre = tie(near, cg0, edge0, parts, pre)
    stay, leave = split(keep, near)
    came = seq_swap(leave, 2)
    closing = (parts, tail, sums, hsum, *bsums)
    cg1, edge1, _, last = norm_backward(1, closing, meta, frames_in, low, high, pre, table, xc, rc, utts)
    came, cg1, edge1, last, spec = tie(came, cg1, edge1, last, spec)
    record(stay, came, begins, count)
    chunks = to_slots(slot_of, keeps, cames, tuple(bounds), owners * slots)
    edges = jnp.stack([edge0, edge1])

    state = {}

    def work(stage, *ready):
        if stage == 0:
            feed = tie(spec, *ready)[0]
            state["low"] = shifted(edges[:, 1], 1)
            state["high"] = shifted(edges[:, 0], -1)
            state["wave"] = wave_forward(0, None, meta, feed, halo, synth, win, rows, utts)
            return state["wave"]
        if stage == 1:
            feed = tie(cg0, *ready)[0]
            state["grad"] = conv_backward(
                0, None, meta, feed, state["low"], state["high"], resg, table, rows, utts
            )
            return state["grad"]
        if stage == 2:
            feed = tie(cg1, *ready)[0]
            state["grad"] = conv_backward(
                1, state["grad"], meta, feed, state["low"], state["high"], resg, table, rows, utts
            )
            return state["grad"]
        if stage == 3:
            feed = tie(spec, *ready)[0]
            state["wave"] = wave_forward(1, state["wave"], meta, feed, halo, synth, win, rows, utts)
            return state["wave"]
        return state["wave"]

    if ring:
        cut = {o: chunks[i * slots : (i + 1) * slots] for i, o in enumerate(offsets)}
        up, down = cut[-half_ring], cut[1 - half_ring]
        for hop in range(half_ring):
            left_over = half_ring - 1 - hop
            source = (up, down, last)
            up = lax.ppermute(up, AXES, ring_step(ring, 1, seqs))
            if hop < half_ring - 1:
                down = lax.ppermute(down, AXES, ring_step(ring, -1, seqs))
            if hop < 2:
                last = last + seq_swap(last, 1 << hop)
            else:
                last = last + rows_swap(last, 1 << (hop - 2))
            done = work(hop, *source)
            if hop in (0, 3):
                up, down, last, state["wave"] = tie(up, down, last, done)
            else:
                up, down, last, state["grad"] = tie(up, down, last, done)
            if left_over:
                up = plus(up, cut[left_over])
                if hop < half_ring - 2:
                    down = plus(down, cut[1 - left_over])
        own = plus(cut[0], up, down)
    else:
        own = lax.psum_scatter(chunks, "rows", scatter_dimension=0, tiled=True)
        last = lax.psum(last, AXES)
        for hop in range(4):
            work(hop, own)
    far = seq_swap(own, 2)
    near = seq_swap(own, 1)
    if ring:
        last = last + rows_swap(last, 4)
    waveform = state["wave"].reshape(rows, frames * HOP)
    far, waveform = tie(far, waveform)
    cross = seq_swap(far, 1)
    where_at = jnp.stack([core, plane]).astype(jnp.int32)
    new_master, new_first, new_second = adam(
        held, where_at, (own, near, far, cross), last, master, moment1, moment2
    )
    return waveform, state["grad"], new_master, new_first, new_second


def solution(mesh):
    in_specs = (
        P("rows", "seq", None),
        P("rows", None),
        P("rows", None),
        P(),
        P("rows", None, None),
        P("rows", None, None),
        P("rows", None, None),
        P("rows", "seq"),
    )
    out_specs = (
        P("rows", "seq"),
        P("rows", "seq", None),
        P("rows", None, None),
        P("rows", None, None),
        P("rows", None, None),
    )
    return jax.shard_map(local, mesh=mesh, in_specs=in_specs, out_specs=out_specs, check_vma=False)
```

```python
import functools
import math

import jax
import jax.numpy as jnp
import numpy as np
from jax import lax
from jax.experimental import pallas as pl
from jax.experimental.pallas import tpu as pltpu
from jax.sharding import PartitionSpec as P

FF = 1536
NFFT = 1280
HOP = 320
NBW = 4
KW = 7
UTT = 4
BR = 32
STEP_COUNT = 6
BINS = 641
NOUT = 1282
VROWS = 20
IN_ROWS = 3
HEAD_ROWS = 3
NB = 137

NORM_EPS = 1e-06
ENV_FLOOR = 0.5
BETA_ONE = 0.8
BETA_TWO = 0.9
LEARN_RATE = 0.04
WEIGHT_DECAY = 0.01
ADAM_EPS = 1e-08

LAPS = NFFT // HOP
RIM = (KW - 1) // 2
LAP_PAD = 384
BIN_PAD = 768
HALF = BR // 2
QUART = BR // 4
EDGE = 16
TILE = 256
CHUNK = 768
HALF_BIN = 384
PAIR = 5
LANE = 128
AXES = ("rows", "seq")

F32 = jnp.float32
BF16 = jnp.bfloat16
MIB = 1 << 20
VMEM_BYTES = 60 * MIB


def bin_order():
    order = np.full(BIN_PAD, -1)
    order[: (BINS + 1) // 2] = np.arange(0, BINS, 2)
    order[HALF_BIN : HALF_BIN + BINS // 2] = np.arange(1, BINS, 2)
    return order


def order_table():
    return (np.arange(BIN_PAD)[:, None] == bin_order()[None, :]).astype(jnp.bfloat16)


def synthesis_table():
    n = np.arange(2 * HOP)[None, :]
    order = bin_order()
    out = np.zeros((2, 2, HALF_BIN, 2, LAP_PAD), np.float32)
    for parity in range(2):
        k = order[parity * HALF_BIN : (parity + 1) * HALF_BIN]
        k = k[k >= 0][:, None]
        angle = (k * n % NFFT) * (2.0 * math.pi / NFFT)
        factor = np.where((k == 0) | (k == NFFT // 2), 1.0, 2.0) / NFFT
        out[parity, 0, : len(k), :, :HOP] = (factor * np.cos(angle)).reshape(-1, 2, HOP)
        out[parity, 1, : len(k), :, :HOP] = (-factor * np.sin(angle)).reshape(-1, 2, HOP)
    return out.reshape(2, BIN_PAD, 2 * LAP_PAD).astype(jnp.bfloat16)


def window_tables():
    window = 0.5 - 0.5 * np.cos(np.arange(NFFT) * (2.0 * math.pi / NFFT))
    rows = np.zeros((LAPS, LAP_PAD), np.float64)
    rows[:, :HOP] = window.reshape(LAPS, HOP)
    envelope = np.cumsum(rows**2, axis=0)
    return np.concatenate([rows, 1.0 / np.maximum(envelope, ENV_FLOOR)], axis=0).astype(np.float32)


def ring_of(count):
    if count != 8:
        return None
    return [0, 2, 4, 6, 7, 5, 3, 1]


def ring_step(ring, shift, seq_count):
    where = {r: i for i, r in enumerate(ring)}
    pairs = []
    for r in ring:
        target = ring[(where[r] + shift) % len(ring)]
        pairs += [(r * seq_count + s, target * seq_count + s) for s in range(seq_count)]
    return pairs


def seq_swap(value, bit):
    count = lax.axis_size("seq")
    return lax.ppermute(value, "seq", [(s, s ^ bit) for s in range(count)])


def rows_swap(value, bit):
    count = lax.axis_size("rows")
    return lax.ppermute(value, "rows", [(r, r ^ bit) for r in range(count)])


def shifted(value, distance):
    devices = range(lax.axis_size("seq"))
    return lax.ppermute(
        value, "seq", [(i - distance, i) for i in devices if i - distance in devices]
    )


def dot(a, b, dims):
    return lax.dot_general(a, b, (dims, ((), ())), preferred_element_type=F32)


NN = ((1,), (0,))
NT = ((1,), (1,))
TN = ((0,), (0,))


def frame_reach(meta, row, first, count, utts):
    index = first + lax.broadcasted_iota(jnp.int32, (count, 128), 0)
    start = jnp.zeros_like(index)
    end = jnp.zeros_like(index) + meta[row, 1]
    for u in range(1, utts):
        inside = index >= meta[row, u]
        start = jnp.where(inside, meta[row, u], start)
        end = jnp.where(inside, meta[row, u + 1], end)
    return index - start, end - 1 - index


def spans(count, size):
    return [(at, min(size, count - at)) for at in range(0, count, size)]


def over(table, base, reach, lane_tile, width=LANE):
    cut = slice(lane_tile * LANE, lane_tile * LANE + width)
    picked = jnp.broadcast_to(table[base + LAPS - 1 : base + LAPS, cut], (reach.shape[0], width))
    for j in range(LAPS - 2, -1, -1):
        picked = jnp.where(reach[:, :width] == j, table[base + j : base + j + 1, cut], picked)
    return picked


def keep_within(values, reach, left, offset):
    if offset < 0:
        return jnp.where(reach >= -offset, values, 0.0)
    if offset > 0:
        return jnp.where(left >= offset, values, 0.0)
    return values


def row_mean(values):
    return jnp.mean(values, axis=1, keepdims=True)


def fold(values):
    rows, columns = values.shape
    return jnp.sum(values.reshape(rows // 8, 8, columns), axis=0)


def sincos(angle):
    turns = jnp.round(angle * (0.5 / math.pi))
    rest = angle * 0.5 - turns * 3.1416015625
    rest = rest + turns * 8.908910206761537e-06
    sq = rest * rest
    sine = 1.0 + sq * (
        -0.16666656732559204
        + sq * (0.008333033882081509 + sq * (-0.00019807791977655143 + sq * 2.6022808015113696e-06))
    )
    cosine = 1.0 + sq * (
        -0.4999992549419403
        + sq * (0.04166382923722267 + sq * (-0.001385461655445397 + sq * 2.3163083824329078e-05))
    )
    sine = rest * sine
    double = sine + sine
    return double * cosine, 1.0 - double * sine


ANGLE_LIMIT = 1024.0


def params():
    return pltpu.CompilerParams(vmem_limit_bytes=VMEM_BYTES)


def cost(flops, bytes_accessed, transcendentals=0):
    return pl.CostEstimate(
        flops=int(flops), bytes_accessed=int(bytes_accessed), transcendentals=int(transcendentals)
    )


WHOLE = pl.BlockSpec(memory_space=pltpu.VMEM)
SCALARS = pl.BlockSpec(memory_space=pltpu.SMEM)
ANYWHERE = pl.BlockSpec(memory_space=pl.ANY)
shape_of = jax.ShapeDtypeStruct


def pre_body(meta, wave_ref, halo_ref, synth_ref, win_ref, *rest, start, tiles, rows, utts):
    out_ref, flat, scaled_all, even_all, odd_all = rest[-5:]
    step = pl.program_id(0)
    tile = start + step
    lines = PAIR * TILE
    extra = PAIR * EDGE
    count = TILE + EDGE
    lane = lax.broadcasted_iota(jnp.int32, (count // 2, LANE), 1)
    for at, size in spans(lines, 320):
        rows_at = pl.ds(pl.multiple_of(tile * lines + at, 16), size)
        flat[at : at + size, :] = wave_ref[rows_at, :].astype(F32)
    after = jnp.minimum((tile + 1) * lines, tiles * lines - extra)
    following = wave_ref[pl.ds(pl.multiple_of(after, 16), extra), :]
    flat[lines:, :] = jnp.where(tile == tiles - 1, halo_ref[...], following).astype(F32)
    for r in range(rows):
        scaled, even, odd = scaled_all.at[r], even_all.at[r], odd_all.at[r]
        base = meta[r, 2 * utts + 1] + tile * TILE
        part = [flat[pl.ds(2 * k + r, count // 2, stride=2 * PAIR), :] for k in range(PAIR)]
        turned = [pltpu.roll(v, LANE // 2, 1) for v in part[2:]]
        front = lane < LANE // 2
        frame = (
            part[0],
            part[1],
            jnp.where(front, part[2], 0.0),
            jnp.where(front, turned[0], turned[1]),
            jnp.where(front, turned[1], turned[2]),
            jnp.where(front, turned[2], 0.0),
        )
        for c in range(3):
            scaled[c, pl.ds(0, count // 2, stride=2), :] = frame[c]
            scaled[c, pl.ds(1, count // 2, stride=2), :] = frame[3 + c]
        for at, size in spans(count, 32):
            reach, _ = frame_reach(meta, r, base + at, size, utts)
            for c in range(3):
                scaled[c, at : at + size, :] = scaled[c, at : at + size, :] * over(win_ref, LAPS, reach, c)
        for at, size in spans(TILE, 32):
            _, left = frame_reach(meta, r, base + at, size, utts)
            for j in range(2):
                for c in range(3):
                    span = slice(c * LANE, (c + 1) * LANE)

                    def lap(i):
                        value = scaled[c, at + i : at + i + size, :] * win_ref[i : i + 1, span]
                        return keep_within(value, None, left, i).astype(BF16).astype(F32)

                    one, two = lap(j), lap(j + 2)
                    column = slice(j * LAP_PAD + c * LANE, j * LAP_PAD + (c + 1) * LANE)
                    even[at : at + size, column] = (one + two).astype(BF16)
                    odd[at : at + size, column] = (one - two).astype(BF16)
        out_ref[r, :, 0:BIN_PAD] = dot(even[...], synth_ref[0], NT).astype(BF16)
        out_ref[r, :, BIN_PAD:] = dot(odd[...], synth_ref[1], NT).astype(BF16)


def spectrum_cotangent(start, stop, before, meta, wave, halo, synth, win, rows, utts):
    tiles = wave.shape[0] // (PAIR * TILE)
    frames = tiles * TILE
    more = [] if before is None else [before]
    steps = stop - start
    return pl.pallas_call(
        functools.partial(pre_body, start=start, tiles=tiles, rows=rows, utts=utts),
        grid=(steps,),
        in_specs=[SCALARS, WHOLE, WHOLE, WHOLE, WHOLE] + [ANYWHERE] * len(more),
        out_specs=pl.BlockSpec((rows, TILE, 2 * BIN_PAD), lambda i: (0, start + i, 0)),
        out_shape=shape_of((rows, frames, 2 * BIN_PAD), BF16),
        input_output_aliases={5: 0} if more else {},
        scratch_shapes=[
            pltpu.VMEM((PAIR * (TILE + EDGE), LANE), F32),
            pltpu.VMEM((rows, LAP_PAD // LANE, TILE + EDGE, LANE), F32),
            pltpu.VMEM((rows, TILE, BIN_PAD), BF16),
            pltpu.VMEM((rows, TILE, BIN_PAD), BF16),
        ],
        compiler_params=params(),
        cost_estimate=cost(4 * rows * steps * TILE * 768 * 768, rows * steps * TILE * 3072 + 4 * MIB),
        name=f"spectrum_cotangent_{start}",
    )(meta, wave, halo, synth, win, *more)


def place_parts(places, counts, core, pieces, table, sem, slots, owners, start):
    for index, ref in enumerate(pieces):
        side = core if index % 2 == 0 else 1 - core
        owner = owners[index // 2]

        def one(s, carry, ref=ref, side=side, owner=owner):
            bucket = places[0, owner * slots + s]
            at = pl.multiple_of(bucket * BR + side * HALF, HALF)
            copy = pltpu.make_async_copy(ref.at[s], table.at[pl.ds(at, HALF), :], sem)
            if start:
                copy.start()
            else:
                copy.wait()
            return carry

        lax.fori_loop(0, counts[0, owner], one, 0)


def assemble_body(places, counts, core, *refs, slots, owners):
    pieces, table, sem = refs[: 2 * len(owners)], refs[-2], refs[-1]
    place_parts(places, counts, core[0], pieces, table, sem, slots, owners, True)
    place_parts(places, counts, core[0], pieces, table, sem, slots, owners, False)


def assemble(owners, places, counts, core, pieces, slots):
    channels = pieces[0].shape[2]
    return pl.pallas_call(
        functools.partial(assemble_body, slots=slots, owners=owners),
        in_specs=[SCALARS, SCALARS, SCALARS] + [ANYWHERE] * len(pieces),
        out_specs=WHOLE,
        out_shape=shape_of((NB * BR, channels), BF16),
        scratch_shapes=[pltpu.SemaphoreType.DMA],
        compiler_params=params(),
        cost_estimate=cost(0, 12 * MIB),
        name="assemble",
    )(places, counts, core, *pieces)


def take_body(slot_of, ref, out, sem):
    def copy(b):
        return pltpu.make_async_copy(ref.at[slot_of[0, b]], out.at[b], sem)

    def start(b, carry):
        copy(b).start()
        return carry

    def wait(b, carry):
        copy(b).wait()
        return carry

    lax.fori_loop(0, NB, start, 0)
    lax.fori_loop(0, NB, wait, 0)


def take_slots(slot_of, gathered):
    return pl.pallas_call(
        take_body,
        in_specs=[SCALARS, ANYWHERE],
        out_specs=WHOLE,
        out_shape=shape_of((NB, *gathered.shape[1:]), BF16),
        scratch_shapes=[pltpu.SemaphoreType.DMA],
        compiler_params=params(),
        cost_estimate=cost(0, 6 * MIB),
        name="take_slots",
    )(slot_of, gathered)


def fill_frames(xs, x_ref, low_ref, high_ref, row, tile, tiles, channels):
    first = pl.multiple_of(tile * TILE, TILE)

    def put(at, block):
        block = block.astype(F32)
        for c in range(channels // LANE):
            xs[c, at : at + block.shape[0], :] = block[:, c * LANE : (c + 1) * LANE]

    for at, size in spans(TILE, 64):
        put(EDGE + at, x_ref[row, pl.ds(pl.multiple_of(first + at, 64), size), :])

    before = x_ref[row, pl.ds(pl.multiple_of(jnp.maximum(first - EDGE, 0), EDGE), EDGE), :]
    put(0, jnp.where(tile == 0, low_ref[row], before))
    end = jnp.minimum(first + TILE, (tiles - 1) * TILE)
    after = x_ref[row, pl.ds(pl.multiple_of(end, EDGE), EDGE), :]
    put(EDGE + TILE, jnp.where(tile == tiles - 1, high_ref[row], after))


def by_utterance(meta, row, utts, index, rows_of):
    value = jnp.broadcast_to(rows_of(0), (index.shape[0], LANE))
    for u in range(1, utts):
        value = jnp.where(index >= meta[row, u], rows_of(u), value)
    return value


def pick_rows(meta, row, utts, vec, out, channels):
    for u in range(utts):
        wanted = meta[row, utts + 1 + u]
        for at, offset in ((u, KW + 1), (utts + u, KW + 1 + NBW)):
            value = vec(offset)
            for b in range(1, NBW):
                value = jnp.where(wanted == b, vec(offset + b), value)
            out[at : at + 1, :] = value


def interleave(ones, others):
    at = 0
    for i, one in enumerate(ones):
        one()
        until = (i + 1) * len(others) // len(ones)
        for other in others[at:until]:
            other()
        at = until


def forward_body(meta, places, counts, x_ref, low_ref, high_ref, order_ref, cot_ref, *rest, owners, slots, tiles, count, utts):
    pieces = rest[: 2 * len(owners)]
    table_in = rest[2 * len(owners)]
    (
        table_out,
        spec_ref,
        act_ref,
        pre_ref,
        ada_ref,
        lowg_ref,
        resg_ref,
        xc_ref,
        rc_ref,
        send_ref,
        keep_ref,
        tail_ref,
        sums_ref,
        bsum_ref,
        table,
        xs,
        w_head,
        b_head,
        vecs,
        picks,
        grad,
        lines,
        hg,
        hg_old,
        logs_ref,
        angle_ref,
        ngrad_ref,
        slim,
        xn_ref,
        normed,
        normed_old,
        branch_ref,
        rn_ref,
        slow,
        sem,
        sems,
    ) = rest[2 * len(owners) + 1 :]
    step = pl.program_id(0)
    core = meta[0, 2 * utts + 2]
    channels = x_ref.shape[2]
    lane_tiles = channels // LANE
    now = jnp.minimum(step, count - 1)
    row, tile = now // tiles, now % tiles
    vec = lambda v: vecs[2 + v : 3 + v, :]
    vec_at = KW + 1 + 2 * NBW
    head_at = 2 * FF

    def store():
        return pltpu.make_async_copy(table, table_out, sems.at[1])

    @pl.when(step == 0)
    def _():
        whole = pltpu.make_async_copy(table_in, table, sems.at[0])
        whole.start()
        normed[...] = jnp.zeros_like(normed)
        w_head[...] = jnp.zeros_like(w_head)
        b_head[...] = jnp.zeros_like(b_head)
        whole.wait()
        place_parts(places, counts, core, pieces, table, sem, slots, owners, True)
        place_parts(places, counts, core, pieces, table, sem, slots, owners, False)
        store().start()
        vecs[...] = table[head_at + 1280 : head_at + 1280 + BR, :].astype(F32)

    @pl.when(step == 1)
    def _():
        sums_ref[...] = jnp.zeros_like(sums_ref)
        bsum_ref[...] = jnp.zeros_like(bsum_ref)

    @pl.when(step == 2)
    def _():
        grad[...] = jnp.zeros_like(grad)

    @pl.when(tile == 0)
    def _():
        pick_rows(meta, row, utts, vec, picks, channels)

    base = meta[row, 2 * utts + 1] + tile * TILE
    fill_frames(xs, x_ref, low_ref, high_ref, row, tile, tiles, channels)

    def convolve(at, size):
        reach, left = frame_reach(meta, row, base + at, size, utts)
        index = base + at + lax.broadcasted_iota(jnp.int32, (size, LANE), 0)
        conv = []
        for c in range(lane_tiles):
            cut = slice(c * LANE, (c + 1) * LANE)
            total = vecs[2 + KW : 3 + KW, cut]
            for k in range(KW):
                offset = k - RIM
                moved = xs[c, EDGE + offset + at : EDGE + offset + at + size, :]
                total = total + keep_within(moved, reach, left, offset) * vecs[2 + k : 3 + k, cut]
            conv.append(total)
        mean = jnp.sum(sum(conv), axis=1, keepdims=True) * (1.0 / channels)
        conv = [v - mean for v in conv]
        square = jnp.sum(sum([v * v for v in conv]), axis=1, keepdims=True) * (1.0 / channels)
        rc = jnp.broadcast_to(lax.rsqrt(square + NORM_EPS), (size, LANE))
        rc_ref[at : at + size, :] = rc
        for c in range(lane_tiles):
            cut = slice(c * LANE, (c + 1) * LANE)
            xc = conv[c] * rc
            xc_ref[at : at + size, cut] = xc
            scale = by_utterance(meta, row, utts, index, lambda u: picks[u : u + 1, cut])
            shift = by_utterance(meta, row, utts, index, lambda u: picks[utts + u : utts + u + 1, cut])
            ada_ref[at : at + size, cut] = (xc * scale + shift).astype(BF16)

    def head(at, size, turn):
        span = slice(at, at + size)
        for c in range(0, BIN_PAD, LANE):
            bins, angles = slice(c, c + LANE), slice(BIN_PAD + c, BIN_PAD + c + LANE)
            parity, inner = c // HALF_BIN, c % HALF_BIN
            reals = slice(parity * BIN_PAD + inner, parity * BIN_PAD + inner + LANE)
            imags = slice(reals.start + HALF_BIN, reals.stop + HALF_BIN)
            angle = angle_ref[span, bins] + b_head[0:1, angles]
            scale = jnp.exp(logs_ref[span, bins] + b_head[0:1, bins])
            sine, cosine = turn(angle)
            real, imag = scale * cosine, scale * sine
            spec_ref[span, reals] = real.astype(BF16)
            spec_ref[span, imags] = imag.astype(BF16)
            dre = cot_ref[span, reals].astype(F32)
            dim = cot_ref[span, imags].astype(F32)
            hg[span, bins] = (dre * real + dim * imag).astype(BF16)
            hg[span, angles] = (dim * real - dre * imag).astype(BF16)

    def gelu(at, size, c):
        for d in range(c * 512, (c + 1) * 512, 256):
            cut = slice(d, d + 256)
            bias = vecs[2 + VROWS + c : 3 + VROWS + c, d - c * 512 : d - c * 512 + 256]
            pre = pre_ref[at : at + size, cut] + bias
            phi = 0.5 + 0.5 * lax.erf(pre * math.sqrt(0.5))
            act_ref[at : at + size, cut] = (pre * phi).astype(BF16)

    def second_norm(at, size):
        span = slice(at, at + size)
        branch = slim[span, :] + vec(vec_at)
        branch_ref[span, :] = branch
        x = jnp.concatenate([xs[c, EDGE + at : EDGE + at + size, :] for c in range(lane_tiles)], axis=1)
        residual = x + vec(vec_at + 1) * branch
        residual = residual - row_mean(residual)
        rn = lax.rsqrt(row_mean(residual * residual) + NORM_EPS)
        rn_ref[span, :] = jnp.broadcast_to(rn, (size, LANE))
        xn = residual * rn
        xn_ref[span, :] = xn
        normed[span, :] = (xn * vec(vec_at + 2) + vec(vec_at + 3)).astype(BF16)

    def second_norm_back(at, size, sums):
        span = slice(at, at + size)
        ngrad = ngrad_ref[span, :]
        xn = xn_ref[span, :]
        e = ngrad * vec(vec_at + 2)
        resg = rn_ref[span, 0:1] * (e - row_mean(e) - xn * row_mean(e * xn))
        resg_ref[span, :] = resg
        low = (vec(vec_at + 1) * resg).astype(BF16)
        lowg_ref[span, :] = low
        return (
            sums[0] + fold(low.astype(F32)),
            sums[1] + fold(resg * branch_ref[span, :]),
            sums[2] + fold(ngrad * xn),
            sums[3] + fold(ngrad),
        )

    def head_dots(ref, begin):
        def one(c):
            ref[:, c : c + 256] = dot(normed[...], w_head[begin + c : begin + c + 256, :], NT)

        return [functools.partial(one, c) for c in range(0, BIN_PAD, 256)]

    def hidden_dot(c):
        pre_ref[:, c : c + 256] = dot(ada_ref[...], table[c : c + 256, :], NT)

    def grad_dot(c):
        grad[c : c + 256, :] += dot(hg_old[:, c : c + 256], normed_old[...], TN)

    interleave(
        head_dots(logs_ref, 0) + head_dots(angle_ref, BIN_PAD),
        [functools.partial(convolve, at, size) for at, size in spans(TILE, 32)],
    )
    interleave(
        [functools.partial(hidden_dot, c) for c in range(0, FF, 256)]
        + [functools.partial(grad_dot, c) for c in range(0, 2 * BIN_PAD, 256)],
        [functools.partial(head, at, size, sincos) for at, size in spans(TILE, 16)],
    )

    @pl.when((step > 0) & (slow[0] > 0))
    def _():
        def again(i, carry):
            rows = pl.ds(pl.multiple_of(i * 32, 32), 32)
            for c in range(0, BIN_PAD, LANE):
                bins, angles = slice(c, c + LANE), slice(BIN_PAD + c, BIN_PAD + c + LANE)
                parity, inner = c // HALF_BIN, c % HALF_BIN
                reals = slice(parity * BIN_PAD + inner, parity * BIN_PAD + inner + LANE)
                imags = slice(reals.start + HALF_BIN, reals.stop + HALF_BIN)
                angle = angle_ref[rows, bins] + b_head[0:1, angles]
                scale = jnp.exp(logs_ref[rows, bins] + b_head[0:1, bins])
                real, imag = scale * jnp.cos(angle), scale * jnp.sin(angle)
                spec_ref[rows, reals] = real.astype(BF16)
                spec_ref[rows, imags] = imag.astype(BF16)
                dre = cot_ref[rows, reals].astype(F32)
                dim = cot_ref[rows, imags].astype(F32)
                hg[rows, bins] = (dre * real + dim * imag).astype(BF16)
                hg[rows, angles] = (dim * real - dre * imag).astype(BF16)
            return carry

        lax.fori_loop(0, TILE // 32, again, 0)

    @pl.when(step == 0)
    def _():
        last = vecs[...]
        line = jnp.concatenate([last[25:26], last[26:27], last[27:28]], axis=1)
        line = jnp.broadcast_to(line, (16, 3 * channels))
        moved = pltpu.roll(line, 3 * channels - BINS, 1)
        for at, value in ((0, line), (BIN_PAD, moved)):
            picked = dot(value[:, 0:BIN_PAD].astype(BF16), order_ref[...], NN)
            b_head[:, at : at + BIN_PAD] = picked[0:8]
        inside = lax.broadcasted_iota(jnp.int32, (336, LANE), 0)
        for c in range(lane_tiles):
            cut = slice(c * LANE, (c + 1) * LANE)
            lines[c, 0:1312, :] = table[head_at : head_at + 1312, cut].astype(F32)
            lines[c, 1312:, :] = jnp.zeros((lines.shape[1] - 1312, LANE), F32)
            for part, start in ((0, 0), (BIN_PAD, BINS)):
                evens = lines[c, pl.ds(start, 336, stride=2), :]
                w_head[part : part + 336, cut] = jnp.where(inside < (BINS + 1) // 2, evens, 0.0).astype(BF16)
                odds = lines[c, pl.ds(start + 1, 320, stride=2), :]
                w_head[part + HALF_BIN : part + HALF_BIN + 320, cut] = odds.astype(BF16)
        longest = jnp.zeros((8, 1), F32)
        for at, size in spans(BIN_PAD, 64):
            weights = w_head[BIN_PAD + at : BIN_PAD + at + size, :].astype(F32)
            length = jnp.sum(weights * weights, axis=1, keepdims=True)
            longest = jnp.maximum(longest, jnp.max(length.reshape(size // 8, 8, 1), axis=0))
        gain, shift = jnp.abs(vec(vec_at + 2)), vec(vec_at + 3)
        normed_length = math.sqrt(channels) * jnp.max(gain) + jnp.sqrt(jnp.sum(shift * shift, keepdims=True))[0, 0]
        bound = 1.05 * normed_length * jnp.max(jnp.sqrt(longest)) + jnp.max(jnp.abs(b_head[:, BIN_PAD:]))
        slow[0] = jnp.where(bound < ANGLE_LIMIT, 0, 1)

    def ngrad_dot(c):
        ngrad_ref[:, c : c + 256] = dot(hg[...], w_head[:, c : c + 256], NN)

    def branch_dot(c):
        slim[:, c : c + 256] = dot(act_ref[...], table[FF : 2 * FF, c : c + 256], NN)

    interleave(
        [functools.partial(ngrad_dot, c) for c in range(0, channels, 256)],
        [functools.partial(gelu, at, size, c) for c in range(IN_ROWS) for at, size in spans(TILE, 32)],
    )
    sums = [sums_ref[v] for v in range(4)]

    def back(at, size):
        sums[:] = second_norm_back(at, size, sums)

    interleave(
        [functools.partial(branch_dot, c) for c in range(0, channels, 256)],
        [functools.partial(back, at, size) for at, size in spans(TILE, 16)],
    )
    for v in range(4):
        sums_ref[v] = sums[v]
    for c in range(0, 2 * BIN_PAD, 512):
        total = bsum_ref[:, c : c + 512]
        for at, size in spans(TILE, 32):
            total = total + fold(hg[at : at + size, c : c + 512].astype(F32))
        bsum_ref[:, c : c + 512] = total
    hg_old[...] = hg[...]
    normed_old[...] = normed[...]
    for at, size in spans(TILE, 16):
        second_norm(at, size)

    @pl.when(step == count)
    def _():
        for c in range(0, 2 * BIN_PAD, 256):
            grad_dot(c)
        for c in range(lane_tiles):
            cut = slice(c * LANE, (c + 1) * LANE)
            for part, start in ((0, 0), (BIN_PAD, BINS)):
                lines[c, pl.ds(start + 1, 320, stride=2), :] = grad[part + HALF_BIN : part + HALF_BIN + 320, cut]
                lines[c, pl.ds(start, 320, stride=2), :] = grad[part : part + 320, cut]
                lines[c, start + 640 : start + 641, :] = grad[part + 320 : part + 321, cut]
            for b in range(40):
                low_half = lines[c, b * BR : b * BR + HALF, :].astype(BF16)
                high_half = lines[c, b * BR + HALF : b * BR + BR, :].astype(BF16)
                keep_ref[b, :, cut] = jnp.where(core == 0, low_half, high_half)
                send_ref[b, :, cut] = jnp.where(core == 0, high_half, low_half)
            tail_ref[:, cut] = lines[c, 1280:1288, :]
        store().wait()


def forward(owners, meta, places, counts, x, low, high, order, cot, pieces, table, utts):
    rows, frames, channels = x.shape
    tiles = frames // TILE
    steps = rows * tiles
    count = rows * frames
    slots = pieces[0].shape[0]
    ahead = lambda i: jnp.minimum(i, steps - 1)
    behind = lambda i: jnp.maximum(i - 1, 0)
    wide = pl.BlockSpec((TILE, FF), lambda i: (ahead(i), 0))
    wide_late = pl.BlockSpec((None, TILE, FF), lambda i: (behind(i) // tiles, behind(i) % tiles, 0))
    slim = pl.BlockSpec((TILE, channels), lambda i: (ahead(i), 0))
    slim_late = pl.BlockSpec((TILE, channels), lambda i: (behind(i), 0))
    return pl.pallas_call(
        functools.partial(forward_body, owners=owners, slots=slots, tiles=tiles, count=steps, utts=utts),
        grid=(steps + 1,),
        in_specs=[SCALARS, SCALARS, SCALARS, WHOLE, WHOLE, WHOLE, WHOLE, wide_late]
        + [ANYWHERE] * (len(pieces) + 1),
        out_specs=[ANYWHERE, wide_late, wide, wide, slim, slim_late, slim_late, slim]
        + [pl.BlockSpec((TILE, LANE), lambda i: (ahead(i), 0))]
        + [WHOLE] * 5,
        out_shape=[
            shape_of((NB * BR, channels), BF16),
            shape_of((rows, frames, 2 * BIN_PAD), BF16),
            shape_of((count, FF), BF16),
            shape_of((count, FF), F32),
            shape_of((count, channels), BF16),
            shape_of((count, channels), BF16),
            shape_of((count, channels), F32),
            shape_of((count, channels), F32),
            shape_of((count, LANE), F32),
            shape_of((40, HALF, channels), BF16),
            shape_of((40, HALF, channels), BF16),
            shape_of((8, channels), F32),
            shape_of((4, 8, channels), F32),
            shape_of((8, 2 * BIN_PAD), F32),
        ],
        scratch_shapes=[
            pltpu.VMEM((NB * BR, channels), BF16),
            pltpu.VMEM((channels // LANE, TILE + 2 * EDGE, LANE), F32),
            pltpu.VMEM((2 * BIN_PAD, channels), BF16),
            pltpu.VMEM((8, 2 * BIN_PAD), F32),
            pltpu.VMEM((BR, channels), F32),
            pltpu.VMEM((2 * utts, channels), F32),
            pltpu.VMEM((2 * BIN_PAD, channels), F32),
            pltpu.VMEM((channels // LANE, 1344, LANE), F32),
            pltpu.VMEM((TILE, 2 * BIN_PAD), BF16),
            pltpu.VMEM((TILE, 2 * BIN_PAD), BF16),
            pltpu.VMEM((TILE, BIN_PAD), F32),
            pltpu.VMEM((TILE, BIN_PAD), F32),
            pltpu.VMEM((TILE, channels), F32),
            pltpu.VMEM((TILE, channels), F32),
            pltpu.VMEM((TILE, channels), F32),
            pltpu.VMEM((TILE, channels), BF16),
            pltpu.VMEM((TILE, channels), BF16),
            pltpu.VMEM((TILE, channels), F32),
            pltpu.VMEM((TILE, LANE), F32),
            pltpu.SMEM((1,), jnp.int32),
            pltpu.SemaphoreType.DMA,
            pltpu.SemaphoreType.DMA((2,)),
        ],
        compiler_params=params(),
        cost_estimate=cost(10 * count * 1536 * 512, 40 * MIB, count * 4096),
        name="forward",
    )(meta, places, counts, x, low, high, order, cot, *pieces, table)


def mlp_body(meta, low_ref, act_ref, hidden_ref, ada_ref, wout_ref, last_ref, *rest, chunk, utts):
    pre_ref, send_ref, keep_ref, bsum_ref, gout, gin, agrad, bias = rest[-8:]
    step = pl.program_id(0)
    core = meta[0, 2 * utts + 2]
    tile, channels = low_ref.shape

    @pl.when(step == 0)
    def _():
        gout[...] = jnp.zeros_like(gout)
        gin[...] = jnp.zeros_like(gin)
        bsum_ref[...] = jnp.zeros_like(bsum_ref)
        last = last_ref[...].astype(F32)
        line = jnp.concatenate([last[2 + VROWS + c : 3 + VROWS + c] for c in range(IN_ROWS)], axis=1)
        bias[...] = jnp.broadcast_to(line[:, chunk * CHUNK : (chunk + 1) * CHUNK], (8, CHUNK))

    def agrad_dot(c):
        agrad[:, c : c + 256] = dot(low_ref[...], wout_ref[c : c + 256, :], NT)

    def gout_dot(c):
        gout[c : c + 256, :] += dot(act_ref[:, c : c + 256], low_ref[...], TN)

    def gin_dot(c):
        gin[c : c + 256, :] += dot(pre_ref[:, c : c + 256], ada_ref[...], TN)

    def slope(c):
        cut = slice(c, c + 256)
        total = bsum_ref[:, cut]
        for at, size in spans(tile, 32):
            span = slice(at, at + size)
            value = hidden_ref[span, cut] + bias[0:1, cut]
            phi = 0.5 + 0.5 * lax.erf(value * math.sqrt(0.5))
            bell = jnp.exp(-0.5 * value * value) * (1.0 / math.sqrt(2.0 * math.pi))
            pre = (agrad[span, cut] * (phi + value * bell)).astype(BF16)
            pre_ref[span, cut] = pre
            total = total + fold(pre.astype(F32))
        bsum_ref[:, cut] = total

    cuts = range(0, CHUNK, 256)
    for c in cuts:
        agrad_dot(c)
    interleave([functools.partial(gout_dot, c) for c in cuts], [functools.partial(slope, c) for c in cuts])
    for c in cuts:
        gin_dot(c)

    @pl.when(step == pl.num_programs(0) - 1)
    def _():
        buckets = CHUNK // BR
        for at, ref in ((0, gin), (buckets, gout)):
            for b in range(buckets):
                low_half = ref[b * BR : b * BR + HALF, :].astype(BF16)
                high_half = ref[b * BR + HALF : b * BR + BR, :].astype(BF16)
                keep_ref[at + b] = jnp.where(core == 0, low_half, high_half)
                send_ref[at + b] = jnp.where(core == 0, high_half, low_half)


def mlp_backward(chunk, before, meta, low, act, hidden, ada, table, utts):
    count, channels = low.shape
    tile = 512
    slim = pl.BlockSpec((tile, channels), lambda i: (i, 0))
    part = pl.BlockSpec((tile, CHUNK), lambda i: (i, chunk))
    buckets = 2 * CHUNK // BR
    more = [] if before is None else [before]
    return pl.pallas_call(
        functools.partial(mlp_body, chunk=chunk, utts=utts),
        grid=(count // tile,),
        in_specs=[
            SCALARS,
            slim,
            part,
            part,
            slim,
            pl.BlockSpec((CHUNK, channels), lambda i: (FF // CHUNK + chunk, 0)),
            pl.BlockSpec((BR, channels), lambda i: (NB - 1, 0)),
        ]
        + [ANYWHERE] * len(more),
        out_specs=[part, WHOLE, WHOLE, WHOLE],
        out_shape=[
            shape_of((count, FF), BF16),
            shape_of((buckets, HALF, channels), BF16),
            shape_of((buckets, HALF, channels), BF16),
            shape_of((8, CHUNK), F32),
        ],
        input_output_aliases={7: 0} if more else {},
        scratch_shapes=[
            pltpu.VMEM((CHUNK, channels), F32),
            pltpu.VMEM((CHUNK, channels), F32),
            pltpu.VMEM((tile, CHUNK), F32),
            pltpu.VMEM((8, CHUNK), F32),
        ],
        compiler_params=params(),
        cost_estimate=cost(6 * count * CHUNK * 512, 16 * MIB),
        name=f"mlp_backward_{chunk}",
    )(meta, low, act, hidden, ada, table, table, *more)


def norm_body(
    meta, x_ref, low_ref, high_ref, pre_ref, w_in, last_ref, xc_ref, rc_ref, *rest, row, tiles, utts, closing
):
    more = rest[: 7 if closing else 0]
    outs = rest[len(more) :]
    cg_ref, edge_ref, part_ref = outs[:3]
    xs, vecs, picks, agrad, cg, reaches = outs[-6:]
    tile = pl.program_id(0)
    channels = x_ref.shape[2]
    lane_tiles = channels // LANE
    base = meta[row, 2 * utts + 1] + tile * TILE
    vec = lambda v: vecs[2 + v : 3 + v, :]

    @pl.when(tile == 0)
    def _():
        vecs[...] = last_ref[...].astype(F32)
        part_ref[...] = more[0][...] if closing else jnp.zeros_like(part_ref)
        pick_rows(meta, row, utts, vec, picks, channels)

    agrad[...] = dot(pre_ref[...], w_in[...], NN)
    fill_frames(xs, x_ref, low_ref, high_ref, row, tile, tiles, channels)
    for at, size in spans(TILE, 32):
        span = slice(at, at + size)
        reach, left = frame_reach(meta, row, base + at, size, utts)
        reaches[0, span, :] = reach
        reaches[1, span, :] = left
        index = base + at + lax.broadcasted_iota(jnp.int32, (size, LANE), 0)
        ecs, xcs = [], []
        for c in range(lane_tiles):
            cut = slice(c * LANE, (c + 1) * LANE)
            scale = by_utterance(meta, row, utts, index, lambda u: picks[u : u + 1, cut])
            ecs.append(agrad[span, cut] * scale)
            xcs.append(xc_ref[span, cut])
        m_one = jnp.sum(sum(ecs), axis=1, keepdims=True) * (1.0 / channels)
        m_two = jnp.sum(sum([e * v for e, v in zip(ecs, xcs)]), axis=1, keepdims=True) * (1.0 / channels)
        rc = rc_ref[span, :]
        for c in range(lane_tiles):
            cut = slice(c * LANE, (c + 1) * LANE)
            value = rc * (ecs[c] - m_one - xcs[c] * m_two)
            cg[c, span, :] = value
            cg_ref[span, cut] = value
    for u in range(utts):
        begin, end = meta[row, u], meta[row, u + 1]

        @pl.when((begin < base + TILE) & (end > base))
        def _(u=u, begin=begin, end=end):
            wanted = meta[row, utts + 1 + u]
            for c in range(lane_tiles):
                cut = slice(c * LANE, (c + 1) * LANE)
                one = jnp.zeros((8, LANE), F32)
                two = jnp.zeros((8, LANE), F32)
                for at, size in spans(TILE, 64):
                    span = slice(at, at + size)
                    index = base + at + lax.broadcasted_iota(jnp.int32, (size, LANE), 0)
                    value = jnp.where((index >= begin) & (index < end), agrad[span, cut], 0.0)
                    one = one + fold(value * xc_ref[span, cut])
                    two = two + fold(value)
                part_ref[KW + 1 + wanted, :, cut] += one
                part_ref[KW + 1 + NBW + wanted, :, cut] += two

    for c in range(lane_tiles):
        cut = slice(c * LANE, (c + 1) * LANE)
        sums = [part_ref[k, :, cut] for k in range(KW + 1)]
        for at, size in spans(TILE, 32):
            span = slice(at, at + size)
            reach, left = reaches[0, span, :], reaches[1, span, :]
            value = cg[c, span, :]
            for k in range(KW):
                offset = k - RIM
                moved = xs[c, EDGE + offset + at : EDGE + offset + at + size, :] * value
                sums[k] = sums[k] + fold(keep_within(moved, reach, left, offset))
            sums[KW] = sums[KW] + fold(value)
        for k in range(KW + 1):
            part_ref[k, :, cut] = sums[k]

    @pl.when(tile == 0)
    def _():
        edge_ref[0] = cg_ref[0:8, :]

    @pl.when(tile == tiles - 1)
    def _():
        edge_ref[1] = cg_ref[TILE - 8 : TILE, :]

    if closing:
        _, tail_ref, sums_ref, hsum_ref, bsum0, bsum1, order_ref = more
        vec_ref = outs[3]

        @pl.when(tile == tiles - 1)
        def _():
            vec_ref[0:8, :] = jnp.zeros((8, channels), F32)
            vec_ref[0:2, :] = tail_ref[0:2, :]
            for v in range(VROWS):
                at = v - (KW + 1 + 2 * NBW)
                rows_of = part_ref[v] if at < 0 else sums_ref[at]
                vec_ref[2 + v : 3 + v, :] = jnp.sum(rows_of, axis=0, keepdims=True)
            line = jnp.concatenate([bsum0[...], bsum1[...]], axis=1)
            for c in range(IN_ROWS):
                at = 2 + VROWS + c
                vec_ref[at : at + 1, :] = jnp.sum(
                    line[:, c * channels : (c + 1) * channels], axis=0, keepdims=True
                )

            def bins(value):
                value = jnp.broadcast_to(jnp.sum(value, axis=0, keepdims=True), (16, BIN_PAD))
                total = jnp.zeros((16, BIN_PAD), F32)
                for _ in range(3):
                    part = value.astype(BF16)
                    value = value - part.astype(F32)
                    total = total + dot(part, order_ref[...], NT)
                return total[0:8]

            flat = jnp.concatenate([bins(hsum_ref[:, 0:BIN_PAD]), bins(hsum_ref[:, BIN_PAD:])], axis=1)
            column = lax.broadcasted_iota(jnp.int32, (8, 3 * channels), 1)
            moved = pltpu.roll(flat, 2 * BIN_PAD - (BIN_PAD - BINS), 1)
            joined = jnp.where(column < BINS, flat, moved)
            joined = jnp.where(column < NOUT, joined, 0.0)
            for c in range(HEAD_ROWS):
                at = 2 + VROWS + IN_ROWS + c
                vec_ref[at : at + 1, :] = joined[0:1, c * channels : (c + 1) * channels]
            vec_ref[28:32, :] = jnp.zeros((4, channels), F32)


def norm_backward(row, closing, meta, x, low, high, pre, table, xc, rc, utts):
    rows, frames, channels = x.shape
    tiles = frames // TILE
    block = lambda width: pl.BlockSpec((TILE, width), lambda i: (row * tiles + i, 0))
    sums = KW + 1 + 2 * NBW
    out_specs = [pl.BlockSpec((TILE, channels), lambda i: (i, 0)), WHOLE, WHOLE]
    out_shape = [
        shape_of((frames, channels), F32),
        shape_of((2, 8, channels), F32),
        shape_of((sums, 8, channels), F32),
    ]
    if closing:
        out_specs.append(WHOLE)
        out_shape.append(shape_of((BR, channels), F32))
    return pl.pallas_call(
        functools.partial(norm_body, row=row, tiles=tiles, utts=utts, closing=bool(closing)),
        grid=(tiles,),
        in_specs=[SCALARS, WHOLE, WHOLE, WHOLE, block(FF)]
        + [
            pl.BlockSpec((FF, channels), lambda i: (0, 0)),
            pl.BlockSpec((BR, channels), lambda i: (NB - 1, 0)),
            block(channels),
            block(LANE),
        ]
        + [WHOLE] * len(closing),
        out_specs=out_specs,
        out_shape=out_shape,
        scratch_shapes=[
            pltpu.VMEM((channels // LANE, TILE + 2 * EDGE, LANE), F32),
            pltpu.VMEM((BR, channels), F32),
            pltpu.VMEM((2 * utts, channels), F32),
            pltpu.VMEM((TILE, channels), F32),
            pltpu.VMEM((channels // LANE, TILE, LANE), F32),
            pltpu.VMEM((2, TILE, LANE), jnp.int32),
        ],
        compiler_params=params(),
        cost_estimate=cost(2 * frames * 1536 * 512, 12 * MIB),
        name=f"norm_backward_{row}",
    )(meta, x, low, high, pre, table, table, xc, rc, *closing)


def conv_body(meta, cg_ref, before_ref, after_ref, low_ref, high_ref, resg_ref, last_ref, *rest, row, tiles, utts):
    out_ref, cs, vecs = rest[-3:]
    tile = pl.program_id(0)
    channels = cg_ref.shape[1]
    base = meta[row, 2 * utts + 1] + tile * TILE

    @pl.when(tile == 0)
    def _():
        vecs[...] = last_ref[...].astype(F32)

    for c in range(channels // LANE):
        cut = slice(c * LANE, (c + 1) * LANE)
        cs[c, 8 : 8 + TILE, :] = cg_ref[:, cut]
        cs[c, 0:8, :] = jnp.where(tile == 0, low_ref[row, :, cut], before_ref[:, cut])
        cs[c, 8 + TILE :, :] = jnp.where(tile == tiles - 1, high_ref[row, :, cut], after_ref[:, cut])
    for at, size in spans(TILE, 32):
        span = slice(at, at + size)
        reach, left = frame_reach(meta, row, base + at, size, utts)
        for c in range(channels // LANE):
            cut = slice(c * LANE, (c + 1) * LANE)
            total = resg_ref[span, cut]
            for k in range(KW):
                offset = RIM - k
                moved = cs[c, 8 + offset + at : 8 + offset + at + size, :]
                total = total + keep_within(moved, reach, left, offset) * vecs[2 + k : 3 + k, cut]
            out_ref[0, span, cut] = total


def conv_backward(row, before, meta, cg, low, high, resg, table, rows, utts):
    frames, channels = cg.shape
    tiles = frames // TILE
    per = TILE // 8
    more = [] if before is None else [before]
    return pl.pallas_call(
        functools.partial(conv_body, row=row, tiles=tiles, utts=utts),
        grid=(tiles,),
        in_specs=[
            SCALARS,
            pl.BlockSpec((TILE, channels), lambda i: (i, 0)),
            pl.BlockSpec((8, channels), lambda i: (jnp.maximum(i * per - 1, 0), 0)),
            pl.BlockSpec((8, channels), lambda i: (jnp.minimum((i + 1) * per, tiles * per - 1), 0)),
            WHOLE,
            WHOLE,
            pl.BlockSpec((TILE, channels), lambda i: (row * tiles + i, 0)),
            pl.BlockSpec((BR, channels), lambda i: (NB - 1, 0)),
        ]
        + [ANYWHERE] * len(more),
        out_specs=pl.BlockSpec((1, TILE, channels), lambda i: (row, i, 0)),
        out_shape=shape_of((rows, frames, channels), F32),
        input_output_aliases={8: 0} if more else {},
        scratch_shapes=[
            pltpu.VMEM((channels // LANE, TILE + 16, LANE), F32),
            pltpu.VMEM((BR, channels), F32),
        ],
        compiler_params=params(),
        cost_estimate=cost(16 * frames * 512, 6 * MIB),
        name=f"conv_backward_{row}",
    )(meta, cg, cg, cg, low, high, resg, table, *more)


def wave_body(meta, spec_ref, prev_ref, halo_ref, synth_ref, win_ref, *rest, start, rows, utts):
    out_ref, spec_all, held_all, done_all = rest[-4:]
    tile = start + pl.program_id(0)
    lane = lax.broadcasted_iota(jnp.int32, (TILE // 2, LANE), 1)
    front = lane < LANE // 2
    for r in range(rows):
        spec, held, done = spec_all.at[r], held_all.at[r], done_all.at[r]
        base = meta[r, 2 * utts + 1] + tile * TILE
        spec[EDGE:, :] = spec_ref[r]
        spec[0:EDGE, :] = jnp.where(tile == 0, halo_ref[r], prev_ref[r])
        for parity in range(2):
            half = slice(parity * BIN_PAD, (parity + 1) * BIN_PAD)
            piece = dot(spec[:, half], synth_ref[parity], NN)
            for c in range(BIN_PAD // LANE):
                held[parity, c] = piece[:, c * LANE : (c + 1) * LANE]
        for at, size in spans(TILE, 32):
            reach, _ = frame_reach(meta, r, base + at, size, utts)
            for c in range(3):
                cut = slice(c * LANE, (c + 1) * LANE)
                total = None
                for j in range(LAPS):
                    rows_at = slice(EDGE + at - j, EDGE + at - j + size)
                    of = (j % 2) * 3 + c
                    one, two = held[0, of, rows_at, :], held[1, of, rows_at, :]
                    piece = (one + two if j < 2 else one - two) * win_ref[j : j + 1, cut]
                    total = piece if j == 0 else total + jnp.where(reach >= j, piece, 0.0)
                done[c, at : at + size, :] = total * over(win_ref, LAPS, reach, c)
        even = [done[c, pl.ds(0, TILE // 2, stride=2), :] for c in range(3)]
        odd = [pltpu.roll(done[c, pl.ds(1, TILE // 2, stride=2), :], LANE // 2, 1) for c in range(3)]
        part = (
            even[0],
            even[1],
            jnp.where(front, even[2], odd[0]),
            jnp.where(front, odd[0], odd[1]),
            jnp.where(front, odd[1], odd[2]),
        )
        for k in range(PAIR):
            out_ref[pl.ds(2 * k + r, TILE // 2, stride=2 * PAIR), :] = part[k]


def wave_forward(start, stop, before, meta, spec, halo, synth, win, utts):
    rows, frames, _ = spec.shape
    tiles = frames // TILE
    per = TILE // EDGE
    more = [] if before is None else [before]
    return pl.pallas_call(
        functools.partial(wave_body, start=start, rows=rows, utts=utts),
        grid=(stop - start,),
        in_specs=[
            SCALARS,
            pl.BlockSpec((rows, TILE, 2 * BIN_PAD), lambda i: (0, start + i, 0)),
            pl.BlockSpec((rows, EDGE, 2 * BIN_PAD), lambda i: (0, jnp.maximum((start + i) * per - 1, 0), 0)),
            WHOLE,
            WHOLE,
            WHOLE,
        ]
        + [ANYWHERE] * len(more),
        out_specs=pl.BlockSpec((PAIR * TILE, LANE), lambda i: (start + i, 0)),
        out_shape=shape_of((PAIR * TILE * tiles, LANE), F32),
        input_output_aliases={6: 0} if more else {},
        scratch_shapes=[
            pltpu.VMEM((rows, TILE + EDGE, 2 * BIN_PAD), BF16),
            pltpu.VMEM((rows, 2, BIN_PAD // LANE, TILE + EDGE, LANE), F32),
            pltpu.VMEM((rows, LAP_PAD // LANE, TILE, LANE), F32),
        ],
        compiler_params=params(),
        cost_estimate=cost(4 * rows * (stop - start) * TILE * 768 * 768, 10 * MIB),
        name=f"wave_forward_{start}",
    )(meta, spec, spec, halo, synth, win, *more)


def slot_body(slot_of, *refs, bounds):
    count = len(bounds)
    out = refs[-1]
    for (start, stop), keep, came in zip(bounds, refs[:count], refs[count : 2 * count]):

        def one(b, carry, start=start, keep=keep, came=came):
            value = keep[b].astype(F32) + came[b].astype(F32)
            out[slot_of[0, start + b]] = value.astype(BF16)
            return carry

        lax.fori_loop(0, stop - start, one, 0)


def to_slots(slot_of, keeps, cames, bounds, total):
    channels = keeps[0].shape[2]
    return pl.pallas_call(
        functools.partial(slot_body, bounds=bounds),
        in_specs=[SCALARS] + [WHOLE] * (2 * len(bounds)),
        out_specs=WHOLE,
        out_shape=shape_of((total, QUART, channels), BF16),
        compiler_params=params(),
        cost_estimate=cost(0, 6 * MIB),
        name="to_slots",
    )(slot_of, *keeps, *cames)


def adam_body(places, spot, own, near, far, cross, last_ref, master, first, second, *outs, block):
    out_master, out_first, out_second = outs
    core, plane = spot[0], spot[1]
    one_fix = 1.0 / (1.0 - BETA_ONE**STEP_COUNT)
    two_fix = 1.0 / (1.0 - BETA_TWO**STEP_COUNT)
    for s in range(block):
        bucket = places[0, pl.program_id(0) * block + s]
        for ref, c, p in (
            (own, core, plane),
            (near, 1 - core, plane),
            (far, core, 1 - plane),
            (cross, 1 - core, 1 - plane),
        ):
            rows = pl.ds(pl.multiple_of(c * HALF + p * QUART, QUART), QUART)
            grad = ref[s].astype(F32)
            grad = jnp.where(bucket == NB - 1, last_ref[rows, :], grad)
            grad = jnp.where(bucket < NB, grad, 0.0)
            old = master[s, rows, :]
            one = BETA_ONE * first[s, rows, :] + (1.0 - BETA_ONE) * grad
            two = BETA_TWO * second[s, rows, :] + (1.0 - BETA_TWO) * grad * grad
            out_first[s, rows, :] = one
            out_second[s, rows, :] = two
            step = one * one_fix / (jnp.sqrt(two * two_fix) + ADAM_EPS)
            out_master[s, rows, :] = old - LEARN_RATE * (step + WEIGHT_DECAY * old)


def adam(places, spot, quarters, last, master, first, second):
    slots, depth, channels = master.shape
    block = max(b for b in range(1, 10) if slots % b == 0)
    full = pl.BlockSpec((block, depth, channels), lambda i: (i, 0, 0))
    part = pl.BlockSpec((block, QUART, channels), lambda i: (i, 0, 0))
    return pl.pallas_call(
        functools.partial(adam_body, block=block),
        grid=(slots // block,),
        in_specs=[SCALARS, SCALARS] + [part] * 4 + [WHOLE, full, full, full],
        out_specs=[full] * 3,
        out_shape=[shape_of(master.shape, F32)] * 3,
        compiler_params=params(),
        cost_estimate=cost(0, 12 * MIB),
        name="adam",
    )(places, spot, *quarters, last, master, first, second)


def tie(*values):
    return lax.optimization_barrier(values)


def plus(*values):
    return sum([v.astype(F32) for v in values]).astype(BF16)


def local(frames_in, lengths, bw_ids, owner_list, master, moment1, moment2, wave_grad):
    rows, frames, channels = frames_in.shape
    slots = master.shape[0]
    utts = lengths.shape[1]
    owners = lax.axis_size("rows")
    seqs = lax.axis_size("seq")
    row_at = lax.axis_index("rows")
    seq_at = lax.axis_index("seq")
    core, plane = seq_at % 2, seq_at // 2
    ring = ring_of(owners)
    half_ring = owners // 2

    mine = lax.dynamic_slice_in_dim(master, core * HALF, HALF, axis=1).astype(BF16)

    starts = [jnp.zeros((rows, 1), jnp.int32)]
    for u in range(utts):
        starts.append(starts[-1] + lengths[:, u : u + 1])
    spot = jnp.broadcast_to(jnp.stack([seq_at * frames, core])[None, :], (rows, 2)).astype(jnp.int32)
    meta = jnp.concatenate(starts + [bw_ids, spot], axis=1)
    lines = wave_grad.reshape(rows, frames * HOP // LANE, LANE).transpose(1, 0, 2).reshape(-1, LANE)
    order = jnp.asarray(order_table())
    synth = jnp.asarray(synthesis_table())
    win = jnp.asarray(window_tables())

    low = shifted(frames_in[:, frames - EDGE :], 1)
    high = shifted(frames_in[:, :EDGE], -1)
    later = shifted(lines[: PAIR * EDGE], -1)
    bucket_index = jnp.arange(NB, dtype=jnp.int32)
    same = owner_list[None, :] == owner_list[:, None]
    rank = jnp.sum((same & (bucket_index[None, :] < bucket_index[:, None])).astype(jnp.int32), axis=1)
    ids = jnp.arange(owners, dtype=jnp.int32)
    if ring:
        offsets = [0]
        for hop in range(1, half_ring):
            offsets += [-hop, hop]
        offsets.append(-half_ring)
        order_ids = jnp.asarray(ring, jnp.int32)
        where = jnp.sum(jnp.where(order_ids == row_at, ids, 0))
        at = (where + jnp.asarray(offsets, jnp.int32)) % owners
        owner_ids = jnp.sum(jnp.where(at[:, None] == ids[None, :], order_ids[None, :], 0), axis=1)
    else:
        owner_ids = ids

    def held_by(wanted):
        targets = (wanted[:, None] * slots + jnp.arange(slots, dtype=jnp.int32)[None, :]).reshape(-1)
        match = (owner_list * slots + rank)[None, :] == targets[:, None]
        return (NB + jnp.sum(match.astype(jnp.int32) * (bucket_index[None, :] - NB), axis=1))[None, :]

    places = held_by(jnp.concatenate([owner_ids, row_at[None].astype(jnp.int32)]))
    places, held = places[:, : owners * slots], places[:, owners * slots :]
    rel = jnp.sum(jnp.where(owner_list[:, None] == owner_ids[None, :], ids[None, :], 0), axis=1)
    slot_of = (rel * slots + rank)[None, :]
    counts = jnp.sum((owner_list[None, :] == owner_ids[:, None]).astype(jnp.int32), axis=1)[None, :]
    at_core = core[None].astype(jnp.int32)

    cot = None
    tiles = frames // TILE
    if ring:
        ahead = back = mine
        arrived = [mine, seq_swap(mine, 1)]
        for hop in range(half_ring):
            source = (ahead, back)
            ahead = lax.ppermute(ahead, AXES, ring_step(ring, 1, seqs))
            if hop < half_ring - 1:
                back = lax.ppermute(back, AXES, ring_step(ring, -1, seqs))
            if hop in (1, 2):
                feed = tie(lines, *source)[0]
                begin, end = ((0, tiles // 2), (tiles // 2, tiles))[hop - 1]
                cot = spectrum_cotangent(begin, end, cot, meta, feed, later, synth, win, rows, utts)
                ahead, back, cot = tie(ahead, back, cot)
            if hop == half_ring - 1:
                fed = tie(places, *source)[0]
                partial_table = assemble(tuple(range(owners - 1)), fed, counts, at_core, arrived, slots)
                ahead, partial_table = tie(ahead, partial_table)
            else:
                arrived += [ahead, seq_swap(ahead, 1), back, seq_swap(back, 1)]
        arrived = [ahead, seq_swap(ahead, 1)]
        owned = (owners - 1,)
        part_places, part_counts = places, counts
    else:
        gathered = lax.all_gather(mine, "rows", axis=0, tiled=True)
        arrived = [gathered, seq_swap(gathered, 1)]
        owned = (0,)
        arrived = [take_slots(slot_of, a) for a in arrived]
        part_places = jnp.arange(NB, dtype=jnp.int32)[None, :]
        part_counts = jnp.full((1, 1), NB, jnp.int32)
        partial_table = jnp.zeros((NB * BR, channels), BF16)
        cot = spectrum_cotangent(0, tiles, cot, meta, lines, later, synth, win, rows, utts)

    (table, spec, act, hidden, ada, low_grad, resg, xc, rc, send, keep, tail, sums, hsum) = forward(
        owned, meta, part_places, part_counts, frames_in, low, high, order, cot, arrived, partial_table, utts
    )
    halo = shifted(spec[:, frames - EDGE :], 1)

    keeps, cames, bounds = [], [], []

    def split(keep, came):
        both = plus(keep, came)
        stay = lax.dynamic_slice_in_dim(both, plane * QUART, QUART, axis=1)
        leave = lax.dynamic_slice_in_dim(both, (1 - plane) * QUART, QUART, axis=1)
        return stay, leave

    def record(stay, came, begins, per):
        for at, begin in enumerate(begins):
            keeps.append(stay[at * per : (at + 1) * per])
            cames.append(came[at * per : (at + 1) * per])
            bounds.append((begin, begin + per))

    per = CHUNK // BR
    pre, bsums = None, []
    begins, count = (2 * FF // BR,), 40
    for chunk in range(FF // CHUNK):
        near = seq_swap(send, 1)
        pre, next_send, next_keep, bsum = mlp_backward(chunk, pre, meta, low_grad, act, hidden, ada, table, utts)
        near, pre, next_send, next_keep = tie(near, pre, next_send, next_keep)
        bsums.append(bsum)
        stay, leave = split(keep, near)
        record(stay, seq_swap(leave, 2), begins, count)
        send, keep = next_send, next_keep
        begins, count = (chunk * per, FF // BR + chunk * per), per

    near = seq_swap(send, 1)
    cg0, edge0, parts = norm_backward(0, (), meta, frames_in, low, high, pre, table, xc, rc, utts)
    near, cg0, edge0, parts, pre = tie(near, cg0, edge0, parts, pre)
    stay, leave = split(keep, near)
    came = seq_swap(leave, 2)
    closing = (parts, tail, sums, hsum, *bsums, order)
    cg1, edge1, _, last = norm_backward(1, closing, meta, frames_in, low, high, pre, table, xc, rc, utts)
    came, cg1, edge1, last, spec = tie(came, cg1, edge1, last, spec)
    record(stay, came, begins, count)
    chunks = to_slots(slot_of, keeps, cames, tuple(bounds), owners * slots)
    edges = jnp.stack([edge0, edge1])

    state = {}

    def work(stage, *ready):
        if stage == 0:
            feed = tie(spec, *ready)[0]
            state["low"] = shifted(edges[:, 1], 1)
            state["high"] = shifted(edges[:, 0], -1)
            state["wave"] = wave_forward(0, tiles // 2, None, meta, feed, halo, synth, win, utts)
            return state["wave"]
        if stage == 1:
            feed = tie(cg0, *ready)[0]
            state["grad"] = conv_backward(
                0, None, meta, feed, state["low"], state["high"], resg, table, rows, utts
            )
            return state["grad"]
        if stage == 2:
            feed = tie(cg1, *ready)[0]
            state["grad"] = conv_backward(
                1, state["grad"], meta, feed, state["low"], state["high"], resg, table, rows, utts
            )
            return state["grad"]
        if stage == 3:
            feed = tie(spec, *ready)[0]
            state["wave"] = wave_forward(tiles // 2, tiles, state["wave"], meta, feed, halo, synth, win, utts)
            return state["wave"]
        return state["wave"]

    if ring:
        cut = {o: chunks[i * slots : (i + 1) * slots] for i, o in enumerate(offsets)}
        up, down = cut[-half_ring], cut[1 - half_ring]
        for hop in range(half_ring):
            left_over = half_ring - 1 - hop
            source = (up, down, last)
            up = lax.ppermute(up, AXES, ring_step(ring, 1, seqs))
            if hop < half_ring - 1:
                down = lax.ppermute(down, AXES, ring_step(ring, -1, seqs))
            if hop < 2:
                last = last + seq_swap(last, 1 << hop)
            else:
                last = last + rows_swap(last, 1 << (hop - 2))
            done = work(hop, *source)
            if hop in (0, 3):
                up, down, last, state["wave"] = tie(up, down, last, done)
            else:
                up, down, last, state["grad"] = tie(up, down, last, done)
            if left_over:
                up = plus(up, cut[left_over])
                if hop < half_ring - 2:
                    down = plus(down, cut[1 - left_over])
        own = plus(cut[0], up, down)
    else:
        own = lax.psum_scatter(chunks, "rows", scatter_dimension=0, tiled=True)
        last = lax.psum(last, AXES)
        for hop in range(4):
            work(hop, own)
    far = seq_swap(own, 2)
    near = seq_swap(own, 1)
    if ring:
        last = last + rows_swap(last, 4)
    waveform = state["wave"].reshape(-1, rows, LANE).transpose(1, 0, 2).reshape(rows, frames * HOP)
    cross = seq_swap(far, 1)
    where_at = jnp.stack([core, plane]).astype(jnp.int32)
    new_master, new_first, new_second = adam(
        held, where_at, (own, near, far, cross), last, master, moment1, moment2
    )
    return waveform, state["grad"], new_master, new_first, new_second


def solution(mesh):
    in_specs = (
        P("rows", "seq", None),
        P("rows", None),
        P("rows", None),
        P(),
        P("rows", None, None),
        P("rows", None, None),
        P("rows", None, None),
        P("rows", "seq"),
    )
    out_specs = (
        P("rows", "seq"),
        P("rows", "seq", None),
        P("rows", None, None),
        P("rows", None, None),
        P("rows", None, None),
    )
    return jax.shard_map(local, mesh=mesh, in_specs=in_specs, out_specs=out_specs, check_vma=False)
```

```python
import functools
import math

import jax
import jax.numpy as jnp
import numpy as np
from jax import lax
from jax.experimental import pallas as pl
from jax.experimental.pallas import tpu as pltpu
from jax.sharding import PartitionSpec as P

FF = 1536
NFFT = 1280
HOP = 320
NBW = 4
KW = 7
UTT = 4
BR = 32
STEP_COUNT = 6
BINS = 641
NOUT = 1282
VROWS = 20
IN_ROWS = 3
HEAD_ROWS = 3
NB = 137

NORM_EPS = 1e-06
ENV_FLOOR = 0.5
BETA_ONE = 0.8
BETA_TWO = 0.9
LEARN_RATE = 0.04
WEIGHT_DECAY = 0.01
ADAM_EPS = 1e-08

LAPS = NFFT // HOP
RIM = (KW - 1) // 2
LAP_PAD = 384
BIN_PAD = 768
HALF = BR // 2
QUART = BR // 4
EDGE = 16
TILE = 256
CHUNK = 768
HALF_BIN = 384
PAIR = 5
LANE = 128
AXES = ("rows", "seq")

F32 = jnp.float32
BF16 = jnp.bfloat16
MIB = 1 << 20
VMEM_BYTES = 60 * MIB


def bin_order():
    order = np.full(BIN_PAD, -1)
    order[: (BINS + 1) // 2] = np.arange(0, BINS, 2)
    order[HALF_BIN : HALF_BIN + BINS // 2] = np.arange(1, BINS, 2)
    return order


def order_table():
    return (np.arange(BIN_PAD)[:, None] == bin_order()[None, :]).astype(jnp.bfloat16)


def synthesis_table():
    n = np.arange(2 * HOP)[None, :]
    order = bin_order()
    out = np.zeros((2, 2, HALF_BIN, 2, LAP_PAD), np.float32)
    for parity in range(2):
        k = order[parity * HALF_BIN : (parity + 1) * HALF_BIN]
        k = k[k >= 0][:, None]
        angle = (k * n % NFFT) * (2.0 * math.pi / NFFT)
        factor = np.where((k == 0) | (k == NFFT // 2), 1.0, 2.0) / NFFT
        out[parity, 0, : len(k), :, :HOP] = (factor * np.cos(angle)).reshape(-1, 2, HOP)
        out[parity, 1, : len(k), :, :HOP] = (-factor * np.sin(angle)).reshape(-1, 2, HOP)
    return out.reshape(2, BIN_PAD, 2 * LAP_PAD).astype(jnp.bfloat16)


def window_tables():
    window = 0.5 - 0.5 * np.cos(np.arange(NFFT) * (2.0 * math.pi / NFFT))
    rows = np.zeros((LAPS, LAP_PAD), np.float64)
    rows[:, :HOP] = window.reshape(LAPS, HOP)
    envelope = np.cumsum(rows**2, axis=0)
    return np.concatenate([rows, 1.0 / np.maximum(envelope, ENV_FLOOR)], axis=0).astype(np.float32)


def ring_of(count):
    if count != 8:
        return None
    return [0, 2, 4, 6, 7, 5, 3, 1]


def ring_step(ring, shift, seq_count):
    where = {r: i for i, r in enumerate(ring)}
    pairs = []
    for r in ring:
        target = ring[(where[r] + shift) % len(ring)]
        pairs += [(r * seq_count + s, target * seq_count + s) for s in range(seq_count)]
    return pairs


def seq_swap(value, bit):
    count = lax.axis_size("seq")
    return lax.ppermute(value, "seq", [(s, s ^ bit) for s in range(count)])


def rows_swap(value, bit):
    count = lax.axis_size("rows")
    return lax.ppermute(value, "rows", [(r, r ^ bit) for r in range(count)])


def shifted(value, distance):
    devices = range(lax.axis_size("seq"))
    return lax.ppermute(
        value, "seq", [(i - distance, i) for i in devices if i - distance in devices]
    )


def dot(a, b, dims):
    return lax.dot_general(a, b, (dims, ((), ())), preferred_element_type=F32)


NN = ((1,), (0,))
NT = ((1,), (1,))
TN = ((0,), (0,))


def frame_reach(meta, row, first, count, utts):
    index = first + lax.broadcasted_iota(jnp.int32, (count, 128), 0)
    start = jnp.zeros_like(index)
    end = jnp.zeros_like(index) + meta[row, 1]
    for u in range(1, utts):
        inside = index >= meta[row, u]
        start = jnp.where(inside, meta[row, u], start)
        end = jnp.where(inside, meta[row, u + 1], end)
    return index - start, end - 1 - index


def spans(count, size):
    return [(at, min(size, count - at)) for at in range(0, count, size)]


def over(table, base, reach, lane_tile, width=LANE):
    cut = slice(lane_tile * LANE, lane_tile * LANE + width)
    picked = jnp.broadcast_to(table[base + LAPS - 1 : base + LAPS, cut], (reach.shape[0], width))
    for j in range(LAPS - 2, -1, -1):
        picked = jnp.where(reach[:, :width] == j, table[base + j : base + j + 1, cut], picked)
    return picked


def keep_within(values, reach, left, offset):
    if offset < 0:
        return jnp.where(reach >= -offset, values, 0.0)
    if offset > 0:
        return jnp.where(left >= offset, values, 0.0)
    return values


def row_mean(values):
    return jnp.mean(values, axis=1, keepdims=True)


def fold(values):
    rows, columns = values.shape
    return jnp.sum(values.reshape(rows // 8, 8, columns), axis=0)


def sincos(angle):
    turns = jnp.round(angle * (0.5 / math.pi))
    rest = angle * 0.5 - turns * 3.1416015625
    rest = rest + turns * 8.908910206761537e-06
    sq = rest * rest
    sine = 1.0 + sq * (
        -0.16666656732559204
        + sq * (0.008333033882081509 + sq * (-0.00019807791977655143 + sq * 2.6022808015113696e-06))
    )
    cosine = 1.0 + sq * (
        -0.4999992549419403
        + sq * (0.04166382923722267 + sq * (-0.001385461655445397 + sq * 2.3163083824329078e-05))
    )
    sine = rest * sine
    double = sine + sine
    return double * cosine, 1.0 - double * sine


ANGLE_LIMIT = 1024.0


def params():
    return pltpu.CompilerParams(vmem_limit_bytes=VMEM_BYTES)


def cost(flops, bytes_accessed, transcendentals=0):
    return pl.CostEstimate(
        flops=int(flops), bytes_accessed=int(bytes_accessed), transcendentals=int(transcendentals)
    )


WHOLE = pl.BlockSpec(memory_space=pltpu.VMEM)
SCALARS = pl.BlockSpec(memory_space=pltpu.SMEM)
ANYWHERE = pl.BlockSpec(memory_space=pl.ANY)
shape_of = jax.ShapeDtypeStruct


def pre_body(meta, wave_ref, halo_ref, synth_ref, win_ref, *rest, start, tiles, rows, utts):
    out_ref, flat, scaled_all, even_all, odd_all = rest[-5:]
    step = pl.program_id(0)
    tile = start + step
    lines = PAIR * TILE
    extra = PAIR * EDGE
    count = TILE + EDGE
    lane = lax.broadcasted_iota(jnp.int32, (count // 2, LANE), 1)
    for at, size in spans(lines, 320):
        rows_at = pl.ds(pl.multiple_of(tile * lines + at, 16), size)
        flat[at : at + size, :] = wave_ref[rows_at, :].astype(F32)
    after = jnp.minimum((tile + 1) * lines, tiles * lines - extra)
    following = wave_ref[pl.ds(pl.multiple_of(after, 16), extra), :]
    flat[lines:, :] = jnp.where(tile == tiles - 1, halo_ref[...], following).astype(F32)
    for r in range(rows):
        scaled, even, odd = scaled_all.at[r], even_all.at[r], odd_all.at[r]
        base = meta[r, 2 * utts + 1] + tile * TILE
        part = [flat[pl.ds(2 * k + r, count // 2, stride=2 * PAIR), :] for k in range(PAIR)]
        turned = [pltpu.roll(v, LANE // 2, 1) for v in part[2:]]
        front = lane < LANE // 2
        frame = (
            part[0],
            part[1],
            jnp.where(front, part[2], 0.0),
            jnp.where(front, turned[0], turned[1]),
            jnp.where(front, turned[1], turned[2]),
            jnp.where(front, turned[2], 0.0),
        )
        for c in range(3):
            scaled[c, pl.ds(0, count // 2, stride=2), :] = frame[c]
            scaled[c, pl.ds(1, count // 2, stride=2), :] = frame[3 + c]
        for at, size in spans(count, 32):
            reach, _ = frame_reach(meta, r, base + at, size, utts)
            for c in range(3):
                scaled[c, at : at + size, :] = scaled[c, at : at + size, :] * over(win_ref, LAPS, reach, c)
        for at, size in spans(TILE, 32):
            _, left = frame_reach(meta, r, base + at, size, utts)
            for j in range(2):
                for c in range(3):
                    span = slice(c * LANE, (c + 1) * LANE)

                    def lap(i):
                        value = scaled[c, at + i : at + i + size, :] * win_ref[i : i + 1, span]
                        return keep_within(value, None, left, i).astype(BF16).astype(F32)

                    one, two = lap(j), lap(j + 2)
                    column = slice(j * LAP_PAD + c * LANE, j * LAP_PAD + (c + 1) * LANE)
                    even[at : at + size, column] = (one + two).astype(BF16)
                    odd[at : at + size, column] = (one - two).astype(BF16)
        out_ref[r, :, 0:BIN_PAD] = dot(even[...], synth_ref[0], NT).astype(BF16)
        out_ref[r, :, BIN_PAD:] = dot(odd[...], synth_ref[1], NT).astype(BF16)


def spectrum_cotangent(start, stop, before, meta, wave, halo, synth, win, rows, utts):
    tiles = wave.shape[0] // (PAIR * TILE)
    frames = tiles * TILE
    more = [] if before is None else [before]
    steps = stop - start
    return pl.pallas_call(
        functools.partial(pre_body, start=start, tiles=tiles, rows=rows, utts=utts),
        grid=(steps,),
        in_specs=[SCALARS, WHOLE, WHOLE, WHOLE, WHOLE] + [ANYWHERE] * len(more),
        out_specs=pl.BlockSpec((rows, TILE, 2 * BIN_PAD), lambda i: (0, start + i, 0)),
        out_shape=shape_of((rows, frames, 2 * BIN_PAD), BF16),
        input_output_aliases={5: 0} if more else {},
        scratch_shapes=[
            pltpu.VMEM((PAIR * (TILE + EDGE), LANE), F32),
            pltpu.VMEM((rows, LAP_PAD // LANE, TILE + EDGE, LANE), F32),
            pltpu.VMEM((rows, TILE, BIN_PAD), BF16),
            pltpu.VMEM((rows, TILE, BIN_PAD), BF16),
        ],
        compiler_params=params(),
        cost_estimate=cost(4 * rows * steps * TILE * 768 * 768, rows * steps * TILE * 3072 + 4 * MIB),
        name=f"spectrum_cotangent_{start}",
    )(meta, wave, halo, synth, win, *more)


def place_parts(places, counts, core, pieces, table, sem, slots, owners, start):
    for index, ref in enumerate(pieces):
        side = core if index % 2 == 0 else 1 - core
        owner = owners[index // 2]

        def one(s, carry, ref=ref, side=side, owner=owner):
            bucket = places[0, owner * slots + s]
            at = pl.multiple_of(bucket * BR + side * HALF, HALF)
            copy = pltpu.make_async_copy(ref.at[s], table.at[pl.ds(at, HALF), :], sem)
            if start:
                copy.start()
            else:
                copy.wait()
            return carry

        lax.fori_loop(0, counts[0, owner], one, 0)


def assemble_body(places, counts, core, *refs, slots, owners):
    pieces, table, sem = refs[: 2 * len(owners)], refs[-2], refs[-1]
    place_parts(places, counts, core[0], pieces, table, sem, slots, owners, True)
    place_parts(places, counts, core[0], pieces, table, sem, slots, owners, False)


def assemble(owners, places, counts, core, pieces, slots):
    channels = pieces[0].shape[2]
    return pl.pallas_call(
        functools.partial(assemble_body, slots=slots, owners=owners),
        in_specs=[SCALARS, SCALARS, SCALARS] + [ANYWHERE] * len(pieces),
        out_specs=WHOLE,
        out_shape=shape_of((NB * BR, channels), BF16),
        scratch_shapes=[pltpu.SemaphoreType.DMA],
        compiler_params=params(),
        cost_estimate=cost(0, 12 * MIB),
        name="assemble",
    )(places, counts, core, *pieces)


def take_body(slot_of, ref, out, sem):
    def copy(b):
        return pltpu.make_async_copy(ref.at[slot_of[0, b]], out.at[b], sem)

    def start(b, carry):
        copy(b).start()
        return carry

    def wait(b, carry):
        copy(b).wait()
        return carry

    lax.fori_loop(0, NB, start, 0)
    lax.fori_loop(0, NB, wait, 0)


def take_slots(slot_of, gathered):
    return pl.pallas_call(
        take_body,
        in_specs=[SCALARS, ANYWHERE],
        out_specs=WHOLE,
        out_shape=shape_of((NB, *gathered.shape[1:]), BF16),
        scratch_shapes=[pltpu.SemaphoreType.DMA],
        compiler_params=params(),
        cost_estimate=cost(0, 6 * MIB),
        name="take_slots",
    )(slot_of, gathered)


def fill_frames(xs, x_ref, low_ref, high_ref, row, tile, tiles, channels):
    first = pl.multiple_of(tile * TILE, TILE)

    def put(at, block):
        block = block.astype(F32)
        for c in range(channels // LANE):
            xs[c, at : at + block.shape[0], :] = block[:, c * LANE : (c + 1) * LANE]

    for at, size in spans(TILE, 64):
        put(EDGE + at, x_ref[row, pl.ds(pl.multiple_of(first + at, 64), size), :])

    before = x_ref[row, pl.ds(pl.multiple_of(jnp.maximum(first - EDGE, 0), EDGE), EDGE), :]
    put(0, jnp.where(tile == 0, low_ref[row], before))
    end = jnp.minimum(first + TILE, (tiles - 1) * TILE)
    after = x_ref[row, pl.ds(pl.multiple_of(end, EDGE), EDGE), :]
    put(EDGE + TILE, jnp.where(tile == tiles - 1, high_ref[row], after))


def by_utterance(meta, row, utts, index, rows_of):
    value = jnp.broadcast_to(rows_of(0), (index.shape[0], LANE))
    for u in range(1, utts):
        value = jnp.where(index >= meta[row, u], rows_of(u), value)
    return value


def pick_rows(meta, row, utts, vec, out, channels):
    for u in range(utts):
        wanted = meta[row, utts + 1 + u]
        for at, offset in ((u, KW + 1), (utts + u, KW + 1 + NBW)):
            value = vec(offset)
            for b in range(1, NBW):
                value = jnp.where(wanted == b, vec(offset + b), value)
            out[at : at + 1, :] = value


def interleave(ones, others):
    at = 0
    for i, one in enumerate(ones):
        one()
        until = (i + 1) * len(others) // len(ones)
        for other in others[at:until]:
            other()
        at = until


def forward_body(meta, places, counts, x_ref, low_ref, high_ref, order_ref, cot_ref, *rest, owners, slots, tiles, count, utts):
    pieces = rest[: 2 * len(owners)]
    table_in = rest[2 * len(owners)]
    (
        table_out,
        spec_ref,
        act_ref,
        der_ref,
        ada_ref,
        lowg_ref,
        resg_ref,
        xc_ref,
        rc_ref,
        send_ref,
        keep_ref,
        tail_ref,
        sums_ref,
        bsum_ref,
        table,
        xs,
        w_head,
        b_head,
        vecs,
        picks,
        grad,
        lines,
        hg,
        hg_old,
        pre_ref,
        logs_ref,
        angle_ref,
        ngrad_ref,
        slim,
        xn_ref,
        normed,
        normed_old,
        branch_ref,
        rn_ref,
        slow,
        sem,
        sems,
    ) = rest[2 * len(owners) + 1 :]
    step = pl.program_id(0)
    core = meta[0, 2 * utts + 2]
    channels = x_ref.shape[2]
    lane_tiles = channels // LANE
    now = jnp.minimum(step, count - 1)
    row, tile = now // tiles, now % tiles
    vec = lambda v: vecs[2 + v : 3 + v, :]
    vec_at = KW + 1 + 2 * NBW
    head_at = 2 * FF

    def store():
        return pltpu.make_async_copy(table, table_out, sems.at[1])

    @pl.when(step == 0)
    def _():
        whole = pltpu.make_async_copy(table_in, table, sems.at[0])
        whole.start()
        normed[...] = jnp.zeros_like(normed)
        w_head[...] = jnp.zeros_like(w_head)
        b_head[...] = jnp.zeros_like(b_head)
        whole.wait()
        place_parts(places, counts, core, pieces, table, sem, slots, owners, True)
        place_parts(places, counts, core, pieces, table, sem, slots, owners, False)
        store().start()
        vecs[...] = table[head_at + 1280 : head_at + 1280 + BR, :].astype(F32)

    @pl.when(step == 1)
    def _():
        sums_ref[...] = jnp.zeros_like(sums_ref)
        bsum_ref[...] = jnp.zeros_like(bsum_ref)

    @pl.when(step == 2)
    def _():
        grad[...] = jnp.zeros_like(grad)

    @pl.when(tile == 0)
    def _():
        pick_rows(meta, row, utts, vec, picks, channels)

    base = meta[row, 2 * utts + 1] + tile * TILE
    fill_frames(xs, x_ref, low_ref, high_ref, row, tile, tiles, channels)

    def convolve(at, size):
        reach, left = frame_reach(meta, row, base + at, size, utts)
        index = base + at + lax.broadcasted_iota(jnp.int32, (size, LANE), 0)
        conv = []
        for c in range(lane_tiles):
            cut = slice(c * LANE, (c + 1) * LANE)
            total = vecs[2 + KW : 3 + KW, cut]
            for k in range(KW):
                offset = k - RIM
                moved = xs[c, EDGE + offset + at : EDGE + offset + at + size, :]
                total = total + keep_within(moved, reach, left, offset) * vecs[2 + k : 3 + k, cut]
            conv.append(total)
        mean = jnp.sum(sum(conv), axis=1, keepdims=True) * (1.0 / channels)
        conv = [v - mean for v in conv]
        square = jnp.sum(sum([v * v for v in conv]), axis=1, keepdims=True) * (1.0 / channels)
        rc = jnp.broadcast_to(lax.rsqrt(square + NORM_EPS), (size, LANE))
        rc_ref[at : at + size, :] = rc
        for c in range(lane_tiles):
            cut = slice(c * LANE, (c + 1) * LANE)
            xc = conv[c] * rc
            xc_ref[at : at + size, cut] = xc.astype(BF16)
            scale = by_utterance(meta, row, utts, index, lambda u: picks[u : u + 1, cut])
            shift = by_utterance(meta, row, utts, index, lambda u: picks[utts + u : utts + u + 1, cut])
            ada_ref[at : at + size, cut] = (xc * scale + shift).astype(BF16)

    def head(at, size, turn):
        span = slice(at, at + size)
        for c in range(0, BIN_PAD, LANE):
            bins, angles = slice(c, c + LANE), slice(BIN_PAD + c, BIN_PAD + c + LANE)
            parity, inner = c // HALF_BIN, c % HALF_BIN
            reals = slice(parity * BIN_PAD + inner, parity * BIN_PAD + inner + LANE)
            imags = slice(reals.start + HALF_BIN, reals.stop + HALF_BIN)
            angle = angle_ref[span, bins] + b_head[0:1, angles]
            scale = jnp.exp(logs_ref[span, bins] + b_head[0:1, bins])
            sine, cosine = turn(angle)
            real, imag = scale * cosine, scale * sine
            spec_ref[span, reals] = real.astype(BF16)
            spec_ref[span, imags] = imag.astype(BF16)
            dre = cot_ref[span, reals].astype(F32)
            dim = cot_ref[span, imags].astype(F32)
            hg[span, bins] = (dre * real + dim * imag).astype(BF16)
            hg[span, angles] = (dim * real - dre * imag).astype(BF16)

    def gelu(at, size, c):
        for d in range(c * 512, (c + 1) * 512, 256):
            cut = slice(d, d + 256)
            bias = vecs[2 + VROWS + c : 3 + VROWS + c, d - c * 512 : d - c * 512 + 256]
            pre = pre_ref[at : at + size, cut] + bias
            phi = 0.5 + 0.5 * lax.erf(pre * math.sqrt(0.5))
            bell = jnp.exp(-0.5 * pre * pre) * (1.0 / math.sqrt(2.0 * math.pi))
            act_ref[at : at + size, cut] = (pre * phi).astype(BF16)
            der_ref[at : at + size, cut] = (phi + pre * bell).astype(BF16)

    def second_norm(at, size):
        span = slice(at, at + size)
        branch = slim[span, :] + vec(vec_at)
        branch_ref[span, :] = branch
        x = jnp.concatenate([xs[c, EDGE + at : EDGE + at + size, :] for c in range(lane_tiles)], axis=1)
        residual = x + vec(vec_at + 1) * branch
        residual = residual - row_mean(residual)
        rn = lax.rsqrt(row_mean(residual * residual) + NORM_EPS)
        rn_ref[span, :] = jnp.broadcast_to(rn, (size, LANE))
        xn = residual * rn
        xn_ref[span, :] = xn
        normed[span, :] = (xn * vec(vec_at + 2) + vec(vec_at + 3)).astype(BF16)

    def second_norm_back(at, size, sums):
        span = slice(at, at + size)
        ngrad = ngrad_ref[span, :]
        xn = xn_ref[span, :]
        e = ngrad * vec(vec_at + 2)
        resg = rn_ref[span, 0:1] * (e - row_mean(e) - xn * row_mean(e * xn))
        resg_ref[span, :] = resg.astype(BF16)
        low = (vec(vec_at + 1) * resg).astype(BF16)
        lowg_ref[span, :] = low
        return (
            sums[0] + fold(low.astype(F32)),
            sums[1] + fold(resg * branch_ref[span, :]),
            sums[2] + fold(ngrad * xn),
            sums[3] + fold(ngrad),
        )

    def head_dots(ref, begin):
        def one(c):
            ref[:, c : c + 256] = dot(normed[...], w_head[begin + c : begin + c + 256, :], NT)

        return [functools.partial(one, c) for c in range(0, BIN_PAD, 256)]

    def hidden_dot(c):
        pre_ref[:, c : c + 256] = dot(ada_ref[...], table[c : c + 256, :], NT)

    def grad_dot(c):
        grad[c : c + 256, :] += dot(hg_old[:, c : c + 256], normed_old[...], TN)

    interleave(
        head_dots(logs_ref, 0) + head_dots(angle_ref, BIN_PAD),
        [functools.partial(convolve, at, size) for at, size in spans(TILE, 32)],
    )
    interleave(
        [functools.partial(hidden_dot, c) for c in range(0, FF, 256)]
        + [functools.partial(grad_dot, c) for c in range(0, 2 * BIN_PAD, 256)],
        [functools.partial(head, at, size, sincos) for at, size in spans(TILE, 16)],
    )

    @pl.when((step > 0) & (slow[0] > 0))
    def _():
        def again(i, carry):
            rows = pl.ds(pl.multiple_of(i * 32, 32), 32)
            for c in range(0, BIN_PAD, LANE):
                bins, angles = slice(c, c + LANE), slice(BIN_PAD + c, BIN_PAD + c + LANE)
                parity, inner = c // HALF_BIN, c % HALF_BIN
                reals = slice(parity * BIN_PAD + inner, parity * BIN_PAD + inner + LANE)
                imags = slice(reals.start + HALF_BIN, reals.stop + HALF_BIN)
                angle = angle_ref[rows, bins] + b_head[0:1, angles]
                scale = jnp.exp(logs_ref[rows, bins] + b_head[0:1, bins])
                real, imag = scale * jnp.cos(angle), scale * jnp.sin(angle)
                spec_ref[rows, reals] = real.astype(BF16)
                spec_ref[rows, imags] = imag.astype(BF16)
                dre = cot_ref[rows, reals].astype(F32)
                dim = cot_ref[rows, imags].astype(F32)
                hg[rows, bins] = (dre * real + dim * imag).astype(BF16)
                hg[rows, angles] = (dim * real - dre * imag).astype(BF16)
            return carry

        lax.fori_loop(0, TILE // 32, again, 0)

    @pl.when(step == 0)
    def _():
        last = vecs[...]
        line = jnp.concatenate([last[25:26], last[26:27], last[27:28]], axis=1)
        line = jnp.broadcast_to(line, (16, 3 * channels))
        moved = pltpu.roll(line, 3 * channels - BINS, 1)
        for at, value in ((0, line), (BIN_PAD, moved)):
            picked = dot(value[:, 0:BIN_PAD].astype(BF16), order_ref[...], NN)
            b_head[:, at : at + BIN_PAD] = picked[0:8]
        inside = lax.broadcasted_iota(jnp.int32, (336, LANE), 0)
        for c in range(lane_tiles):
            cut = slice(c * LANE, (c + 1) * LANE)
            lines[c, 0:1312, :] = table[head_at : head_at + 1312, cut].astype(F32)
            lines[c, 1312:, :] = jnp.zeros((lines.shape[1] - 1312, LANE), F32)
            for part, start in ((0, 0), (BIN_PAD, BINS)):
                evens = lines[c, pl.ds(start, 336, stride=2), :]
                w_head[part : part + 336, cut] = jnp.where(inside < (BINS + 1) // 2, evens, 0.0).astype(BF16)
                odds = lines[c, pl.ds(start + 1, 320, stride=2), :]
                w_head[part + HALF_BIN : part + HALF_BIN + 320, cut] = odds.astype(BF16)
        longest = jnp.zeros((8, 1), F32)
        for at, size in spans(BIN_PAD, 64):
            weights = w_head[BIN_PAD + at : BIN_PAD + at + size, :].astype(F32)
            length = jnp.sum(weights * weights, axis=1, keepdims=True)
            longest = jnp.maximum(longest, jnp.max(length.reshape(size // 8, 8, 1), axis=0))
        gain, shift = jnp.abs(vec(vec_at + 2)), vec(vec_at + 3)
        normed_length = math.sqrt(channels) * jnp.max(gain) + jnp.sqrt(jnp.sum(shift * shift, keepdims=True))[0, 0]
        bound = 1.05 * normed_length * jnp.max(jnp.sqrt(longest)) + jnp.max(jnp.abs(b_head[:, BIN_PAD:]))
        slow[0] = jnp.where(bound < ANGLE_LIMIT, 0, 1)

    def ngrad_dot(c):
        ngrad_ref[:, c : c + 256] = dot(hg[...], w_head[:, c : c + 256], NN)

    def branch_dot(c):
        slim[:, c : c + 256] = dot(act_ref[...], table[FF : 2 * FF, c : c + 256], NN)

    interleave(
        [functools.partial(ngrad_dot, c) for c in range(0, channels, 256)],
        [functools.partial(gelu, at, size, c) for c in range(IN_ROWS) for at, size in spans(TILE, 32)],
    )
    sums = [sums_ref[v] for v in range(4)]

    def back(at, size):
        sums[:] = second_norm_back(at, size, sums)

    interleave(
        [functools.partial(branch_dot, c) for c in range(0, channels, 256)],
        [functools.partial(back, at, size) for at, size in spans(TILE, 16)],
    )
    for v in range(4):
        sums_ref[v] = sums[v]
    for c in range(0, 2 * BIN_PAD, 512):
        total = bsum_ref[:, c : c + 512]
        for at, size in spans(TILE, 32):
            total = total + fold(hg[at : at + size, c : c + 512].astype(F32))
        bsum_ref[:, c : c + 512] = total
    hg_old[...] = hg[...]
    normed_old[...] = normed[...]
    for at, size in spans(TILE, 16):
        second_norm(at, size)

    @pl.when(step == count)
    def _():
        for c in range(0, 2 * BIN_PAD, 256):
            grad_dot(c)
        for c in range(lane_tiles):
            cut = slice(c * LANE, (c + 1) * LANE)
            for part, start in ((0, 0), (BIN_PAD, BINS)):
                lines[c, pl.ds(start + 1, 320, stride=2), :] = grad[part + HALF_BIN : part + HALF_BIN + 320, cut]
                lines[c, pl.ds(start, 320, stride=2), :] = grad[part : part + 320, cut]
                lines[c, start + 640 : start + 641, :] = grad[part + 320 : part + 321, cut]
            for b in range(40):
                low_half = lines[c, b * BR : b * BR + HALF, :].astype(BF16)
                high_half = lines[c, b * BR + HALF : b * BR + BR, :].astype(BF16)
                keep_ref[b, :, cut] = jnp.where(core == 0, low_half, high_half)
                send_ref[b, :, cut] = jnp.where(core == 0, high_half, low_half)
            tail_ref[:, cut] = lines[c, 1280:1288, :]
        store().wait()


def forward(owners, meta, places, counts, x, low, high, order, cot, pieces, table, utts):
    rows, frames, channels = x.shape
    tiles = frames // TILE
    steps = rows * tiles
    count = rows * frames
    slots = pieces[0].shape[0]
    ahead = lambda i: jnp.minimum(i, steps - 1)
    behind = lambda i: jnp.maximum(i - 1, 0)
    wide = pl.BlockSpec((TILE, FF), lambda i: (ahead(i), 0))
    wide_late = pl.BlockSpec((None, TILE, FF), lambda i: (behind(i) // tiles, behind(i) % tiles, 0))
    slim = pl.BlockSpec((TILE, channels), lambda i: (ahead(i), 0))
    slim_late = pl.BlockSpec((TILE, channels), lambda i: (behind(i), 0))
    return pl.pallas_call(
        functools.partial(forward_body, owners=owners, slots=slots, tiles=tiles, count=steps, utts=utts),
        grid=(steps + 1,),
        in_specs=[SCALARS, SCALARS, SCALARS, WHOLE, WHOLE, WHOLE, WHOLE, wide_late]
        + [ANYWHERE] * (len(pieces) + 1),
        out_specs=[ANYWHERE, wide_late, wide, wide, slim, slim_late, slim_late, slim]
        + [pl.BlockSpec((TILE, LANE), lambda i: (ahead(i), 0))]
        + [WHOLE] * 5,
        out_shape=[
            shape_of((NB * BR, channels), BF16),
            shape_of((rows, frames, 2 * BIN_PAD), BF16),
            shape_of((count, FF), BF16),
            shape_of((count, FF), BF16),
            shape_of((count, channels), BF16),
            shape_of((count, channels), BF16),
            shape_of((count, channels), BF16),
            shape_of((count, channels), BF16),
            shape_of((count, LANE), F32),
            shape_of((40, HALF, channels), BF16),
            shape_of((40, HALF, channels), BF16),
            shape_of((8, channels), F32),
            shape_of((4, 8, channels), F32),
            shape_of((8, 2 * BIN_PAD), F32),
        ],
        scratch_shapes=[
            pltpu.VMEM((NB * BR, channels), BF16),
            pltpu.VMEM((channels // LANE, TILE + 2 * EDGE, LANE), F32),
            pltpu.VMEM((2 * BIN_PAD, channels), BF16),
            pltpu.VMEM((8, 2 * BIN_PAD), F32),
            pltpu.VMEM((BR, channels), F32),
            pltpu.VMEM((2 * utts, channels), F32),
            pltpu.VMEM((2 * BIN_PAD, channels), F32),
            pltpu.VMEM((channels // LANE, 1344, LANE), F32),
            pltpu.VMEM((TILE, 2 * BIN_PAD), BF16),
            pltpu.VMEM((TILE, 2 * BIN_PAD), BF16),
            pltpu.VMEM((TILE, FF), F32),
            pltpu.VMEM((TILE, BIN_PAD), F32),
            pltpu.VMEM((TILE, BIN_PAD), F32),
            pltpu.VMEM((TILE, channels), F32),
            pltpu.VMEM((TILE, channels), F32),
            pltpu.VMEM((TILE, channels), F32),
            pltpu.VMEM((TILE, channels), BF16),
            pltpu.VMEM((TILE, channels), BF16),
            pltpu.VMEM((TILE, channels), F32),
            pltpu.VMEM((TILE, LANE), F32),
            pltpu.SMEM((1,), jnp.int32),
            pltpu.SemaphoreType.DMA,
            pltpu.SemaphoreType.DMA((2,)),
        ],
        compiler_params=params(),
        cost_estimate=cost(10 * count * 1536 * 512, 40 * MIB, count * 4096),
        name="forward",
    )(meta, places, counts, x, low, high, order, cot, *pieces, table)


def mlp_body(meta, low_ref, act_ref, der_ref, ada_ref, wout_ref, *rest, utts):
    pre_ref, send_ref, keep_ref, bsum_ref, gout, gin, agrad = rest[-7:]
    step = pl.program_id(0)
    core = meta[0, 2 * utts + 2]
    tile = low_ref.shape[0]

    @pl.when(step == 0)
    def _():
        gout[...] = jnp.zeros_like(gout)
        gin[...] = jnp.zeros_like(gin)
        bsum_ref[...] = jnp.zeros_like(bsum_ref)

    def agrad_dot(c):
        agrad[:, c : c + 256] = dot(low_ref[...], wout_ref[c : c + 256, :], NT)

    def gout_dot(c):
        gout[c : c + 256, :] += dot(act_ref[:, c : c + 256], low_ref[...], TN)

    def gin_dot(c):
        gin[c : c + 256, :] += dot(pre_ref[:, c : c + 256], ada_ref[...], TN)

    def slope(c):
        cut = slice(c, c + 256)
        total = bsum_ref[:, cut]
        for at, size in spans(tile, 32):
            span = slice(at, at + size)
            pre = (agrad[span, cut] * der_ref[span, cut].astype(F32)).astype(BF16)
            pre_ref[span, cut] = pre
            total = total + fold(pre.astype(F32))
        bsum_ref[:, cut] = total

    cuts = range(0, CHUNK, 256)
    for c in cuts:
        agrad_dot(c)
    interleave([functools.partial(gout_dot, c) for c in cuts], [functools.partial(slope, c) for c in cuts])
    for c in cuts:
        gin_dot(c)

    @pl.when(step == pl.num_programs(0) - 1)
    def _():
        buckets = CHUNK // BR
        for at, ref in ((0, gin), (buckets, gout)):
            for b in range(buckets):
                low_half = ref[b * BR : b * BR + HALF, :].astype(BF16)
                high_half = ref[b * BR + HALF : b * BR + BR, :].astype(BF16)
                keep_ref[at + b] = jnp.where(core == 0, low_half, high_half)
                send_ref[at + b] = jnp.where(core == 0, high_half, low_half)


def mlp_backward(chunk, before, meta, low, act, der, ada, table, utts):
    count, channels = low.shape
    tile = 512
    slim = pl.BlockSpec((tile, channels), lambda i: (i, 0))
    part = pl.BlockSpec((tile, CHUNK), lambda i: (i, chunk))
    buckets = 2 * CHUNK // BR
    more = [] if before is None else [before]
    return pl.pallas_call(
        functools.partial(mlp_body, utts=utts),
        grid=(count // tile,),
        in_specs=[
            SCALARS,
            slim,
            part,
            part,
            slim,
            pl.BlockSpec((CHUNK, channels), lambda i: (FF // CHUNK + chunk, 0)),
        ]
        + [ANYWHERE] * len(more),
        out_specs=[part, WHOLE, WHOLE, WHOLE],
        out_shape=[
            shape_of((count, FF), BF16),
            shape_of((buckets, HALF, channels), BF16),
            shape_of((buckets, HALF, channels), BF16),
            shape_of((8, CHUNK), F32),
        ],
        input_output_aliases={6: 0} if more else {},
        scratch_shapes=[
            pltpu.VMEM((CHUNK, channels), F32),
            pltpu.VMEM((CHUNK, channels), F32),
            pltpu.VMEM((tile, CHUNK), F32),
        ],
        compiler_params=params(),
        cost_estimate=cost(6 * count * CHUNK * 512, 16 * MIB),
        name=f"mlp_backward_{chunk}",
    )(meta, low, act, der, ada, table, *more)


def norm_body(
    meta, x_ref, low_ref, high_ref, pre_ref, w_in, last_ref, xc_ref, rc_ref, *rest, row, tiles, utts, closing
):
    more = rest[: 7 if closing else 0]
    outs = rest[len(more) :]
    cg_ref, edge_ref, part_ref = outs[:3]
    xs, vecs, picks, agrad, cg, reaches = outs[-6:]
    tile = pl.program_id(0)
    channels = x_ref.shape[2]
    lane_tiles = channels // LANE
    base = meta[row, 2 * utts + 1] + tile * TILE
    vec = lambda v: vecs[2 + v : 3 + v, :]

    @pl.when(tile == 0)
    def _():
        vecs[...] = last_ref[...].astype(F32)
        part_ref[...] = more[0][...] if closing else jnp.zeros_like(part_ref)
        pick_rows(meta, row, utts, vec, picks, channels)

    agrad[...] = dot(pre_ref[...], w_in[...], NN)
    fill_frames(xs, x_ref, low_ref, high_ref, 0, tile, tiles, channels)
    for at, size in spans(TILE, 32):
        span = slice(at, at + size)
        reach, left = frame_reach(meta, row, base + at, size, utts)
        reaches[0, span, :] = reach
        reaches[1, span, :] = left
        index = base + at + lax.broadcasted_iota(jnp.int32, (size, LANE), 0)
        ecs, xcs = [], []
        for c in range(lane_tiles):
            cut = slice(c * LANE, (c + 1) * LANE)
            scale = by_utterance(meta, row, utts, index, lambda u: picks[u : u + 1, cut])
            ecs.append(agrad[span, cut] * scale)
            xcs.append(xc_ref[span, cut].astype(F32))
        m_one = jnp.sum(sum(ecs), axis=1, keepdims=True) * (1.0 / channels)
        m_two = jnp.sum(sum([e * v for e, v in zip(ecs, xcs)]), axis=1, keepdims=True) * (1.0 / channels)
        rc = rc_ref[span, :]
        for c in range(lane_tiles):
            cut = slice(c * LANE, (c + 1) * LANE)
            value = rc * (ecs[c] - m_one - xcs[c] * m_two)
            cg[c, span, :] = value
            cg_ref[span, cut] = value.astype(BF16)
    for u in range(utts):
        begin, end = meta[row, u], meta[row, u + 1]

        @pl.when((begin < base + TILE) & (end > base))
        def _(u=u, begin=begin, end=end):
            wanted = meta[row, utts + 1 + u]
            for c in range(lane_tiles):
                cut = slice(c * LANE, (c + 1) * LANE)
                one = jnp.zeros((8, LANE), F32)
                two = jnp.zeros((8, LANE), F32)
                for at, size in spans(TILE, 64):
                    span = slice(at, at + size)
                    index = base + at + lax.broadcasted_iota(jnp.int32, (size, LANE), 0)
                    value = jnp.where((index >= begin) & (index < end), agrad[span, cut], 0.0)
                    one = one + fold(value * xc_ref[span, cut].astype(F32))
                    two = two + fold(value)
                part_ref[KW + 1 + wanted, :, cut] += one
                part_ref[KW + 1 + NBW + wanted, :, cut] += two

    for c in range(lane_tiles):
        cut = slice(c * LANE, (c + 1) * LANE)
        sums = [part_ref[k, :, cut] for k in range(KW + 1)]
        for at, size in spans(TILE, 32):
            span = slice(at, at + size)
            reach, left = reaches[0, span, :], reaches[1, span, :]
            value = cg[c, span, :]
            for k in range(KW):
                offset = k - RIM
                moved = xs[c, EDGE + offset + at : EDGE + offset + at + size, :] * value
                sums[k] = sums[k] + fold(keep_within(moved, reach, left, offset))
            sums[KW] = sums[KW] + fold(value)
        for k in range(KW + 1):
            part_ref[k, :, cut] = sums[k]

    @pl.when(tile == 0)
    def _():
        edge_ref[0] = cg_ref[0:EDGE, :]

    @pl.when(tile == tiles - 1)
    def _():
        edge_ref[1] = cg_ref[TILE - EDGE : TILE, :]

    if closing:
        _, tail_ref, sums_ref, hsum_ref, bsum0, bsum1, order_ref = more
        vec_ref, quarter_refs = outs[-7], outs[3:7]
        core, plane = meta[0, 2 * utts + 2], meta[0, 2 * utts + 3]

        @pl.when(tile == tiles - 1)
        def _():
            vec_ref[0:8, :] = jnp.zeros((8, channels), F32)
            vec_ref[0:2, :] = tail_ref[0:2, :]
            for v in range(VROWS):
                at = v - (KW + 1 + 2 * NBW)
                rows_of = part_ref[v] if at < 0 else sums_ref[at]
                vec_ref[2 + v : 3 + v, :] = jnp.sum(rows_of, axis=0, keepdims=True)
            line = jnp.concatenate([bsum0[...], bsum1[...]], axis=1)
            for c in range(IN_ROWS):
                at = 2 + VROWS + c
                vec_ref[at : at + 1, :] = jnp.sum(
                    line[:, c * channels : (c + 1) * channels], axis=0, keepdims=True
                )

            def bins(value):
                value = jnp.broadcast_to(jnp.sum(value, axis=0, keepdims=True), (16, BIN_PAD))
                total = jnp.zeros((16, BIN_PAD), F32)
                for _ in range(3):
                    part = value.astype(BF16)
                    value = value - part.astype(F32)
                    total = total + dot(part, order_ref[...], NT)
                return total[0:8]

            flat = jnp.concatenate([bins(hsum_ref[:, 0:BIN_PAD]), bins(hsum_ref[:, BIN_PAD:])], axis=1)
            column = lax.broadcasted_iota(jnp.int32, (8, 3 * channels), 1)
            moved = pltpu.roll(flat, 2 * BIN_PAD - (BIN_PAD - BINS), 1)
            joined = jnp.where(column < BINS, flat, moved)
            joined = jnp.where(column < NOUT, joined, 0.0)
            for c in range(HEAD_ROWS):
                at = 2 + VROWS + IN_ROWS + c
                vec_ref[at : at + 1, :] = joined[0:1, c * channels : (c + 1) * channels]
            vec_ref[28:32, :] = jnp.zeros((4, channels), F32)
            for ref, c, p in zip(
                quarter_refs,
                (core, 1 - core, core, 1 - core),
                (plane, plane, 1 - plane, 1 - plane),
            ):
                ref[...] = vec_ref[pl.ds(pl.multiple_of(c * HALF + p * QUART, QUART), QUART), :]


def norm_backward(row, closing, meta, x, low, high, pre, table, xc, rc, utts):
    rows, frames, channels = x.shape
    tiles = frames // TILE
    block = lambda width: pl.BlockSpec((TILE, width), lambda i: (row * tiles + i, 0))
    sums = KW + 1 + 2 * NBW
    out_specs = [pl.BlockSpec((TILE, channels), lambda i: (i, 0)), WHOLE, WHOLE]
    out_shape = [
        shape_of((frames, channels), BF16),
        shape_of((2, EDGE, channels), BF16),
        shape_of((sums, 8, channels), F32),
    ]
    if closing:
        out_specs += [WHOLE] * 4
        out_shape += [shape_of((QUART, channels), F32)] * 4
    return pl.pallas_call(
        functools.partial(norm_body, row=row, tiles=tiles, utts=utts, closing=bool(closing)),
        grid=(tiles,),
        in_specs=[SCALARS]
        + [pl.BlockSpec((1, frames, channels), lambda i: (row, 0, 0))]
        + [pl.BlockSpec((1, EDGE, channels), lambda i: (row, 0, 0))] * 2
        + [block(FF)]
        + [
            pl.BlockSpec((FF, channels), lambda i: (0, 0)),
            pl.BlockSpec((BR, channels), lambda i: (NB - 1, 0)),
            block(channels),
            block(LANE),
        ]
        + [WHOLE] * len(closing),
        out_specs=out_specs,
        out_shape=out_shape,
        scratch_shapes=([pltpu.VMEM((BR, channels), F32)] if closing else [])
        + [
            pltpu.VMEM((channels // LANE, TILE + 2 * EDGE, LANE), F32),
            pltpu.VMEM((BR, channels), F32),
            pltpu.VMEM((2 * utts, channels), F32),
            pltpu.VMEM((TILE, channels), F32),
            pltpu.VMEM((channels // LANE, TILE, LANE), F32),
            pltpu.VMEM((2, TILE, LANE), jnp.int32),
        ],
        compiler_params=params(),
        cost_estimate=cost(2 * frames * 1536 * 512, 12 * MIB),
        name=f"norm_backward_{row}",
    )(meta, x, low, high, pre, table, table, xc, rc, *closing)


def conv_body(meta, cg_ref, before_ref, after_ref, low_ref, high_ref, resg_ref, last_ref, *rest, row, tiles, utts):
    out_ref, cs, vecs = rest[-3:]
    tile = pl.program_id(0)
    channels = cg_ref.shape[1]
    base = meta[row, 2 * utts + 1] + tile * TILE

    @pl.when(tile == 0)
    def _():
        vecs[...] = last_ref[...].astype(F32)

    for c in range(channels // LANE):
        cut = slice(c * LANE, (c + 1) * LANE)
        cs[c, EDGE : EDGE + TILE, :] = cg_ref[:, cut].astype(F32)
        cs[c, 0:EDGE, :] = jnp.where(tile == 0, low_ref[row, :, cut], before_ref[:, cut]).astype(F32)
        after = jnp.where(tile == tiles - 1, high_ref[row, :, cut], after_ref[:, cut])
        cs[c, EDGE + TILE :, :] = after.astype(F32)
    for at, size in spans(TILE, 32):
        span = slice(at, at + size)
        reach, left = frame_reach(meta, row, base + at, size, utts)
        for c in range(channels // LANE):
            cut = slice(c * LANE, (c + 1) * LANE)
            total = resg_ref[span, cut].astype(F32)
            for k in range(KW):
                offset = RIM - k
                moved = cs[c, EDGE + offset + at : EDGE + offset + at + size, :]
                total = total + keep_within(moved, reach, left, offset) * vecs[2 + k : 3 + k, cut]
            out_ref[0, span, cut] = total


def conv_backward(row, before, meta, cg, low, high, resg, table, rows, utts):
    frames, channels = cg.shape
    tiles = frames // TILE
    per = TILE // EDGE
    more = [] if before is None else [before]
    return pl.pallas_call(
        functools.partial(conv_body, row=row, tiles=tiles, utts=utts),
        grid=(tiles,),
        in_specs=[
            SCALARS,
            pl.BlockSpec((TILE, channels), lambda i: (i, 0)),
            pl.BlockSpec((EDGE, channels), lambda i: (jnp.maximum(i * per - 1, 0), 0)),
            pl.BlockSpec((EDGE, channels), lambda i: (jnp.minimum((i + 1) * per, tiles * per - 1), 0)),
            WHOLE,
            WHOLE,
            pl.BlockSpec((TILE, channels), lambda i: (row * tiles + i, 0)),
            pl.BlockSpec((BR, channels), lambda i: (NB - 1, 0)),
        ]
        + [ANYWHERE] * len(more),
        out_specs=pl.BlockSpec((1, TILE, channels), lambda i: (row, i, 0)),
        out_shape=shape_of((rows, frames, channels), F32),
        input_output_aliases={8: 0} if more else {},
        scratch_shapes=[
            pltpu.VMEM((channels // LANE, TILE + 2 * EDGE, LANE), F32),
            pltpu.VMEM((BR, channels), F32),
        ],
        compiler_params=params(),
        cost_estimate=cost(16 * frames * 512, 6 * MIB),
        name=f"conv_backward_{row}",
    )(meta, cg, cg, cg, low, high, resg, table, *more)


def wave_body(meta, spec_ref, prev_ref, halo_ref, synth_ref, win_ref, *rest, start, rows, utts):
    out_ref, spec_all, held_all, done_all = rest[-4:]
    tile = start + pl.program_id(0)
    lane = lax.broadcasted_iota(jnp.int32, (TILE // 2, LANE), 1)
    front = lane < LANE // 2
    for r in range(rows):
        spec, held, done = spec_all.at[r], held_all.at[r], done_all.at[r]
        base = meta[r, 2 * utts + 1] + tile * TILE
        spec[EDGE:, :] = spec_ref[r]
        spec[0:EDGE, :] = jnp.where(tile == 0, halo_ref[r], prev_ref[r])
        for parity in range(2):
            half = slice(parity * BIN_PAD, (parity + 1) * BIN_PAD)
            piece = dot(spec[:, half], synth_ref[parity], NN)
            for c in range(BIN_PAD // LANE):
                held[parity, c] = piece[:, c * LANE : (c + 1) * LANE]
        for at, size in spans(TILE, 32):
            reach, _ = frame_reach(meta, r, base + at, size, utts)
            for c in range(3):
                cut = slice(c * LANE, (c + 1) * LANE)
                total = None
                for j in range(LAPS):
                    rows_at = slice(EDGE + at - j, EDGE + at - j + size)
                    of = (j % 2) * 3 + c
                    one, two = held[0, of, rows_at, :], held[1, of, rows_at, :]
                    piece = (one + two if j < 2 else one - two) * win_ref[j : j + 1, cut]
                    total = piece if j == 0 else total + jnp.where(reach >= j, piece, 0.0)
                done[c, at : at + size, :] = total * over(win_ref, LAPS, reach, c)
        even = [done[c, pl.ds(0, TILE // 2, stride=2), :] for c in range(3)]
        odd = [pltpu.roll(done[c, pl.ds(1, TILE // 2, stride=2), :], LANE // 2, 1) for c in range(3)]
        part = (
            even[0],
            even[1],
            jnp.where(front, even[2], odd[0]),
            jnp.where(front, odd[0], odd[1]),
            jnp.where(front, odd[1], odd[2]),
        )
        for k in range(PAIR):
            out_ref[pl.ds(2 * k + r, TILE // 2, stride=2 * PAIR), :] = part[k]


def wave_forward(start, stop, before, meta, spec, halo, synth, win, utts):
    rows, frames, _ = spec.shape
    tiles = frames // TILE
    per = TILE // EDGE
    more = [] if before is None else [before]
    return pl.pallas_call(
        functools.partial(wave_body, start=start, rows=rows, utts=utts),
        grid=(stop - start,),
        in_specs=[
            SCALARS,
            pl.BlockSpec((rows, TILE, 2 * BIN_PAD), lambda i: (0, start + i, 0)),
            pl.BlockSpec((rows, EDGE, 2 * BIN_PAD), lambda i: (0, jnp.maximum((start + i) * per - 1, 0), 0)),
            WHOLE,
            WHOLE,
            WHOLE,
        ]
        + [ANYWHERE] * len(more),
        out_specs=pl.BlockSpec((PAIR * TILE, LANE), lambda i: (start + i, 0)),
        out_shape=shape_of((PAIR * TILE * tiles, LANE), F32),
        input_output_aliases={6: 0} if more else {},
        scratch_shapes=[
            pltpu.VMEM((rows, TILE + EDGE, 2 * BIN_PAD), BF16),
            pltpu.VMEM((rows, 2, BIN_PAD // LANE, TILE + EDGE, LANE), F32),
            pltpu.VMEM((rows, LAP_PAD // LANE, TILE, LANE), F32),
        ],
        compiler_params=params(),
        cost_estimate=cost(4 * rows * (stop - start) * TILE * 768 * 768, 10 * MIB),
        name=f"wave_forward_{start}",
    )(meta, spec, spec, halo, synth, win, *more)


def slot_body(slot_of, *refs, bounds):
    count = len(bounds)
    out = refs[-1]
    lasts = refs[2 * count : -1]
    for (start, stop), keep, came in zip(bounds, refs[:count], refs[count : 2 * count]):

        def one(b, carry, start=start, keep=keep, came=came):
            value = keep[b].astype(F32) + came[b].astype(F32)
            out[slot_of[0, start + b]] = value.astype(BF16)
            return carry

        lax.fori_loop(0, stop - start, one, 0)
    out[slot_of[0, NB - 1]] = sum([ref[...] for ref in lasts]).astype(BF16)


def to_slots(slot_of, keeps, cames, lasts, bounds, total):
    channels = keeps[0].shape[2]
    return pl.pallas_call(
        functools.partial(slot_body, bounds=bounds),
        in_specs=[SCALARS] + [WHOLE] * (2 * len(bounds) + len(lasts)),
        out_specs=WHOLE,
        out_shape=shape_of((total, QUART, channels), BF16),
        compiler_params=params(),
        cost_estimate=cost(0, 6 * MIB),
        name="to_slots",
    )(slot_of, *keeps, *cames, *lasts)


def adam_body(places, spot, low_ref, high_ref, master, first, second, *rest, block):
    out_master, out_first, out_second = rest[-3:]
    one_fix = 1.0 / (1.0 - BETA_ONE**STEP_COUNT)
    two_fix = 1.0 / (1.0 - BETA_TWO**STEP_COUNT)
    for s in range(block):
        bucket = places[0, pl.program_id(0) * block + s]
        for half, ref in enumerate((low_ref, high_ref)):
            grad = jnp.where(bucket < NB, ref[s].astype(F32), 0.0)
            old = master[s, half, 0]
            one = BETA_ONE * first[s, half, 0] + (1.0 - BETA_ONE) * grad
            two = BETA_TWO * second[s, half, 0] + (1.0 - BETA_TWO) * grad * grad
            out_first[s, half, 0] = one
            out_second[s, half, 0] = two
            step = one * one_fix / (jnp.sqrt(two * two_fix) + ADAM_EPS)
            out_master[s, half, 0] = old - LEARN_RATE * (step + WEIGHT_DECAY * old)


def adam(places, spot, low, high, master, first, second, before):
    slots, depth, channels = master.shape
    block = max(b for b in range(1, 10) if slots % b == 0)
    cut = lambda v: v.reshape(slots, 2, 2, QUART, channels)
    full = pl.BlockSpec((block, 2, 1, QUART, channels), lambda i, places, spot: (i, 0, spot[0], 0, 0))
    part = pl.BlockSpec((block, QUART, channels), lambda i, places, spot: (i, 0, 0))
    more = [cut(v) for v in before]
    outs = pl.pallas_call(
        functools.partial(adam_body, block=block),
        grid_spec=pltpu.PrefetchScalarGridSpec(
            num_scalar_prefetch=2,
            grid=(slots // block,),
            in_specs=[part] * 2 + [full] * 3 + [ANYWHERE] * len(more),
            out_specs=[full] * 3,
        ),
        out_shape=[shape_of((slots, 2, 2, QUART, channels), F32)] * 3,
        input_output_aliases={7 + v: v for v in range(len(more))},
        compiler_params=params(),
        cost_estimate=cost(0, 6 * MIB),
        name="adam_second" if more else "adam_first",
    )(places, spot, low, high, cut(master), cut(first), cut(second), *more)
    return [v.reshape(slots, depth, channels) for v in outs]


def tie(*values):
    return lax.optimization_barrier(values)


def plus(*values):
    return sum([v.astype(F32) for v in values]).astype(BF16)


def local(frames_in, lengths, bw_ids, owner_list, master, moment1, moment2, wave_grad):
    rows, frames, channels = frames_in.shape
    slots = master.shape[0]
    utts = lengths.shape[1]
    owners = lax.axis_size("rows")
    seqs = lax.axis_size("seq")
    row_at = lax.axis_index("rows")
    seq_at = lax.axis_index("seq")
    core, plane = seq_at % 2, seq_at // 2
    ring = ring_of(owners)
    half_ring = owners // 2

    mine = lax.dynamic_slice_in_dim(master, core * HALF, HALF, axis=1).astype(BF16)

    starts = [jnp.zeros((rows, 1), jnp.int32)]
    for u in range(utts):
        starts.append(starts[-1] + lengths[:, u : u + 1])
    spot = jnp.broadcast_to(jnp.stack([seq_at * frames, core, plane])[None, :], (rows, 3)).astype(jnp.int32)
    meta = jnp.concatenate(starts + [bw_ids, spot], axis=1)
    lines = wave_grad.reshape(rows, frames * HOP // LANE, LANE).transpose(1, 0, 2).reshape(-1, LANE)
    order = jnp.asarray(order_table())
    synth = jnp.asarray(synthesis_table())
    win = jnp.asarray(window_tables())

    low = shifted(frames_in[:, frames - EDGE :], 1)
    high = shifted(frames_in[:, :EDGE], -1)
    later = shifted(lines[: PAIR * EDGE], -1)
    bucket_index = jnp.arange(NB, dtype=jnp.int32)
    same = owner_list[None, :] == owner_list[:, None]
    rank = jnp.sum((same & (bucket_index[None, :] < bucket_index[:, None])).astype(jnp.int32), axis=1)
    ids = jnp.arange(owners, dtype=jnp.int32)
    if ring:
        offsets = [0]
        for hop in range(1, half_ring):
            offsets += [-hop, hop]
        offsets.append(-half_ring)
        order_ids = jnp.asarray(ring, jnp.int32)
        where = jnp.sum(jnp.where(order_ids == row_at, ids, 0))
        at = (where + jnp.asarray(offsets, jnp.int32)) % owners
        owner_ids = jnp.sum(jnp.where(at[:, None] == ids[None, :], order_ids[None, :], 0), axis=1)
    else:
        owner_ids = ids

    def held_by(wanted):
        targets = (wanted[:, None] * slots + jnp.arange(slots, dtype=jnp.int32)[None, :]).reshape(-1)
        match = (owner_list * slots + rank)[None, :] == targets[:, None]
        return (NB + jnp.sum(match.astype(jnp.int32) * (bucket_index[None, :] - NB), axis=1))[None, :]

    places = held_by(jnp.concatenate([owner_ids, row_at[None].astype(jnp.int32)]))
    places, held = places[:, : owners * slots], places[:, owners * slots :]
    rel = jnp.sum(jnp.where(owner_list[:, None] == owner_ids[None, :], ids[None, :], 0), axis=1)
    slot_of = (rel * slots + rank)[None, :]
    counts = jnp.sum((owner_list[None, :] == owner_ids[:, None]).astype(jnp.int32), axis=1)[None, :]
    at_core = core[None].astype(jnp.int32)

    cot = None
    tiles = frames // TILE
    if ring:
        ahead = back = mine
        arrived = [mine, seq_swap(mine, 1)]
        for hop in range(half_ring):
            source = (ahead, back)
            ahead = lax.ppermute(ahead, AXES, ring_step(ring, 1, seqs))
            if hop < half_ring - 1:
                back = lax.ppermute(back, AXES, ring_step(ring, -1, seqs))
            if hop in (1, 2):
                feed, low, high = tie(lines, low, high, *source)[:3]
                begin, end = ((0, tiles // 2), (tiles // 2, tiles))[hop - 1]
                cot = spectrum_cotangent(begin, end, cot, meta, feed, later, synth, win, rows, utts)
                ahead, back, cot = tie(ahead, back, cot)
            if hop == half_ring - 1:
                fed = tie(places, *source)[0]
                partial_table = assemble(tuple(range(owners - 1)), fed, counts, at_core, arrived, slots)
                ahead, partial_table = tie(ahead, partial_table)
            else:
                arrived += [ahead, seq_swap(ahead, 1), back, seq_swap(back, 1)]
        arrived = [ahead, seq_swap(ahead, 1)]
        owned = (owners - 1,)
        part_places, part_counts = places, counts
    else:
        gathered = lax.all_gather(mine, "rows", axis=0, tiled=True)
        arrived = [gathered, seq_swap(gathered, 1)]
        owned = (0,)
        arrived = [take_slots(slot_of, a) for a in arrived]
        part_places = jnp.arange(NB, dtype=jnp.int32)[None, :]
        part_counts = jnp.full((1, 1), NB, jnp.int32)
        partial_table = jnp.zeros((NB * BR, channels), BF16)
        cot = spectrum_cotangent(0, tiles, cot, meta, lines, later, synth, win, rows, utts)

    (table, spec, act, der, ada, low_grad, resg, xc, rc, send, keep, tail, sums, hsum) = forward(
        owned, meta, part_places, part_counts, frames_in, low, high, order, cot, arrived, partial_table, utts
    )
    halo = shifted(spec[:, frames - EDGE :], 1)

    keeps, cames, bounds = [], [], []

    def split(keep, came):
        both = plus(keep, came)
        stay = lax.dynamic_slice_in_dim(both, plane * QUART, QUART, axis=1)
        leave = lax.dynamic_slice_in_dim(both, (1 - plane) * QUART, QUART, axis=1)
        return stay, leave

    def record(stay, came, begins, per):
        for at, begin in enumerate(begins):
            keeps.append(stay[at * per : (at + 1) * per])
            cames.append(came[at * per : (at + 1) * per])
            bounds.append((begin, begin + per))

    per = CHUNK // BR
    pre, bsums = None, []
    begins, count = (2 * FF // BR,), 40
    waiting = []
    for chunk in range(FF // CHUNK):
        near = seq_swap(send, 1)
        pre, next_send, next_keep, bsum = mlp_backward(chunk, pre, meta, low_grad, act, der, ada, table, utts)
        near, pre, next_send, next_keep = tie(near, pre, next_send, next_keep)
        bsums.append(bsum)
        stay, leave = split(keep, near)
        waiting.append((stay, seq_swap(leave, 2), begins, count))
        send, keep = next_send, next_keep
        begins, count = (chunk * per, FF // BR + chunk * per), per

    near = seq_swap(send, 1)
    for stay, came, *where_from in waiting[:-1]:
        pre, came = tie(pre, came)
        record(stay, came, *where_from)
    cg0, edge0, parts = norm_backward(0, (), meta, frames_in, low, high, pre, table, xc, rc, utts)
    kept, came, *where_from = waiting[-1]
    near, cg0, edge0, parts, pre, came = tie(near, cg0, edge0, parts, pre, came)
    record(kept, came, *where_from)
    stay, leave = split(keep, near)
    came = seq_swap(leave, 2)
    closing = (parts, tail, sums, hsum, *bsums, order)
    cg1, edge1, _, own, to_near, to_far, to_cross = norm_backward(
        1, closing, meta, frames_in, low, high, pre, table, xc, rc, utts
    )
    lasts = (own, seq_swap(to_near, 1), seq_swap(to_far, 2), seq_swap(to_cross, 3))
    edges = jnp.stack([edge0, edge1])
    edge_low, edge_high = shifted(edges[:, 1], 1), shifted(edges[:, 0], -1)
    came, spec, edge_low, edge_high, *lasts = tie(came, spec, edge_low, edge_high, *lasts)
    record(stay, came, begins, count)
    chunks = to_slots(slot_of, keeps, cames, lasts, tuple(bounds), owners * slots)

    state = {}

    def work(stage, *ready):
        if stage in (0, 3):
            feed = tie(spec, *ready)[0]
            begin, end, before = ((0, tiles // 2, None), (tiles // 2, tiles, state.get("wave")))[stage // 3]
            state["wave"] = wave_forward(begin, end, before, meta, feed, halo, synth, win, utts)
            return "wave"
        if stage in (1, 4):
            row = stage // 4
            feed = tie((cg0, cg1)[row], *ready)[0]
            state["grad"] = conv_backward(
                row, state.get("grad"), meta, feed, edge_low, edge_high, resg, table, rows, utts
            )
            return "grad"
        return None

    if ring:
        cut = {o: chunks[i * slots : (i + 1) * slots] for i, o in enumerate(offsets)}
        up, down = cut[-half_ring], cut[1 - half_ring]
        for hop in range(half_ring):
            left_over = half_ring - 1 - hop
            source = (up, down)
            up = lax.ppermute(up, AXES, ring_step(ring, 1, seqs))
            if hop < half_ring - 1:
                down = lax.ppermute(down, AXES, ring_step(ring, -1, seqs))
            done = work(hop, *source)
            if done:
                up, down, state[done] = tie(up, down, state[done])
            if left_over:
                up = plus(up, cut[left_over])
                if hop < half_ring - 2:
                    down = plus(down, cut[1 - left_over])
        own = plus(cut[0], up, down)
    else:
        own = lax.psum_scatter(chunks, "rows", scatter_dimension=0, tiled=True)
        for hop in (0, 1, 3):
            work(hop, own)
    near, far = seq_swap(own, 1), seq_swap(own, 2)
    work(4, own)
    near, far, state["grad"] = tie(near, far, state["grad"])
    cross = seq_swap(far, 1)
    waveform = state["wave"].reshape(-1, rows, LANE).transpose(1, 0, 2).reshape(rows, frames * HOP)

    def ordered(mine, other):
        return jnp.where(core == 0, mine, other), jnp.where(core == 0, other, mine)

    here, there = plane[None].astype(jnp.int32), (1 - plane)[None].astype(jnp.int32)
    first = adam(held, here, *ordered(own, near), master, moment1, moment2, ())
    cross, *first = tie(cross, *first)
    new_master, new_first, new_second = adam(held, there, *ordered(far, cross), master, moment1, moment2, first)
    return waveform, state["grad"], new_master, new_first, new_second


def solution(mesh):
    in_specs = (
        P("rows", "seq", None),
        P("rows", None),
        P("rows", None),
        P(),
        P("rows", None, None),
        P("rows", None, None),
        P("rows", None, None),
        P("rows", "seq"),
    )
    out_specs = (
        P("rows", "seq"),
        P("rows", "seq", None),
        P("rows", None, None),
        P("rows", None, None),
        P("rows", None, None),
    )
    return jax.shard_map(local, mesh=mesh, in_specs=in_specs, out_specs=out_specs, check_vma=False)
```

```python
import functools
import math

import jax
import jax.numpy as jnp
import numpy as np
from jax import lax
from jax.experimental import pallas as pl
from jax.experimental.pallas import tpu as pltpu
from jax.sharding import PartitionSpec as P

FF = 1536
NFFT = 1280
HOP = 320
NBW = 4
KW = 7
UTT = 4
BR = 32
STEP_COUNT = 6
BINS = 641
NOUT = 1282
VROWS = 20
IN_ROWS = 3
HEAD_ROWS = 3
NB = 137

NORM_EPS = 1e-06
ENV_FLOOR = 0.5
BETA_ONE = 0.8
BETA_TWO = 0.9
LEARN_RATE = 0.04
WEIGHT_DECAY = 0.01
ADAM_EPS = 1e-08

LAPS = NFFT // HOP
RIM = (KW - 1) // 2
LAP_PAD = 384
BIN_PAD = 768
HALF = BR // 2
QUART = BR // 4
EDGE = 16
TILE = 256
CHUNK = 768
HALF_BIN = 384
PAIR = 5
ADAM_BLOCK = 9
LANE = 128
AXES = ("rows", "seq")

F32 = jnp.float32
BF16 = jnp.bfloat16
MIB = 1 << 20
VMEM_BYTES = 60 * MIB


def bin_order():
    order = np.full(BIN_PAD, -1)
    order[: (BINS + 1) // 2] = np.arange(0, BINS, 2)
    order[HALF_BIN : HALF_BIN + BINS // 2] = np.arange(1, BINS, 2)
    return order


def order_table():
    return (np.arange(BIN_PAD)[:, None] == bin_order()[None, :]).astype(jnp.bfloat16)


def synthesis_table():
    n = np.arange(2 * HOP)[None, :]
    order = bin_order()
    out = np.zeros((2, 2, HALF_BIN, 2, LAP_PAD), np.float32)
    for parity in range(2):
        k = order[parity * HALF_BIN : (parity + 1) * HALF_BIN]
        k = k[k >= 0][:, None]
        angle = (k * n % NFFT) * (2.0 * math.pi / NFFT)
        factor = np.where((k == 0) | (k == NFFT // 2), 1.0, 2.0) / NFFT
        out[parity, 0, : len(k), :, :HOP] = (factor * np.cos(angle)).reshape(-1, 2, HOP)
        out[parity, 1, : len(k), :, :HOP] = (-factor * np.sin(angle)).reshape(-1, 2, HOP)
    return out.reshape(2, BIN_PAD, 2 * LAP_PAD).astype(jnp.bfloat16)


def window_tables():
    window = 0.5 - 0.5 * np.cos(np.arange(NFFT) * (2.0 * math.pi / NFFT))
    rows = np.zeros((LAPS, LAP_PAD), np.float64)
    rows[:, :HOP] = window.reshape(LAPS, HOP)
    envelope = np.cumsum(rows**2, axis=0)
    return np.concatenate([rows, 1.0 / np.maximum(envelope, ENV_FLOOR)], axis=0).astype(np.float32)


def ring_of(count):
    if count != 8:
        return None
    return [0, 2, 4, 6, 7, 5, 3, 1]


def ring_step(ring, shift, seq_count):
    where = {r: i for i, r in enumerate(ring)}
    pairs = []
    for r in ring:
        target = ring[(where[r] + shift) % len(ring)]
        pairs += [(r * seq_count + s, target * seq_count + s) for s in range(seq_count)]
    return pairs


def seq_swap(value, bit):
    count = lax.axis_size("seq")
    return lax.ppermute(value, "seq", [(s, s ^ bit) for s in range(count)])


def rows_swap(value, bit):
    count = lax.axis_size("rows")
    return lax.ppermute(value, "rows", [(r, r ^ bit) for r in range(count)])


def shifted(value, distance):
    devices = range(lax.axis_size("seq"))
    return lax.ppermute(
        value, "seq", [(i - distance, i) for i in devices if i - distance in devices]
    )


def dot(a, b, dims):
    return lax.dot_general(a, b, (dims, ((), ())), preferred_element_type=F32)


NN = ((1,), (0,))
NT = ((1,), (1,))
TN = ((0,), (0,))


def frame_reach(meta, row, first, count, utts):
    index = first + lax.broadcasted_iota(jnp.int32, (count, 128), 0)
    start = jnp.zeros_like(index)
    end = jnp.zeros_like(index) + meta[row, 1]
    for u in range(1, utts):
        inside = index >= meta[row, u]
        start = jnp.where(inside, meta[row, u], start)
        end = jnp.where(inside, meta[row, u + 1], end)
    return index - start, end - 1 - index


def spans(count, size):
    return [(at, min(size, count - at)) for at in range(0, count, size)]


def over(table, base, reach, lane_tile, width=LANE):
    cut = slice(lane_tile * LANE, lane_tile * LANE + width)
    picked = jnp.broadcast_to(table[base + LAPS - 1 : base + LAPS, cut], (reach.shape[0], width))
    for j in range(LAPS - 2, -1, -1):
        picked = jnp.where(reach[:, :width] == j, table[base + j : base + j + 1, cut], picked)
    return picked


def keep_within(values, reach, left, offset):
    if offset < 0:
        return jnp.where(reach >= -offset, values, 0.0)
    if offset > 0:
        return jnp.where(left >= offset, values, 0.0)
    return values


def row_mean(values):
    return jnp.mean(values, axis=1, keepdims=True)


def fold(values):
    rows, columns = values.shape
    return jnp.sum(values.reshape(rows // 8, 8, columns), axis=0)


def sincos(angle):
    turns = jnp.round(angle * (0.5 / math.pi))
    rest = angle * 0.5 - turns * 3.1416015625
    rest = rest + turns * 8.908910206761537e-06
    sq = rest * rest
    sine = 1.0 + sq * (
        -0.16666656732559204
        + sq * (0.008333033882081509 + sq * (-0.00019807791977655143 + sq * 2.6022808015113696e-06))
    )
    cosine = 1.0 + sq * (
        -0.4999992549419403
        + sq * (0.04166382923722267 + sq * (-0.001385461655445397 + sq * 2.3163083824329078e-05))
    )
    sine = rest * sine
    double = sine + sine
    return double * cosine, 1.0 - double * sine


ANGLE_LIMIT = 1024.0


def params():
    return pltpu.CompilerParams(vmem_limit_bytes=VMEM_BYTES)


def cost(flops, bytes_accessed, transcendentals=0):
    return pl.CostEstimate(
        flops=int(flops), bytes_accessed=int(bytes_accessed), transcendentals=int(transcendentals)
    )


WHOLE = pl.BlockSpec(memory_space=pltpu.VMEM)
SCALARS = pl.BlockSpec(memory_space=pltpu.SMEM)
ANYWHERE = pl.BlockSpec(memory_space=pl.ANY)
shape_of = jax.ShapeDtypeStruct


def plan_body(ids, lengths, bw_ids, owner_list, order, offsets, meta, places, held, slot_of, counts, rel, *, frames, ring):
    rows, utts = lengths.shape
    owners, slots = order.shape[0], held.shape[1]
    row_at, seq_at = ids[0], ids[1]
    for r in range(rows):
        start = jnp.int32(0)
        meta[r, 0] = start
        for u in range(utts):
            start = start + lengths[r, u]
            meta[r, u + 1] = start
            meta[r, utts + 1 + u] = bw_ids[r, u]
        meta[r, 2 * utts + 1] = seq_at * frames
        meta[r, 2 * utts + 2] = lax.rem(seq_at, 2)
        meta[r, 2 * utts + 3] = lax.div(seq_at, 2)
    where = jnp.int32(0)
    if ring:
        for i in range(owners):
            where = jnp.where(order[i] == row_at, i, where)

    def name(i, carry):
        rel[order[lax.rem(where + offsets[i] + owners, owners)]] = i
        counts[0, i] = 0
        return carry

    def clear(i, carry):
        places[0, i] = NB
        return carry

    def place(b, carry):
        i = rel[owner_list[b]]
        n = counts[0, i]
        counts[0, i] = n + 1
        places[0, i * slots + n] = b
        slot_of[0, b] = i * slots + n
        return carry

    lax.fori_loop(0, owners, name, 0)
    lax.fori_loop(0, owners * slots, clear, 0)
    lax.fori_loop(0, NB, place, 0)
    own = rel[row_at]

    def keep(n, carry):
        held[0, n] = places[0, own * slots + n]
        return carry

    lax.fori_loop(0, slots, keep, 0)


def plan(ids, lengths, bw_ids, owner_list, order, offsets, slots, frames, ring):
    rows, utts = lengths.shape
    owners = order.shape[0]
    shapes = ((rows, 2 * utts + 4), (1, owners * slots), (1, slots), (1, NB), (1, owners))
    return pl.pallas_call(
        functools.partial(plan_body, frames=frames, ring=ring),
        in_specs=[SCALARS] * 6,
        out_specs=[SCALARS] * 5,
        out_shape=[shape_of(shape, jnp.int32) for shape in shapes],
        scratch_shapes=[pltpu.SMEM((owners,), jnp.int32)],
        compiler_params=params(),
        cost_estimate=cost(8000, 8 * 1024),
        name="plan",
    )(ids, lengths, bw_ids, owner_list, order, offsets)


def pre_body(meta, wave_ref, halo_ref, synth_ref, win_ref, *rest, start, tiles, rows, utts):
    out_ref, flat, scaled_all, even_all, odd_all = rest[-5:]
    step = pl.program_id(0)
    tile = start + step
    lines = PAIR * TILE
    extra = PAIR * EDGE
    count = TILE + EDGE
    lane = lax.broadcasted_iota(jnp.int32, (count // 2, LANE), 1)
    for at, size in spans(lines, 320):
        rows_at = pl.ds(pl.multiple_of(tile * lines + at, 16), size)
        flat[at : at + size, :] = wave_ref[rows_at, :].astype(F32)
    after = jnp.minimum((tile + 1) * lines, tiles * lines - extra)
    following = wave_ref[pl.ds(pl.multiple_of(after, 16), extra), :]
    flat[lines:, :] = jnp.where(tile == tiles - 1, halo_ref[...], following).astype(F32)
    for r in range(rows):
        scaled, even, odd = scaled_all.at[r], even_all.at[r], odd_all.at[r]
        base = meta[r, 2 * utts + 1] + tile * TILE
        part = [flat[pl.ds(2 * k + r, count // 2, stride=2 * PAIR), :] for k in range(PAIR)]
        turned = [pltpu.roll(v, LANE // 2, 1) for v in part[2:]]
        front = lane < LANE // 2
        frame = (
            part[0],
            part[1],
            jnp.where(front, part[2], 0.0),
            jnp.where(front, turned[0], turned[1]),
            jnp.where(front, turned[1], turned[2]),
            jnp.where(front, turned[2], 0.0),
        )
        for c in range(3):
            scaled[c, pl.ds(0, count // 2, stride=2), :] = frame[c]
            scaled[c, pl.ds(1, count // 2, stride=2), :] = frame[3 + c]
        for at, size in spans(count, 32):
            reach, _ = frame_reach(meta, r, base + at, size, utts)
            for c in range(3):
                scaled[c, at : at + size, :] = scaled[c, at : at + size, :] * over(win_ref, LAPS, reach, c)
        for at, size in spans(TILE, 32):
            _, left = frame_reach(meta, r, base + at, size, utts)
            for j in range(2):
                for c in range(3):
                    span = slice(c * LANE, (c + 1) * LANE)

                    def lap(i):
                        value = scaled[c, at + i : at + i + size, :] * win_ref[i : i + 1, span]
                        return keep_within(value, None, left, i).astype(BF16).astype(F32)

                    one, two = lap(j), lap(j + 2)
                    column = slice(j * LAP_PAD + c * LANE, j * LAP_PAD + (c + 1) * LANE)
                    even[at : at + size, column] = (one + two).astype(BF16)
                    odd[at : at + size, column] = (one - two).astype(BF16)
        out_ref[r, :, 0:BIN_PAD] = dot(even[...], synth_ref[0], NT).astype(BF16)
        out_ref[r, :, BIN_PAD:] = dot(odd[...], synth_ref[1], NT).astype(BF16)


def spectrum_cotangent(start, stop, before, meta, wave, halo, synth, win, rows, utts):
    tiles = wave.shape[0] // (PAIR * TILE)
    frames = tiles * TILE
    more = [] if before is None else [before]
    steps = stop - start
    return pl.pallas_call(
        functools.partial(pre_body, start=start, tiles=tiles, rows=rows, utts=utts),
        grid=(steps,),
        in_specs=[SCALARS, WHOLE, WHOLE, WHOLE, WHOLE] + [ANYWHERE] * len(more),
        out_specs=pl.BlockSpec((rows, TILE, 2 * BIN_PAD), lambda i: (0, start + i, 0)),
        out_shape=shape_of((rows, frames, 2 * BIN_PAD), BF16),
        input_output_aliases={5: 0} if more else {},
        scratch_shapes=[
            pltpu.VMEM((PAIR * (TILE + EDGE), LANE), F32),
            pltpu.VMEM((rows, LAP_PAD // LANE, TILE + EDGE, LANE), F32),
            pltpu.VMEM((rows, TILE, BIN_PAD), BF16),
            pltpu.VMEM((rows, TILE, BIN_PAD), BF16),
        ],
        compiler_params=params(),
        cost_estimate=cost(4 * rows * steps * TILE * 768 * 768, rows * steps * TILE * 3072 + 4 * MIB),
        name=f"spectrum_cotangent_{start}",
    )(meta, wave, halo, synth, win, *more)


def place_parts(places, counts, core, pieces, table, sem, slots, owners, start):
    for index, ref in enumerate(pieces):
        side = core if index % 2 == 0 else 1 - core
        owner = owners[index // 2]

        def one(s, carry, ref=ref, side=side, owner=owner):
            bucket = places[0, owner * slots + s]
            at = pl.multiple_of(bucket * BR + side * HALF, HALF)
            copy = pltpu.make_async_copy(ref.at[s], table.at[pl.ds(at, HALF), :], sem)
            if start:
                copy.start()
            else:
                copy.wait()
            return carry

        lax.fori_loop(0, counts[0, owner], one, 0)


def assemble_body(meta, places, counts, *refs, slots, owners):
    pieces, table, sem = refs[: 2 * len(owners)], refs[-2], refs[-1]
    core = meta[0, meta.shape[1] - 2]
    place_parts(places, counts, core, pieces, table, sem, slots, owners, True)
    place_parts(places, counts, core, pieces, table, sem, slots, owners, False)


def assemble(owners, meta, places, counts, pieces, slots):
    channels = pieces[0].shape[2]
    return pl.pallas_call(
        functools.partial(assemble_body, slots=slots, owners=owners),
        in_specs=[SCALARS, SCALARS, SCALARS] + [ANYWHERE] * len(pieces),
        out_specs=WHOLE,
        out_shape=shape_of((NB * BR, channels), BF16),
        scratch_shapes=[pltpu.SemaphoreType.DMA],
        compiler_params=params(),
        cost_estimate=cost(0, 12 * MIB),
        name="assemble",
    )(meta, places, counts, *pieces)


def take_body(slot_of, ref, out, sem):
    def copy(b):
        return pltpu.make_async_copy(ref.at[slot_of[0, b]], out.at[b], sem)

    def start(b, carry):
        copy(b).start()
        return carry

    def wait(b, carry):
        copy(b).wait()
        return carry

    lax.fori_loop(0, NB, start, 0)
    lax.fori_loop(0, NB, wait, 0)


def take_slots(slot_of, gathered):
    return pl.pallas_call(
        take_body,
        in_specs=[SCALARS, ANYWHERE],
        out_specs=WHOLE,
        out_shape=shape_of((NB, *gathered.shape[1:]), BF16),
        scratch_shapes=[pltpu.SemaphoreType.DMA],
        compiler_params=params(),
        cost_estimate=cost(0, 6 * MIB),
        name="take_slots",
    )(slot_of, gathered)


def fill_frames(xs, x_ref, low_ref, high_ref, row, tile, tiles, channels):
    first = pl.multiple_of(tile * TILE, TILE)

    def put(at, block):
        block = block.astype(F32)
        for c in range(channels // LANE):
            xs[c, at : at + block.shape[0], :] = block[:, c * LANE : (c + 1) * LANE]

    for at, size in spans(TILE, 64):
        put(EDGE + at, x_ref[row, pl.ds(pl.multiple_of(first + at, 64), size), :])

    before = x_ref[row, pl.ds(pl.multiple_of(jnp.maximum(first - EDGE, 0), EDGE), EDGE), :]
    put(0, jnp.where(tile == 0, low_ref[row], before))
    end = jnp.minimum(first + TILE, (tiles - 1) * TILE)
    after = x_ref[row, pl.ds(pl.multiple_of(end, EDGE), EDGE), :]
    put(EDGE + TILE, jnp.where(tile == tiles - 1, high_ref[row], after))


def by_utterance(meta, row, utts, index, rows_of):
    value = jnp.broadcast_to(rows_of(0), (index.shape[0], LANE))
    for u in range(1, utts):
        value = jnp.where(index >= meta[row, u], rows_of(u), value)
    return value


def pick_rows(meta, row, utts, vec, out, channels):
    for u in range(utts):
        wanted = meta[row, utts + 1 + u]
        for at, offset in ((u, KW + 1), (utts + u, KW + 1 + NBW)):
            value = vec(offset)
            for b in range(1, NBW):
                value = jnp.where(wanted == b, vec(offset + b), value)
            out[at : at + 1, :] = value


def interleave(ones, others):
    at = 0
    for i, one in enumerate(ones):
        one()
        until = (i + 1) * len(others) // len(ones)
        for other in others[at:until]:
            other()
        at = until


def forward_body(meta, places, counts, x_ref, low_ref, high_ref, order_ref, cot_ref, *rest, owners, slots, tiles, count, utts):
    pieces = rest[: 2 * len(owners)]
    table_in = rest[2 * len(owners)]
    (
        table_out,
        spec_ref,
        act_ref,
        der_ref,
        ada_ref,
        lowg_ref,
        resg_ref,
        xc_ref,
        rc_ref,
        send_ref,
        keep_ref,
        tail_ref,
        sums_ref,
        bsum_ref,
        table,
        xs,
        w_head,
        b_head,
        vecs,
        picks,
        grad,
        lines,
        hg,
        hg_old,
        pre_ref,
        logs_ref,
        angle_ref,
        ngrad_ref,
        slim,
        xn_ref,
        normed,
        normed_old,
        branch_ref,
        rn_ref,
        slow,
        sem,
        sems,
    ) = rest[2 * len(owners) + 1 :]
    step = pl.program_id(0)
    core = meta[0, 2 * utts + 2]
    channels = x_ref.shape[2]
    lane_tiles = channels // LANE
    now = jnp.minimum(step, count - 1)
    row, tile = now // tiles, now % tiles
    vec = lambda v: vecs[2 + v : 3 + v, :]
    vec_at = KW + 1 + 2 * NBW
    head_at = 2 * FF

    def store():
        return pltpu.make_async_copy(table, table_out, sems.at[1])

    @pl.when(step == 0)
    def _():
        whole = pltpu.make_async_copy(table_in, table, sems.at[0])
        whole.start()
        normed[...] = jnp.zeros_like(normed)
        w_head[...] = jnp.zeros_like(w_head)
        b_head[...] = jnp.zeros_like(b_head)
        whole.wait()
        place_parts(places, counts, core, pieces, table, sem, slots, owners, True)
        place_parts(places, counts, core, pieces, table, sem, slots, owners, False)
        store().start()
        vecs[...] = table[head_at + 1280 : head_at + 1280 + BR, :].astype(F32)

    @pl.when(step == 1)
    def _():
        sums_ref[...] = jnp.zeros_like(sums_ref)
        bsum_ref[...] = jnp.zeros_like(bsum_ref)

    @pl.when(step == 2)
    def _():
        grad[...] = jnp.zeros_like(grad)

    @pl.when(tile == 0)
    def _():
        pick_rows(meta, row, utts, vec, picks, channels)

    base = meta[row, 2 * utts + 1] + tile * TILE
    fill_frames(xs, x_ref, low_ref, high_ref, row, tile, tiles, channels)

    def convolve(at, size):
        reach, left = frame_reach(meta, row, base + at, size, utts)
        index = base + at + lax.broadcasted_iota(jnp.int32, (size, LANE), 0)
        conv = []
        for c in range(lane_tiles):
            cut = slice(c * LANE, (c + 1) * LANE)
            total = vecs[2 + KW : 3 + KW, cut]
            for k in range(KW):
                offset = k - RIM
                moved = xs[c, EDGE + offset + at : EDGE + offset + at + size, :]
                total = total + keep_within(moved, reach, left, offset) * vecs[2 + k : 3 + k, cut]
            conv.append(total)
        mean = jnp.sum(sum(conv), axis=1, keepdims=True) * (1.0 / channels)
        conv = [v - mean for v in conv]
        square = jnp.sum(sum([v * v for v in conv]), axis=1, keepdims=True) * (1.0 / channels)
        rc = jnp.broadcast_to(lax.rsqrt(square + NORM_EPS), (size, LANE))
        rc_ref[at : at + size, :] = rc
        for c in range(lane_tiles):
            cut = slice(c * LANE, (c + 1) * LANE)
            xc = conv[c] * rc
            xc_ref[at : at + size, cut] = xc.astype(BF16)
            scale = by_utterance(meta, row, utts, index, lambda u: picks[u : u + 1, cut])
            shift = by_utterance(meta, row, utts, index, lambda u: picks[utts + u : utts + u + 1, cut])
            ada_ref[at : at + size, cut] = (xc * scale + shift).astype(BF16)

    def head(at, size, turn):
        span = slice(at, at + size)
        for c in range(0, BIN_PAD, LANE):
            bins, angles = slice(c, c + LANE), slice(BIN_PAD + c, BIN_PAD + c + LANE)
            parity, inner = c // HALF_BIN, c % HALF_BIN
            reals = slice(parity * BIN_PAD + inner, parity * BIN_PAD + inner + LANE)
            imags = slice(reals.start + HALF_BIN, reals.stop + HALF_BIN)
            angle = angle_ref[span, bins] + b_head[0:1, angles]
            scale = jnp.exp(logs_ref[span, bins] + b_head[0:1, bins])
            sine, cosine = turn(angle)
            real, imag = scale * cosine, scale * sine
            spec_ref[span, reals] = real.astype(BF16)
            spec_ref[span, imags] = imag.astype(BF16)
            dre = cot_ref[span, reals].astype(F32)
            dim = cot_ref[span, imags].astype(F32)
            hg[span, bins] = (dre * real + dim * imag).astype(BF16)
            hg[span, angles] = (dim * real - dre * imag).astype(BF16)

    def gelu(at, size, c):
        for d in range(c * 512, (c + 1) * 512, 256):
            cut = slice(d, d + 256)
            bias = vecs[2 + VROWS + c : 3 + VROWS + c, d - c * 512 : d - c * 512 + 256]
            pre = pre_ref[at : at + size, cut] + bias
            phi = 0.5 + 0.5 * lax.erf(pre * math.sqrt(0.5))
            bell = jnp.exp(-0.5 * pre * pre) * (1.0 / math.sqrt(2.0 * math.pi))
            act_ref[at : at + size, cut] = (pre * phi).astype(BF16)
            der_ref[at : at + size, cut] = (phi + pre * bell).astype(BF16)

    def second_norm(at, size):
        span = slice(at, at + size)
        branch = slim[span, :] + vec(vec_at)
        branch_ref[span, :] = branch
        x = jnp.concatenate([xs[c, EDGE + at : EDGE + at + size, :] for c in range(lane_tiles)], axis=1)
        residual = x + vec(vec_at + 1) * branch
        residual = residual - row_mean(residual)
        rn = lax.rsqrt(row_mean(residual * residual) + NORM_EPS)
        rn_ref[span, :] = jnp.broadcast_to(rn, (size, LANE))
        xn = residual * rn
        xn_ref[span, :] = xn
        normed[span, :] = (xn * vec(vec_at + 2) + vec(vec_at + 3)).astype(BF16)

    def second_norm_back(at, size, sums):
        span = slice(at, at + size)
        ngrad = ngrad_ref[span, :]
        xn = xn_ref[span, :]
        e = ngrad * vec(vec_at + 2)
        resg = rn_ref[span, 0:1] * (e - row_mean(e) - xn * row_mean(e * xn))
        resg_ref[span, :] = resg.astype(BF16)
        low = (vec(vec_at + 1) * resg).astype(BF16)
        lowg_ref[span, :] = low
        return (
            sums[0] + fold(low.astype(F32)),
            sums[1] + fold(resg * branch_ref[span, :]),
            sums[2] + fold(ngrad * xn),
            sums[3] + fold(ngrad),
        )

    def head_dots(ref, begin):
        def one(c):
            ref[:, c : c + 256] = dot(normed[...], w_head[begin + c : begin + c + 256, :], NT)

        return [functools.partial(one, c) for c in range(0, BIN_PAD, 256)]

    def hidden_dot(c):
        pre_ref[:, c : c + 256] = dot(ada_ref[...], table[c : c + 256, :], NT)

    def grad_dot(c):
        grad[c : c + 256, :] += dot(hg_old[:, c : c + 256], normed_old[...], TN)

    interleave(
        head_dots(logs_ref, 0) + head_dots(angle_ref, BIN_PAD),
        [functools.partial(convolve, at, size) for at, size in spans(TILE, 32)],
    )
    interleave(
        [functools.partial(hidden_dot, c) for c in range(0, FF, 256)]
        + [functools.partial(grad_dot, c) for c in range(0, 2 * BIN_PAD, 256)],
        [functools.partial(head, at, size, sincos) for at, size in spans(TILE, 16)],
    )

    @pl.when((step > 0) & (slow[0] > 0))
    def _():
        def again(i, carry):
            rows = pl.ds(pl.multiple_of(i * 32, 32), 32)
            for c in range(0, BIN_PAD, LANE):
                bins, angles = slice(c, c + LANE), slice(BIN_PAD + c, BIN_PAD + c + LANE)
                parity, inner = c // HALF_BIN, c % HALF_BIN
                reals = slice(parity * BIN_PAD + inner, parity * BIN_PAD + inner + LANE)
                imags = slice(reals.start + HALF_BIN, reals.stop + HALF_BIN)
                angle = angle_ref[rows, bins] + b_head[0:1, angles]
                scale = jnp.exp(logs_ref[rows, bins] + b_head[0:1, bins])
                real, imag = scale * jnp.cos(angle), scale * jnp.sin(angle)
                spec_ref[rows, reals] = real.astype(BF16)
                spec_ref[rows, imags] = imag.astype(BF16)
                dre = cot_ref[rows, reals].astype(F32)
                dim = cot_ref[rows, imags].astype(F32)
                hg[rows, bins] = (dre * real + dim * imag).astype(BF16)
                hg[rows, angles] = (dim * real - dre * imag).astype(BF16)
            return carry

        lax.fori_loop(0, TILE // 32, again, 0)

    @pl.when(step == 0)
    def _():
        last = vecs[...]
        line = jnp.concatenate([last[25:26], last[26:27], last[27:28]], axis=1)
        line = jnp.broadcast_to(line, (16, 3 * channels))
        moved = pltpu.roll(line, 3 * channels - BINS, 1)
        for at, value in ((0, line), (BIN_PAD, moved)):
            picked = dot(value[:, 0:BIN_PAD].astype(BF16), order_ref[...], NN)
            b_head[:, at : at + BIN_PAD] = picked[0:8]
        inside = lax.broadcasted_iota(jnp.int32, (336, LANE), 0)
        for c in range(lane_tiles):
            cut = slice(c * LANE, (c + 1) * LANE)
            lines[c, 0:1312, :] = table[head_at : head_at + 1312, cut].astype(F32)
            lines[c, 1312:, :] = jnp.zeros((lines.shape[1] - 1312, LANE), F32)
            for part, start in ((0, 0), (BIN_PAD, BINS)):
                evens = lines[c, pl.ds(start, 336, stride=2), :]
                w_head[part : part + 336, cut] = jnp.where(inside < (BINS + 1) // 2, evens, 0.0).astype(BF16)
                odds = lines[c, pl.ds(start + 1, 320, stride=2), :]
                w_head[part + HALF_BIN : part + HALF_BIN + 320, cut] = odds.astype(BF16)
        longest = jnp.zeros((8, 1), F32)
        for at, size in spans(BIN_PAD, 64):
            weights = w_head[BIN_PAD + at : BIN_PAD + at + size, :].astype(F32)
            length = jnp.sum(weights * weights, axis=1, keepdims=True)
            longest = jnp.maximum(longest, jnp.max(length.reshape(size // 8, 8, 1), axis=0))
        gain, shift = jnp.abs(vec(vec_at + 2)), vec(vec_at + 3)
        normed_length = math.sqrt(channels) * jnp.max(gain) + jnp.sqrt(jnp.sum(shift * shift, keepdims=True))[0, 0]
        bound = 1.05 * normed_length * jnp.max(jnp.sqrt(longest)) + jnp.max(jnp.abs(b_head[:, BIN_PAD:]))
        slow[0] = jnp.where(bound < ANGLE_LIMIT, 0, 1)

    def ngrad_dot(c):
        ngrad_ref[:, c : c + 256] = dot(hg[...], w_head[:, c : c + 256], NN)

    def branch_dot(c):
        slim[:, c : c + 256] = dot(act_ref[...], table[FF : 2 * FF, c : c + 256], NN)

    interleave(
        [functools.partial(ngrad_dot, c) for c in range(0, channels, 256)],
        [functools.partial(gelu, at, size, c) for c in range(IN_ROWS) for at, size in spans(TILE, 32)],
    )
    sums = [sums_ref[v] for v in range(4)]

    def back(at, size):
        sums[:] = second_norm_back(at, size, sums)

    interleave(
        [functools.partial(branch_dot, c) for c in range(0, channels, 256)],
        [functools.partial(back, at, size) for at, size in spans(TILE, 16)],
    )
    for v in range(4):
        sums_ref[v] = sums[v]
    for c in range(0, 2 * BIN_PAD, 512):
        total = bsum_ref[:, c : c + 512]
        for at, size in spans(TILE, 32):
            total = total + fold(hg[at : at + size, c : c + 512].astype(F32))
        bsum_ref[:, c : c + 512] = total
    hg_old[...] = hg[...]
    normed_old[...] = normed[...]
    for at, size in spans(TILE, 16):
        second_norm(at, size)

    @pl.when(step == count)
    def _():
        for c in range(0, 2 * BIN_PAD, 256):
            grad_dot(c)
        for c in range(lane_tiles):
            cut = slice(c * LANE, (c + 1) * LANE)
            for part, start in ((0, 0), (BIN_PAD, BINS)):
                lines[c, pl.ds(start + 1, 320, stride=2), :] = grad[part + HALF_BIN : part + HALF_BIN + 320, cut]
                lines[c, pl.ds(start, 320, stride=2), :] = grad[part : part + 320, cut]
                lines[c, start + 640 : start + 641, :] = grad[part + 320 : part + 321, cut]
            for b in range(40):
                low_half = lines[c, b * BR : b * BR + HALF, :].astype(BF16)
                high_half = lines[c, b * BR + HALF : b * BR + BR, :].astype(BF16)
                keep_ref[b, :, cut] = jnp.where(core == 0, low_half, high_half)
                send_ref[b, :, cut] = jnp.where(core == 0, high_half, low_half)
            tail_ref[:, cut] = lines[c, 1280:1288, :]
        store().wait()


def forward(owners, meta, places, counts, x, low, high, order, cot, pieces, table, utts):
    rows, frames, channels = x.shape
    tiles = frames // TILE
    steps = rows * tiles
    count = rows * frames
    slots = pieces[0].shape[0]
    ahead = lambda i: jnp.minimum(i, steps - 1)
    behind = lambda i: jnp.maximum(i - 1, 0)
    wide = pl.BlockSpec((TILE, FF), lambda i: (ahead(i), 0))
    wide_late = pl.BlockSpec((None, TILE, FF), lambda i: (behind(i) // tiles, behind(i) % tiles, 0))
    slim = pl.BlockSpec((TILE, channels), lambda i: (ahead(i), 0))
    slim_late = pl.BlockSpec((TILE, channels), lambda i: (behind(i), 0))
    return pl.pallas_call(
        functools.partial(forward_body, owners=owners, slots=slots, tiles=tiles, count=steps, utts=utts),
        grid=(steps + 1,),
        in_specs=[SCALARS, SCALARS, SCALARS, WHOLE, WHOLE, WHOLE, WHOLE, wide_late]
        + [ANYWHERE] * (len(pieces) + 1),
        out_specs=[ANYWHERE, wide_late, wide, wide, slim, slim_late, slim_late, slim]
        + [pl.BlockSpec((TILE, LANE), lambda i: (ahead(i), 0))]
        + [WHOLE] * 5,
        out_shape=[
            shape_of((NB * BR, channels), BF16),
            shape_of((rows, frames, 2 * BIN_PAD), BF16),
            shape_of((count, FF), BF16),
            shape_of((count, FF), BF16),
            shape_of((count, channels), BF16),
            shape_of((count, channels), BF16),
            shape_of((count, channels), BF16),
            shape_of((count, channels), BF16),
            shape_of((count, LANE), F32),
            shape_of((40, HALF, channels), BF16),
            shape_of((40, HALF, channels), BF16),
            shape_of((8, channels), F32),
            shape_of((4, 8, channels), F32),
            shape_of((8, 2 * BIN_PAD), F32),
        ],
        scratch_shapes=[
            pltpu.VMEM((NB * BR, channels), BF16),
            pltpu.VMEM((channels // LANE, TILE + 2 * EDGE, LANE), F32),
            pltpu.VMEM((2 * BIN_PAD, channels), BF16),
            pltpu.VMEM((8, 2 * BIN_PAD), F32),
            pltpu.VMEM((BR, channels), F32),
            pltpu.VMEM((2 * utts, channels), F32),
            pltpu.VMEM((2 * BIN_PAD, channels), F32),
            pltpu.VMEM((channels // LANE, 1344, LANE), F32),
            pltpu.VMEM((TILE, 2 * BIN_PAD), BF16),
            pltpu.VMEM((TILE, 2 * BIN_PAD), BF16),
            pltpu.VMEM((TILE, FF), F32),
            pltpu.VMEM((TILE, BIN_PAD), F32),
            pltpu.VMEM((TILE, BIN_PAD), F32),
            pltpu.VMEM((TILE, channels), F32),
            pltpu.VMEM((TILE, channels), F32),
            pltpu.VMEM((TILE, channels), F32),
            pltpu.VMEM((TILE, channels), BF16),
            pltpu.VMEM((TILE, channels), BF16),
            pltpu.VMEM((TILE, channels), F32),
            pltpu.VMEM((TILE, LANE), F32),
            pltpu.SMEM((1,), jnp.int32),
            pltpu.SemaphoreType.DMA,
            pltpu.SemaphoreType.DMA((2,)),
        ],
        compiler_params=params(),
        cost_estimate=cost(10 * count * 1536 * 512, 40 * MIB, count * 4096),
        name="forward",
    )(meta, places, counts, x, low, high, order, cot, *pieces, table)


def mlp_body(meta, low_ref, act_ref, der_ref, ada_ref, wout_ref, *rest, utts):
    pre_ref, send_ref, keep_ref, bsum_ref, gout, gin, agrad = rest[-7:]
    step = pl.program_id(0)
    core = meta[0, 2 * utts + 2]
    tile = low_ref.shape[0]

    @pl.when(step == 0)
    def _():
        gout[...] = jnp.zeros_like(gout)
        gin[...] = jnp.zeros_like(gin)
        bsum_ref[...] = jnp.zeros_like(bsum_ref)

    def agrad_dot(c):
        agrad[:, c : c + 256] = dot(low_ref[...], wout_ref[c : c + 256, :], NT)

    def gout_dot(c):
        gout[c : c + 256, :] += dot(act_ref[:, c : c + 256], low_ref[...], TN)

    def gin_dot(c):
        gin[c : c + 256, :] += dot(pre_ref[:, c : c + 256], ada_ref[...], TN)

    def slope(c):
        cut = slice(c, c + 256)
        total = bsum_ref[:, cut]
        for at, size in spans(tile, 32):
            span = slice(at, at + size)
            pre = (agrad[span, cut] * der_ref[span, cut].astype(F32)).astype(BF16)
            pre_ref[span, cut] = pre
            total = total + fold(pre.astype(F32))
        bsum_ref[:, cut] = total

    cuts = range(0, CHUNK, 256)
    for c in cuts:
        agrad_dot(c)
    interleave([functools.partial(gout_dot, c) for c in cuts], [functools.partial(slope, c) for c in cuts])
    for c in cuts:
        gin_dot(c)

    @pl.when(step == pl.num_programs(0) - 1)
    def _():
        buckets = CHUNK // BR
        for at, ref in ((0, gin), (buckets, gout)):
            for b in range(buckets):
                low_half = ref[b * BR : b * BR + HALF, :].astype(BF16)
                high_half = ref[b * BR + HALF : b * BR + BR, :].astype(BF16)
                keep_ref[at + b] = jnp.where(core == 0, low_half, high_half)
                send_ref[at + b] = jnp.where(core == 0, high_half, low_half)


def mlp_backward(chunk, before, meta, low, act, der, ada, table, utts):
    count, channels = low.shape
    tile = 512
    slim = pl.BlockSpec((tile, channels), lambda i: (i, 0))
    part = pl.BlockSpec((tile, CHUNK), lambda i: (i, chunk))
    buckets = 2 * CHUNK // BR
    more = [] if before is None else [before]
    return pl.pallas_call(
        functools.partial(mlp_body, utts=utts),
        grid=(count // tile,),
        in_specs=[
            SCALARS,
            slim,
            part,
            part,
            slim,
            pl.BlockSpec((CHUNK, channels), lambda i: (FF // CHUNK + chunk, 0)),
        ]
        + [ANYWHERE] * len(more),
        out_specs=[part, WHOLE, WHOLE, WHOLE],
        out_shape=[
            shape_of((count, FF), BF16),
            shape_of((buckets, HALF, channels), BF16),
            shape_of((buckets, HALF, channels), BF16),
            shape_of((8, CHUNK), F32),
        ],
        input_output_aliases={6: 0} if more else {},
        scratch_shapes=[
            pltpu.VMEM((CHUNK, channels), F32),
            pltpu.VMEM((CHUNK, channels), F32),
            pltpu.VMEM((tile, CHUNK), F32),
        ],
        compiler_params=params(),
        cost_estimate=cost(6 * count * CHUNK * 512, 16 * MIB),
        name=f"mlp_backward_{chunk}",
    )(meta, low, act, der, ada, table, *more)


def norm_body(
    meta, x_ref, low_ref, high_ref, pre_ref, w_in, last_ref, xc_ref, rc_ref, *rest, row, tiles, utts, closing
):
    more = rest[: 8 if closing else 0]
    outs = rest[len(more) :]
    cg_ref, edge_ref, part_ref = outs[:3]
    xs, vecs, picks, agrad, cg, reaches = outs[-6:]
    tile = pl.program_id(0)
    channels = x_ref.shape[2]
    lane_tiles = channels // LANE
    base = meta[row, 2 * utts + 1] + tile * TILE
    vec = lambda v: vecs[2 + v : 3 + v, :]

    @pl.when(tile == 0)
    def _():
        vecs[...] = last_ref[...].astype(F32)
        part_ref[...] = more[0][...] if closing else jnp.zeros_like(part_ref)
        pick_rows(meta, row, utts, vec, picks, channels)

    agrad[...] = dot(pre_ref[...], w_in[...], NN)
    fill_frames(xs, x_ref, low_ref, high_ref, 0, tile, tiles, channels)
    for at, size in spans(TILE, 32):
        span = slice(at, at + size)
        reach, left = frame_reach(meta, row, base + at, size, utts)
        reaches[0, span, :] = reach
        reaches[1, span, :] = left
        index = base + at + lax.broadcasted_iota(jnp.int32, (size, LANE), 0)
        ecs, xcs = [], []
        for c in range(lane_tiles):
            cut = slice(c * LANE, (c + 1) * LANE)
            scale = by_utterance(meta, row, utts, index, lambda u: picks[u : u + 1, cut])
            ecs.append(agrad[span, cut] * scale)
            xcs.append(xc_ref[span, cut].astype(F32))
        m_one = jnp.sum(sum(ecs), axis=1, keepdims=True) * (1.0 / channels)
        m_two = jnp.sum(sum([e * v for e, v in zip(ecs, xcs)]), axis=1, keepdims=True) * (1.0 / channels)
        rc = rc_ref[span, :]
        for c in range(lane_tiles):
            cut = slice(c * LANE, (c + 1) * LANE)
            value = rc * (ecs[c] - m_one - xcs[c] * m_two)
            cg[c, span, :] = value
            cg_ref[span, cut] = value.astype(BF16)
    for u in range(utts):
        begin, end = meta[row, u], meta[row, u + 1]

        @pl.when((begin < base + TILE) & (end > base))
        def _(u=u, begin=begin, end=end):
            wanted = meta[row, utts + 1 + u]
            for c in range(lane_tiles):
                cut = slice(c * LANE, (c + 1) * LANE)
                one = jnp.zeros((8, LANE), F32)
                two = jnp.zeros((8, LANE), F32)
                for at, size in spans(TILE, 64):
                    span = slice(at, at + size)
                    index = base + at + lax.broadcasted_iota(jnp.int32, (size, LANE), 0)
                    value = jnp.where((index >= begin) & (index < end), agrad[span, cut], 0.0)
                    one = one + fold(value * xc_ref[span, cut].astype(F32))
                    two = two + fold(value)
                part_ref[KW + 1 + wanted, :, cut] += one
                part_ref[KW + 1 + NBW + wanted, :, cut] += two

    for c in range(lane_tiles):
        cut = slice(c * LANE, (c + 1) * LANE)
        sums = [part_ref[k, :, cut] for k in range(KW + 1)]
        for at, size in spans(TILE, 32):
            span = slice(at, at + size)
            reach, left = reaches[0, span, :], reaches[1, span, :]
            value = cg[c, span, :]
            for k in range(KW):
                offset = k - RIM
                moved = xs[c, EDGE + offset + at : EDGE + offset + at + size, :] * value
                sums[k] = sums[k] + fold(keep_within(moved, reach, left, offset))
            sums[KW] = sums[KW] + fold(value)
        for k in range(KW + 1):
            part_ref[k, :, cut] = sums[k]

    def edge(side, begin):
        for c in range(lane_tiles):
            edge_ref[side, :, c * LANE : (c + 1) * LANE] = cg[c, begin : begin + 8, :]

    @pl.when(tile == 0)
    def _():
        edge(0, 0)

    @pl.when(tile == tiles - 1)
    def _():
        edge(1, TILE - 8)

    if closing:
        _, other_edge, tail_ref, sums_ref, hsum_ref, bsum0, bsum1, order_ref = more
        vec_ref, quarter_refs = outs[-7], outs[3:7]
        core, plane = meta[0, 2 * utts + 2], meta[0, 2 * utts + 3]

        @pl.when(tile == tiles - 1)
        def _():
            vec_ref[0:8, :] = jnp.zeros((8, channels), F32)
            vec_ref[0:2, :] = tail_ref[0:2, :]
            for v in range(VROWS):
                at = v - (KW + 1 + 2 * NBW)
                rows_of = part_ref[v] if at < 0 else sums_ref[at]
                vec_ref[2 + v : 3 + v, :] = jnp.sum(rows_of, axis=0, keepdims=True)
            line = jnp.concatenate([bsum0[...], bsum1[...]], axis=1)
            for c in range(IN_ROWS):
                at = 2 + VROWS + c
                vec_ref[at : at + 1, :] = jnp.sum(
                    line[:, c * channels : (c + 1) * channels], axis=0, keepdims=True
                )

            def bins(value):
                value = jnp.broadcast_to(jnp.sum(value, axis=0, keepdims=True), (16, BIN_PAD))
                total = jnp.zeros((16, BIN_PAD), F32)
                for _ in range(3):
                    part = value.astype(BF16)
                    value = value - part.astype(F32)
                    total = total + dot(part, order_ref[...], NT)
                return total[0:8]

            flat = jnp.concatenate([bins(hsum_ref[:, 0:BIN_PAD]), bins(hsum_ref[:, BIN_PAD:])], axis=1)
            column = lax.broadcasted_iota(jnp.int32, (8, 3 * channels), 1)
            moved = pltpu.roll(flat, 2 * BIN_PAD - (BIN_PAD - BINS), 1)
            joined = jnp.where(column < BINS, flat, moved)
            joined = jnp.where(column < NOUT, joined, 0.0)
            for c in range(HEAD_ROWS):
                at = 2 + VROWS + IN_ROWS + c
                vec_ref[at : at + 1, :] = joined[0:1, c * channels : (c + 1) * channels]
            vec_ref[28:32, :] = jnp.zeros((4, channels), F32)
            for ref, c, p in zip(
                quarter_refs,
                (core, 1 - core, core, 1 - core),
                (plane, plane, 1 - plane, 1 - plane),
            ):
                ref[0:8, :] = vec_ref[pl.ds(pl.multiple_of(c * HALF + p * QUART, QUART), QUART), :]
            for at, ref in ((8, other_edge), (16, edge_ref)):
                quarter_refs[1][at : at + 8, :] = jnp.where(core == 0, ref[1], ref[0])
                quarter_refs[3][at : at + 8, :] = jnp.where(core == 0, ref[0], ref[1])


def norm_backward(row, closing, meta, x, low, high, pre, table, xc, rc, utts):
    rows, frames, channels = x.shape
    tiles = frames // TILE
    block = lambda width: pl.BlockSpec((TILE, width), lambda i: (row * tiles + i, 0))
    sums = KW + 1 + 2 * NBW
    out_specs = [pl.BlockSpec((TILE, channels), lambda i: (i, 0)), WHOLE, WHOLE]
    out_shape = [
        shape_of((frames, channels), BF16),
        shape_of((2, 8, channels), F32),
        shape_of((sums, 8, channels), F32),
    ]
    if closing:
        out_specs += [WHOLE] * 4
        out_shape += [shape_of((8 * n, channels), F32) for n in (1, 3, 1, 3)]
    return pl.pallas_call(
        functools.partial(norm_body, row=row, tiles=tiles, utts=utts, closing=bool(closing)),
        grid=(tiles,),
        in_specs=[SCALARS]
        + [pl.BlockSpec((1, frames, channels), lambda i: (row, 0, 0))]
        + [pl.BlockSpec((1, EDGE, channels), lambda i: (row, 0, 0))] * 2
        + [block(FF)]
        + [
            pl.BlockSpec((FF, channels), lambda i: (0, 0)),
            pl.BlockSpec((BR, channels), lambda i: (NB - 1, 0)),
            block(channels),
            block(LANE),
        ]
        + [WHOLE] * len(closing),
        out_specs=out_specs,
        out_shape=out_shape,
        scratch_shapes=([pltpu.VMEM((BR, channels), F32)] if closing else [])
        + [
            pltpu.VMEM((channels // LANE, TILE + 2 * EDGE, LANE), F32),
            pltpu.VMEM((BR, channels), F32),
            pltpu.VMEM((2 * utts, channels), F32),
            pltpu.VMEM((TILE, channels), F32),
            pltpu.VMEM((channels // LANE, TILE, LANE), F32),
            pltpu.VMEM((2, TILE, LANE), jnp.int32),
        ],
        compiler_params=params(),
        cost_estimate=cost(2 * frames * 1536 * 512, 12 * MIB),
        name=f"norm_backward_{row}",
    )(meta, x, low, high, pre, table, table, xc, rc, *closing)


def conv_body(meta, cg_ref, before_ref, after_ref, near_ref, cross_ref, resg_ref, last_ref, *rest, row, tiles, utts):
    out_ref, cs, vecs = rest[-3:]
    tile = pl.program_id(0)
    channels = cg_ref.shape[1]
    core = meta[0, 2 * utts + 2]
    base = meta[row, 2 * utts + 1] + tile * TILE

    @pl.when(tile == 0)
    def _():
        vecs[...] = last_ref[...].astype(F32)

    for c in range(channels // LANE):
        cut = slice(c * LANE, (c + 1) * LANE)
        cs[c, EDGE : EDGE + TILE, :] = cg_ref[:, cut].astype(F32)
        near, cross = near_ref[8 + 8 * row : 16 + 8 * row, cut], cross_ref[8 + 8 * row : 16 + 8 * row, cut]
        before, after = before_ref[:, cut].astype(F32)[EDGE - 8 :], after_ref[:, cut].astype(F32)[:8]
        cs[c, EDGE - 8 : EDGE, :] = jnp.where(tile == 0, jnp.where(core == 0, cross, near), before)
        after = jnp.where(tile == tiles - 1, jnp.where(core == 0, near, cross), after)
        cs[c, EDGE + TILE : EDGE + TILE + 8, :] = after
    for at, size in spans(TILE, 32):
        span = slice(at, at + size)
        reach, left = frame_reach(meta, row, base + at, size, utts)
        for c in range(channels // LANE):
            cut = slice(c * LANE, (c + 1) * LANE)
            total = resg_ref[span, cut].astype(F32)
            for k in range(KW):
                offset = RIM - k
                moved = cs[c, EDGE + offset + at : EDGE + offset + at + size, :]
                total = total + keep_within(moved, reach, left, offset) * vecs[2 + k : 3 + k, cut]
            out_ref[0, span, cut] = total


def conv_backward(row, before, meta, cg, near, cross, resg, table, rows, utts):
    frames, channels = cg.shape
    tiles = frames // TILE
    per = TILE // EDGE
    more = [] if before is None else [before]
    return pl.pallas_call(
        functools.partial(conv_body, row=row, tiles=tiles, utts=utts),
        grid=(tiles,),
        in_specs=[
            SCALARS,
            pl.BlockSpec((TILE, channels), lambda i: (i, 0)),
            pl.BlockSpec((EDGE, channels), lambda i: (jnp.maximum(i * per - 1, 0), 0)),
            pl.BlockSpec((EDGE, channels), lambda i: (jnp.minimum((i + 1) * per, tiles * per - 1), 0)),
            WHOLE,
            WHOLE,
            pl.BlockSpec((TILE, channels), lambda i: (row * tiles + i, 0)),
            pl.BlockSpec((BR, channels), lambda i: (NB - 1, 0)),
        ]
        + [ANYWHERE] * len(more),
        out_specs=pl.BlockSpec((1, TILE, channels), lambda i: (row, i, 0)),
        out_shape=shape_of((rows, frames, channels), F32),
        input_output_aliases={8: 0} if more else {},
        scratch_shapes=[
            pltpu.VMEM((channels // LANE, TILE + 2 * EDGE, LANE), F32),
            pltpu.VMEM((BR, channels), F32),
        ],
        compiler_params=params(),
        cost_estimate=cost(16 * frames * 512, 6 * MIB),
        name=f"conv_backward_{row}",
    )(meta, cg, cg, cg, near, cross, resg, table, *more)


def wave_body(meta, spec_ref, prev_ref, halo_ref, synth_ref, win_ref, *rest, start, rows, utts):
    out_ref, spec_all, held_all, done_all = rest[-4:]
    tile = start + pl.program_id(0)
    lane = lax.broadcasted_iota(jnp.int32, (TILE // 2, LANE), 1)
    front = lane < LANE // 2
    for r in range(rows):
        spec, held, done = spec_all.at[r], held_all.at[r], done_all.at[r]
        base = meta[r, 2 * utts + 1] + tile * TILE
        spec[EDGE:, :] = spec_ref[r]
        spec[0:EDGE, :] = jnp.where(tile == 0, halo_ref[r], prev_ref[r])
        for parity in range(2):
            half = slice(parity * BIN_PAD, (parity + 1) * BIN_PAD)
            piece = dot(spec[:, half], synth_ref[parity], NN)
            for c in range(BIN_PAD // LANE):
                held[parity, c] = piece[:, c * LANE : (c + 1) * LANE]
        for at, size in spans(TILE, 32):
            reach, _ = frame_reach(meta, r, base + at, size, utts)
            for c in range(3):
                cut = slice(c * LANE, (c + 1) * LANE)
                total = None
                for j in range(LAPS):
                    rows_at = slice(EDGE + at - j, EDGE + at - j + size)
                    of = (j % 2) * 3 + c
                    one, two = held[0, of, rows_at, :], held[1, of, rows_at, :]
                    piece = (one + two if j < 2 else one - two) * win_ref[j : j + 1, cut]
                    total = piece if j == 0 else total + jnp.where(reach >= j, piece, 0.0)
                done[c, at : at + size, :] = total * over(win_ref, LAPS, reach, c)
        even = [done[c, pl.ds(0, TILE // 2, stride=2), :] for c in range(3)]
        odd = [pltpu.roll(done[c, pl.ds(1, TILE // 2, stride=2), :], LANE // 2, 1) for c in range(3)]
        part = (
            even[0],
            even[1],
            jnp.where(front, even[2], odd[0]),
            jnp.where(front, odd[0], odd[1]),
            jnp.where(front, odd[1], odd[2]),
        )
        for k in range(PAIR):
            out_ref[pl.ds(2 * k + r, TILE // 2, stride=2 * PAIR), :] = part[k]


def wave_forward(start, stop, before, meta, spec, halo, synth, win, utts):
    rows, frames, _ = spec.shape
    tiles = frames // TILE
    per = TILE // EDGE
    more = [] if before is None else [before]
    return pl.pallas_call(
        functools.partial(wave_body, start=start, rows=rows, utts=utts),
        grid=(stop - start,),
        in_specs=[
            SCALARS,
            pl.BlockSpec((rows, TILE, 2 * BIN_PAD), lambda i: (0, start + i, 0)),
            pl.BlockSpec((rows, EDGE, 2 * BIN_PAD), lambda i: (0, jnp.maximum((start + i) * per - 1, 0), 0)),
            WHOLE,
            WHOLE,
            WHOLE,
        ]
        + [ANYWHERE] * len(more),
        out_specs=pl.BlockSpec((PAIR * TILE, LANE), lambda i: (start + i, 0)),
        out_shape=shape_of((PAIR * TILE * tiles, LANE), F32),
        input_output_aliases={6: 0} if more else {},
        scratch_shapes=[
            pltpu.VMEM((rows, TILE + EDGE, 2 * BIN_PAD), BF16),
            pltpu.VMEM((rows, 2, BIN_PAD // LANE, TILE + EDGE, LANE), F32),
            pltpu.VMEM((rows, LAP_PAD // LANE, TILE, LANE), F32),
        ],
        compiler_params=params(),
        cost_estimate=cost(4 * rows * (stop - start) * TILE * 768 * 768, 10 * MIB),
        name=f"wave_forward_{start}",
    )(meta, spec, spec, halo, synth, win, *more)


def slot_body(slot_of, *refs, groups, lasts, copies, slots):
    count = max(g[0] for g in groups) + 1
    keeps, cames, last_refs = refs[:count], refs[count : 2 * count], refs[2 * count : 2 * count + lasts]
    out, *more = refs[2 * count + lasts :]
    for index, offset, start, stop in groups:

        def one(b, carry, keep=keeps[index], came=cames[index], offset=offset, start=start):
            value = keep[offset + b].astype(F32) + came[offset + b].astype(F32)
            out[slot_of[0, start + b]] = value.astype(BF16)
            return carry

        lax.fori_loop(0, stop - start, one, 0)
    total = last_refs[0][0:QUART, :]
    for ref in last_refs[1:]:
        total = total + ref[0:QUART, :]
    out[slot_of[0, NB - 1]] = total.astype(BF16)
    for ref, at in zip(more, copies):
        ref[...] = out[at * slots : (at + 1) * slots]


def to_slots(slot_of, keeps, cames, lasts, groups, owners, slots, copies):
    channels = keeps[0].shape[2]
    return pl.pallas_call(
        functools.partial(slot_body, groups=groups, lasts=len(lasts), copies=copies, slots=slots),
        in_specs=[SCALARS] + [WHOLE] * (2 * len(keeps) + len(lasts)),
        out_specs=[WHOLE] * (1 + len(copies)),
        out_shape=[shape_of((owners * slots, QUART, channels), BF16)]
        + [shape_of((slots, QUART, channels), BF16)] * len(copies),
        compiler_params=params(),
        cost_estimate=cost(0, 6 * MIB),
        name="to_slots",
    )(slot_of, *keeps, *cames, *lasts)


def adam_body(places, meta, mine_ref, other_ref, master, first, second, *rest, block):
    out_master, out_first, out_second = rest[-3:]
    one_fix = 1.0 / (1.0 - BETA_ONE**STEP_COUNT)
    two_fix = 1.0 / (1.0 - BETA_TWO**STEP_COUNT)
    core = meta[0, meta.shape[1] - 2]
    for s in range(block):
        bucket = places[0, pl.program_id(0) * block + s]
        mine, other = mine_ref[s].astype(F32), other_ref[s].astype(F32)
        for half in range(2):
            grad = jnp.where(bucket < NB, jnp.where(core == half, mine, other), 0.0)
            old = master[s, half, 0]
            one = BETA_ONE * first[s, half, 0] + (1.0 - BETA_ONE) * grad
            two = BETA_TWO * second[s, half, 0] + (1.0 - BETA_TWO) * grad * grad
            out_first[s, half, 0] = one
            out_second[s, half, 0] = two
            step = one * one_fix / (jnp.sqrt(two * two_fix) + ADAM_EPS)
            out_master[s, half, 0] = old - LEARN_RATE * (step + WEIGHT_DECAY * old)


def adam(places, meta, mine, other, master, first, second, before):
    slots, depth, channels = master.shape
    block = max(b for b in range(1, ADAM_BLOCK + 1) if slots % b == 0)
    plane_at = meta.shape[1] - 1
    cut = lambda v: v.reshape(slots, 2, 2, QUART, channels)
    def at_plane(i, places, meta):
        plane = meta[0, plane_at]
        return i, 0, 1 - plane if before else plane, 0, 0

    full = pl.BlockSpec((block, 2, 1, QUART, channels), at_plane)
    part = pl.BlockSpec((block, QUART, channels), lambda i, places, meta: (i, 0, 0))
    more = [cut(v) for v in before]
    outs = pl.pallas_call(
        functools.partial(adam_body, block=block),
        grid_spec=pltpu.PrefetchScalarGridSpec(
            num_scalar_prefetch=2,
            grid=(slots // block,),
            in_specs=[part] * 2 + [full] * 3 + [ANYWHERE] * len(more),
            out_specs=[full] * 3,
        ),
        out_shape=[shape_of((slots, 2, 2, QUART, channels), F32)] * 3,
        input_output_aliases={7 + v: v for v in range(len(more))},
        compiler_params=params(),
        cost_estimate=cost(0, 6 * MIB),
        name="adam_second" if more else "adam_first",
    )(places, meta, mine, other, cut(master), cut(first), cut(second), *more)
    return [v.reshape(slots, depth, channels) for v in outs]


def tie(*values):
    return lax.optimization_barrier(values)


def plus(*values):
    return sum([v.astype(F32) for v in values]).astype(BF16)


def local(frames_in, lengths, bw_ids, owner_list, master, moment1, moment2, wave_grad):
    rows, frames, channels = frames_in.shape
    slots = master.shape[0]
    utts = lengths.shape[1]
    owners = lax.axis_size("rows")
    seqs = lax.axis_size("seq")
    row_at = lax.axis_index("rows")
    seq_at = lax.axis_index("seq")
    core, plane = seq_at % 2, seq_at // 2
    ring = ring_of(owners)
    half_ring = owners // 2

    mine = lax.dynamic_slice_in_dim(master, core * HALF, HALF, axis=1).astype(BF16)

    lines = wave_grad.reshape(rows, frames * HOP // LANE, LANE).transpose(1, 0, 2).reshape(-1, LANE)
    order = jnp.asarray(order_table())
    synth = jnp.asarray(synthesis_table())
    win = jnp.asarray(window_tables())

    low = shifted(frames_in[:, frames - EDGE :], 1)
    high = shifted(frames_in[:, :EDGE], -1)
    later = shifted(lines[: PAIR * EDGE], -1)
    offsets = [0]
    for hop in range(1, half_ring):
        offsets += [-hop, hop]
    offsets.append(-half_ring)
    names = np.arange(owners, dtype=np.int32)
    ids = jnp.stack([row_at, seq_at]).astype(jnp.int32)
    meta, places, held, slot_of, counts = plan(
        ids,
        lengths,
        bw_ids,
        owner_list,
        jnp.asarray(ring if ring else names, jnp.int32),
        jnp.asarray(offsets if ring else names, jnp.int32),
        slots,
        frames,
        bool(ring),
    )

    cot = None
    tiles = frames // TILE
    if ring:
        ahead = back = mine
        arrived = [mine, seq_swap(mine, 1)]
        for hop in range(half_ring):
            source = (ahead, back)
            ahead = lax.ppermute(ahead, AXES, ring_step(ring, 1, seqs))
            if hop < half_ring - 1:
                back = lax.ppermute(back, AXES, ring_step(ring, -1, seqs))
            if hop == 0:
                ahead, back, low, high, later, meta = tie(ahead, back, low, high, later, meta)
            if hop in (1, 2):
                feed = tie(lines, *source)[0]
                begin, end = ((0, tiles // 2), (tiles // 2, tiles))[hop - 1]
                cot = spectrum_cotangent(begin, end, cot, meta, feed, later, synth, win, rows, utts)
                ahead, back, cot = tie(ahead, back, cot)
            if hop == half_ring - 1:
                fed = tie(places, *source)[0]
                partial_table = assemble(tuple(range(owners - 1)), meta, fed, counts, arrived, slots)
                ahead, partial_table = tie(ahead, partial_table)
            else:
                arrived += [ahead, seq_swap(ahead, 1), back, seq_swap(back, 1)]
        arrived = [ahead, seq_swap(ahead, 1)]
        owned = (owners - 1,)
        part_places, part_counts = places, counts
    else:
        gathered = lax.all_gather(mine, "rows", axis=0, tiled=True)
        arrived = [gathered, seq_swap(gathered, 1)]
        owned = (0,)
        arrived = [take_slots(slot_of, a) for a in arrived]
        part_places = jnp.arange(NB, dtype=jnp.int32)[None, :]
        part_counts = jnp.full((1, 1), NB, jnp.int32)
        partial_table = jnp.zeros((NB * BR, channels), BF16)
        cot = spectrum_cotangent(0, tiles, cot, meta, lines, later, synth, win, rows, utts)

    (table, spec, act, der, ada, low_grad, resg, xc, rc, send, keep, tail, sums, hsum) = forward(
        owned, meta, part_places, part_counts, frames_in, low, high, order, cot, arrived, partial_table, utts
    )
    halo = shifted(spec[:, frames - EDGE :], 1)

    keeps, cames, groups = [], [], []

    def split(keep, came):
        both = plus(keep, came)
        stay = lax.dynamic_slice_in_dim(both, plane * QUART, QUART, axis=1)
        leave = lax.dynamic_slice_in_dim(both, (1 - plane) * QUART, QUART, axis=1)
        return stay, leave

    def record(stay, came, begins, per):
        for at, begin in enumerate(begins):
            groups.append((len(keeps), at * per, begin, begin + per))
        keeps.append(stay)
        cames.append(came)

    per = CHUNK // BR
    pre, bsums = None, []
    begins, count = (2 * FF // BR,), 40
    waiting = []
    for chunk in range(FF // CHUNK):
        near = seq_swap(send, 1)
        pre, next_send, next_keep, bsum = mlp_backward(chunk, pre, meta, low_grad, act, der, ada, table, utts)
        near, pre, next_send, next_keep = tie(near, pre, next_send, next_keep)
        bsums.append(bsum)
        stay, leave = split(keep, near)
        waiting.append((stay, seq_swap(leave, 2), begins, count))
        send, keep = next_send, next_keep
        begins, count = (chunk * per, FF // BR + chunk * per), per

    near = seq_swap(send, 1)
    for stay, came, *where_from in waiting[:-1]:
        pre, came = tie(pre, came)
        record(stay, came, *where_from)
    cg0, edge0, parts = norm_backward(0, (), meta, frames_in, low, high, pre, table, xc, rc, utts)
    kept, came, *where_from = waiting[-1]
    near, cg0, edge0, parts, pre, came = tie(near, cg0, edge0, parts, pre, came)
    record(kept, came, *where_from)
    stay, leave = split(keep, near)
    came = seq_swap(leave, 2)
    closing = (parts, edge0, tail, sums, hsum, *bsums, order)
    cg1, _, _, own, to_near, to_far, to_cross = norm_backward(
        1, closing, meta, frames_in, low, high, pre, table, xc, rc, utts
    )
    lasts = (own, seq_swap(to_near, 1), seq_swap(to_far, 2), seq_swap(to_cross, 3))
    came, spec, *lasts = tie(came, spec, *lasts)
    record(stay, came, begins, count)
    first_sent = (owners - 1, owners - 3) if ring else ()
    chunks, *sent = to_slots(slot_of, keeps, cames, lasts, tuple(groups), owners, slots, first_sent)

    state = {}

    def work(stage, *ready):
        if stage in (0, 2):
            feed = tie(spec, *ready)[0]
            begin, end, before = ((0, tiles // 2, None), (tiles // 2, tiles, state.get("wave")))[stage // 2]
            state["wave"] = wave_forward(begin, end, before, meta, feed, halo, synth, win, utts)
            return "wave"
        if stage in (1, 3):
            row = stage // 2
            feed = tie((cg0, cg1)[row], *ready)[0]
            state["grad"] = conv_backward(
                row, state.get("grad"), meta, feed, lasts[1], lasts[3], resg, table, rows, utts
            )
            return "grad"

    if ring:
        cut = {o: chunks[i * slots : (i + 1) * slots] for i, o in enumerate(offsets)}
        up, down = sent
        for hop in range(half_ring):
            left_over = half_ring - 1 - hop
            source = (up, down)
            up = lax.ppermute(up, AXES, ring_step(ring, 1, seqs))
            if hop < half_ring - 1:
                down = lax.ppermute(down, AXES, ring_step(ring, -1, seqs))
            done = work(hop, *source)
            up, down, state[done] = tie(up, down, state[done])
            if left_over:
                up = plus(up, cut[left_over])
                if hop < half_ring - 2:
                    down = plus(down, cut[1 - left_over])
        own = plus(cut[0], up, down)
    else:
        own = lax.psum_scatter(chunks, "rows", scatter_dimension=0, tiled=True)
        for hop in range(4):
            work(hop, own)
    near, far = seq_swap(own, 1), seq_swap(own, 2)
    cross = seq_swap(far, 1)
    waveform = state["wave"].reshape(-1, rows, LANE).transpose(1, 0, 2).reshape(rows, frames * HOP)

    first = adam(held, meta, own, near, master, moment1, moment2, ())
    cross, *first = tie(cross, *first)
    new_master, new_first, new_second = adam(held, meta, far, cross, master, moment1, moment2, first)
    return waveform, state["grad"], new_master, new_first, new_second


def solution(mesh):
    in_specs = (
        P("rows", "seq", None),
        P("rows", None),
        P("rows", None),
        P(),
        P("rows", None, None),
        P("rows", None, None),
        P("rows", None, None),
        P("rows", "seq"),
    )
    out_specs = (
        P("rows", "seq"),
        P("rows", "seq", None),
        P("rows", None, None),
        P("rows", None, None),
        P("rows", None, None),
    )
    return jax.shard_map(local, mesh=mesh, in_specs=in_specs, out_specs=out_specs, check_vma=False)
```

```python
import functools
import math

import jax
import jax.numpy as jnp
import numpy as np
from jax import lax
from jax.experimental import pallas as pl
from jax.experimental.pallas import tpu as pltpu
from jax.sharding import PartitionSpec as P

FF = 1536
NFFT = 1280
HOP = 320
NBW = 4
KW = 7
UTT = 4
BR = 32
STEP_COUNT = 6
BINS = 641
NOUT = 1282
VROWS = 20
IN_ROWS = 3
HEAD_ROWS = 3
NB = 137

NORM_EPS = 1e-06
ENV_FLOOR = 0.5
BETA_ONE = 0.8
BETA_TWO = 0.9
LEARN_RATE = 0.04
WEIGHT_DECAY = 0.01
ADAM_EPS = 1e-08

LAPS = NFFT // HOP
RIM = (KW - 1) // 2
LAP_PAD = 384
BIN_PAD = 768
HALF = BR // 2
QUART = BR // 4
EDGE = 16
TILE = 256
CHUNK = 768
HALF_BIN = 384
PAIR = 5
ADAM_BLOCK = 27
LANE = 128
AXES = ("rows", "seq")

F32 = jnp.float32
BF16 = jnp.bfloat16
MIB = 1 << 20
VMEM_BYTES = 60 * MIB


def bin_order():
    order = np.full(BIN_PAD, -1)
    order[: (BINS + 1) // 2] = np.arange(0, BINS, 2)
    order[HALF_BIN : HALF_BIN + BINS // 2] = np.arange(1, BINS, 2)
    return order


def order_table():
    return (np.arange(BIN_PAD)[:, None] == bin_order()[None, :]).astype(jnp.bfloat16)


def synthesis_table():
    n = np.arange(2 * HOP)[None, :]
    order = bin_order()
    out = np.zeros((2, 2, HALF_BIN, 2, LAP_PAD), np.float32)
    for parity in range(2):
        k = order[parity * HALF_BIN : (parity + 1) * HALF_BIN]
        k = k[k >= 0][:, None]
        angle = (k * n % NFFT) * (2.0 * math.pi / NFFT)
        factor = np.where((k == 0) | (k == NFFT // 2), 1.0, 2.0) / NFFT
        out[parity, 0, : len(k), :, :HOP] = (factor * np.cos(angle)).reshape(-1, 2, HOP)
        out[parity, 1, : len(k), :, :HOP] = (-factor * np.sin(angle)).reshape(-1, 2, HOP)
    return out.reshape(2, BIN_PAD, 2 * LAP_PAD).astype(jnp.bfloat16)


def window_tables():
    window = 0.5 - 0.5 * np.cos(np.arange(NFFT) * (2.0 * math.pi / NFFT))
    rows = np.zeros((LAPS, LAP_PAD), np.float64)
    rows[:, :HOP] = window.reshape(LAPS, HOP)
    envelope = np.cumsum(rows**2, axis=0)
    return np.concatenate([rows, 1.0 / np.maximum(envelope, ENV_FLOOR)], axis=0).astype(np.float32)


def ring_of(count):
    if count != 8:
        return None
    return [0, 2, 4, 6, 7, 5, 3, 1]


def ring_step(ring, shift, seq_count):
    where = {r: i for i, r in enumerate(ring)}
    pairs = []
    for r in ring:
        target = ring[(where[r] + shift) % len(ring)]
        pairs += [(r * seq_count + s, target * seq_count + s) for s in range(seq_count)]
    return pairs


def seq_swap(value, bit):
    count = lax.axis_size("seq")
    return lax.ppermute(value, "seq", [(s, s ^ bit) for s in range(count)])


def rows_swap(value, bit):
    count = lax.axis_size("rows")
    return lax.ppermute(value, "rows", [(r, r ^ bit) for r in range(count)])


def shifted(value, distance):
    devices = range(lax.axis_size("seq"))
    return lax.ppermute(
        value, "seq", [(i - distance, i) for i in devices if i - distance in devices]
    )


def dot(a, b, dims):
    return lax.dot_general(a, b, (dims, ((), ())), preferred_element_type=F32)


NN = ((1,), (0,))
NT = ((1,), (1,))
TN = ((0,), (0,))


def frame_reach(meta, row, first, count, utts):
    index = first + lax.broadcasted_iota(jnp.int32, (count, 128), 0)
    start = jnp.zeros_like(index)
    end = jnp.zeros_like(index) + meta[row, 1]
    for u in range(1, utts):
        inside = index >= meta[row, u]
        start = jnp.where(inside, meta[row, u], start)
        end = jnp.where(inside, meta[row, u + 1], end)
    return index - start, end - 1 - index


def spans(count, size):
    return [(at, min(size, count - at)) for at in range(0, count, size)]


def over(table, base, reach, lane_tile, width=LANE):
    cut = slice(lane_tile * LANE, lane_tile * LANE + width)
    picked = jnp.broadcast_to(table[base + LAPS - 1 : base + LAPS, cut], (reach.shape[0], width))
    for j in range(LAPS - 2, -1, -1):
        picked = jnp.where(reach[:, :width] == j, table[base + j : base + j + 1, cut], picked)
    return picked


def keep_within(values, reach, left, offset):
    if offset < 0:
        return jnp.where(reach >= -offset, values, 0.0)
    if offset > 0:
        return jnp.where(left >= offset, values, 0.0)
    return values


def row_mean(values):
    return jnp.mean(values, axis=1, keepdims=True)


def fold(values):
    rows, columns = values.shape
    return jnp.sum(values.reshape(rows // 8, 8, columns), axis=0)


def sincos(angle):
    turns = jnp.round(angle * (0.5 / math.pi))
    rest = angle * 0.5 - turns * 3.1416015625
    rest = rest + turns * 8.908910206761537e-06
    sq = rest * rest
    sine = 1.0 + sq * (
        -0.16666656732559204
        + sq * (0.008333033882081509 + sq * (-0.00019807791977655143 + sq * 2.6022808015113696e-06))
    )
    cosine = 1.0 + sq * (
        -0.4999992549419403
        + sq * (0.04166382923722267 + sq * (-0.001385461655445397 + sq * 2.3163083824329078e-05))
    )
    sine = rest * sine
    double = sine + sine
    return double * cosine, 1.0 - double * sine


ANGLE_LIMIT = 1024.0


def params():
    return pltpu.CompilerParams(vmem_limit_bytes=VMEM_BYTES)


def cost(flops, bytes_accessed, transcendentals=0):
    return pl.CostEstimate(
        flops=int(flops), bytes_accessed=int(bytes_accessed), transcendentals=int(transcendentals)
    )


WHOLE = pl.BlockSpec(memory_space=pltpu.VMEM)
SCALARS = pl.BlockSpec(memory_space=pltpu.SMEM)
ANYWHERE = pl.BlockSpec(memory_space=pl.ANY)
shape_of = jax.ShapeDtypeStruct


def plan_body(ids, lengths, bw_ids, owner_list, order, offsets, meta, places, held, slot_of, counts, rel, *, frames, ring):
    rows, utts = lengths.shape
    owners, slots = order.shape[0], held.shape[1]
    row_at, seq_at = ids[0], ids[1]
    for r in range(rows):
        start = jnp.int32(0)
        meta[r, 0] = start
        for u in range(utts):
            start = start + lengths[r, u]
            meta[r, u + 1] = start
            meta[r, utts + 1 + u] = bw_ids[r, u]
        meta[r, 2 * utts + 1] = seq_at * frames
        meta[r, 2 * utts + 2] = lax.rem(seq_at, 2)
        meta[r, 2 * utts + 3] = lax.div(seq_at, 2)
    where = jnp.int32(0)
    if ring:
        for i in range(owners):
            where = jnp.where(order[i] == row_at, i, where)

    def name(i, carry):
        rel[order[lax.rem(where + offsets[i] + owners, owners)]] = i
        counts[0, i] = 0
        return carry

    def clear(i, carry):
        places[0, i] = NB
        return carry

    def place(b, carry):
        i = rel[owner_list[b]]
        n = counts[0, i]
        counts[0, i] = n + 1
        places[0, i * slots + n] = b
        slot_of[0, b] = i * slots + n
        return carry

    lax.fori_loop(0, owners, name, 0)
    lax.fori_loop(0, owners * slots, clear, 0, unroll=8)
    lax.fori_loop(0, NB, place, 0)
    own = rel[row_at]

    def keep(n, carry):
        held[0, n] = places[0, own * slots + n]
        return carry

    lax.fori_loop(0, slots, keep, 0, unroll=True)


def plan(ids, lengths, bw_ids, owner_list, order, offsets, slots, frames, ring):
    rows, utts = lengths.shape
    owners = order.shape[0]
    shapes = ((rows, 2 * utts + 4), (1, owners * slots), (1, slots), (1, NB), (1, owners))
    return pl.pallas_call(
        functools.partial(plan_body, frames=frames, ring=ring),
        in_specs=[SCALARS] * 6,
        out_specs=[SCALARS] * 5,
        out_shape=[shape_of(shape, jnp.int32) for shape in shapes],
        scratch_shapes=[pltpu.SMEM((owners,), jnp.int32)],
        compiler_params=params(),
        cost_estimate=cost(8000, 8 * 1024),
        name="plan",
    )(ids, lengths, bw_ids, owner_list, order, offsets)


def pre_body(meta, wave_ref, halo_ref, synth_ref, win_ref, *rest, start, tiles, rows, utts):
    out_ref, flat, scaled_all, even_all, odd_all = rest[-5:]
    step = pl.program_id(0)
    tile = start + step
    lines = PAIR * TILE
    extra = PAIR * EDGE
    count = TILE + EDGE
    lane = lax.broadcasted_iota(jnp.int32, (count // 2, LANE), 1)
    for at, size in spans(lines, 320):
        rows_at = pl.ds(pl.multiple_of(tile * lines + at, 16), size)
        flat[at : at + size, :] = wave_ref[rows_at, :].astype(F32)
    after = jnp.minimum((tile + 1) * lines, tiles * lines - extra)
    following = wave_ref[pl.ds(pl.multiple_of(after, 16), extra), :]
    flat[lines:, :] = jnp.where(tile == tiles - 1, halo_ref[...], following).astype(F32)
    for r in range(rows):
        scaled, even, odd = scaled_all.at[r], even_all.at[r], odd_all.at[r]
        base = meta[r, 2 * utts + 1] + tile * TILE
        part = [flat[pl.ds(2 * k + r, count // 2, stride=2 * PAIR), :] for k in range(PAIR)]
        turned = [pltpu.roll(v, LANE // 2, 1) for v in part[2:]]
        front = lane < LANE // 2
        frame = (
            part[0],
            part[1],
            jnp.where(front, part[2], 0.0),
            jnp.where(front, turned[0], turned[1]),
            jnp.where(front, turned[1], turned[2]),
            jnp.where(front, turned[2], 0.0),
        )
        for c in range(3):
            scaled[c, pl.ds(0, count // 2, stride=2), :] = frame[c]
            scaled[c, pl.ds(1, count // 2, stride=2), :] = frame[3 + c]
        for at, size in spans(count, 32):
            reach, _ = frame_reach(meta, r, base + at, size, utts)
            for c in range(3):
                scaled[c, at : at + size, :] = scaled[c, at : at + size, :] * over(win_ref, LAPS, reach, c)
        for at, size in spans(TILE, 32):
            _, left = frame_reach(meta, r, base + at, size, utts)
            for j in range(2):
                for c in range(3):
                    span = slice(c * LANE, (c + 1) * LANE)

                    def lap(i):
                        value = scaled[c, at + i : at + i + size, :] * win_ref[i : i + 1, span]
                        return keep_within(value, None, left, i).astype(BF16).astype(F32)

                    one, two = lap(j), lap(j + 2)
                    column = slice(j * LAP_PAD + c * LANE, j * LAP_PAD + (c + 1) * LANE)
                    even[at : at + size, column] = (one + two).astype(BF16)
                    odd[at : at + size, column] = (one - two).astype(BF16)
        out_ref[r, :, 0:BIN_PAD] = dot(even[...], synth_ref[0], NT).astype(BF16)
        out_ref[r, :, BIN_PAD:] = dot(odd[...], synth_ref[1], NT).astype(BF16)


def spectrum_cotangent(start, stop, before, meta, wave, halo, synth, win, rows, utts):
    tiles = wave.shape[0] // (PAIR * TILE)
    frames = tiles * TILE
    more = [] if before is None else [before]
    steps = stop - start
    return pl.pallas_call(
        functools.partial(pre_body, start=start, tiles=tiles, rows=rows, utts=utts),
        grid=(steps,),
        in_specs=[SCALARS, WHOLE, WHOLE, WHOLE, WHOLE] + [ANYWHERE] * len(more),
        out_specs=pl.BlockSpec((rows, TILE, 2 * BIN_PAD), lambda i: (0, start + i, 0)),
        out_shape=shape_of((rows, frames, 2 * BIN_PAD), BF16),
        input_output_aliases={5: 0} if more else {},
        scratch_shapes=[
            pltpu.VMEM((PAIR * (TILE + EDGE), LANE), F32),
            pltpu.VMEM((rows, LAP_PAD // LANE, TILE + EDGE, LANE), F32),
            pltpu.VMEM((rows, TILE, BIN_PAD), BF16),
            pltpu.VMEM((rows, TILE, BIN_PAD), BF16),
        ],
        compiler_params=params(),
        cost_estimate=cost(4 * rows * steps * TILE * 768 * 768, rows * steps * TILE * 3072 + 4 * MIB),
        name=f"spectrum_cotangent_{start}",
    )(meta, wave, halo, synth, win, *more)


def place_parts(places, counts, core, pieces, table, sem, slots, owners, start):
    done = {}
    for index, ref in enumerate(pieces):
        side = core if index % 2 == 0 else 1 - core
        owner = owners[index // 2]
        first = done.get((owner, index % 2), 0)
        done[owner, index % 2] = first + ref.shape[0]

        def one(s, carry, ref=ref, side=side, owner=owner, first=first):
            bucket = places[0, owner * slots + first + s]
            at = pl.multiple_of(bucket * BR + side * HALF, HALF)
            copy = pltpu.make_async_copy(ref.at[s], table.at[pl.ds(at, HALF), :], sem)
            if start:
                copy.start()
            else:
                copy.wait()
            return carry

        held = jnp.clip(counts[0, owner] - first, 0, ref.shape[0])
        lax.fori_loop(0, held, one, 0)


def assemble_body(meta, places, counts, *refs, slots, owners):
    pieces, table, sem = refs[: 2 * len(owners)], refs[-2], refs[-1]
    core = meta[0, meta.shape[1] - 2]
    place_parts(places, counts, core, pieces, table, sem, slots, owners, True)
    place_parts(places, counts, core, pieces, table, sem, slots, owners, False)


def assemble(owners, meta, places, counts, pieces, slots):
    channels = pieces[0].shape[2]
    return pl.pallas_call(
        functools.partial(assemble_body, slots=slots, owners=owners),
        in_specs=[SCALARS, SCALARS, SCALARS] + [ANYWHERE] * len(pieces),
        out_specs=WHOLE,
        out_shape=shape_of((NB * BR, channels), BF16),
        scratch_shapes=[pltpu.SemaphoreType.DMA],
        compiler_params=params(),
        cost_estimate=cost(0, 12 * MIB),
        name="assemble",
    )(meta, places, counts, *pieces)


def take_body(slot_of, ref, out, sem):
    def copy(b):
        return pltpu.make_async_copy(ref.at[slot_of[0, b]], out.at[b], sem)

    def start(b, carry):
        copy(b).start()
        return carry

    def wait(b, carry):
        copy(b).wait()
        return carry

    lax.fori_loop(0, NB, start, 0)
    lax.fori_loop(0, NB, wait, 0)


def take_slots(slot_of, gathered):
    return pl.pallas_call(
        take_body,
        in_specs=[SCALARS, ANYWHERE],
        out_specs=WHOLE,
        out_shape=shape_of((NB, *gathered.shape[1:]), BF16),
        scratch_shapes=[pltpu.SemaphoreType.DMA],
        compiler_params=params(),
        cost_estimate=cost(0, 6 * MIB),
        name="take_slots",
    )(slot_of, gathered)


def fill_frames(xs, x_ref, low_ref, high_ref, row, tile, tiles, channels):
    first = pl.multiple_of(tile * TILE, TILE)

    def put(at, block):
        block = block.astype(F32)
        for c in range(channels // LANE):
            xs[c, at : at + block.shape[0], :] = block[:, c * LANE : (c + 1) * LANE]

    for at, size in spans(TILE, 64):
        put(EDGE + at, x_ref[row, pl.ds(pl.multiple_of(first + at, 64), size), :])

    before = x_ref[row, pl.ds(pl.multiple_of(jnp.maximum(first - EDGE, 0), EDGE), EDGE), :]
    put(0, jnp.where(tile == 0, low_ref[row], before))
    end = jnp.minimum(first + TILE, (tiles - 1) * TILE)
    after = x_ref[row, pl.ds(pl.multiple_of(end, EDGE), EDGE), :]
    put(EDGE + TILE, jnp.where(tile == tiles - 1, high_ref[row], after))


def by_utterance(meta, row, utts, index, rows_of):
    value = jnp.broadcast_to(rows_of(0), (index.shape[0], LANE))
    for u in range(1, utts):
        value = jnp.where(index >= meta[row, u], rows_of(u), value)
    return value


def pick_rows(meta, row, utts, vec, out, channels):
    for u in range(utts):
        wanted = meta[row, utts + 1 + u]
        for at, offset in ((u, KW + 1), (utts + u, KW + 1 + NBW)):
            value = vec(offset)
            for b in range(1, NBW):
                value = jnp.where(wanted == b, vec(offset + b), value)
            out[at : at + 1, :] = value


def interleave(ones, others):
    at = 0
    for i, one in enumerate(ones):
        one()
        until = (i + 1) * len(others) // len(ones)
        for other in others[at:until]:
            other()
        at = until
    for other in others[at:]:
        other()


def forward_body(meta, places, counts, x_ref, low_ref, high_ref, order_ref, cot_ref, *rest, owners, slots, tiles, count, utts):
    pieces = rest[: 2 * len(owners)]
    table_in = rest[2 * len(owners)]
    (
        table_out,
        spec_ref,
        act_ref,
        der_ref,
        ada_ref,
        lowg_ref,
        resg_ref,
        xc_ref,
        rc_ref,
        send_ref,
        keep_ref,
        tail_ref,
        sums_ref,
        bsum_ref,
        table,
        xs,
        w_head,
        b_head,
        vecs,
        picks,
        grad,
        lines,
        hg,
        hg_old,
        pre_ref,
        logs_ref,
        angle_ref,
        ngrad_ref,
        slim,
        xn_ref,
        normed,
        normed_old,
        branch_ref,
        rn_ref,
        slow,
        sem,
        sems,
    ) = rest[2 * len(owners) + 1 :]
    step = pl.program_id(0)
    core = meta[0, 2 * utts + 2]
    channels = x_ref.shape[2]
    lane_tiles = channels // LANE
    now = jnp.minimum(step, count - 1)
    row, tile = now // tiles, now % tiles
    vec = lambda v: vecs[2 + v : 3 + v, :]
    vec_at = KW + 1 + 2 * NBW
    head_at = 2 * FF

    def store():
        return pltpu.make_async_copy(table, table_out, sems.at[1])

    @pl.when(step == 0)
    def _():
        whole = pltpu.make_async_copy(table_in, table, sems.at[0])
        whole.start()
        normed[...] = jnp.zeros_like(normed)
        w_head[...] = jnp.zeros_like(w_head)
        b_head[...] = jnp.zeros_like(b_head)
        whole.wait()
        place_parts(places, counts, core, pieces, table, sem, slots, owners, True)
        place_parts(places, counts, core, pieces, table, sem, slots, owners, False)
        store().start()
        vecs[...] = table[head_at + 1280 : head_at + 1280 + BR, :].astype(F32)

    @pl.when(step == 1)
    def _():
        sums_ref[...] = jnp.zeros_like(sums_ref)
        bsum_ref[...] = jnp.zeros_like(bsum_ref)

    @pl.when(step == 2)
    def _():
        grad[...] = jnp.zeros_like(grad)

    @pl.when(tile == 0)
    def _():
        pick_rows(meta, row, utts, vec, picks, channels)

    base = meta[row, 2 * utts + 1] + tile * TILE
    fill_frames(xs, x_ref, low_ref, high_ref, row, tile, tiles, channels)

    def convolve(at, size):
        reach, left = frame_reach(meta, row, base + at, size, utts)
        index = base + at + lax.broadcasted_iota(jnp.int32, (size, LANE), 0)
        conv = []
        for c in range(lane_tiles):
            cut = slice(c * LANE, (c + 1) * LANE)
            total = vecs[2 + KW : 3 + KW, cut]
            for k in range(KW):
                offset = k - RIM
                moved = xs[c, EDGE + offset + at : EDGE + offset + at + size, :]
                total = total + keep_within(moved, reach, left, offset) * vecs[2 + k : 3 + k, cut]
            conv.append(total)
        mean = jnp.sum(sum(conv), axis=1, keepdims=True) * (1.0 / channels)
        conv = [v - mean for v in conv]
        square = jnp.sum(sum([v * v for v in conv]), axis=1, keepdims=True) * (1.0 / channels)
        rc = jnp.broadcast_to(lax.rsqrt(square + NORM_EPS), (size, LANE))
        rc_ref[at : at + size, :] = rc
        for c in range(lane_tiles):
            cut = slice(c * LANE, (c + 1) * LANE)
            xc = conv[c] * rc
            xc_ref[at : at + size, cut] = xc.astype(BF16)
            scale = by_utterance(meta, row, utts, index, lambda u: picks[u : u + 1, cut])
            shift = by_utterance(meta, row, utts, index, lambda u: picks[utts + u : utts + u + 1, cut])
            ada_ref[at : at + size, cut] = (xc * scale + shift).astype(BF16)

    def head(at, size, turn):
        span = slice(at, at + size)
        for c in range(0, BIN_PAD, LANE):
            bins, angles = slice(c, c + LANE), slice(BIN_PAD + c, BIN_PAD + c + LANE)
            parity, inner = c // HALF_BIN, c % HALF_BIN
            reals = slice(parity * BIN_PAD + inner, parity * BIN_PAD + inner + LANE)
            imags = slice(reals.start + HALF_BIN, reals.stop + HALF_BIN)
            angle = angle_ref[span, bins] + b_head[0:1, angles]
            scale = jnp.exp(logs_ref[span, bins] + b_head[0:1, bins])
            sine, cosine = turn(angle)
            real, imag = scale * cosine, scale * sine
            spec_ref[span, reals] = real.astype(BF16)
            spec_ref[span, imags] = imag.astype(BF16)
            dre = cot_ref[span, reals].astype(F32)
            dim = cot_ref[span, imags].astype(F32)
            hg[span, bins] = (dre * real + dim * imag).astype(BF16)
            hg[span, angles] = (dim * real - dre * imag).astype(BF16)

    def gelu(at, size, c):
        for d in range(c * 512, (c + 1) * 512, 256):
            cut = slice(d, d + 256)
            bias = vecs[2 + VROWS + c : 3 + VROWS + c, d - c * 512 : d - c * 512 + 256]
            pre = pre_ref[at : at + size, cut] + bias
            phi = 0.5 + 0.5 * lax.erf(pre * math.sqrt(0.5))
            bell = jnp.exp(-0.5 * pre * pre) * (1.0 / math.sqrt(2.0 * math.pi))
            act_ref[at : at + size, cut] = (pre * phi).astype(BF16)
            der_ref[at : at + size, cut] = (phi + pre * bell).astype(BF16)

    def second_norm(at, size):
        span = slice(at, at + size)
        branch = slim[span, :] + vec(vec_at)
        branch_ref[span, :] = branch
        x = jnp.concatenate([xs[c, EDGE + at : EDGE + at + size, :] for c in range(lane_tiles)], axis=1)
        residual = x + vec(vec_at + 1) * branch
        residual = residual - row_mean(residual)
        rn = lax.rsqrt(row_mean(residual * residual) + NORM_EPS)
        rn_ref[span, :] = jnp.broadcast_to(rn, (size, LANE))
        xn = residual * rn
        xn_ref[span, :] = xn
        normed[span, :] = (xn * vec(vec_at + 2) + vec(vec_at + 3)).astype(BF16)

    def second_norm_back(at, size, sums):
        span = slice(at, at + size)
        ngrad = ngrad_ref[span, :]
        xn = xn_ref[span, :]
        e = ngrad * vec(vec_at + 2)
        resg = rn_ref[span, 0:1] * (e - row_mean(e) - xn * row_mean(e * xn))
        resg_ref[span, :] = resg.astype(BF16)
        low = (vec(vec_at + 1) * resg).astype(BF16)
        lowg_ref[span, :] = low
        return (
            sums[0] + fold(low.astype(F32)),
            sums[1] + fold(resg * branch_ref[span, :]),
            sums[2] + fold(ngrad * xn),
            sums[3] + fold(ngrad),
        )

    def head_dots(ref, begin):
        def one(c):
            ref[:, c : c + 256] = dot(normed[...], w_head[begin + c : begin + c + 256, :], NT)

        return [functools.partial(one, c) for c in range(0, BIN_PAD, 256)]

    def hidden_dot(c):
        pre_ref[:, c : c + 256] = dot(ada_ref[...], table[c : c + 256, :], NT)

    def grad_dot(c):
        grad[c : c + 256, :] += dot(hg_old[:, c : c + 256], normed_old[...], TN)

    def ngrad_dot(c):
        ngrad_ref[:, c : c + 256] = dot(hg[...], w_head[:, c : c + 256], NN)

    def branch_dot(c):
        slim[:, c : c + 256] = dot(act_ref[...], table[FF : 2 * FF, c : c + 256], NN)

    def head_again():
        def again(i, carry):
            rows = pl.ds(pl.multiple_of(i * 32, 32), 32)
            for c in range(0, BIN_PAD, LANE):
                bins, angles = slice(c, c + LANE), slice(BIN_PAD + c, BIN_PAD + c + LANE)
                parity, inner = c // HALF_BIN, c % HALF_BIN
                reals = slice(parity * BIN_PAD + inner, parity * BIN_PAD + inner + LANE)
                imags = slice(reals.start + HALF_BIN, reals.stop + HALF_BIN)
                angle = angle_ref[rows, bins] + b_head[0:1, angles]
                scale = jnp.exp(logs_ref[rows, bins] + b_head[0:1, bins])
                real, imag = scale * jnp.cos(angle), scale * jnp.sin(angle)
                spec_ref[rows, reals] = real.astype(BF16)
                spec_ref[rows, imags] = imag.astype(BF16)
                dre = cot_ref[rows, reals].astype(F32)
                dim = cot_ref[rows, imags].astype(F32)
                hg[rows, bins] = (dre * real + dim * imag).astype(BF16)
                hg[rows, angles] = (dim * real - dre * imag).astype(BF16)
            return carry

        lax.fori_loop(0, TILE // 32, again, 0)

    def build_head():
        last = vecs[...]
        line = jnp.concatenate([last[25:26], last[26:27], last[27:28]], axis=1)
        line = jnp.broadcast_to(line, (16, 3 * channels))
        moved = pltpu.roll(line, 3 * channels - BINS, 1)
        for at, value in ((0, line), (BIN_PAD, moved)):
            picked = dot(value[:, 0:BIN_PAD].astype(BF16), order_ref[...], NN)
            b_head[:, at : at + BIN_PAD] = picked[0:8]
        inside = lax.broadcasted_iota(jnp.int32, (336, LANE), 0)
        for c in range(lane_tiles):
            cut = slice(c * LANE, (c + 1) * LANE)
            lines[c, 0:1312, :] = table[head_at : head_at + 1312, cut].astype(F32)
            lines[c, 1312:, :] = jnp.zeros((lines.shape[1] - 1312, LANE), F32)
            for part, start in ((0, 0), (BIN_PAD, BINS)):
                evens = lines[c, pl.ds(start, 336, stride=2), :]
                w_head[part : part + 336, cut] = jnp.where(inside < (BINS + 1) // 2, evens, 0.0).astype(BF16)
                odds = lines[c, pl.ds(start + 1, 320, stride=2), :]
                w_head[part + HALF_BIN : part + HALF_BIN + 320, cut] = odds.astype(BF16)
        longest = jnp.zeros((8, 1), F32)
        for at, size in spans(BIN_PAD, 64):
            weights = w_head[BIN_PAD + at : BIN_PAD + at + size, :].astype(F32)
            length = jnp.sum(weights * weights, axis=1, keepdims=True)
            longest = jnp.maximum(longest, jnp.max(length.reshape(size // 8, 8, 1), axis=0))
        gain, shift = jnp.abs(vec(vec_at + 2)), vec(vec_at + 3)
        normed_length = math.sqrt(channels) * jnp.max(gain) + jnp.sqrt(jnp.sum(shift * shift, keepdims=True))[0, 0]
        bound = 1.05 * normed_length * jnp.max(jnp.sqrt(longest)) + jnp.max(jnp.abs(b_head[:, BIN_PAD:]))
        slow[0] = jnp.where(bound < ANGLE_LIMIT, 0, 1)

    def over_all(call, values):
        return [functools.partial(call, v) for v in values]

    def in_spans(call, size, *more):
        return [functools.partial(call, at, length, *more) for at, length in spans(TILE, size)]

    def work(first, second):
        interleave(
            head_dots(logs_ref, 0) + head_dots(angle_ref, BIN_PAD) if second else [],
            in_spans(convolve, 32) if first else [],
        )
        interleave(
            (over_all(hidden_dot, range(0, FF, 256)) if first else [])
            + (over_all(grad_dot, range(0, 2 * BIN_PAD, 256)) if second else []),
            in_spans(head, 16, sincos) if second else [],
        )
        if second:
            pl.when(slow[0] > 0)(head_again)
        interleave(
            over_all(ngrad_dot, range(0, channels, 256)) if second else [],
            [call for c in range(IN_ROWS) for call in in_spans(gelu, 32, c)] if first else [],
        )
        sums = [sums_ref[v] for v in range(4)]

        def back(at, size):
            sums[:] = second_norm_back(at, size, sums)

        interleave(
            over_all(branch_dot, range(0, channels, 256)) if first else [],
            in_spans(back, 16) if second else [],
        )
        if second:
            for v in range(4):
                sums_ref[v] = sums[v]
            for c in range(0, 2 * BIN_PAD, 512):
                total = bsum_ref[:, c : c + 512]
                for at, size in spans(TILE, 32):
                    total = total + fold(hg[at : at + size, c : c + 512].astype(F32))
                bsum_ref[:, c : c + 512] = total
            hg_old[...] = hg[...]
            normed_old[...] = normed[...]
        if first:
            interleave([], in_spans(second_norm, 16))

    @pl.when(step == 0)
    def _():
        work(True, False)
        build_head()

    @pl.when((step > 0) & (step < count))
    def _():
        work(True, True)

    @pl.when(step == count)
    def _():
        work(False, True)

    @pl.when(step == count)
    def _():
        for c in range(0, 2 * BIN_PAD, 256):
            grad_dot(c)
        for c in range(lane_tiles):
            cut = slice(c * LANE, (c + 1) * LANE)
            for part, start in ((0, 0), (BIN_PAD, BINS)):
                lines[c, pl.ds(start + 1, 320, stride=2), :] = grad[part + HALF_BIN : part + HALF_BIN + 320, cut]
                lines[c, pl.ds(start, 320, stride=2), :] = grad[part : part + 320, cut]
                lines[c, start + 640 : start + 641, :] = grad[part + 320 : part + 321, cut]
            for b in range(40):
                low_half = lines[c, b * BR : b * BR + HALF, :].astype(BF16)
                high_half = lines[c, b * BR + HALF : b * BR + BR, :].astype(BF16)
                keep_ref[b, :, cut] = jnp.where(core == 0, low_half, high_half)
                send_ref[b, :, cut] = jnp.where(core == 0, high_half, low_half)
            tail_ref[:, cut] = lines[c, 1280:1288, :]
        store().wait()


def forward(owners, slots, meta, places, counts, x, low, high, order, cot, pieces, table, utts):
    rows, frames, channels = x.shape
    tiles = frames // TILE
    steps = rows * tiles
    count = rows * frames
    ahead = lambda i: jnp.minimum(i, steps - 1)
    behind = lambda i: jnp.maximum(i - 1, 0)
    wide = pl.BlockSpec((TILE, FF), lambda i: (ahead(i), 0))
    wide_late = pl.BlockSpec((None, TILE, FF), lambda i: (behind(i) // tiles, behind(i) % tiles, 0))
    slim = pl.BlockSpec((TILE, channels), lambda i: (ahead(i), 0))
    slim_late = pl.BlockSpec((TILE, channels), lambda i: (behind(i), 0))
    return pl.pallas_call(
        functools.partial(forward_body, owners=owners, slots=slots, tiles=tiles, count=steps, utts=utts),
        grid=(steps + 1,),
        in_specs=[SCALARS, SCALARS, SCALARS, WHOLE, WHOLE, WHOLE, WHOLE, wide_late]
        + [ANYWHERE] * (len(pieces) + 1),
        out_specs=[ANYWHERE, wide_late, wide, wide, slim, slim_late, slim_late, slim]
        + [pl.BlockSpec((TILE, LANE), lambda i: (ahead(i), 0))]
        + [WHOLE] * 5,
        out_shape=[
            shape_of((NB * BR, channels), BF16),
            shape_of((rows, frames, 2 * BIN_PAD), BF16),
            shape_of((count, FF), BF16),
            shape_of((count, FF), BF16),
            shape_of((count, channels), BF16),
            shape_of((count, channels), BF16),
            shape_of((count, channels), BF16),
            shape_of((count, channels), BF16),
            shape_of((count, LANE), F32),
            shape_of((40, HALF, channels), BF16),
            shape_of((40, HALF, channels), BF16),
            shape_of((8, channels), F32),
            shape_of((4, 8, channels), F32),
            shape_of((8, 2 * BIN_PAD), F32),
        ],
        scratch_shapes=[
            pltpu.VMEM((NB * BR, channels), BF16),
            pltpu.VMEM((channels // LANE, TILE + 2 * EDGE, LANE), F32),
            pltpu.VMEM((2 * BIN_PAD, channels), BF16),
            pltpu.VMEM((8, 2 * BIN_PAD), F32),
            pltpu.VMEM((BR, channels), F32),
            pltpu.VMEM((2 * utts, channels), F32),
            pltpu.VMEM((2 * BIN_PAD, channels), F32),
            pltpu.VMEM((channels // LANE, 1344, LANE), F32),
            pltpu.VMEM((TILE, 2 * BIN_PAD), BF16),
            pltpu.VMEM((TILE, 2 * BIN_PAD), BF16),
            pltpu.VMEM((TILE, FF), F32),
            pltpu.VMEM((TILE, BIN_PAD), F32),
            pltpu.VMEM((TILE, BIN_PAD), F32),
            pltpu.VMEM((TILE, channels), F32),
            pltpu.VMEM((TILE, channels), F32),
            pltpu.VMEM((TILE, channels), F32),
            pltpu.VMEM((TILE, channels), BF16),
            pltpu.VMEM((TILE, channels), BF16),
            pltpu.VMEM((TILE, channels), F32),
            pltpu.VMEM((TILE, LANE), F32),
            pltpu.SMEM((1,), jnp.int32),
            pltpu.SemaphoreType.DMA,
            pltpu.SemaphoreType.DMA((2,)),
        ],
        compiler_params=params(),
        cost_estimate=cost(10 * count * 1536 * 512, 40 * MIB, count * 4096),
        name="forward",
    )(meta, places, counts, x, low, high, order, cot, *pieces, table)


def mlp_body(meta, low_ref, act_ref, der_ref, ada_ref, wout_ref, *rest, utts):
    pre_ref, send_ref, keep_ref, bsum_ref, gout, gin, agrad = rest[-7:]
    step = pl.program_id(0)
    core = meta[0, 2 * utts + 2]
    tile = low_ref.shape[0]

    @pl.when(step == 0)
    def _():
        gout[...] = jnp.zeros_like(gout)
        gin[...] = jnp.zeros_like(gin)
        bsum_ref[...] = jnp.zeros_like(bsum_ref)

    def agrad_dot(c):
        agrad[:, c : c + 256] = dot(low_ref[...], wout_ref[c : c + 256, :], NT)

    def gout_dot(c):
        gout[c : c + 256, :] += dot(act_ref[:, c : c + 256], low_ref[...], TN)

    def gin_dot(c):
        gin[c : c + 256, :] += dot(pre_ref[:, c : c + 256], ada_ref[...], TN)

    def slope(c):
        cut = slice(c, c + 256)
        total = bsum_ref[:, cut]
        for at, size in spans(tile, 32):
            span = slice(at, at + size)
            pre = (agrad[span, cut] * der_ref[span, cut].astype(F32)).astype(BF16)
            pre_ref[span, cut] = pre
            total = total + fold(pre.astype(F32))
        bsum_ref[:, cut] = total

    cuts = range(0, CHUNK, 256)
    for c in cuts:
        agrad_dot(c)
    interleave([functools.partial(gout_dot, c) for c in cuts], [functools.partial(slope, c) for c in cuts])
    for c in cuts:
        gin_dot(c)

    @pl.when(step == pl.num_programs(0) - 1)
    def _():
        buckets = CHUNK // BR
        for at, ref in ((0, gin), (buckets, gout)):
            for b in range(buckets):
                low_half = ref[b * BR : b * BR + HALF, :].astype(BF16)
                high_half = ref[b * BR + HALF : b * BR + BR, :].astype(BF16)
                keep_ref[at + b] = jnp.where(core == 0, low_half, high_half)
                send_ref[at + b] = jnp.where(core == 0, high_half, low_half)


def mlp_backward(chunk, before, meta, low, act, der, ada, table, utts):
    count, channels = low.shape
    tile = 512
    slim = pl.BlockSpec((tile, channels), lambda i: (i, 0))
    part = pl.BlockSpec((tile, CHUNK), lambda i: (i, chunk))
    buckets = 2 * CHUNK // BR
    more = [] if before is None else [before]
    return pl.pallas_call(
        functools.partial(mlp_body, utts=utts),
        grid=(count // tile,),
        in_specs=[
            SCALARS,
            slim,
            part,
            part,
            slim,
            pl.BlockSpec((CHUNK, channels), lambda i: (FF // CHUNK + chunk, 0)),
        ]
        + [ANYWHERE] * len(more),
        out_specs=[part, WHOLE, WHOLE, WHOLE],
        out_shape=[
            shape_of((count, FF), BF16),
            shape_of((buckets, HALF, channels), BF16),
            shape_of((buckets, HALF, channels), BF16),
            shape_of((8, CHUNK), F32),
        ],
        input_output_aliases={6: 0} if more else {},
        scratch_shapes=[
            pltpu.VMEM((CHUNK, channels), F32),
            pltpu.VMEM((CHUNK, channels), F32),
            pltpu.VMEM((tile, CHUNK), F32),
        ],
        compiler_params=params(),
        cost_estimate=cost(6 * count * CHUNK * 512, 16 * MIB),
        name=f"mlp_backward_{chunk}",
    )(meta, low, act, der, ada, table, *more)


def norm_body(
    meta,
    x_ref,
    low_ref,
    high_ref,
    pre_ref,
    w_in,
    last_ref,
    xc_ref,
    rc_ref,
    tail_ref,
    sums_ref,
    hsum_ref,
    bsum0,
    bsum1,
    order_ref,
    cg_ref,
    own_ref,
    near_ref,
    far_ref,
    cross_ref,
    part_ref,
    edge_ref,
    vec_ref,
    xs,
    vecs,
    picks,
    agrad,
    cg,
    reaches,
    *,
    tiles,
    utts,
):
    step = pl.program_id(0)
    row, tile = step // tiles, step % tiles
    rows = x_ref.shape[0]
    channels = x_ref.shape[2]
    lane_tiles = channels // LANE
    base = meta[row, 2 * utts + 1] + tile * TILE
    vec = lambda v: vecs[2 + v : 3 + v, :]

    @pl.when(step == 0)
    def _():
        vecs[...] = last_ref[...].astype(F32)
        part_ref[...] = jnp.zeros_like(part_ref)

    @pl.when(tile == 0)
    def _():
        pick_rows(meta, row, utts, vec, picks, channels)

    agrad[...] = dot(pre_ref[...], w_in[...], NN)
    fill_frames(xs, x_ref, low_ref, high_ref, row, tile, tiles, channels)
    for at, size in spans(TILE, 32):
        span = slice(at, at + size)
        reach, left = frame_reach(meta, row, base + at, size, utts)
        reaches[0, span, :] = reach
        reaches[1, span, :] = left
        index = base + at + lax.broadcasted_iota(jnp.int32, (size, LANE), 0)
        ecs, xcs = [], []
        for c in range(lane_tiles):
            cut = slice(c * LANE, (c + 1) * LANE)
            scale = by_utterance(meta, row, utts, index, lambda u: picks[u : u + 1, cut])
            ecs.append(agrad[span, cut] * scale)
            xcs.append(xc_ref[span, cut].astype(F32))
        m_one = jnp.sum(sum(ecs), axis=1, keepdims=True) * (1.0 / channels)
        m_two = jnp.sum(sum([e * v for e, v in zip(ecs, xcs)]), axis=1, keepdims=True) * (1.0 / channels)
        rc = rc_ref[span, :]
        for c in range(lane_tiles):
            cut = slice(c * LANE, (c + 1) * LANE)
            value = rc * (ecs[c] - m_one - xcs[c] * m_two)
            cg[c, span, :] = value
            cg_ref[span, cut] = value.astype(BF16)
    for u in range(utts):
        begin, end = meta[row, u], meta[row, u + 1]

        @pl.when((begin < base + TILE) & (end > base))
        def _(u=u, begin=begin, end=end):
            wanted = meta[row, utts + 1 + u]
            for c in range(lane_tiles):
                cut = slice(c * LANE, (c + 1) * LANE)
                one = jnp.zeros((8, LANE), F32)
                two = jnp.zeros((8, LANE), F32)
                for at, size in spans(TILE, 64):
                    span = slice(at, at + size)
                    index = base + at + lax.broadcasted_iota(jnp.int32, (size, LANE), 0)
                    value = jnp.where((index >= begin) & (index < end), agrad[span, cut], 0.0)
                    one = one + fold(value * xc_ref[span, cut].astype(F32))
                    two = two + fold(value)
                part_ref[KW + 1 + wanted, :, cut] += one
                part_ref[KW + 1 + NBW + wanted, :, cut] += two

    for c in range(lane_tiles):
        cut = slice(c * LANE, (c + 1) * LANE)
        sums = [part_ref[k, :, cut] for k in range(KW + 1)]
        for at, size in spans(TILE, 32):
            span = slice(at, at + size)
            reach, left = reaches[0, span, :], reaches[1, span, :]
            value = cg[c, span, :]
            for k in range(KW):
                offset = k - RIM
                moved = xs[c, EDGE + offset + at : EDGE + offset + at + size, :] * value
                sums[k] = sums[k] + fold(keep_within(moved, reach, left, offset))
            sums[KW] = sums[KW] + fold(value)
        for k in range(KW + 1):
            part_ref[k, :, cut] = sums[k]

    def edge(side, begin):
        for c in range(lane_tiles):
            edge_ref[row, side, :, c * LANE : (c + 1) * LANE] = cg[c, begin : begin + 8, :]

    @pl.when(tile == 0)
    def _():
        edge(0, 0)

    @pl.when(tile == tiles - 1)
    def _():
        edge(1, TILE - 8)

    core, plane = meta[0, 2 * utts + 2], meta[0, 2 * utts + 3]

    @pl.when(step == rows * tiles - 1)
    def _():
        vec_ref[0:8, :] = jnp.zeros((8, channels), F32)
        vec_ref[0:2, :] = tail_ref[0:2, :]
        for v in range(VROWS):
            at = v - (KW + 1 + 2 * NBW)
            rows_of = part_ref[v] if at < 0 else sums_ref[at]
            vec_ref[2 + v : 3 + v, :] = jnp.sum(rows_of, axis=0, keepdims=True)
        line = jnp.concatenate([bsum0[...], bsum1[...]], axis=1)
        for c in range(IN_ROWS):
            at = 2 + VROWS + c
            vec_ref[at : at + 1, :] = jnp.sum(
                line[:, c * channels : (c + 1) * channels], axis=0, keepdims=True
            )

        def bins(value):
            value = jnp.broadcast_to(jnp.sum(value, axis=0, keepdims=True), (16, BIN_PAD))
            total = jnp.zeros((16, BIN_PAD), F32)
            for _ in range(3):
                part = value.astype(BF16)
                value = value - part.astype(F32)
                total = total + dot(part, order_ref[...], NT)
            return total[0:8]

        flat = jnp.concatenate([bins(hsum_ref[:, 0:BIN_PAD]), bins(hsum_ref[:, BIN_PAD:])], axis=1)
        column = lax.broadcasted_iota(jnp.int32, (8, 3 * channels), 1)
        moved = pltpu.roll(flat, 2 * BIN_PAD - (BIN_PAD - BINS), 1)
        joined = jnp.where(column < BINS, flat, moved)
        joined = jnp.where(column < NOUT, joined, 0.0)
        for c in range(HEAD_ROWS):
            at = 2 + VROWS + IN_ROWS + c
            vec_ref[at : at + 1, :] = joined[0:1, c * channels : (c + 1) * channels]
        vec_ref[28:32, :] = jnp.zeros((4, channels), F32)
        for ref, c, p in zip(
            (own_ref, near_ref, far_ref, cross_ref),
            (core, 1 - core, core, 1 - core),
            (plane, plane, 1 - plane, 1 - plane),
        ):
            ref[0:8, :] = vec_ref[pl.ds(pl.multiple_of(c * HALF + p * QUART, QUART), QUART), :]
        for r in range(rows):
            at = 8 + 8 * r
            near_ref[at : at + 8, :] = jnp.where(core == 0, edge_ref[r, 1], edge_ref[r, 0])
            cross_ref[at : at + 8, :] = jnp.where(core == 0, edge_ref[r, 0], edge_ref[r, 1])


def norm_backward(meta, x, low, high, pre, table, xc, rc, tail, sums, hsum, bsums, order, utts):
    rows, frames, channels = x.shape
    tiles = frames // TILE
    block = lambda width: pl.BlockSpec((TILE, width), lambda i: (i, 0))
    return pl.pallas_call(
        functools.partial(norm_body, tiles=tiles, utts=utts),
        grid=(rows * tiles,),
        in_specs=[SCALARS, WHOLE, WHOLE, WHOLE, block(FF)]
        + [
            pl.BlockSpec((FF, channels), lambda i: (0, 0)),
            pl.BlockSpec((BR, channels), lambda i: (NB - 1, 0)),
            block(channels),
            block(LANE),
        ]
        + [WHOLE] * 6,
        out_specs=[block(channels)] + [WHOLE] * 4,
        out_shape=[shape_of((rows * frames, channels), BF16)]
        + [shape_of((8 * n, channels), F32) for n in (1, 1 + rows, 1, 1 + rows)],
        scratch_shapes=[
            pltpu.VMEM((KW + 1 + 2 * NBW, 8, channels), F32),
            pltpu.VMEM((rows, 2, 8, channels), F32),
            pltpu.VMEM((BR, channels), F32),
            pltpu.VMEM((channels // LANE, TILE + 2 * EDGE, LANE), F32),
            pltpu.VMEM((BR, channels), F32),
            pltpu.VMEM((2 * utts, channels), F32),
            pltpu.VMEM((TILE, channels), F32),
            pltpu.VMEM((channels // LANE, TILE, LANE), F32),
            pltpu.VMEM((2, TILE, LANE), jnp.int32),
        ],
        compiler_params=params(),
        cost_estimate=cost(2 * rows * frames * 1536 * 512, 20 * MIB),
        name="norm_backward",
    )(meta, x, low, high, pre, table, table, xc, rc, tail, sums, hsum, *bsums, order)


def conv_body(meta, cg_ref, before_ref, after_ref, near_ref, cross_ref, resg_ref, last_ref, *rest, row, tiles, utts):
    out_ref, cs, vecs = rest[-3:]
    tile = pl.program_id(0)
    channels = cg_ref.shape[1]
    core = meta[0, 2 * utts + 2]
    base = meta[row, 2 * utts + 1] + tile * TILE

    @pl.when(tile == 0)
    def _():
        vecs[...] = last_ref[...].astype(F32)

    for c in range(channels // LANE):
        cut = slice(c * LANE, (c + 1) * LANE)
        cs[c, EDGE : EDGE + TILE, :] = cg_ref[:, cut].astype(F32)
        near, cross = near_ref[8 + 8 * row : 16 + 8 * row, cut], cross_ref[8 + 8 * row : 16 + 8 * row, cut]
        before, after = before_ref[:, cut].astype(F32)[EDGE - 8 :], after_ref[:, cut].astype(F32)[:8]
        cs[c, EDGE - 8 : EDGE, :] = jnp.where(tile == 0, jnp.where(core == 0, cross, near), before)
        after = jnp.where(tile == tiles - 1, jnp.where(core == 0, near, cross), after)
        cs[c, EDGE + TILE : EDGE + TILE + 8, :] = after
    for at, size in spans(TILE, 32):
        span = slice(at, at + size)
        reach, left = frame_reach(meta, row, base + at, size, utts)
        for c in range(channels // LANE):
            cut = slice(c * LANE, (c + 1) * LANE)
            total = resg_ref[span, cut].astype(F32)
            for k in range(KW):
                offset = RIM - k
                moved = cs[c, EDGE + offset + at : EDGE + offset + at + size, :]
                total = total + keep_within(moved, reach, left, offset) * vecs[2 + k : 3 + k, cut]
            out_ref[0, span, cut] = total


def conv_backward(row, before, meta, cg, near, cross, resg, table, rows, utts):
    frames, channels = cg.shape[0] // rows, cg.shape[1]
    tiles = frames // TILE
    per = TILE // EDGE
    more = [] if before is None else [before]
    return pl.pallas_call(
        functools.partial(conv_body, row=row, tiles=tiles, utts=utts),
        grid=(tiles,),
        in_specs=[
            SCALARS,
            pl.BlockSpec((TILE, channels), lambda i: (row * tiles + i, 0)),
            pl.BlockSpec((EDGE, channels), lambda i: (row * tiles * per + jnp.maximum(i * per - 1, 0), 0)),
            pl.BlockSpec((EDGE, channels), lambda i: (row * tiles * per + jnp.minimum((i + 1) * per, tiles * per - 1), 0)),
            WHOLE,
            WHOLE,
            pl.BlockSpec((TILE, channels), lambda i: (row * tiles + i, 0)),
            pl.BlockSpec((BR, channels), lambda i: (NB - 1, 0)),
        ]
        + [ANYWHERE] * len(more),
        out_specs=pl.BlockSpec((1, TILE, channels), lambda i: (row, i, 0)),
        out_shape=shape_of((rows, frames, channels), F32),
        input_output_aliases={8: 0} if more else {},
        scratch_shapes=[
            pltpu.VMEM((channels // LANE, TILE + 2 * EDGE, LANE), F32),
            pltpu.VMEM((BR, channels), F32),
        ],
        compiler_params=params(),
        cost_estimate=cost(16 * frames * 512, 6 * MIB),
        name=f"conv_backward_{row}",
    )(meta, cg, cg, cg, near, cross, resg, table, *more)


def wave_body(meta, spec_ref, prev_ref, halo_ref, synth_ref, win_ref, *rest, start, rows, utts):
    out_ref, spec_all, held_all, done_all = rest[-4:]
    tile = start + pl.program_id(0)
    lane = lax.broadcasted_iota(jnp.int32, (TILE // 2, LANE), 1)
    front = lane < LANE // 2
    for r in range(rows):
        spec, held, done = spec_all.at[r], held_all.at[r], done_all.at[r]
        base = meta[r, 2 * utts + 1] + tile * TILE
        spec[EDGE:, :] = spec_ref[r]
        spec[0:EDGE, :] = jnp.where(tile == 0, halo_ref[r], prev_ref[r])
        for parity in range(2):
            half = slice(parity * BIN_PAD, (parity + 1) * BIN_PAD)
            piece = dot(spec[:, half], synth_ref[parity], NN)
            for c in range(BIN_PAD // LANE):
                held[parity, c] = piece[:, c * LANE : (c + 1) * LANE]
        for at, size in spans(TILE, 32):
            reach, _ = frame_reach(meta, r, base + at, size, utts)
            for c in range(3):
                cut = slice(c * LANE, (c + 1) * LANE)
                total = None
                for j in range(LAPS):
                    rows_at = slice(EDGE + at - j, EDGE + at - j + size)
                    of = (j % 2) * 3 + c
                    one, two = held[0, of, rows_at, :], held[1, of, rows_at, :]
                    piece = (one + two if j < 2 else one - two) * win_ref[j : j + 1, cut]
                    total = piece if j == 0 else total + jnp.where(reach >= j, piece, 0.0)
                done[c, at : at + size, :] = total * over(win_ref, LAPS, reach, c)
        even = [done[c, pl.ds(0, TILE // 2, stride=2), :] for c in range(3)]
        odd = [pltpu.roll(done[c, pl.ds(1, TILE // 2, stride=2), :], LANE // 2, 1) for c in range(3)]
        part = (
            even[0],
            even[1],
            jnp.where(front, even[2], odd[0]),
            jnp.where(front, odd[0], odd[1]),
            jnp.where(front, odd[1], odd[2]),
        )
        for k in range(PAIR):
            out_ref[pl.ds(2 * k + r, TILE // 2, stride=2 * PAIR), :] = part[k]


def wave_forward(start, stop, before, meta, spec, halo, synth, win, utts):
    rows, frames, _ = spec.shape
    tiles = frames // TILE
    per = TILE // EDGE
    more = [] if before is None else [before]
    return pl.pallas_call(
        functools.partial(wave_body, start=start, rows=rows, utts=utts),
        grid=(stop - start,),
        in_specs=[
            SCALARS,
            pl.BlockSpec((rows, TILE, 2 * BIN_PAD), lambda i: (0, start + i, 0)),
            pl.BlockSpec((rows, EDGE, 2 * BIN_PAD), lambda i: (0, jnp.maximum((start + i) * per - 1, 0), 0)),
            WHOLE,
            WHOLE,
            WHOLE,
        ]
        + [ANYWHERE] * len(more),
        out_specs=pl.BlockSpec((PAIR * TILE, LANE), lambda i: (start + i, 0)),
        out_shape=shape_of((PAIR * TILE * tiles, LANE), F32),
        input_output_aliases={6: 0} if more else {},
        scratch_shapes=[
            pltpu.VMEM((rows, TILE + EDGE, 2 * BIN_PAD), BF16),
            pltpu.VMEM((rows, 2, BIN_PAD // LANE, TILE + EDGE, LANE), F32),
            pltpu.VMEM((rows, LAP_PAD // LANE, TILE, LANE), F32),
        ],
        compiler_params=params(),
        cost_estimate=cost(4 * rows * (stop - start) * TILE * 768 * 768, 10 * MIB),
        name=f"wave_forward_{start}",
    )(meta, spec, spec, halo, synth, win, *more)


def slot_body(slot_of, *refs, groups, lasts, copies, slots):
    count = max(g[0] for g in groups) + 1
    keeps, cames, last_refs = refs[:count], refs[count : 2 * count], refs[2 * count : 2 * count + lasts]
    out, *more = refs[2 * count + lasts :]
    for index, offset, start, stop in groups:

        def one(b, carry, keep=keeps[index], came=cames[index], offset=offset, start=start):
            value = keep[offset + b].astype(F32) + came[offset + b].astype(F32)
            out[slot_of[0, start + b]] = value.astype(BF16)
            return carry

        lax.fori_loop(0, stop - start, one, 0, unroll=8)
    total = last_refs[0][0:QUART, :]
    for ref in last_refs[1:]:
        total = total + ref[0:QUART, :]
    out[slot_of[0, NB - 1]] = total.astype(BF16)
    for ref, at in zip(more, copies):
        ref[...] = out[at * slots : (at + 1) * slots]


def to_slots(slot_of, keeps, cames, lasts, groups, owners, slots, copies):
    channels = keeps[0].shape[2]
    return pl.pallas_call(
        functools.partial(slot_body, groups=groups, lasts=len(lasts), copies=copies, slots=slots),
        in_specs=[SCALARS] + [WHOLE] * (2 * len(keeps) + len(lasts)),
        out_specs=[WHOLE] * (1 + len(copies)),
        out_shape=[shape_of((owners * slots, QUART, channels), BF16)]
        + [shape_of((slots, QUART, channels), BF16)] * len(copies),
        compiler_params=params(),
        cost_estimate=cost(0, 6 * MIB),
        name="to_slots",
    )(slot_of, *keeps, *cames, *lasts)


def adam_body(places, meta, mine_ref, other_ref, master, first, second, *rest, block):
    out_master, out_first, out_second = rest[-3:]
    one_fix = 1.0 / (1.0 - BETA_ONE**STEP_COUNT)
    two_fix = 1.0 / (1.0 - BETA_TWO**STEP_COUNT)
    core = meta[0, meta.shape[1] - 2]
    for s in range(block):
        bucket = places[0, pl.program_id(0) * block + s]
        mine, other = mine_ref[s].astype(F32), other_ref[s].astype(F32)
        for half in range(2):
            grad = jnp.where(bucket < NB, jnp.where(core == half, mine, other), 0.0)
            old = master[s, half, 0]
            one = BETA_ONE * first[s, half, 0] + (1.0 - BETA_ONE) * grad
            two = BETA_TWO * second[s, half, 0] + (1.0 - BETA_TWO) * grad * grad
            out_first[s, half, 0] = one
            out_second[s, half, 0] = two
            step = one * one_fix / (jnp.sqrt(two * two_fix) + ADAM_EPS)
            out_master[s, half, 0] = old - LEARN_RATE * (step + WEIGHT_DECAY * old)


def adam(places, meta, mine, other, master, first, second, before):
    slots, depth, channels = master.shape
    block = max(b for b in range(1, ADAM_BLOCK + 1) if slots % b == 0)
    plane_at = meta.shape[1] - 1
    cut = lambda v: v.reshape(slots, 2, 2, QUART, channels)
    def at_plane(i, places, meta):
        plane = meta[0, plane_at]
        return i, 0, 1 - plane if before else plane, 0, 0

    full = pl.BlockSpec((block, 2, 1, QUART, channels), at_plane)
    part = pl.BlockSpec((block, QUART, channels), lambda i, places, meta: (i, 0, 0))
    more = [cut(v) for v in before]
    outs = pl.pallas_call(
        functools.partial(adam_body, block=block),
        grid_spec=pltpu.PrefetchScalarGridSpec(
            num_scalar_prefetch=2,
            grid=(slots // block,),
            in_specs=[part] * 2 + [full] * 3 + [ANYWHERE] * len(more),
            out_specs=[full] * 3,
        ),
        out_shape=[shape_of((slots, 2, 2, QUART, channels), F32)] * 3,
        input_output_aliases={7 + v: v for v in range(len(more))},
        compiler_params=params(),
        cost_estimate=cost(0, 6 * MIB),
        name="adam_second" if more else "adam_first",
    )(places, meta, mine, other, cut(master), cut(first), cut(second), *more)
    return [v.reshape(slots, depth, channels) for v in outs]


def tie(*values):
    return lax.optimization_barrier(values)


def plus(*values):
    return sum([v.astype(F32) for v in values]).astype(BF16)


def local(frames_in, lengths, bw_ids, owner_list, master, moment1, moment2, wave_grad):
    rows, frames, channels = frames_in.shape
    slots = master.shape[0]
    utts = lengths.shape[1]
    owners = lax.axis_size("rows")
    seqs = lax.axis_size("seq")
    row_at = lax.axis_index("rows")
    seq_at = lax.axis_index("seq")
    core, plane = seq_at % 2, seq_at // 2
    ring = ring_of(owners)
    half_ring = owners // 2

    mine = lax.dynamic_slice_in_dim(master, core * HALF, HALF, axis=1).astype(BF16)

    lines = wave_grad.reshape(rows, frames * HOP // LANE, LANE).transpose(1, 0, 2).reshape(-1, LANE)
    order = jnp.asarray(order_table())
    synth = jnp.asarray(synthesis_table())
    win = jnp.asarray(window_tables())

    later = shifted(lines[: PAIR * EDGE], -1)
    offsets = [0]
    for hop in range(1, half_ring):
        offsets += [-hop, hop]
    offsets.append(-half_ring)
    names = np.arange(owners, dtype=np.int32)
    ids = jnp.stack([row_at, seq_at]).astype(jnp.int32)
    meta, places, held, slot_of, counts = plan(
        ids,
        lengths,
        bw_ids,
        owner_list,
        jnp.asarray(ring if ring else names, jnp.int32),
        jnp.asarray(offsets if ring else names, jnp.int32),
        slots,
        frames,
        bool(ring),
    )

    cot = None
    tiles = frames // TILE
    if ring:
        ahead = back = mine
        arrived = [mine, seq_swap(mine, 1)]
        for hop in range(half_ring):
            source = (ahead, back)
            ahead = lax.ppermute(ahead, AXES, ring_step(ring, 1, seqs))
            if hop < half_ring - 1:
                back = lax.ppermute(back, AXES, ring_step(ring, -1, seqs))
            if hop == 0:
                ahead, back, later, meta = tie(ahead, back, later, meta)
            if hop == 1:
                edges = tie(frames_in, *source)[0]
                low = shifted(edges[:, frames - EDGE :], 1)
                high = shifted(edges[:, :EDGE], -1)
                ahead, back, low, high = tie(ahead, back, low, high)
            if hop in (1, 2):
                feed = tie(lines, *source)[0]
                begin, end = ((0, tiles // 2), (tiles // 2, tiles))[hop - 1]
                cot = spectrum_cotangent(begin, end, cot, meta, feed, later, synth, win, rows, utts)
                ahead, back, cot = tie(ahead, back, cot)
            if hop == half_ring - 1:
                fed = tie(places, *source)[0]
                partial_table = assemble(tuple(range(owners - 1)), meta, fed, counts, arrived, slots)
                ahead, back, partial_table = tie(ahead, back, partial_table)
            else:
                arrived += [ahead, seq_swap(ahead, 1), back, seq_swap(back, 1)]
        arrived = [ahead, seq_swap(ahead, 1)]
        owned = (owners - 1,)
        part_places, part_counts, part_slots = places, counts, slots
    else:
        low = shifted(frames_in[:, frames - EDGE :], 1)
        high = shifted(frames_in[:, :EDGE], -1)
        gathered = lax.all_gather(mine, "rows", axis=0, tiled=True)
        arrived = [gathered, seq_swap(gathered, 1)]
        owned = (0,)
        arrived = [take_slots(slot_of, a) for a in arrived]
        part_places = jnp.arange(NB, dtype=jnp.int32)[None, :]
        part_counts, part_slots = jnp.full((1, 1), NB, jnp.int32), NB
        partial_table = jnp.zeros((NB * BR, channels), BF16)
        cot = spectrum_cotangent(0, tiles, cot, meta, lines, later, synth, win, rows, utts)

    (table, spec, act, der, ada, low_grad, resg, xc, rc, send, keep, tail, sums, hsum) = forward(
        owned, part_slots, meta, part_places, part_counts, frames_in, low, high, order, cot, arrived, partial_table, utts
    )
    halo = shifted(spec[:, frames - EDGE :], 1)

    keeps, cames, groups = [], [], []

    def split(keep, came):
        both = plus(keep, came)
        stay = lax.dynamic_slice_in_dim(both, plane * QUART, QUART, axis=1)
        leave = lax.dynamic_slice_in_dim(both, (1 - plane) * QUART, QUART, axis=1)
        return stay, leave

    def record(stay, came, begins, per):
        for at, begin in enumerate(begins):
            groups.append((len(keeps), at * per, begin, begin + per))
        keeps.append(stay)
        cames.append(came)

    per = CHUNK // BR
    pre, bsums = None, []
    begins, count = (2 * FF // BR,), 40
    waiting = []
    for chunk in range(FF // CHUNK):
        near = seq_swap(send, 1)
        pre, next_send, next_keep, bsum = mlp_backward(chunk, pre, meta, low_grad, act, der, ada, table, utts)
        near, pre, next_send, next_keep = tie(near, pre, next_send, next_keep)
        bsums.append(bsum)
        stay, leave = split(keep, near)
        waiting.append((stay, seq_swap(leave, 2), begins, count))
        send, keep = next_send, next_keep
        begins, count = (chunk * per, FF // BR + chunk * per), per

    state = {"wave": None, "grad": None}

    def wave_piece(n, *ready):
        feed = tie(spec, *ready)[0]
        begin, end = n * tiles // 2, (n + 1) * tiles // 2
        state["wave"] = wave_forward(begin, end, state["wave"], meta, feed, halo, synth, win, utts)
        return "wave"

    def conv_piece(row, *ready):
        feed = tie(cg, *ready)[0]
        state["grad"] = conv_backward(row, state["grad"], meta, feed, lasts[1], lasts[3], resg, table, rows, utts)
        return "grad"

    near = seq_swap(send, 1)
    for stay, came, *where_from in waiting[:-1]:
        pre, came = tie(pre, came)
        record(stay, came, *where_from)
    cg, own, to_near, to_far, to_cross = norm_backward(
        meta, frames_in, low, high, pre, table, xc, rc, tail, sums, hsum, bsums, order, utts
    )
    kept, came, *where_from = waiting[-1]
    near, came, cg, own, to_near, to_far, to_cross = tie(near, came, cg, own, to_near, to_far, to_cross)
    record(kept, came, *where_from)
    stay, leave = split(keep, near)
    came = seq_swap(leave, 2)
    lasts = [own, seq_swap(to_near, 1), seq_swap(to_far, 2), seq_swap(to_cross, 3)]
    wave_piece(0, own)
    came, state["wave"], *lasts = tie(came, state["wave"], *lasts)
    record(stay, came, begins, count)
    first_sent = (owners - 1, owners - 3) if ring else ()
    chunks, *sent = to_slots(slot_of, keeps, cames, lasts, tuple(groups), owners, slots, first_sent)
    if ring:
        cut = {o: chunks[i * slots : (i + 1) * slots] for i, o in enumerate(offsets)}
        up, down = sent
        for hop in range(half_ring):
            left_over = half_ring - 1 - hop
            source = (up, down)
            up = lax.ppermute(up, AXES, ring_step(ring, 1, seqs))
            if hop < half_ring - 1:
                down = lax.ppermute(down, AXES, ring_step(ring, -1, seqs))
            if hop < 2:
                done = conv_piece(hop, *source)
                up, down, state[done] = tie(up, down, state[done])
            elif hop == 2:
                done = wave_piece(1, *source)
                up, down, state[done] = tie(up, down, state[done])
            if left_over:
                up = plus(up, cut[left_over])
                if hop < half_ring - 2:
                    down = plus(down, cut[1 - left_over])
        own = plus(cut[0], up, down)
    else:
        own = lax.psum_scatter(chunks, "rows", scatter_dimension=0, tiled=True)
        conv_piece(0, own)
        conv_piece(1, own)
        wave_piece(1, own)
    near, far = seq_swap(own, 1), seq_swap(own, 2)
    cross = seq_swap(far, 1)
    waveform = state["wave"].reshape(-1, rows, LANE).transpose(1, 0, 2).reshape(rows, frames * HOP)

    first = adam(held, meta, own, near, master, moment1, moment2, ())
    cross, *first = tie(cross, *first)
    new_master, new_first, new_second = adam(held, meta, far, cross, master, moment1, moment2, first)
    return waveform, state["grad"], new_master, new_first, new_second


def solution(mesh):
    in_specs = (
        P("rows", "seq", None),
        P("rows", None),
        P("rows", None),
        P(),
        P("rows", None, None),
        P("rows", None, None),
        P("rows", None, None),
        P("rows", "seq"),
    )
    out_specs = (
        P("rows", "seq"),
        P("rows", "seq", None),
        P("rows", None, None),
        P("rows", None, None),
        P("rows", None, None),
    )
    return jax.shard_map(local, mesh=mesh, in_specs=in_specs, out_specs=out_specs, check_vma=False)
```

```python
import functools
import math

import jax
import jax.numpy as jnp
import numpy as np
from jax import lax
from jax.experimental import pallas as pl
from jax.experimental.pallas import tpu as pltpu
from jax.sharding import PartitionSpec as P

FF = 1536
NFFT = 1280
HOP = 320
NBW = 4
KW = 7
UTT = 4
BR = 32
STEP_COUNT = 6
BINS = 641
NOUT = 1282
VROWS = 20
IN_ROWS = 3
HEAD_ROWS = 3
NB = 137

NORM_EPS = 1e-06
ENV_FLOOR = 0.5
BETA_ONE = 0.8
BETA_TWO = 0.9
LEARN_RATE = 0.04
WEIGHT_DECAY = 0.01
ADAM_EPS = 1e-08

LAPS = NFFT // HOP
RIM = (KW - 1) // 2
LAP_PAD = 384
BIN_PAD = 768
HALF = BR // 2
QUART = BR // 4
EDGE = 16
TILE = 256
CHUNK = 768
HALF_BIN = 384
PAIR = 5
ADAM_BLOCK = 27
LANE = 128
AXES = ("rows", "seq")

F32 = jnp.float32
BF16 = jnp.bfloat16
MIB = 1 << 20
VMEM_BYTES = 60 * MIB


def bin_order():
    order = np.full(BIN_PAD, -1)
    order[: (BINS + 1) // 2] = np.arange(0, BINS, 2)
    order[HALF_BIN : HALF_BIN + BINS // 2] = np.arange(1, BINS, 2)
    return order


def order_table():
    return (np.arange(BIN_PAD)[:, None] == bin_order()[None, :]).astype(jnp.bfloat16)


def synthesis_table():
    n = np.arange(2 * HOP)[None, :]
    order = bin_order()
    out = np.zeros((2, 2, HALF_BIN, 2, LAP_PAD), np.float32)
    for parity in range(2):
        k = order[parity * HALF_BIN : (parity + 1) * HALF_BIN]
        k = k[k >= 0][:, None]
        angle = (k * n % NFFT) * (2.0 * math.pi / NFFT)
        factor = np.where((k == 0) | (k == NFFT // 2), 1.0, 2.0) / NFFT
        out[parity, 0, : len(k), :, :HOP] = (factor * np.cos(angle)).reshape(-1, 2, HOP)
        out[parity, 1, : len(k), :, :HOP] = (-factor * np.sin(angle)).reshape(-1, 2, HOP)
    return out.reshape(2, BIN_PAD, 2 * LAP_PAD).astype(jnp.bfloat16)


def window_tables():
    window = 0.5 - 0.5 * np.cos(np.arange(NFFT) * (2.0 * math.pi / NFFT))
    rows = np.zeros((LAPS, LAP_PAD), np.float64)
    rows[:, :HOP] = window.reshape(LAPS, HOP)
    envelope = np.cumsum(rows**2, axis=0)
    return np.concatenate([rows, 1.0 / np.maximum(envelope, ENV_FLOOR)], axis=0).astype(np.float32)


def ring_of(count):
    if count != 8:
        return None
    return [0, 2, 4, 6, 7, 5, 3, 1]


def ring_step(ring, shift, seq_count):
    where = {r: i for i, r in enumerate(ring)}
    pairs = []
    for r in ring:
        target = ring[(where[r] + shift) % len(ring)]
        pairs += [(r * seq_count + s, target * seq_count + s) for s in range(seq_count)]
    return pairs


def seq_swap(value, bit):
    count = lax.axis_size("seq")
    return lax.ppermute(value, "seq", [(s, s ^ bit) for s in range(count)])


def rows_swap(value, bit):
    count = lax.axis_size("rows")
    return lax.ppermute(value, "rows", [(r, r ^ bit) for r in range(count)])


def shifted(value, distance):
    devices = range(lax.axis_size("seq"))
    return lax.ppermute(
        value, "seq", [(i - distance, i) for i in devices if i - distance in devices]
    )


def dot(a, b, dims):
    return lax.dot_general(a, b, (dims, ((), ())), preferred_element_type=F32)


NN = ((1,), (0,))
NT = ((1,), (1,))
TN = ((0,), (0,))


def frame_reach(meta, row, first, count, utts):
    index = first + lax.broadcasted_iota(jnp.int32, (count, 128), 0)
    start = jnp.zeros_like(index)
    end = jnp.zeros_like(index) + meta[row, 1]
    for u in range(1, utts):
        inside = index >= meta[row, u]
        start = jnp.where(inside, meta[row, u], start)
        end = jnp.where(inside, meta[row, u + 1], end)
    return index - start, end - 1 - index


def spans(count, size):
    return [(at, min(size, count - at)) for at in range(0, count, size)]


def over(table, base, reach, lane_tile, width=LANE):
    cut = slice(lane_tile * LANE, lane_tile * LANE + width)
    picked = jnp.broadcast_to(table[base + LAPS - 1 : base + LAPS, cut], (reach.shape[0], width))
    for j in range(LAPS - 2, -1, -1):
        picked = jnp.where(reach[:, :width] == j, table[base + j : base + j + 1, cut], picked)
    return picked


def keep_within(values, reach, left, offset):
    if offset < 0:
        return jnp.where(reach >= -offset, values, 0.0)
    if offset > 0:
        return jnp.where(left >= offset, values, 0.0)
    return values


def row_mean(values):
    return jnp.mean(values, axis=1, keepdims=True)


def fold(values):
    rows, columns = values.shape
    return jnp.sum(values.reshape(rows // 8, 8, columns), axis=0)


def sincos(angle):
    turns = jnp.round(angle * (0.5 / math.pi))
    rest = angle * 0.5 - turns * 3.1416015625
    rest = rest + turns * 8.908910206761537e-06
    sq = rest * rest
    sine = 1.0 + sq * (
        -0.16666656732559204
        + sq * (0.008333033882081509 + sq * (-0.00019807791977655143 + sq * 2.6022808015113696e-06))
    )
    cosine = 1.0 + sq * (
        -0.4999992549419403
        + sq * (0.04166382923722267 + sq * (-0.001385461655445397 + sq * 2.3163083824329078e-05))
    )
    sine = rest * sine
    double = sine + sine
    return double * cosine, 1.0 - double * sine


ANGLE_LIMIT = 1024.0


def params():
    return pltpu.CompilerParams(vmem_limit_bytes=VMEM_BYTES)


def cost(flops, bytes_accessed, transcendentals=0):
    return pl.CostEstimate(
        flops=int(flops), bytes_accessed=int(bytes_accessed), transcendentals=int(transcendentals)
    )


WHOLE = pl.BlockSpec(memory_space=pltpu.VMEM)
SCALARS = pl.BlockSpec(memory_space=pltpu.SMEM)
ANYWHERE = pl.BlockSpec(memory_space=pl.ANY)
shape_of = jax.ShapeDtypeStruct


def plan_body(ids, lengths, bw_ids, owner_list, order, offsets, meta, places, held, slot_of, counts, rel, *, frames, ring):
    rows, utts = lengths.shape
    owners, slots = order.shape[0], held.shape[1]
    row_at, seq_at = ids[0], ids[1]
    for r in range(rows):
        start = jnp.int32(0)
        meta[r, 0] = start
        for u in range(utts):
            start = start + lengths[r, u]
            meta[r, u + 1] = start
            meta[r, utts + 1 + u] = bw_ids[r, u]
        meta[r, 2 * utts + 1] = seq_at * frames
        meta[r, 2 * utts + 2] = lax.rem(seq_at, 2)
        meta[r, 2 * utts + 3] = lax.div(seq_at, 2)
    where = jnp.int32(0)
    if ring:
        for i in range(owners):
            where = jnp.where(order[i] == row_at, i, where)

    def name(i, carry):
        rel[order[lax.rem(where + offsets[i] + owners, owners)]] = i
        counts[0, i] = 0
        return carry

    def clear(i, carry):
        places[0, i] = NB
        return carry

    def place(b, carry):
        i = rel[owner_list[b]]
        n = counts[0, i]
        counts[0, i] = n + 1
        places[0, i * slots + n] = b
        slot_of[0, b] = i * slots + n
        return carry

    lax.fori_loop(0, owners, name, 0)
    lax.fori_loop(0, owners * slots, clear, 0, unroll=8)
    lax.fori_loop(0, NB, place, 0)
    own = rel[row_at]

    def keep(n, carry):
        held[0, n] = places[0, own * slots + n]
        return carry

    lax.fori_loop(0, slots, keep, 0)


def plan(ids, lengths, bw_ids, owner_list, order, offsets, slots, frames, ring):
    rows, utts = lengths.shape
    owners = order.shape[0]
    shapes = ((rows, 2 * utts + 4), (1, owners * slots), (1, slots), (1, NB), (1, owners))
    return pl.pallas_call(
        functools.partial(plan_body, frames=frames, ring=ring),
        in_specs=[SCALARS] * 6,
        out_specs=[SCALARS] * 5,
        out_shape=[shape_of(shape, jnp.int32) for shape in shapes],
        scratch_shapes=[pltpu.SMEM((owners,), jnp.int32)],
        compiler_params=params(),
        cost_estimate=cost(8000, 8 * 1024),
        name="plan",
    )(ids, lengths, bw_ids, owner_list, order, offsets)


def pre_body(meta, wave_ref, halo_ref, synth_ref, win_ref, *rest, start, tiles, rows, utts):
    out_ref, flat, scaled_all, even_all, odd_all = rest[-5:]
    step = pl.program_id(0)
    tile = start + step
    lines = PAIR * TILE
    extra = PAIR * EDGE
    count = TILE + EDGE
    lane = lax.broadcasted_iota(jnp.int32, (count // 2, LANE), 1)
    for at, size in spans(lines, 320):
        rows_at = pl.ds(pl.multiple_of(tile * lines + at, 16), size)
        flat[at : at + size, :] = wave_ref[rows_at, :].astype(F32)
    after = jnp.minimum((tile + 1) * lines, tiles * lines - extra)
    following = wave_ref[pl.ds(pl.multiple_of(after, 16), extra), :]
    flat[lines:, :] = jnp.where(tile == tiles - 1, halo_ref[...], following).astype(F32)
    for r in range(rows):
        scaled, even, odd = scaled_all.at[r], even_all.at[r], odd_all.at[r]
        base = meta[r, 2 * utts + 1] + tile * TILE
        part = [flat[pl.ds(2 * k + r, count // 2, stride=2 * PAIR), :] for k in range(PAIR)]
        turned = [pltpu.roll(v, LANE // 2, 1) for v in part[2:]]
        front = lane < LANE // 2
        frame = (
            part[0],
            part[1],
            jnp.where(front, part[2], 0.0),
            jnp.where(front, turned[0], turned[1]),
            jnp.where(front, turned[1], turned[2]),
            jnp.where(front, turned[2], 0.0),
        )
        for c in range(3):
            scaled[c, pl.ds(0, count // 2, stride=2), :] = frame[c]
            scaled[c, pl.ds(1, count // 2, stride=2), :] = frame[3 + c]
        for at, size in spans(count, 32):
            reach, _ = frame_reach(meta, r, base + at, size, utts)
            for c in range(3):
                scaled[c, at : at + size, :] = scaled[c, at : at + size, :] * over(win_ref, LAPS, reach, c)
        for at, size in spans(TILE, 32):
            _, left = frame_reach(meta, r, base + at, size, utts)
            for j in range(2):
                for c in range(3):
                    span = slice(c * LANE, (c + 1) * LANE)

                    def lap(i):
                        value = scaled[c, at + i : at + i + size, :] * win_ref[i : i + 1, span]
                        return keep_within(value, None, left, i).astype(BF16).astype(F32)

                    one, two = lap(j), lap(j + 2)
                    column = slice(j * LAP_PAD + c * LANE, j * LAP_PAD + (c + 1) * LANE)
                    even[at : at + size, column] = (one + two).astype(BF16)
                    odd[at : at + size, column] = (one - two).astype(BF16)
        out_ref[r, :, 0:BIN_PAD] = dot(even[...], synth_ref[0], NT).astype(BF16)
        out_ref[r, :, BIN_PAD:] = dot(odd[...], synth_ref[1], NT).astype(BF16)


def spectrum_cotangent(start, stop, before, meta, wave, halo, synth, win, rows, utts):
    tiles = wave.shape[0] // (PAIR * TILE)
    frames = tiles * TILE
    more = [] if before is None else [before]
    steps = stop - start
    return pl.pallas_call(
        functools.partial(pre_body, start=start, tiles=tiles, rows=rows, utts=utts),
        grid=(steps,),
        in_specs=[SCALARS, WHOLE, WHOLE, WHOLE, WHOLE] + [ANYWHERE] * len(more),
        out_specs=pl.BlockSpec((rows, TILE, 2 * BIN_PAD), lambda i: (0, start + i, 0)),
        out_shape=shape_of((rows, frames, 2 * BIN_PAD), BF16),
        input_output_aliases={5: 0} if more else {},
        scratch_shapes=[
            pltpu.VMEM((PAIR * (TILE + EDGE), LANE), F32),
            pltpu.VMEM((rows, LAP_PAD // LANE, TILE + EDGE, LANE), F32),
            pltpu.VMEM((rows, TILE, BIN_PAD), BF16),
            pltpu.VMEM((rows, TILE, BIN_PAD), BF16),
        ],
        compiler_params=params(),
        cost_estimate=cost(4 * rows * steps * TILE * 768 * 768, rows * steps * TILE * 3072 + 4 * MIB),
        name=f"spectrum_cotangent_{start}",
    )(meta, wave, halo, synth, win, *more)


def place_parts(places, counts, core, pieces, table, sem, slots, owners, start):
    done = {}
    for index, ref in enumerate(pieces):
        side = core if index % 2 == 0 else 1 - core
        owner = owners[index // 2]
        first = done.get((owner, index % 2), 0)
        done[owner, index % 2] = first + ref.shape[0]

        def one(s, carry, ref=ref, side=side, owner=owner, first=first):
            bucket = places[0, owner * slots + first + s]
            at = pl.multiple_of(bucket * BR + side * HALF, HALF)
            copy = pltpu.make_async_copy(ref.at[s], table.at[pl.ds(at, HALF), :], sem)
            if start:
                copy.start()
            else:
                copy.wait()
            return carry

        held = jnp.clip(counts[0, owner] - first, 0, ref.shape[0])
        lax.fori_loop(0, held, one, 0)


def assemble_body(meta, places, counts, *refs, slots, owners):
    pieces, table, sem = refs[: 2 * len(owners)], refs[-2], refs[-1]
    core = meta[0, meta.shape[1] - 2]
    place_parts(places, counts, core, pieces, table, sem, slots, owners, True)
    place_parts(places, counts, core, pieces, table, sem, slots, owners, False)


def assemble(owners, meta, places, counts, pieces, slots):
    channels = pieces[0].shape[2]
    return pl.pallas_call(
        functools.partial(assemble_body, slots=slots, owners=owners),
        in_specs=[SCALARS, SCALARS, SCALARS] + [ANYWHERE] * len(pieces),
        out_specs=WHOLE,
        out_shape=shape_of((NB * BR, channels), BF16),
        scratch_shapes=[pltpu.SemaphoreType.DMA],
        compiler_params=params(),
        cost_estimate=cost(0, 12 * MIB),
        name="assemble",
    )(meta, places, counts, *pieces)


def take_body(slot_of, ref, out, sem):
    def copy(b):
        return pltpu.make_async_copy(ref.at[slot_of[0, b]], out.at[b], sem)

    def start(b, carry):
        copy(b).start()
        return carry

    def wait(b, carry):
        copy(b).wait()
        return carry

    lax.fori_loop(0, NB, start, 0)
    lax.fori_loop(0, NB, wait, 0)


def take_slots(slot_of, gathered):
    return pl.pallas_call(
        take_body,
        in_specs=[SCALARS, ANYWHERE],
        out_specs=WHOLE,
        out_shape=shape_of((NB, *gathered.shape[1:]), BF16),
        scratch_shapes=[pltpu.SemaphoreType.DMA],
        compiler_params=params(),
        cost_estimate=cost(0, 6 * MIB),
        name="take_slots",
    )(slot_of, gathered)


def fill_frames(xs, x_ref, low_ref, high_ref, row, tile, tiles, channels):
    first = pl.multiple_of(tile * TILE, TILE)

    def put(at, block):
        block = block.astype(F32)
        for c in range(channels // LANE):
            xs[c, at : at + block.shape[0], :] = block[:, c * LANE : (c + 1) * LANE]

    for at, size in spans(TILE, 64):
        put(EDGE + at, x_ref[row, pl.ds(pl.multiple_of(first + at, 64), size), :])

    before = x_ref[row, pl.ds(pl.multiple_of(jnp.maximum(first - EDGE, 0), EDGE), EDGE), :]
    put(0, jnp.where(tile == 0, low_ref[row], before))
    end = jnp.minimum(first + TILE, (tiles - 1) * TILE)
    after = x_ref[row, pl.ds(pl.multiple_of(end, EDGE), EDGE), :]
    put(EDGE + TILE, jnp.where(tile == tiles - 1, high_ref[row], after))


def by_utterance(meta, row, utts, index, rows_of):
    value = jnp.broadcast_to(rows_of(0), (index.shape[0], LANE))
    for u in range(1, utts):
        value = jnp.where(index >= meta[row, u], rows_of(u), value)
    return value


def pick_rows(meta, row, utts, vec, out, channels):
    for u in range(utts):
        wanted = meta[row, utts + 1 + u]
        for at, offset in ((u, KW + 1), (utts + u, KW + 1 + NBW)):
            value = vec(offset)
            for b in range(1, NBW):
                value = jnp.where(wanted == b, vec(offset + b), value)
            out[at : at + 1, :] = value


def interleave(ones, others):
    at = 0
    for i, one in enumerate(ones):
        one()
        until = (i + 1) * len(others) // len(ones)
        for other in others[at:until]:
            other()
        at = until
    for other in others[at:]:
        other()


def forward_body(meta, places, counts, x_ref, low_ref, high_ref, order_ref, cot_ref, *rest, owners, slots, tiles, count, utts):
    pieces = rest[: 2 * len(owners)]
    table_in = rest[2 * len(owners)]
    (
        table_out,
        spec_ref,
        act_ref,
        der_ref,
        ada_ref,
        lowg_ref,
        resg_ref,
        xc_ref,
        rc_ref,
        send_ref,
        keep_ref,
        tail_ref,
        sums_ref,
        bsum_ref,
        table,
        xs,
        w_head,
        b_head,
        vecs,
        picks,
        grad,
        lines,
        hg,
        hg_old,
        pre_ref,
        logs_ref,
        angle_ref,
        ngrad_ref,
        slim,
        xn_ref,
        normed,
        normed_old,
        branch_ref,
        rn_ref,
        slow,
        sem,
        sems,
    ) = rest[2 * len(owners) + 1 :]
    step = pl.program_id(0)
    core = meta[0, 2 * utts + 2]
    channels = x_ref.shape[2]
    lane_tiles = channels // LANE
    now = jnp.minimum(step, count - 1)
    row, tile = now // tiles, now % tiles
    vec = lambda v: vecs[2 + v : 3 + v, :]
    vec_at = KW + 1 + 2 * NBW
    head_at = 2 * FF

    def store():
        return pltpu.make_async_copy(table, table_out, sems.at[1])

    @pl.when(step == 0)
    def _():
        whole = pltpu.make_async_copy(table_in, table, sems.at[0])
        whole.start()
        normed[...] = jnp.zeros_like(normed)
        w_head[...] = jnp.zeros_like(w_head)
        b_head[...] = jnp.zeros_like(b_head)
        whole.wait()
        place_parts(places, counts, core, pieces, table, sem, slots, owners, True)
        place_parts(places, counts, core, pieces, table, sem, slots, owners, False)
        store().start()
        vecs[...] = table[head_at + 1280 : head_at + 1280 + BR, :].astype(F32)

    @pl.when(step == 1)
    def _():
        sums_ref[...] = jnp.zeros_like(sums_ref)
        bsum_ref[...] = jnp.zeros_like(bsum_ref)

    @pl.when(step == 2)
    def _():
        grad[...] = jnp.zeros_like(grad)

    @pl.when(tile == 0)
    def _():
        pick_rows(meta, row, utts, vec, picks, channels)

    base = meta[row, 2 * utts + 1] + tile * TILE
    fill_frames(xs, x_ref, low_ref, high_ref, row, tile, tiles, channels)

    def convolve(at, size):
        reach, left = frame_reach(meta, row, base + at, size, utts)
        index = base + at + lax.broadcasted_iota(jnp.int32, (size, LANE), 0)
        conv = []
        for c in range(lane_tiles):
            cut = slice(c * LANE, (c + 1) * LANE)
            total = vecs[2 + KW : 3 + KW, cut]
            for k in range(KW):
                offset = k - RIM
                moved = xs[c, EDGE + offset + at : EDGE + offset + at + size, :]
                total = total + keep_within(moved, reach, left, offset) * vecs[2 + k : 3 + k, cut]
            conv.append(total)
        mean = jnp.sum(sum(conv), axis=1, keepdims=True) * (1.0 / channels)
        conv = [v - mean for v in conv]
        square = jnp.sum(sum([v * v for v in conv]), axis=1, keepdims=True) * (1.0 / channels)
        rc = jnp.broadcast_to(lax.rsqrt(square + NORM_EPS), (size, LANE))
        rc_ref[at : at + size, :] = rc
        for c in range(lane_tiles):
            cut = slice(c * LANE, (c + 1) * LANE)
            xc = conv[c] * rc
            xc_ref[at : at + size, cut] = xc.astype(BF16)
            scale = by_utterance(meta, row, utts, index, lambda u: picks[u : u + 1, cut])
            shift = by_utterance(meta, row, utts, index, lambda u: picks[utts + u : utts + u + 1, cut])
            ada_ref[at : at + size, cut] = (xc * scale + shift).astype(BF16)

    def head(at, size, turn):
        span = slice(at, at + size)
        for c in range(0, BIN_PAD, LANE):
            bins, angles = slice(c, c + LANE), slice(BIN_PAD + c, BIN_PAD + c + LANE)
            parity, inner = c // HALF_BIN, c % HALF_BIN
            reals = slice(parity * BIN_PAD + inner, parity * BIN_PAD + inner + LANE)
            imags = slice(reals.start + HALF_BIN, reals.stop + HALF_BIN)
            angle = angle_ref[span, bins] + b_head[0:1, angles]
            scale = jnp.exp(logs_ref[span, bins] + b_head[0:1, bins])
            sine, cosine = turn(angle)
            real, imag = scale * cosine, scale * sine
            spec_ref[span, reals] = real.astype(BF16)
            spec_ref[span, imags] = imag.astype(BF16)
            dre = cot_ref[span, reals].astype(F32)
            dim = cot_ref[span, imags].astype(F32)
            hg[span, bins] = (dre * real + dim * imag).astype(BF16)
            hg[span, angles] = (dim * real - dre * imag).astype(BF16)

    def gelu(at, size, c):
        for d in range(c * 512, (c + 1) * 512, 256):
            cut = slice(d, d + 256)
            bias = vecs[2 + VROWS + c : 3 + VROWS + c, d - c * 512 : d - c * 512 + 256]
            pre = pre_ref[at : at + size, cut] + bias
            phi = 0.5 + 0.5 * lax.erf(pre * math.sqrt(0.5))
            bell = jnp.exp(-0.5 * pre * pre) * (1.0 / math.sqrt(2.0 * math.pi))
            act_ref[at : at + size, cut] = (pre * phi).astype(BF16)
            der_ref[at : at + size, cut] = (phi + pre * bell).astype(BF16)

    def second_norm(at, size):
        span = slice(at, at + size)
        branch = slim[span, :] + vec(vec_at)
        branch_ref[span, :] = branch
        x = jnp.concatenate([xs[c, EDGE + at : EDGE + at + size, :] for c in range(lane_tiles)], axis=1)
        residual = x + vec(vec_at + 1) * branch
        residual = residual - row_mean(residual)
        rn = lax.rsqrt(row_mean(residual * residual) + NORM_EPS)
        rn_ref[span, :] = jnp.broadcast_to(rn, (size, LANE))
        xn = residual * rn
        xn_ref[span, :] = xn
        normed[span, :] = (xn * vec(vec_at + 2) + vec(vec_at + 3)).astype(BF16)

    def second_norm_back(at, size, sums):
        span = slice(at, at + size)
        ngrad = ngrad_ref[span, :]
        xn = xn_ref[span, :]
        e = ngrad * vec(vec_at + 2)
        resg = rn_ref[span, 0:1] * (e - row_mean(e) - xn * row_mean(e * xn))
        resg_ref[span, :] = resg.astype(BF16)
        low = (vec(vec_at + 1) * resg).astype(BF16)
        lowg_ref[span, :] = low
        return (
            sums[0] + fold(low.astype(F32)),
            sums[1] + fold(resg * branch_ref[span, :]),
            sums[2] + fold(ngrad * xn),
            sums[3] + fold(ngrad),
        )

    def head_dots(ref, begin):
        def one(c):
            ref[:, c : c + 256] = dot(normed[...], w_head[begin + c : begin + c + 256, :], NT)

        return [functools.partial(one, c) for c in range(0, BIN_PAD, 256)]

    def hidden_dot(c):
        pre_ref[:, c : c + 256] = dot(ada_ref[...], table[c : c + 256, :], NT)

    def grad_dot(c):
        grad[c : c + 256, :] += dot(hg_old[:, c : c + 256], normed_old[...], TN)

    def ngrad_dot(c):
        ngrad_ref[:, c : c + 256] = dot(hg[...], w_head[:, c : c + 256], NN)

    def branch_dot(c):
        slim[:, c : c + 256] = dot(act_ref[...], table[FF : 2 * FF, c : c + 256], NN)

    def head_again():
        def again(i, carry):
            rows = pl.ds(pl.multiple_of(i * 32, 32), 32)
            for c in range(0, BIN_PAD, LANE):
                bins, angles = slice(c, c + LANE), slice(BIN_PAD + c, BIN_PAD + c + LANE)
                parity, inner = c // HALF_BIN, c % HALF_BIN
                reals = slice(parity * BIN_PAD + inner, parity * BIN_PAD + inner + LANE)
                imags = slice(reals.start + HALF_BIN, reals.stop + HALF_BIN)
                angle = angle_ref[rows, bins] + b_head[0:1, angles]
                scale = jnp.exp(logs_ref[rows, bins] + b_head[0:1, bins])
                real, imag = scale * jnp.cos(angle), scale * jnp.sin(angle)
                spec_ref[rows, reals] = real.astype(BF16)
                spec_ref[rows, imags] = imag.astype(BF16)
                dre = cot_ref[rows, reals].astype(F32)
                dim = cot_ref[rows, imags].astype(F32)
                hg[rows, bins] = (dre * real + dim * imag).astype(BF16)
                hg[rows, angles] = (dim * real - dre * imag).astype(BF16)
            return carry

        lax.fori_loop(0, TILE // 32, again, 0)

    def build_head():
        last = vecs[...]
        line = jnp.concatenate([last[25:26], last[26:27], last[27:28]], axis=1)
        line = jnp.broadcast_to(line, (16, 3 * channels))
        moved = pltpu.roll(line, 3 * channels - BINS, 1)
        for at, value in ((0, line), (BIN_PAD, moved)):
            picked = dot(value[:, 0:BIN_PAD].astype(BF16), order_ref[...], NN)
            b_head[:, at : at + BIN_PAD] = picked[0:8]
        inside = lax.broadcasted_iota(jnp.int32, (336, LANE), 0)
        for c in range(lane_tiles):
            cut = slice(c * LANE, (c + 1) * LANE)
            lines[c, 0:1312, :] = table[head_at : head_at + 1312, cut].astype(F32)
            lines[c, 1312:, :] = jnp.zeros((lines.shape[1] - 1312, LANE), F32)
            for part, start in ((0, 0), (BIN_PAD, BINS)):
                evens = lines[c, pl.ds(start, 336, stride=2), :]
                w_head[part : part + 336, cut] = jnp.where(inside < (BINS + 1) // 2, evens, 0.0).astype(BF16)
                odds = lines[c, pl.ds(start + 1, 320, stride=2), :]
                w_head[part + HALF_BIN : part + HALF_BIN + 320, cut] = odds.astype(BF16)
        longest = jnp.zeros((8, 1), F32)
        for at, size in spans(BIN_PAD, 64):
            weights = w_head[BIN_PAD + at : BIN_PAD + at + size, :].astype(F32)
            length = jnp.sum(weights * weights, axis=1, keepdims=True)
            longest = jnp.maximum(longest, jnp.max(length.reshape(size // 8, 8, 1), axis=0))
        gain, shift = jnp.abs(vec(vec_at + 2)), vec(vec_at + 3)
        normed_length = math.sqrt(channels) * jnp.max(gain) + jnp.sqrt(jnp.sum(shift * shift, keepdims=True))[0, 0]
        bound = 1.05 * normed_length * jnp.max(jnp.sqrt(longest)) + jnp.max(jnp.abs(b_head[:, BIN_PAD:]))
        slow[0] = jnp.where(bound < ANGLE_LIMIT, 0, 1)

    def over_all(call, values):
        return [functools.partial(call, v) for v in values]

    def in_spans(call, size, *more):
        return [functools.partial(call, at, length, *more) for at, length in spans(TILE, size)]

    def work(first, second):
        interleave(
            head_dots(logs_ref, 0) + head_dots(angle_ref, BIN_PAD) if second else [],
            in_spans(convolve, 32) if first else [],
        )
        interleave(
            (over_all(hidden_dot, range(0, FF, 256)) if first else [])
            + (over_all(grad_dot, range(0, 2 * BIN_PAD, 256)) if second else []),
            in_spans(head, 16, sincos) if second else [],
        )
        if second:
            pl.when(slow[0] > 0)(head_again)
        interleave(
            over_all(ngrad_dot, range(0, channels, 256)) if second else [],
            [call for c in range(IN_ROWS) for call in in_spans(gelu, 32, c)] if first else [],
        )
        sums = [sums_ref[v] for v in range(4)]

        def back(at, size):
            sums[:] = second_norm_back(at, size, sums)

        interleave(
            over_all(branch_dot, range(0, channels, 256)) if first else [],
            in_spans(back, 16) if second else [],
        )
        if second:
            for v in range(4):
                sums_ref[v] = sums[v]
            for c in range(0, 2 * BIN_PAD, 512):
                total = bsum_ref[:, c : c + 512]
                for at, size in spans(TILE, 32):
                    total = total + fold(hg[at : at + size, c : c + 512].astype(F32))
                bsum_ref[:, c : c + 512] = total
            hg_old[...] = hg[...]
            normed_old[...] = normed[...]
        if first:
            interleave([], in_spans(second_norm, 16))

    @pl.when(step == 0)
    def _():
        work(True, False)
        build_head()

    @pl.when((step > 0) & (step < count))
    def _():
        work(True, True)

    @pl.when(step == count)
    def _():
        work(False, True)

    @pl.when(step == count)
    def _():
        for c in range(0, 2 * BIN_PAD, 256):
            grad_dot(c)
        for c in range(lane_tiles):
            cut = slice(c * LANE, (c + 1) * LANE)
            for part, start in ((0, 0), (BIN_PAD, BINS)):
                lines[c, pl.ds(start + 1, 320, stride=2), :] = grad[part + HALF_BIN : part + HALF_BIN + 320, cut]
                lines[c, pl.ds(start, 320, stride=2), :] = grad[part : part + 320, cut]
                lines[c, start + 640 : start + 641, :] = grad[part + 320 : part + 321, cut]
            for b in range(40):
                low_half = lines[c, b * BR : b * BR + HALF, :].astype(BF16)
                high_half = lines[c, b * BR + HALF : b * BR + BR, :].astype(BF16)
                keep_ref[b, :, cut] = jnp.where(core == 0, low_half, high_half)
                send_ref[b, :, cut] = jnp.where(core == 0, high_half, low_half)
            tail_ref[:, cut] = lines[c, 1280:1288, :]
        store().wait()


def forward(owners, slots, meta, places, counts, x, low, high, order, cot, pieces, table, utts):
    rows, frames, channels = x.shape
    tiles = frames // TILE
    steps = rows * tiles
    count = rows * frames
    ahead = lambda i: jnp.minimum(i, steps - 1)
    behind = lambda i: jnp.maximum(i - 1, 0)
    wide = pl.BlockSpec((TILE, FF), lambda i: (ahead(i), 0))
    wide_late = pl.BlockSpec((None, TILE, FF), lambda i: (behind(i) // tiles, behind(i) % tiles, 0))
    slim = pl.BlockSpec((TILE, channels), lambda i: (ahead(i), 0))
    slim_late = pl.BlockSpec((TILE, channels), lambda i: (behind(i), 0))
    return pl.pallas_call(
        functools.partial(forward_body, owners=owners, slots=slots, tiles=tiles, count=steps, utts=utts),
        grid=(steps + 1,),
        in_specs=[SCALARS, SCALARS, SCALARS, WHOLE, WHOLE, WHOLE, WHOLE, wide_late]
        + [ANYWHERE] * (len(pieces) + 1),
        out_specs=[ANYWHERE, wide_late, wide, wide, slim, slim_late, slim_late, slim]
        + [pl.BlockSpec((TILE, LANE), lambda i: (ahead(i), 0))]
        + [WHOLE] * 5,
        out_shape=[
            shape_of((NB * BR, channels), BF16),
            shape_of((rows, frames, 2 * BIN_PAD), BF16),
            shape_of((count, FF), BF16),
            shape_of((count, FF), BF16),
            shape_of((count, channels), BF16),
            shape_of((count, channels), BF16),
            shape_of((count, channels), BF16),
            shape_of((count, channels), BF16),
            shape_of((count, LANE), F32),
            shape_of((40, HALF, channels), BF16),
            shape_of((40, HALF, channels), BF16),
            shape_of((8, channels), F32),
            shape_of((4, 8, channels), F32),
            shape_of((8, 2 * BIN_PAD), F32),
        ],
        scratch_shapes=[
            pltpu.VMEM((NB * BR, channels), BF16),
            pltpu.VMEM((channels // LANE, TILE + 2 * EDGE, LANE), F32),
            pltpu.VMEM((2 * BIN_PAD, channels), BF16),
            pltpu.VMEM((8, 2 * BIN_PAD), F32),
            pltpu.VMEM((BR, channels), F32),
            pltpu.VMEM((2 * utts, channels), F32),
            pltpu.VMEM((2 * BIN_PAD, channels), F32),
            pltpu.VMEM((channels // LANE, 1344, LANE), F32),
            pltpu.VMEM((TILE, 2 * BIN_PAD), BF16),
            pltpu.VMEM((TILE, 2 * BIN_PAD), BF16),
            pltpu.VMEM((TILE, FF), F32),
            pltpu.VMEM((TILE, BIN_PAD), F32),
            pltpu.VMEM((TILE, BIN_PAD), F32),
            pltpu.VMEM((TILE, channels), F32),
            pltpu.VMEM((TILE, channels), F32),
            pltpu.VMEM((TILE, channels), F32),
            pltpu.VMEM((TILE, channels), BF16),
            pltpu.VMEM((TILE, channels), BF16),
            pltpu.VMEM((TILE, channels), F32),
            pltpu.VMEM((TILE, LANE), F32),
            pltpu.SMEM((1,), jnp.int32),
            pltpu.SemaphoreType.DMA,
            pltpu.SemaphoreType.DMA((2,)),
        ],
        compiler_params=params(),
        cost_estimate=cost(10 * count * 1536 * 512, 40 * MIB, count * 4096),
        name="forward",
    )(meta, places, counts, x, low, high, order, cot, *pieces, table)


def mlp_body(meta, low_ref, act_ref, der_ref, ada_ref, wout_ref, *rest, utts):
    pre_ref, send_ref, keep_ref, bsum_ref, gout, gin, agrad = rest[-7:]
    step = pl.program_id(0)
    core = meta[0, 2 * utts + 2]
    tile = low_ref.shape[0]

    @pl.when(step == 0)
    def _():
        gout[...] = jnp.zeros_like(gout)
        gin[...] = jnp.zeros_like(gin)
        bsum_ref[...] = jnp.zeros_like(bsum_ref)

    def agrad_dot(c):
        agrad[:, c : c + 256] = dot(low_ref[...], wout_ref[c : c + 256, :], NT)

    def gout_dot(c):
        gout[c : c + 256, :] += dot(act_ref[:, c : c + 256], low_ref[...], TN)

    def gin_dot(c):
        gin[c : c + 256, :] += dot(pre_ref[:, c : c + 256], ada_ref[...], TN)

    def slope(c):
        cut = slice(c, c + 256)
        total = bsum_ref[:, cut]
        for at, size in spans(tile, 32):
            span = slice(at, at + size)
            pre = (agrad[span, cut] * der_ref[span, cut].astype(F32)).astype(BF16)
            pre_ref[span, cut] = pre
            total = total + fold(pre.astype(F32))
        bsum_ref[:, cut] = total

    cuts = range(0, CHUNK, 256)
    for c in cuts:
        agrad_dot(c)
    interleave([functools.partial(gout_dot, c) for c in cuts], [functools.partial(slope, c) for c in cuts])
    for c in cuts:
        gin_dot(c)

    @pl.when(step == pl.num_programs(0) - 1)
    def _():
        buckets = CHUNK // BR
        for at, ref in ((0, gin), (buckets, gout)):
            for b in range(buckets):
                low_half = ref[b * BR : b * BR + HALF, :].astype(BF16)
                high_half = ref[b * BR + HALF : b * BR + BR, :].astype(BF16)
                keep_ref[at + b] = jnp.where(core == 0, low_half, high_half)
                send_ref[at + b] = jnp.where(core == 0, high_half, low_half)


def mlp_backward(chunk, before, meta, low, act, der, ada, table, utts):
    count, channels = low.shape
    tile = 512
    slim = pl.BlockSpec((tile, channels), lambda i: (i, 0))
    part = pl.BlockSpec((tile, CHUNK), lambda i: (i, chunk))
    buckets = 2 * CHUNK // BR
    more = [] if before is None else [before]
    return pl.pallas_call(
        functools.partial(mlp_body, utts=utts),
        grid=(count // tile,),
        in_specs=[
            SCALARS,
            slim,
            part,
            part,
            slim,
            pl.BlockSpec((CHUNK, channels), lambda i: (FF // CHUNK + chunk, 0)),
        ]
        + [ANYWHERE] * len(more),
        out_specs=[part, WHOLE, WHOLE, WHOLE],
        out_shape=[
            shape_of((count, FF), BF16),
            shape_of((buckets, HALF, channels), BF16),
            shape_of((buckets, HALF, channels), BF16),
            shape_of((8, CHUNK), F32),
        ],
        input_output_aliases={6: 0} if more else {},
        scratch_shapes=[
            pltpu.VMEM((CHUNK, channels), F32),
            pltpu.VMEM((CHUNK, channels), F32),
            pltpu.VMEM((tile, CHUNK), F32),
        ],
        compiler_params=params(),
        cost_estimate=cost(6 * count * CHUNK * 512, 16 * MIB),
        name=f"mlp_backward_{chunk}",
    )(meta, low, act, der, ada, table, *more)


def norm_body(
    meta, x_ref, low_ref, high_ref, pre_ref, w_in, last_ref, xc_ref, rc_ref, *rest, row, tiles, utts, closing
):
    more = rest[: 8 if closing else 0]
    outs = rest[len(more) :]
    cg_ref, edge_ref, part_ref = outs[:3]
    xs, vecs, picks, agrad, cg, reaches = outs[-6:]
    tile = pl.program_id(0)
    channels = x_ref.shape[2]
    lane_tiles = channels // LANE
    base = meta[row, 2 * utts + 1] + tile * TILE
    vec = lambda v: vecs[2 + v : 3 + v, :]

    @pl.when(tile == 0)
    def _():
        vecs[...] = last_ref[...].astype(F32)
        part_ref[...] = more[0][...] if closing else jnp.zeros_like(part_ref)
        pick_rows(meta, row, utts, vec, picks, channels)

    agrad[...] = dot(pre_ref[...], w_in[...], NN)
    fill_frames(xs, x_ref, low_ref, high_ref, 0, tile, tiles, channels)
    for at, size in spans(TILE, 32):
        span = slice(at, at + size)
        reach, left = frame_reach(meta, row, base + at, size, utts)
        reaches[0, span, :] = reach
        reaches[1, span, :] = left
        index = base + at + lax.broadcasted_iota(jnp.int32, (size, LANE), 0)
        ecs, xcs = [], []
        for c in range(lane_tiles):
            cut = slice(c * LANE, (c + 1) * LANE)
            scale = by_utterance(meta, row, utts, index, lambda u: picks[u : u + 1, cut])
            ecs.append(agrad[span, cut] * scale)
            xcs.append(xc_ref[span, cut].astype(F32))
        m_one = jnp.sum(sum(ecs), axis=1, keepdims=True) * (1.0 / channels)
        m_two = jnp.sum(sum([e * v for e, v in zip(ecs, xcs)]), axis=1, keepdims=True) * (1.0 / channels)
        rc = rc_ref[span, :]
        for c in range(lane_tiles):
            cut = slice(c * LANE, (c + 1) * LANE)
            value = rc * (ecs[c] - m_one - xcs[c] * m_two)
            cg[c, span, :] = value
            cg_ref[span, cut] = value.astype(BF16)
    for u in range(utts):
        begin, end = meta[row, u], meta[row, u + 1]

        @pl.when((begin < base + TILE) & (end > base))
        def _(u=u, begin=begin, end=end):
            wanted = meta[row, utts + 1 + u]
            for c in range(lane_tiles):
                cut = slice(c * LANE, (c + 1) * LANE)
                one = jnp.zeros((8, LANE), F32)
                two = jnp.zeros((8, LANE), F32)
                for at, size in spans(TILE, 64):
                    span = slice(at, at + size)
                    index = base + at + lax.broadcasted_iota(jnp.int32, (size, LANE), 0)
                    value = jnp.where((index >= begin) & (index < end), agrad[span, cut], 0.0)
                    one = one + fold(value * xc_ref[span, cut].astype(F32))
                    two = two + fold(value)
                part_ref[KW + 1 + wanted, :, cut] += one
                part_ref[KW + 1 + NBW + wanted, :, cut] += two

    for c in range(lane_tiles):
        cut = slice(c * LANE, (c + 1) * LANE)
        sums = [part_ref[k, :, cut] for k in range(KW + 1)]
        for at, size in spans(TILE, 32):
            span = slice(at, at + size)
            reach, left = reaches[0, span, :], reaches[1, span, :]
            value = cg[c, span, :]
            for k in range(KW):
                offset = k - RIM
                moved = xs[c, EDGE + offset + at : EDGE + offset + at + size, :] * value
                sums[k] = sums[k] + fold(keep_within(moved, reach, left, offset))
            sums[KW] = sums[KW] + fold(value)
        for k in range(KW + 1):
            part_ref[k, :, cut] = sums[k]

    def edge(side, begin):
        for c in range(lane_tiles):
            edge_ref[side, :, c * LANE : (c + 1) * LANE] = cg[c, begin : begin + 8, :]

    @pl.when(tile == 0)
    def _():
        edge(0, 0)

    @pl.when(tile == tiles - 1)
    def _():
        edge(1, TILE - 8)

    if closing:
        _, other_edge, tail_ref, sums_ref, hsum_ref, bsum0, bsum1, order_ref = more
        vec_ref, quarter_refs = outs[-7], outs[3:7]
        core, plane = meta[0, 2 * utts + 2], meta[0, 2 * utts + 3]

        @pl.when(tile == tiles - 1)
        def _():
            vec_ref[0:8, :] = jnp.zeros((8, channels), F32)
            vec_ref[0:2, :] = tail_ref[0:2, :]
            for v in range(VROWS):
                at = v - (KW + 1 + 2 * NBW)
                rows_of = part_ref[v] if at < 0 else sums_ref[at]
                vec_ref[2 + v : 3 + v, :] = jnp.sum(rows_of, axis=0, keepdims=True)
            line = jnp.concatenate([bsum0[...], bsum1[...]], axis=1)
            for c in range(IN_ROWS):
                at = 2 + VROWS + c
                vec_ref[at : at + 1, :] = jnp.sum(
                    line[:, c * channels : (c + 1) * channels], axis=0, keepdims=True
                )

            def bins(value):
                value = jnp.broadcast_to(jnp.sum(value, axis=0, keepdims=True), (16, BIN_PAD))
                total = jnp.zeros((16, BIN_PAD), F32)
                for _ in range(3):
                    part = value.astype(BF16)
                    value = value - part.astype(F32)
                    total = total + dot(part, order_ref[...], NT)
                return total[0:8]

            flat = jnp.concatenate([bins(hsum_ref[:, 0:BIN_PAD]), bins(hsum_ref[:, BIN_PAD:])], axis=1)
            column = lax.broadcasted_iota(jnp.int32, (8, 3 * channels), 1)
            moved = pltpu.roll(flat, 2 * BIN_PAD - (BIN_PAD - BINS), 1)
            joined = jnp.where(column < BINS, flat, moved)
            joined = jnp.where(column < NOUT, joined, 0.0)
            for c in range(HEAD_ROWS):
                at = 2 + VROWS + IN_ROWS + c
                vec_ref[at : at + 1, :] = joined[0:1, c * channels : (c + 1) * channels]
            vec_ref[28:32, :] = jnp.zeros((4, channels), F32)
            for ref, c, p in zip(
                quarter_refs,
                (core, 1 - core, core, 1 - core),
                (plane, plane, 1 - plane, 1 - plane),
            ):
                ref[0:8, :] = vec_ref[pl.ds(pl.multiple_of(c * HALF + p * QUART, QUART), QUART), :]
            for at, ref in ((8, other_edge), (16, edge_ref)):
                quarter_refs[1][at : at + 8, :] = jnp.where(core == 0, ref[1], ref[0])
                quarter_refs[3][at : at + 8, :] = jnp.where(core == 0, ref[0], ref[1])


def norm_backward(row, closing, meta, x, low, high, pre, table, xc, rc, utts):
    rows, frames, channels = x.shape
    tiles = frames // TILE
    block = lambda width: pl.BlockSpec((TILE, width), lambda i: (row * tiles + i, 0))
    sums = KW + 1 + 2 * NBW
    out_specs = [pl.BlockSpec((TILE, channels), lambda i: (i, 0)), WHOLE, WHOLE]
    out_shape = [
        shape_of((frames, channels), BF16),
        shape_of((2, 8, channels), F32),
        shape_of((sums, 8, channels), F32),
    ]
    if closing:
        out_specs += [WHOLE] * 4
        out_shape += [shape_of((8 * n, channels), F32) for n in (1, 3, 1, 3)]
    return pl.pallas_call(
        functools.partial(norm_body, row=row, tiles=tiles, utts=utts, closing=bool(closing)),
        grid=(tiles,),
        in_specs=[SCALARS]
        + [pl.BlockSpec((1, frames, channels), lambda i: (row, 0, 0))]
        + [pl.BlockSpec((1, EDGE, channels), lambda i: (row, 0, 0))] * 2
        + [block(FF)]
        + [
            pl.BlockSpec((FF, channels), lambda i: (0, 0)),
            pl.BlockSpec((BR, channels), lambda i: (NB - 1, 0)),
            block(channels),
            block(LANE),
        ]
        + [WHOLE] * len(closing),
        out_specs=out_specs,
        out_shape=out_shape,
        scratch_shapes=([pltpu.VMEM((BR, channels), F32)] if closing else [])
        + [
            pltpu.VMEM((channels // LANE, TILE + 2 * EDGE, LANE), F32),
            pltpu.VMEM((BR, channels), F32),
            pltpu.VMEM((2 * utts, channels), F32),
            pltpu.VMEM((TILE, channels), F32),
            pltpu.VMEM((channels // LANE, TILE, LANE), F32),
            pltpu.VMEM((2, TILE, LANE), jnp.int32),
        ],
        compiler_params=params(),
        cost_estimate=cost(2 * frames * 1536 * 512, 12 * MIB),
        name=f"norm_backward_{row}",
    )(meta, x, low, high, pre, table, table, xc, rc, *closing)


def conv_body(meta, cg_ref, before_ref, after_ref, near_ref, cross_ref, resg_ref, last_ref, *rest, row, tiles, utts):
    out_ref, cs, vecs = rest[-3:]
    tile = pl.program_id(0)
    channels = cg_ref.shape[1]
    core = meta[0, 2 * utts + 2]
    base = meta[row, 2 * utts + 1] + tile * TILE

    @pl.when(tile == 0)
    def _():
        vecs[...] = last_ref[...].astype(F32)

    for c in range(channels // LANE):
        cut = slice(c * LANE, (c + 1) * LANE)
        cs[c, EDGE : EDGE + TILE, :] = cg_ref[:, cut].astype(F32)
        near, cross = near_ref[8 + 8 * row : 16 + 8 * row, cut], cross_ref[8 + 8 * row : 16 + 8 * row, cut]
        before, after = before_ref[:, cut].astype(F32)[EDGE - 8 :], after_ref[:, cut].astype(F32)[:8]
        cs[c, EDGE - 8 : EDGE, :] = jnp.where(tile == 0, jnp.where(core == 0, cross, near), before)
        after = jnp.where(tile == tiles - 1, jnp.where(core == 0, near, cross), after)
        cs[c, EDGE + TILE : EDGE + TILE + 8, :] = after
    for at, size in spans(TILE, 32):
        span = slice(at, at + size)
        reach, left = frame_reach(meta, row, base + at, size, utts)
        for c in range(channels // LANE):
            cut = slice(c * LANE, (c + 1) * LANE)
            total = resg_ref[span, cut].astype(F32)
            for k in range(KW):
                offset = RIM - k
                moved = cs[c, EDGE + offset + at : EDGE + offset + at + size, :]
                total = total + keep_within(moved, reach, left, offset) * vecs[2 + k : 3 + k, cut]
            out_ref[0, span, cut] = total


def conv_backward(row, before, meta, cg, near, cross, resg, table, rows, utts):
    frames, channels = cg.shape
    tiles = frames // TILE
    per = TILE // EDGE
    more = [] if before is None else [before]
    return pl.pallas_call(
        functools.partial(conv_body, row=row, tiles=tiles, utts=utts),
        grid=(tiles,),
        in_specs=[
            SCALARS,
            pl.BlockSpec((TILE, channels), lambda i: (i, 0)),
            pl.BlockSpec((EDGE, channels), lambda i: (jnp.maximum(i * per - 1, 0), 0)),
            pl.BlockSpec((EDGE, channels), lambda i: (jnp.minimum((i + 1) * per, tiles * per - 1), 0)),
            WHOLE,
            WHOLE,
            pl.BlockSpec((TILE, channels), lambda i: (row * tiles + i, 0)),
            pl.BlockSpec((BR, channels), lambda i: (NB - 1, 0)),
        ]
        + [ANYWHERE] * len(more),
        out_specs=pl.BlockSpec((1, TILE, channels), lambda i: (row, i, 0)),
        out_shape=shape_of((rows, frames, channels), F32),
        input_output_aliases={8: 0} if more else {},
        scratch_shapes=[
            pltpu.VMEM((channels // LANE, TILE + 2 * EDGE, LANE), F32),
            pltpu.VMEM((BR, channels), F32),
        ],
        compiler_params=params(),
        cost_estimate=cost(16 * frames * 512, 6 * MIB),
        name=f"conv_backward_{row}",
    )(meta, cg, cg, cg, near, cross, resg, table, *more)


def wave_body(meta, spec_ref, prev_ref, halo_ref, synth_ref, win_ref, *rest, start, rows, utts):
    out_ref, spec_all, held_all, done_all = rest[-4:]
    tile = start + pl.program_id(0)
    lane = lax.broadcasted_iota(jnp.int32, (TILE // 2, LANE), 1)
    front = lane < LANE // 2
    for r in range(rows):
        spec, held, done = spec_all.at[r], held_all.at[r], done_all.at[r]
        base = meta[r, 2 * utts + 1] + tile * TILE
        spec[EDGE:, :] = spec_ref[r]
        spec[0:EDGE, :] = jnp.where(tile == 0, halo_ref[r], prev_ref[r])
        for parity in range(2):
            half = slice(parity * BIN_PAD, (parity + 1) * BIN_PAD)
            piece = dot(spec[:, half], synth_ref[parity], NN)
            for c in range(BIN_PAD // LANE):
                held[parity, c] = piece[:, c * LANE : (c + 1) * LANE]
        for at, size in spans(TILE, 32):
            reach, _ = frame_reach(meta, r, base + at, size, utts)
            for c in range(3):
                cut = slice(c * LANE, (c + 1) * LANE)
                total = None
                for j in range(LAPS):
                    rows_at = slice(EDGE + at - j, EDGE + at - j + size)
                    of = (j % 2) * 3 + c
                    one, two = held[0, of, rows_at, :], held[1, of, rows_at, :]
                    piece = (one + two if j < 2 else one - two) * win_ref[j : j + 1, cut]
                    total = piece if j == 0 else total + jnp.where(reach >= j, piece, 0.0)
                done[c, at : at + size, :] = total * over(win_ref, LAPS, reach, c)
        even = [done[c, pl.ds(0, TILE // 2, stride=2), :] for c in range(3)]
        odd = [pltpu.roll(done[c, pl.ds(1, TILE // 2, stride=2), :], LANE // 2, 1) for c in range(3)]
        part = (
            even[0],
            even[1],
            jnp.where(front, even[2], odd[0]),
            jnp.where(front, odd[0], odd[1]),
            jnp.where(front, odd[1], odd[2]),
        )
        for k in range(PAIR):
            out_ref[pl.ds(2 * k + r, TILE // 2, stride=2 * PAIR), :] = part[k]


def wave_forward(start, stop, before, meta, spec, halo, synth, win, utts):
    rows, frames, _ = spec.shape
    tiles = frames // TILE
    per = TILE // EDGE
    more = [] if before is None else [before]
    return pl.pallas_call(
        functools.partial(wave_body, start=start, rows=rows, utts=utts),
        grid=(stop - start,),
        in_specs=[
            SCALARS,
            pl.BlockSpec((rows, TILE, 2 * BIN_PAD), lambda i: (0, start + i, 0)),
            pl.BlockSpec((rows, EDGE, 2 * BIN_PAD), lambda i: (0, jnp.maximum((start + i) * per - 1, 0), 0)),
            WHOLE,
            WHOLE,
            WHOLE,
        ]
        + [ANYWHERE] * len(more),
        out_specs=pl.BlockSpec((PAIR * TILE, LANE), lambda i: (start + i, 0)),
        out_shape=shape_of((PAIR * TILE * tiles, LANE), F32),
        input_output_aliases={6: 0} if more else {},
        scratch_shapes=[
            pltpu.VMEM((rows, TILE + EDGE, 2 * BIN_PAD), BF16),
            pltpu.VMEM((rows, 2, BIN_PAD // LANE, TILE + EDGE, LANE), F32),
            pltpu.VMEM((rows, LAP_PAD // LANE, TILE, LANE), F32),
        ],
        compiler_params=params(),
        cost_estimate=cost(4 * rows * (stop - start) * TILE * 768 * 768, 10 * MIB),
        name=f"wave_forward_{start}",
    )(meta, spec, spec, halo, synth, win, *more)


def slot_body(slot_of, *refs, groups, lasts, copies, slots):
    count = max(g[0] for g in groups) + 1
    keeps, cames, last_refs = refs[:count], refs[count : 2 * count], refs[2 * count : 2 * count + lasts]
    out, *more = refs[2 * count + lasts :]
    for index, offset, start, stop in groups:

        def one(b, carry, keep=keeps[index], came=cames[index], offset=offset, start=start):
            value = keep[offset + b].astype(F32) + came[offset + b].astype(F32)
            out[slot_of[0, start + b]] = value.astype(BF16)
            return carry

        lax.fori_loop(0, stop - start, one, 0, unroll=8)
    total = last_refs[0][0:QUART, :]
    for ref in last_refs[1:]:
        total = total + ref[0:QUART, :]
    out[slot_of[0, NB - 1]] = total.astype(BF16)
    for ref, at in zip(more, copies):
        ref[...] = out[at * slots : (at + 1) * slots]


def to_slots(slot_of, keeps, cames, lasts, groups, owners, slots, copies):
    channels = keeps[0].shape[2]
    return pl.pallas_call(
        functools.partial(slot_body, groups=groups, lasts=len(lasts), copies=copies, slots=slots),
        in_specs=[SCALARS] + [WHOLE] * (2 * len(keeps) + len(lasts)),
        out_specs=[WHOLE] * (1 + len(copies)),
        out_shape=[shape_of((owners * slots, QUART, channels), BF16)]
        + [shape_of((slots, QUART, channels), BF16)] * len(copies),
        compiler_params=params(),
        cost_estimate=cost(0, 6 * MIB),
        name="to_slots",
    )(slot_of, *keeps, *cames, *lasts)


def adam_body(places, meta, mine_ref, other_ref, master, first, second, *rest, block):
    out_master, out_first, out_second = rest[-3:]
    one_fix = 1.0 / (1.0 - BETA_ONE**STEP_COUNT)
    two_fix = 1.0 / (1.0 - BETA_TWO**STEP_COUNT)
    core = meta[0, meta.shape[1] - 2]
    for s in range(block):
        bucket = places[0, pl.program_id(0) * block + s]
        mine, other = mine_ref[s].astype(F32), other_ref[s].astype(F32)
        for half in range(2):
            grad = jnp.where(bucket < NB, jnp.where(core == half, mine, other), 0.0)
            old = master[s, half, 0]
            one = BETA_ONE * first[s, half, 0] + (1.0 - BETA_ONE) * grad
            two = BETA_TWO * second[s, half, 0] + (1.0 - BETA_TWO) * grad * grad
            out_first[s, half, 0] = one
            out_second[s, half, 0] = two
            step = one * one_fix / (jnp.sqrt(two * two_fix) + ADAM_EPS)
            out_master[s, half, 0] = old - LEARN_RATE * (step + WEIGHT_DECAY * old)


def adam(places, meta, mine, other, master, first, second, before):
    slots, depth, channels = master.shape
    block = max(b for b in range(1, ADAM_BLOCK + 1) if slots % b == 0)
    plane_at = meta.shape[1] - 1
    cut = lambda v: v.reshape(slots, 2, 2, QUART, channels)
    def at_plane(i, places, meta):
        plane = meta[0, plane_at]
        return i, 0, 1 - plane if before else plane, 0, 0

    full = pl.BlockSpec((block, 2, 1, QUART, channels), at_plane)
    part = pl.BlockSpec((block, QUART, channels), lambda i, places, meta: (i, 0, 0))
    more = [cut(v) for v in before]
    outs = pl.pallas_call(
        functools.partial(adam_body, block=block),
        grid_spec=pltpu.PrefetchScalarGridSpec(
            num_scalar_prefetch=2,
            grid=(slots // block,),
            in_specs=[part] * 2 + [full] * 3 + [ANYWHERE] * len(more),
            out_specs=[full] * 3,
        ),
        out_shape=[shape_of((slots, 2, 2, QUART, channels), F32)] * 3,
        input_output_aliases={7 + v: v for v in range(len(more))},
        compiler_params=params(),
        cost_estimate=cost(0, 6 * MIB),
        name="adam_second" if more else "adam_first",
    )(places, meta, mine, other, cut(master), cut(first), cut(second), *more)
    return [v.reshape(slots, depth, channels) for v in outs]


def tie(*values):
    return lax.optimization_barrier(values)


def plus(*values):
    return sum([v.astype(F32) for v in values]).astype(BF16)


def local(frames_in, lengths, bw_ids, owner_list, master, moment1, moment2, wave_grad):
    rows, frames, channels = frames_in.shape
    slots = master.shape[0]
    utts = lengths.shape[1]
    owners = lax.axis_size("rows")
    seqs = lax.axis_size("seq")
    row_at = lax.axis_index("rows")
    seq_at = lax.axis_index("seq")
    core, plane = seq_at % 2, seq_at // 2
    ring = ring_of(owners)
    half_ring = owners // 2

    mine = lax.dynamic_slice_in_dim(master, core * HALF, HALF, axis=1).astype(BF16)

    lines = wave_grad.reshape(rows, frames * HOP // LANE, LANE).transpose(1, 0, 2).reshape(-1, LANE)
    order = jnp.asarray(order_table())
    synth = jnp.asarray(synthesis_table())
    win = jnp.asarray(window_tables())

    low = shifted(frames_in[:, frames - EDGE :], 1)
    high = shifted(frames_in[:, :EDGE], -1)
    later = shifted(lines[: PAIR * EDGE], -1)
    offsets = [0]
    for hop in range(1, half_ring):
        offsets += [-hop, hop]
    offsets.append(-half_ring)
    names = np.arange(owners, dtype=np.int32)
    ids = jnp.stack([row_at, seq_at]).astype(jnp.int32)
    meta, places, held, slot_of, counts = plan(
        ids,
        lengths,
        bw_ids,
        owner_list,
        jnp.asarray(ring if ring else names, jnp.int32),
        jnp.asarray(offsets if ring else names, jnp.int32),
        slots,
        frames,
        bool(ring),
    )

    cot = None
    tiles = frames // TILE
    if ring:
        ahead = back = mine
        arrived = [mine, seq_swap(mine, 1)]
        for hop in range(half_ring):
            source = (ahead, back)
            ahead = lax.ppermute(ahead, AXES, ring_step(ring, 1, seqs))
            if hop < half_ring - 1:
                back = lax.ppermute(back, AXES, ring_step(ring, -1, seqs))
            if hop == 0:
                ahead, back, low, high, later, meta = tie(ahead, back, low, high, later, meta)
            if hop in (1, 2):
                feed = tie(lines, *source)[0]
                begin, end = ((0, tiles // 2), (tiles // 2, tiles))[hop - 1]
                cot = spectrum_cotangent(begin, end, cot, meta, feed, later, synth, win, rows, utts)
                ahead, back, cot = tie(ahead, back, cot)
            if hop == half_ring - 1:
                fed = tie(places, *source)[0]
                partial_table = assemble(tuple(range(owners - 1)), meta, fed, counts, arrived, slots)
                ahead, partial_table = tie(ahead, partial_table)
            else:
                arrived += [ahead, seq_swap(ahead, 1), back, seq_swap(back, 1)]
        arrived = [ahead, seq_swap(ahead, 1)]
        owned = (owners - 1,)
        part_places, part_counts, part_slots = places, counts, slots
    else:
        gathered = lax.all_gather(mine, "rows", axis=0, tiled=True)
        arrived = [gathered, seq_swap(gathered, 1)]
        owned = (0,)
        arrived = [take_slots(slot_of, a) for a in arrived]
        part_places = jnp.arange(NB, dtype=jnp.int32)[None, :]
        part_counts, part_slots = jnp.full((1, 1), NB, jnp.int32), NB
        partial_table = jnp.zeros((NB * BR, channels), BF16)
        cot = spectrum_cotangent(0, tiles, cot, meta, lines, later, synth, win, rows, utts)

    (table, spec, act, der, ada, low_grad, resg, xc, rc, send, keep, tail, sums, hsum) = forward(
        owned, part_slots, meta, part_places, part_counts, frames_in, low, high, order, cot, arrived, partial_table, utts
    )
    halo = shifted(spec[:, frames - EDGE :], 1)

    keeps, cames, groups = [], [], []

    def split(keep, came):
        both = plus(keep, came)
        stay = lax.dynamic_slice_in_dim(both, plane * QUART, QUART, axis=1)
        leave = lax.dynamic_slice_in_dim(both, (1 - plane) * QUART, QUART, axis=1)
        return stay, leave

    def record(stay, came, begins, per):
        for at, begin in enumerate(begins):
            groups.append((len(keeps), at * per, begin, begin + per))
        keeps.append(stay)
        cames.append(came)

    per = CHUNK // BR
    pre, bsums = None, []
    begins, count = (2 * FF // BR,), 40
    waiting = []
    for chunk in range(FF // CHUNK):
        near = seq_swap(send, 1)
        pre, next_send, next_keep, bsum = mlp_backward(chunk, pre, meta, low_grad, act, der, ada, table, utts)
        near, pre, next_send, next_keep = tie(near, pre, next_send, next_keep)
        bsums.append(bsum)
        stay, leave = split(keep, near)
        waiting.append((stay, seq_swap(leave, 2), begins, count))
        send, keep = next_send, next_keep
        begins, count = (chunk * per, FF // BR + chunk * per), per

    near = seq_swap(send, 1)
    for stay, came, *where_from in waiting[:-1]:
        pre, came = tie(pre, came)
        record(stay, came, *where_from)
    cg0, edge0, parts = norm_backward(0, (), meta, frames_in, low, high, pre, table, xc, rc, utts)
    kept, came, *where_from = waiting[-1]
    near, cg0, edge0, parts, pre, came = tie(near, cg0, edge0, parts, pre, came)
    record(kept, came, *where_from)
    stay, leave = split(keep, near)
    came = seq_swap(leave, 2)
    closing = (parts, edge0, tail, sums, hsum, *bsums, order)
    cg1, _, _, own, to_near, to_far, to_cross = norm_backward(
        1, closing, meta, frames_in, low, high, pre, table, xc, rc, utts
    )
    lasts = (own, seq_swap(to_near, 1), seq_swap(to_far, 2), seq_swap(to_cross, 3))
    came, spec, *lasts = tie(came, spec, *lasts)
    record(stay, came, begins, count)
    first_sent = (owners - 1, owners - 3) if ring else ()
    chunks, *sent = to_slots(slot_of, keeps, cames, lasts, tuple(groups), owners, slots, first_sent)

    state = {}

    def work(stage, *ready):
        if stage in (0, 2):
            feed = tie(spec, *ready)[0]
            begin, end, before = ((0, tiles // 2, None), (tiles // 2, tiles, state.get("wave")))[stage // 2]
            state["wave"] = wave_forward(begin, end, before, meta, feed, halo, synth, win, utts)
            return "wave"
        if stage in (1, 3):
            row = stage // 2
            feed = tie((cg0, cg1)[row], *ready)[0]
            state["grad"] = conv_backward(
                row, state.get("grad"), meta, feed, lasts[1], lasts[3], resg, table, rows, utts
            )
            return "grad"

    if ring:
        cut = {o: chunks[i * slots : (i + 1) * slots] for i, o in enumerate(offsets)}
        up, down = sent
        for hop in range(half_ring):
            left_over = half_ring - 1 - hop
            source = (up, down)
            up = lax.ppermute(up, AXES, ring_step(ring, 1, seqs))
            if hop < half_ring - 1:
                down = lax.ppermute(down, AXES, ring_step(ring, -1, seqs))
            done = work(hop, *source)
            up, down, state[done] = tie(up, down, state[done])
            if left_over:
                up = plus(up, cut[left_over])
                if hop < half_ring - 2:
                    down = plus(down, cut[1 - left_over])
        own = plus(cut[0], up, down)
    else:
        own = lax.psum_scatter(chunks, "rows", scatter_dimension=0, tiled=True)
        for hop in range(4):
            work(hop, own)
    near, far = seq_swap(own, 1), seq_swap(own, 2)
    cross = seq_swap(far, 1)
    waveform = state["wave"].reshape(-1, rows, LANE).transpose(1, 0, 2).reshape(rows, frames * HOP)

    first = adam(held, meta, own, near, master, moment1, moment2, ())
    cross, *first = tie(cross, *first)
    new_master, new_first, new_second = adam(held, meta, far, cross, master, moment1, moment2, first)
    return waveform, state["grad"], new_master, new_first, new_second


def solution(mesh):
    in_specs = (
        P("rows", "seq", None),
        P("rows", None),
        P("rows", None),
        P(),
        P("rows", None, None),
        P("rows", None, None),
        P("rows", None, None),
        P("rows", "seq"),
    )
    out_specs = (
        P("rows", "seq"),
        P("rows", "seq", None),
        P("rows", None, None),
        P("rows", None, None),
        P("rows", None, None),
    )
    return jax.shard_map(local, mesh=mesh, in_specs=in_specs, out_specs=out_specs, check_vma=False)
```

```python
import functools
import math

import jax
import jax.numpy as jnp
import numpy as np
from jax import lax
from jax.experimental import pallas as pl
from jax.experimental.pallas import tpu as pltpu
from jax.sharding import PartitionSpec as P

FF = 1536
NFFT = 1280
HOP = 320
NBW = 4
KW = 7
UTT = 4
BR = 32
STEP_COUNT = 6
BINS = 641
NOUT = 1282
VROWS = 20
IN_ROWS = 3
HEAD_ROWS = 3
NB = 137

NORM_EPS = 1e-06
ENV_FLOOR = 0.5
BETA_ONE = 0.8
BETA_TWO = 0.9
LEARN_RATE = 0.04
WEIGHT_DECAY = 0.01
ADAM_EPS = 1e-08

LAPS = NFFT // HOP
RIM = (KW - 1) // 2
LAP_PAD = 384
BIN_PAD = 768
HALF = BR // 2
QUART = BR // 4
EDGE = 16
TILE = 256
CHUNK = 768
HALF_BIN = 384
PAIR = 5
ADAM_BLOCK = 27
LANE = 128
AXES = ("rows", "seq")

F32 = jnp.float32
BF16 = jnp.bfloat16
MIB = 1 << 20
VMEM_BYTES = 60 * MIB


def bin_order():
    order = np.full(BIN_PAD, -1)
    order[: (BINS + 1) // 2] = np.arange(0, BINS, 2)
    order[HALF_BIN : HALF_BIN + BINS // 2] = np.arange(1, BINS, 2)
    return order


def order_table():
    return (np.arange(BIN_PAD)[:, None] == bin_order()[None, :]).astype(jnp.bfloat16)


def synthesis_table():
    n = np.arange(2 * HOP)[None, :]
    order = bin_order()
    out = np.zeros((2, 2, HALF_BIN, 2, LAP_PAD), np.float32)
    for parity in range(2):
        k = order[parity * HALF_BIN : (parity + 1) * HALF_BIN]
        k = k[k >= 0][:, None]
        angle = (k * n % NFFT) * (2.0 * math.pi / NFFT)
        factor = np.where((k == 0) | (k == NFFT // 2), 1.0, 2.0) / NFFT
        out[parity, 0, : len(k), :, :HOP] = (factor * np.cos(angle)).reshape(-1, 2, HOP)
        out[parity, 1, : len(k), :, :HOP] = (-factor * np.sin(angle)).reshape(-1, 2, HOP)
    return out.reshape(2, BIN_PAD, 2 * LAP_PAD).astype(jnp.bfloat16)


def window_tables():
    window = 0.5 - 0.5 * np.cos(np.arange(NFFT) * (2.0 * math.pi / NFFT))
    rows = np.zeros((LAPS, LAP_PAD), np.float64)
    rows[:, :HOP] = window.reshape(LAPS, HOP)
    envelope = np.cumsum(rows**2, axis=0)
    return np.concatenate([rows, 1.0 / np.maximum(envelope, ENV_FLOOR)], axis=0).astype(np.float32)


def ring_of(count):
    if count != 8:
        return None
    return [0, 2, 4, 6, 7, 5, 3, 1]


def ring_step(ring, shift, seq_count):
    where = {r: i for i, r in enumerate(ring)}
    pairs = []
    for r in ring:
        target = ring[(where[r] + shift) % len(ring)]
        pairs += [(r * seq_count + s, target * seq_count + s) for s in range(seq_count)]
    return pairs


def seq_swap(value, bit):
    count = lax.axis_size("seq")
    return lax.ppermute(value, "seq", [(s, s ^ bit) for s in range(count)])


def rows_swap(value, bit):
    count = lax.axis_size("rows")
    return lax.ppermute(value, "rows", [(r, r ^ bit) for r in range(count)])


def shifted(value, distance):
    devices = range(lax.axis_size("seq"))
    return lax.ppermute(
        value, "seq", [(i - distance, i) for i in devices if i - distance in devices]
    )


def dot(a, b, dims):
    return lax.dot_general(a, b, (dims, ((), ())), preferred_element_type=F32)


NN = ((1,), (0,))
NT = ((1,), (1,))
TN = ((0,), (0,))


def frame_reach(meta, row, first, count, utts):
    index = first + lax.broadcasted_iota(jnp.int32, (count, 128), 0)
    start = jnp.zeros_like(index)
    end = jnp.zeros_like(index) + meta[row, 1]
    for u in range(1, utts):
        inside = index >= meta[row, u]
        start = jnp.where(inside, meta[row, u], start)
        end = jnp.where(inside, meta[row, u + 1], end)
    return index - start, end - 1 - index


def spans(count, size):
    return [(at, min(size, count - at)) for at in range(0, count, size)]


def over(table, base, reach, lane_tile, width=LANE):
    cut = slice(lane_tile * LANE, lane_tile * LANE + width)
    picked = jnp.broadcast_to(table[base + LAPS - 1 : base + LAPS, cut], (reach.shape[0], width))
    for j in range(LAPS - 2, -1, -1):
        picked = jnp.where(reach[:, :width] == j, table[base + j : base + j + 1, cut], picked)
    return picked


def keep_within(values, reach, left, offset):
    if offset < 0:
        return jnp.where(reach >= -offset, values, 0.0)
    if offset > 0:
        return jnp.where(left >= offset, values, 0.0)
    return values


def row_mean(values):
    return jnp.mean(values, axis=1, keepdims=True)


def fold(values):
    rows, columns = values.shape
    return jnp.sum(values.reshape(rows // 8, 8, columns), axis=0)


def sincos(angle):
    turns = jnp.round(angle * (0.5 / math.pi))
    rest = angle * 0.5 - turns * 3.1416015625
    rest = rest + turns * 8.908910206761537e-06
    sq = rest * rest
    sine = 1.0 + sq * (
        -0.16666656732559204
        + sq * (0.008333033882081509 + sq * (-0.00019807791977655143 + sq * 2.6022808015113696e-06))
    )
    cosine = 1.0 + sq * (
        -0.4999992549419403
        + sq * (0.04166382923722267 + sq * (-0.001385461655445397 + sq * 2.3163083824329078e-05))
    )
    sine = rest * sine
    double = sine + sine
    return double * cosine, 1.0 - double * sine


ANGLE_LIMIT = 1024.0


def params():
    return pltpu.CompilerParams(vmem_limit_bytes=VMEM_BYTES)


def cost(flops, bytes_accessed, transcendentals=0):
    return pl.CostEstimate(
        flops=int(flops), bytes_accessed=int(bytes_accessed), transcendentals=int(transcendentals)
    )


WHOLE = pl.BlockSpec(memory_space=pltpu.VMEM)
SCALARS = pl.BlockSpec(memory_space=pltpu.SMEM)
ANYWHERE = pl.BlockSpec(memory_space=pl.ANY)
shape_of = jax.ShapeDtypeStruct


def plan_body(ids, lengths, bw_ids, owner_list, order, offsets, meta, places, held, slot_of, counts, rel, *, frames, ring):
    rows, utts = lengths.shape
    owners, slots = order.shape[0], held.shape[1]
    row_at, seq_at = ids[0], ids[1]
    for r in range(rows):
        start = jnp.int32(0)
        meta[r, 0] = start
        for u in range(utts):
            start = start + lengths[r, u]
            meta[r, u + 1] = start
            meta[r, utts + 1 + u] = bw_ids[r, u]
        meta[r, 2 * utts + 1] = seq_at * frames
        meta[r, 2 * utts + 2] = lax.rem(seq_at, 2)
        meta[r, 2 * utts + 3] = lax.div(seq_at, 2)
    where = jnp.int32(0)
    if ring:
        for i in range(owners):
            where = jnp.where(order[i] == row_at, i, where)

    def name(i, carry):
        rel[order[lax.rem(where + offsets[i] + owners, owners)]] = i
        counts[0, i] = 0
        return carry

    def clear(i, carry):
        places[0, i] = NB
        return carry

    def place(b, carry):
        i = rel[owner_list[b]]
        n = counts[0, i]
        counts[0, i] = n + 1
        places[0, i * slots + n] = b
        slot_of[0, b] = i * slots + n
        return carry

    lax.fori_loop(0, owners, name, 0)
    lax.fori_loop(0, owners * slots, clear, 0, unroll=8)
    lax.fori_loop(0, NB, place, 0)
    own = rel[row_at]

    def keep(n, carry):
        held[0, n] = places[0, own * slots + n]
        return carry

    lax.fori_loop(0, slots, keep, 0)


def plan(ids, lengths, bw_ids, owner_list, order, offsets, slots, frames, ring):
    rows, utts = lengths.shape
    owners = order.shape[0]
    shapes = ((rows, 2 * utts + 4), (1, owners * slots), (1, slots), (1, NB), (1, owners))
    return pl.pallas_call(
        functools.partial(plan_body, frames=frames, ring=ring),
        in_specs=[SCALARS] * 6,
        out_specs=[SCALARS] * 5,
        out_shape=[shape_of(shape, jnp.int32) for shape in shapes],
        scratch_shapes=[pltpu.SMEM((owners,), jnp.int32)],
        compiler_params=params(),
        cost_estimate=cost(8000, 8 * 1024),
        name="plan",
    )(ids, lengths, bw_ids, owner_list, order, offsets)


def pre_body(meta, wave_ref, halo_ref, synth_ref, win_ref, *rest, start, tiles, rows, utts):
    out_ref, flat, scaled_all, even_all, odd_all = rest[-5:]
    step = pl.program_id(0)
    tile = start + step
    lines = PAIR * TILE
    extra = PAIR * EDGE
    count = TILE + EDGE
    lane = lax.broadcasted_iota(jnp.int32, (count // 2, LANE), 1)
    for at, size in spans(lines, 320):
        rows_at = pl.ds(pl.multiple_of(tile * lines + at, 16), size)
        flat[at : at + size, :] = wave_ref[rows_at, :].astype(F32)
    after = jnp.minimum((tile + 1) * lines, tiles * lines - extra)
    following = wave_ref[pl.ds(pl.multiple_of(after, 16), extra), :]
    flat[lines:, :] = jnp.where(tile == tiles - 1, halo_ref[...], following).astype(F32)
    for r in range(rows):
        scaled, even, odd = scaled_all.at[r], even_all.at[r], odd_all.at[r]
        base = meta[r, 2 * utts + 1] + tile * TILE
        part = [flat[pl.ds(2 * k + r, count // 2, stride=2 * PAIR), :] for k in range(PAIR)]
        turned = [pltpu.roll(v, LANE // 2, 1) for v in part[2:]]
        front = lane < LANE // 2
        frame = (
            part[0],
            part[1],
            jnp.where(front, part[2], 0.0),
            jnp.where(front, turned[0], turned[1]),
            jnp.where(front, turned[1], turned[2]),
            jnp.where(front, turned[2], 0.0),
        )
        for c in range(3):
            scaled[c, pl.ds(0, count // 2, stride=2), :] = frame[c]
            scaled[c, pl.ds(1, count // 2, stride=2), :] = frame[3 + c]
        for at, size in spans(count, 32):
            reach, _ = frame_reach(meta, r, base + at, size, utts)
            for c in range(3):
                scaled[c, at : at + size, :] = scaled[c, at : at + size, :] * over(win_ref, LAPS, reach, c)
        for at, size in spans(TILE, 32):
            _, left = frame_reach(meta, r, base + at, size, utts)
            for j in range(2):
                for c in range(3):
                    span = slice(c * LANE, (c + 1) * LANE)

                    def lap(i):
                        value = scaled[c, at + i : at + i + size, :] * win_ref[i : i + 1, span]
                        return keep_within(value, None, left, i).astype(BF16).astype(F32)

                    one, two = lap(j), lap(j + 2)
                    column = slice(j * LAP_PAD + c * LANE, j * LAP_PAD + (c + 1) * LANE)
                    even[at : at + size, column] = (one + two).astype(BF16)
                    odd[at : at + size, column] = (one - two).astype(BF16)
        out_ref[r, :, 0:BIN_PAD] = dot(even[...], synth_ref[0], NT).astype(BF16)
        out_ref[r, :, BIN_PAD:] = dot(odd[...], synth_ref[1], NT).astype(BF16)


def spectrum_cotangent(start, stop, before, meta, wave, halo, synth, win, rows, utts):
    tiles = wave.shape[0] // (PAIR * TILE)
    frames = tiles * TILE
    more = [] if before is None else [before]
    steps = stop - start
    return pl.pallas_call(
        functools.partial(pre_body, start=start, tiles=tiles, rows=rows, utts=utts),
        grid=(steps,),
        in_specs=[SCALARS, WHOLE, WHOLE, WHOLE, WHOLE] + [ANYWHERE] * len(more),
        out_specs=pl.BlockSpec((rows, TILE, 2 * BIN_PAD), lambda i: (0, start + i, 0)),
        out_shape=shape_of((rows, frames, 2 * BIN_PAD), BF16),
        input_output_aliases={5: 0} if more else {},
        scratch_shapes=[
            pltpu.VMEM((PAIR * (TILE + EDGE), LANE), F32),
            pltpu.VMEM((rows, LAP_PAD // LANE, TILE + EDGE, LANE), F32),
            pltpu.VMEM((rows, TILE, BIN_PAD), BF16),
            pltpu.VMEM((rows, TILE, BIN_PAD), BF16),
        ],
        compiler_params=params(),
        cost_estimate=cost(4 * rows * steps * TILE * 768 * 768, rows * steps * TILE * 3072 + 4 * MIB),
        name=f"spectrum_cotangent_{start}",
    )(meta, wave, halo, synth, win, *more)


def place_parts(places, counts, core, pieces, table, sem, slots, owners, start):
    done = {}
    for index, ref in enumerate(pieces):
        side = core if index % 2 == 0 else 1 - core
        owner = owners[index // 2]
        first = done.get((owner, index % 2), 0)
        done[owner, index % 2] = first + ref.shape[0]

        def one(s, carry, ref=ref, side=side, owner=owner, first=first):
            bucket = places[0, owner * slots + first + s]
            at = pl.multiple_of(bucket * BR + side * HALF, HALF)
            copy = pltpu.make_async_copy(ref.at[s], table.at[pl.ds(at, HALF), :], sem)
            if start:
                copy.start()
            else:
                copy.wait()
            return carry

        held = jnp.clip(counts[0, owner] - first, 0, ref.shape[0])
        lax.fori_loop(0, held, one, 0)


def assemble_body(meta, places, counts, *refs, slots, owners):
    pieces, table, sem = refs[: 2 * len(owners)], refs[-2], refs[-1]
    core = meta[0, meta.shape[1] - 2]
    place_parts(places, counts, core, pieces, table, sem, slots, owners, True)
    place_parts(places, counts, core, pieces, table, sem, slots, owners, False)


def assemble(owners, meta, places, counts, pieces, slots):
    channels = pieces[0].shape[2]
    return pl.pallas_call(
        functools.partial(assemble_body, slots=slots, owners=owners),
        in_specs=[SCALARS, SCALARS, SCALARS] + [ANYWHERE] * len(pieces),
        out_specs=WHOLE,
        out_shape=shape_of((NB * BR, channels), BF16),
        scratch_shapes=[pltpu.SemaphoreType.DMA],
        compiler_params=params(),
        cost_estimate=cost(0, 12 * MIB),
        name="assemble",
    )(meta, places, counts, *pieces)


def take_body(slot_of, ref, out, sem):
    def copy(b):
        return pltpu.make_async_copy(ref.at[slot_of[0, b]], out.at[b], sem)

    def start(b, carry):
        copy(b).start()
        return carry

    def wait(b, carry):
        copy(b).wait()
        return carry

    lax.fori_loop(0, NB, start, 0)
    lax.fori_loop(0, NB, wait, 0)


def take_slots(slot_of, gathered):
    return pl.pallas_call(
        take_body,
        in_specs=[SCALARS, ANYWHERE],
        out_specs=WHOLE,
        out_shape=shape_of((NB, *gathered.shape[1:]), BF16),
        scratch_shapes=[pltpu.SemaphoreType.DMA],
        compiler_params=params(),
        cost_estimate=cost(0, 6 * MIB),
        name="take_slots",
    )(slot_of, gathered)


def fill_frames(xs, x_ref, low_ref, high_ref, row, tile, tiles, channels):
    first = pl.multiple_of(tile * TILE, TILE)

    def put(at, block):
        block = block.astype(F32)
        for c in range(channels // LANE):
            xs[c, at : at + block.shape[0], :] = block[:, c * LANE : (c + 1) * LANE]

    for at, size in spans(TILE, 64):
        put(EDGE + at, x_ref[row, pl.ds(pl.multiple_of(first + at, 64), size), :])

    before = x_ref[row, pl.ds(pl.multiple_of(jnp.maximum(first - EDGE, 0), EDGE), EDGE), :]
    put(0, jnp.where(tile == 0, low_ref[row], before))
    end = jnp.minimum(first + TILE, (tiles - 1) * TILE)
    after = x_ref[row, pl.ds(pl.multiple_of(end, EDGE), EDGE), :]
    put(EDGE + TILE, jnp.where(tile == tiles - 1, high_ref[row], after))


def by_utterance(meta, row, utts, index, rows_of):
    value = jnp.broadcast_to(rows_of(0), (index.shape[0], LANE))
    for u in range(1, utts):
        value = jnp.where(index >= meta[row, u], rows_of(u), value)
    return value


def pick_rows(meta, row, utts, vec, out, channels):
    for u in range(utts):
        wanted = meta[row, utts + 1 + u]
        for at, offset in ((u, KW + 1), (utts + u, KW + 1 + NBW)):
            value = vec(offset)
            for b in range(1, NBW):
                value = jnp.where(wanted == b, vec(offset + b), value)
            out[at : at + 1, :] = value


def interleave(ones, others):
    at = 0
    for i, one in enumerate(ones):
        one()
        until = (i + 1) * len(others) // len(ones)
        for other in others[at:until]:
            other()
        at = until
    for other in others[at:]:
        other()


def forward_body(meta, places, counts, x_ref, low_ref, high_ref, order_ref, cot_ref, *rest, owners, slots, tiles, count, utts):
    pieces = rest[: 2 * len(owners)]
    table_in = rest[2 * len(owners)]
    (
        table_out,
        spec_ref,
        act_ref,
        der_ref,
        ada_ref,
        lowg_ref,
        resg_ref,
        xc_ref,
        rc_ref,
        send_ref,
        keep_ref,
        tail_ref,
        sums_ref,
        bsum_ref,
        table,
        xs,
        w_head,
        b_head,
        vecs,
        picks,
        grad,
        lines,
        hg,
        hg_old,
        pre_ref,
        logs_ref,
        angle_ref,
        ngrad_ref,
        slim,
        xn_ref,
        normed,
        normed_old,
        branch_ref,
        rn_ref,
        slow,
        sem,
        sems,
    ) = rest[2 * len(owners) + 1 :]
    step = pl.program_id(0)
    core = meta[0, 2 * utts + 2]
    channels = x_ref.shape[2]
    lane_tiles = channels // LANE
    now = jnp.minimum(step, count - 1)
    row, tile = now // tiles, now % tiles
    vec = lambda v: vecs[2 + v : 3 + v, :]
    vec_at = KW + 1 + 2 * NBW
    head_at = 2 * FF

    def store():
        return pltpu.make_async_copy(table, table_out, sems.at[1])

    @pl.when(step == 0)
    def _():
        whole = pltpu.make_async_copy(table_in, table, sems.at[0])
        whole.start()
        normed[...] = jnp.zeros_like(normed)
        w_head[...] = jnp.zeros_like(w_head)
        b_head[...] = jnp.zeros_like(b_head)
        whole.wait()
        place_parts(places, counts, core, pieces, table, sem, slots, owners, True)
        place_parts(places, counts, core, pieces, table, sem, slots, owners, False)
        store().start()
        vecs[...] = table[head_at + 1280 : head_at + 1280 + BR, :].astype(F32)

    @pl.when(step == 1)
    def _():
        sums_ref[...] = jnp.zeros_like(sums_ref)
        bsum_ref[...] = jnp.zeros_like(bsum_ref)

    @pl.when(step == 2)
    def _():
        grad[...] = jnp.zeros_like(grad)

    @pl.when(tile == 0)
    def _():
        pick_rows(meta, row, utts, vec, picks, channels)

    base = meta[row, 2 * utts + 1] + tile * TILE
    fill_frames(xs, x_ref, low_ref, high_ref, row, tile, tiles, channels)

    def convolve(at, size):
        reach, left = frame_reach(meta, row, base + at, size, utts)
        index = base + at + lax.broadcasted_iota(jnp.int32, (size, LANE), 0)
        conv = []
        for c in range(lane_tiles):
            cut = slice(c * LANE, (c + 1) * LANE)
            total = vecs[2 + KW : 3 + KW, cut]
            for k in range(KW):
                offset = k - RIM
                moved = xs[c, EDGE + offset + at : EDGE + offset + at + size, :]
                total = total + keep_within(moved, reach, left, offset) * vecs[2 + k : 3 + k, cut]
            conv.append(total)
        mean = jnp.sum(sum(conv), axis=1, keepdims=True) * (1.0 / channels)
        conv = [v - mean for v in conv]
        square = jnp.sum(sum([v * v for v in conv]), axis=1, keepdims=True) * (1.0 / channels)
        rc = jnp.broadcast_to(lax.rsqrt(square + NORM_EPS), (size, LANE))
        rc_ref[at : at + size, :] = rc
        for c in range(lane_tiles):
            cut = slice(c * LANE, (c + 1) * LANE)
            xc = conv[c] * rc
            xc_ref[at : at + size, cut] = xc.astype(BF16)
            scale = by_utterance(meta, row, utts, index, lambda u: picks[u : u + 1, cut])
            shift = by_utterance(meta, row, utts, index, lambda u: picks[utts + u : utts + u + 1, cut])
            ada_ref[at : at + size, cut] = (xc * scale + shift).astype(BF16)

    def head(at, size, turn):
        span = slice(at, at + size)
        for c in range(0, BIN_PAD, LANE):
            bins, angles = slice(c, c + LANE), slice(BIN_PAD + c, BIN_PAD + c + LANE)
            parity, inner = c // HALF_BIN, c % HALF_BIN
            reals = slice(parity * BIN_PAD + inner, parity * BIN_PAD + inner + LANE)
            imags = slice(reals.start + HALF_BIN, reals.stop + HALF_BIN)
            angle = angle_ref[span, bins] + b_head[0:1, angles]
            scale = jnp.exp(logs_ref[span, bins] + b_head[0:1, bins])
            sine, cosine = turn(angle)
            real, imag = scale * cosine, scale * sine
            spec_ref[span, reals] = real.astype(BF16)
            spec_ref[span, imags] = imag.astype(BF16)
            dre = cot_ref[span, reals].astype(F32)
            dim = cot_ref[span, imags].astype(F32)
            hg[span, bins] = (dre * real + dim * imag).astype(BF16)
            hg[span, angles] = (dim * real - dre * imag).astype(BF16)

    def gelu(at, size, c):
        for d in range(c * 512, (c + 1) * 512, 256):
            cut = slice(d, d + 256)
            bias = vecs[2 + VROWS + c : 3 + VROWS + c, d - c * 512 : d - c * 512 + 256]
            pre = pre_ref[at : at + size, cut] + bias
            phi = 0.5 + 0.5 * lax.erf(pre * math.sqrt(0.5))
            bell = jnp.exp(-0.5 * pre * pre) * (1.0 / math.sqrt(2.0 * math.pi))
            act_ref[at : at + size, cut] = (pre * phi).astype(BF16)
            der_ref[at : at + size, cut] = (phi + pre * bell).astype(BF16)

    def second_norm(at, size):
        span = slice(at, at + size)
        branch = slim[span, :] + vec(vec_at)
        branch_ref[span, :] = branch
        x = jnp.concatenate([xs[c, EDGE + at : EDGE + at + size, :] for c in range(lane_tiles)], axis=1)
        residual = x + vec(vec_at + 1) * branch
        residual = residual - row_mean(residual)
        rn = lax.rsqrt(row_mean(residual * residual) + NORM_EPS)
        rn_ref[span, :] = jnp.broadcast_to(rn, (size, LANE))
        xn = residual * rn
        xn_ref[span, :] = xn
        normed[span, :] = (xn * vec(vec_at + 2) + vec(vec_at + 3)).astype(BF16)

    def second_norm_back(at, size, sums):
        span = slice(at, at + size)
        ngrad = ngrad_ref[span, :]
        xn = xn_ref[span, :]
        e = ngrad * vec(vec_at + 2)
        resg = rn_ref[span, 0:1] * (e - row_mean(e) - xn * row_mean(e * xn))
        resg_ref[span, :] = resg.astype(BF16)
        low = (vec(vec_at + 1) * resg).astype(BF16)
        lowg_ref[span, :] = low
        return (
            sums[0] + fold(low.astype(F32)),
            sums[1] + fold(resg * branch_ref[span, :]),
            sums[2] + fold(ngrad * xn),
            sums[3] + fold(ngrad),
        )

    def head_dots(ref, begin):
        def one(c):
            ref[:, c : c + 256] = dot(normed[...], w_head[begin + c : begin + c + 256, :], NT)

        return [functools.partial(one, c) for c in range(0, BIN_PAD, 256)]

    def hidden_dot(c):
        pre_ref[:, c : c + 256] = dot(ada_ref[...], table[c : c + 256, :], NT)

    def grad_dot(c):
        grad[c : c + 256, :] += dot(hg_old[:, c : c + 256], normed_old[...], TN)

    def ngrad_dot(c):
        ngrad_ref[:, c : c + 256] = dot(hg[...], w_head[:, c : c + 256], NN)

    def branch_dot(c):
        slim[:, c : c + 256] = dot(act_ref[...], table[FF : 2 * FF, c : c + 256], NN)

    def head_again():
        def again(i, carry):
            rows = pl.ds(pl.multiple_of(i * 32, 32), 32)
            for c in range(0, BIN_PAD, LANE):
                bins, angles = slice(c, c + LANE), slice(BIN_PAD + c, BIN_PAD + c + LANE)
                parity, inner = c // HALF_BIN, c % HALF_BIN
                reals = slice(parity * BIN_PAD + inner, parity * BIN_PAD + inner + LANE)
                imags = slice(reals.start + HALF_BIN, reals.stop + HALF_BIN)
                angle = angle_ref[rows, bins] + b_head[0:1, angles]
                scale = jnp.exp(logs_ref[rows, bins] + b_head[0:1, bins])
                real, imag = scale * jnp.cos(angle), scale * jnp.sin(angle)
                spec_ref[rows, reals] = real.astype(BF16)
                spec_ref[rows, imags] = imag.astype(BF16)
                dre = cot_ref[rows, reals].astype(F32)
                dim = cot_ref[rows, imags].astype(F32)
                hg[rows, bins] = (dre * real + dim * imag).astype(BF16)
                hg[rows, angles] = (dim * real - dre * imag).astype(BF16)
            return carry

        lax.fori_loop(0, TILE // 32, again, 0)

    def build_head():
        last = vecs[...]
        line = jnp.concatenate([last[25:26], last[26:27], last[27:28]], axis=1)
        line = jnp.broadcast_to(line, (16, 3 * channels))
        moved = pltpu.roll(line, 3 * channels - BINS, 1)
        both = jnp.concatenate([line[0:8, 0:BIN_PAD], moved[0:8, 0:BIN_PAD]], axis=0)
        picked = dot(both.astype(BF16), order_ref[...], NN)
        b_head[:, 0:BIN_PAD] = picked[0:8]
        b_head[:, BIN_PAD:] = picked[8:16]
        inside = lax.broadcasted_iota(jnp.int32, (336, LANE), 0)
        for c in range(lane_tiles):
            cut = slice(c * LANE, (c + 1) * LANE)
            lines[c, 0:1312, :] = table[head_at : head_at + 1312, cut].astype(F32)
            lines[c, 1312:, :] = jnp.zeros((lines.shape[1] - 1312, LANE), F32)
            for part, start in ((0, 0), (BIN_PAD, BINS)):
                evens = lines[c, pl.ds(start, 336, stride=2), :]
                w_head[part : part + 336, cut] = jnp.where(inside < (BINS + 1) // 2, evens, 0.0).astype(BF16)
                odds = lines[c, pl.ds(start + 1, 320, stride=2), :]
                w_head[part + HALF_BIN : part + HALF_BIN + 320, cut] = odds.astype(BF16)
        longest = jnp.zeros((8, 1), F32)
        for at, size in spans(BIN_PAD, 64):
            weights = w_head[BIN_PAD + at : BIN_PAD + at + size, :].astype(F32)
            length = jnp.sum(weights * weights, axis=1, keepdims=True)
            longest = jnp.maximum(longest, jnp.max(length.reshape(size // 8, 8, 1), axis=0))
        gain, shift = jnp.abs(vec(vec_at + 2)), vec(vec_at + 3)
        normed_length = math.sqrt(channels) * jnp.max(gain) + jnp.sqrt(jnp.sum(shift * shift, keepdims=True))[0, 0]
        bound = 1.05 * normed_length * jnp.max(jnp.sqrt(longest)) + jnp.max(jnp.abs(b_head[:, BIN_PAD:]))
        slow[0] = jnp.where(bound < ANGLE_LIMIT, 0, 1)

    def over_all(call, values):
        return [functools.partial(call, v) for v in values]

    def in_spans(call, size, *more):
        return [functools.partial(call, at, length, *more) for at, length in spans(TILE, size)]

    def work(first, second):
        interleave(
            head_dots(logs_ref, 0) + head_dots(angle_ref, BIN_PAD) if second else [],
            in_spans(convolve, 32) if first else [],
        )
        interleave(
            (over_all(hidden_dot, range(0, FF, 256)) if first else [])
            + (over_all(grad_dot, range(0, 2 * BIN_PAD, 256)) if second else []),
            in_spans(head, 16, sincos) if second else [],
        )
        if second:
            pl.when(slow[0] > 0)(head_again)
        interleave(
            over_all(ngrad_dot, range(0, channels, 256)) if second else [],
            [call for c in range(IN_ROWS) for call in in_spans(gelu, 32, c)] if first else [],
        )
        sums = [sums_ref[v] for v in range(4)]

        def back(at, size):
            sums[:] = second_norm_back(at, size, sums)

        interleave(
            over_all(branch_dot, range(0, channels, 256)) if first else [],
            in_spans(back, 16) if second else [],
        )
        if second:
            for v in range(4):
                sums_ref[v] = sums[v]
            for c in range(0, 2 * BIN_PAD, 512):
                total = bsum_ref[:, c : c + 512]
                for at, size in spans(TILE, 32):
                    total = total + fold(hg[at : at + size, c : c + 512].astype(F32))
                bsum_ref[:, c : c + 512] = total
            hg_old[...] = hg[...]
            normed_old[...] = normed[...]
        if first:
            interleave([], in_spans(second_norm, 16))

    @pl.when(step == 0)
    def _():
        work(True, False)
        build_head()

    @pl.when((step > 0) & (step < count))
    def _():
        work(True, True)

    @pl.when(step == count)
    def _():
        work(False, True)

    @pl.when(step == count)
    def _():
        for c in range(0, 2 * BIN_PAD, 256):
            grad_dot(c)
        for c in range(lane_tiles):
            cut = slice(c * LANE, (c + 1) * LANE)
            for part, start in ((0, 0), (BIN_PAD, BINS)):
                lines[c, pl.ds(start + 1, 320, stride=2), :] = grad[part + HALF_BIN : part + HALF_BIN + 320, cut]
                lines[c, pl.ds(start, 320, stride=2), :] = grad[part : part + 320, cut]
                lines[c, start + 640 : start + 641, :] = grad[part + 320 : part + 321, cut]
            for b in range(40):
                low_half = lines[c, b * BR : b * BR + HALF, :].astype(BF16)
                high_half = lines[c, b * BR + HALF : b * BR + BR, :].astype(BF16)
                keep_ref[b, :, cut] = jnp.where(core == 0, low_half, high_half)
                send_ref[b, :, cut] = jnp.where(core == 0, high_half, low_half)
            tail_ref[:, cut] = lines[c, 1280:1288, :]
        store().wait()


def forward(owners, slots, meta, places, counts, x, low, high, order, cot, pieces, table, utts):
    rows, frames, channels = x.shape
    tiles = frames // TILE
    steps = rows * tiles
    count = rows * frames
    ahead = lambda i: jnp.minimum(i, steps - 1)
    behind = lambda i: jnp.maximum(i - 1, 0)
    wide = pl.BlockSpec((TILE, FF), lambda i: (ahead(i), 0))
    wide_late = pl.BlockSpec((None, TILE, FF), lambda i: (behind(i) // tiles, behind(i) % tiles, 0))
    slim = pl.BlockSpec((TILE, channels), lambda i: (ahead(i), 0))
    slim_late = pl.BlockSpec((TILE, channels), lambda i: (behind(i), 0))
    return pl.pallas_call(
        functools.partial(forward_body, owners=owners, slots=slots, tiles=tiles, count=steps, utts=utts),
        grid=(steps + 1,),
        in_specs=[SCALARS, SCALARS, SCALARS, WHOLE, WHOLE, WHOLE, WHOLE, wide_late]
        + [ANYWHERE] * (len(pieces) + 1),
        out_specs=[ANYWHERE, wide_late, wide, wide, slim, slim_late, slim_late, slim]
        + [pl.BlockSpec((TILE, LANE), lambda i: (ahead(i), 0))]
        + [WHOLE] * 5,
        out_shape=[
            shape_of((NB * BR, channels), BF16),
            shape_of((rows, frames, 2 * BIN_PAD), BF16),
            shape_of((count, FF), BF16),
            shape_of((count, FF), BF16),
            shape_of((count, channels), BF16),
            shape_of((count, channels), BF16),
            shape_of((count, channels), BF16),
            shape_of((count, channels), BF16),
            shape_of((count, LANE), F32),
            shape_of((40, HALF, channels), BF16),
            shape_of((40, HALF, channels), BF16),
            shape_of((8, channels), F32),
            shape_of((4, 8, channels), F32),
            shape_of((8, 2 * BIN_PAD), F32),
        ],
        scratch_shapes=[
            pltpu.VMEM((NB * BR, channels), BF16),
            pltpu.VMEM((channels // LANE, TILE + 2 * EDGE, LANE), F32),
            pltpu.VMEM((2 * BIN_PAD, channels), BF16),
            pltpu.VMEM((8, 2 * BIN_PAD), F32),
            pltpu.VMEM((BR, channels), F32),
            pltpu.VMEM((2 * utts, channels), F32),
            pltpu.VMEM((2 * BIN_PAD, channels), F32),
            pltpu.VMEM((channels // LANE, 1344, LANE), F32),
            pltpu.VMEM((TILE, 2 * BIN_PAD), BF16),
            pltpu.VMEM((TILE, 2 * BIN_PAD), BF16),
            pltpu.VMEM((TILE, FF), F32),
            pltpu.VMEM((TILE, BIN_PAD), F32),
            pltpu.VMEM((TILE, BIN_PAD), F32),
            pltpu.VMEM((TILE, channels), F32),
            pltpu.VMEM((TILE, channels), F32),
            pltpu.VMEM((TILE, channels), F32),
            pltpu.VMEM((TILE, channels), BF16),
            pltpu.VMEM((TILE, channels), BF16),
            pltpu.VMEM((TILE, channels), F32),
            pltpu.VMEM((TILE, LANE), F32),
            pltpu.SMEM((1,), jnp.int32),
            pltpu.SemaphoreType.DMA,
            pltpu.SemaphoreType.DMA((2,)),
        ],
        compiler_params=params(),
        cost_estimate=cost(10 * count * 1536 * 512, 40 * MIB, count * 4096),
        name="forward",
    )(meta, places, counts, x, low, high, order, cot, *pieces, table)


def mlp_body(meta, low_ref, act_ref, der_ref, ada_ref, wout_ref, *rest, utts):
    pre_ref, send_ref, keep_ref, bsum_ref, gout, gin, agrad = rest[-7:]
    step = pl.program_id(0)
    core = meta[0, 2 * utts + 2]
    tile = low_ref.shape[0]

    @pl.when(step == 0)
    def _():
        gout[...] = jnp.zeros_like(gout)
        gin[...] = jnp.zeros_like(gin)
        bsum_ref[...] = jnp.zeros_like(bsum_ref)

    def agrad_dot(c):
        agrad[:, c : c + 256] = dot(low_ref[...], wout_ref[c : c + 256, :], NT)

    def gout_dot(c):
        gout[c : c + 256, :] += dot(act_ref[:, c : c + 256], low_ref[...], TN)

    def gin_dot(c):
        gin[c : c + 256, :] += dot(pre_ref[:, c : c + 256], ada_ref[...], TN)

    def slope(c):
        cut = slice(c, c + 256)
        total = bsum_ref[:, cut]
        for at, size in spans(tile, 32):
            span = slice(at, at + size)
            pre = (agrad[span, cut] * der_ref[span, cut].astype(F32)).astype(BF16)
            pre_ref[span, cut] = pre
            total = total + fold(pre.astype(F32))
        bsum_ref[:, cut] = total

    cuts = range(0, CHUNK, 256)
    for c in cuts:
        agrad_dot(c)
    interleave([functools.partial(gout_dot, c) for c in cuts], [functools.partial(slope, c) for c in cuts])
    for c in cuts:
        gin_dot(c)

    @pl.when(step == pl.num_programs(0) - 1)
    def _():
        buckets = CHUNK // BR
        for at, ref in ((0, gin), (buckets, gout)):
            for b in range(buckets):
                low_half = ref[b * BR : b * BR + HALF, :].astype(BF16)
                high_half = ref[b * BR + HALF : b * BR + BR, :].astype(BF16)
                keep_ref[at + b] = jnp.where(core == 0, low_half, high_half)
                send_ref[at + b] = jnp.where(core == 0, high_half, low_half)


def mlp_backward(chunk, before, meta, low, act, der, ada, table, utts):
    count, channels = low.shape
    tile = 512
    slim = pl.BlockSpec((tile, channels), lambda i: (i, 0))
    part = pl.BlockSpec((tile, CHUNK), lambda i: (i, chunk))
    buckets = 2 * CHUNK // BR
    more = [] if before is None else [before]
    return pl.pallas_call(
        functools.partial(mlp_body, utts=utts),
        grid=(count // tile,),
        in_specs=[
            SCALARS,
            slim,
            part,
            part,
            slim,
            pl.BlockSpec((CHUNK, channels), lambda i: (FF // CHUNK + chunk, 0)),
        ]
        + [ANYWHERE] * len(more),
        out_specs=[part, WHOLE, WHOLE, WHOLE],
        out_shape=[
            shape_of((count, FF), BF16),
            shape_of((buckets, HALF, channels), BF16),
            shape_of((buckets, HALF, channels), BF16),
            shape_of((8, CHUNK), F32),
        ],
        input_output_aliases={6: 0} if more else {},
        scratch_shapes=[
            pltpu.VMEM((CHUNK, channels), F32),
            pltpu.VMEM((CHUNK, channels), F32),
            pltpu.VMEM((tile, CHUNK), F32),
        ],
        compiler_params=params(),
        cost_estimate=cost(6 * count * CHUNK * 512, 16 * MIB),
        name=f"mlp_backward_{chunk}",
    )(meta, low, act, der, ada, table, *more)


def norm_body(
    meta, x_ref, low_ref, high_ref, pre_ref, w_in, last_ref, xc_ref, rc_ref, *rest, row, tiles, utts, closing
):
    more = rest[: 8 if closing else 0]
    outs = rest[len(more) :]
    cg_ref, edge_ref, part_ref = outs[:3]
    xs, vecs, picks, agrad, cg, reaches = outs[-6:]
    tile = pl.program_id(0)
    channels = x_ref.shape[2]
    lane_tiles = channels // LANE
    base = meta[row, 2 * utts + 1] + tile * TILE
    vec = lambda v: vecs[2 + v : 3 + v, :]

    @pl.when(tile == 0)
    def _():
        vecs[...] = last_ref[...].astype(F32)
        part_ref[...] = more[0][...] if closing else jnp.zeros_like(part_ref)
        pick_rows(meta, row, utts, vec, picks, channels)

    agrad[...] = dot(pre_ref[...], w_in[...], NN)
    fill_frames(xs, x_ref, low_ref, high_ref, 0, tile, tiles, channels)
    for at, size in spans(TILE, 32):
        span = slice(at, at + size)
        reach, left = frame_reach(meta, row, base + at, size, utts)
        reaches[0, span, :] = reach
        reaches[1, span, :] = left
        index = base + at + lax.broadcasted_iota(jnp.int32, (size, LANE), 0)
        ecs, xcs = [], []
        for c in range(lane_tiles):
            cut = slice(c * LANE, (c + 1) * LANE)
            scale = by_utterance(meta, row, utts, index, lambda u: picks[u : u + 1, cut])
            ecs.append(agrad[span, cut] * scale)
            xcs.append(xc_ref[span, cut].astype(F32))
        m_one = jnp.sum(sum(ecs), axis=1, keepdims=True) * (1.0 / channels)
        m_two = jnp.sum(sum([e * v for e, v in zip(ecs, xcs)]), axis=1, keepdims=True) * (1.0 / channels)
        rc = rc_ref[span, :]
        for c in range(lane_tiles):
            cut = slice(c * LANE, (c + 1) * LANE)
            value = rc * (ecs[c] - m_one - xcs[c] * m_two)
            cg[c, span, :] = value
            cg_ref[span, cut] = value.astype(BF16)
    for u in range(utts):
        begin, end = meta[row, u], meta[row, u + 1]

        @pl.when((begin < base + TILE) & (end > base))
        def _(u=u, begin=begin, end=end):
            wanted = meta[row, utts + 1 + u]
            for c in range(lane_tiles):
                cut = slice(c * LANE, (c + 1) * LANE)
                one = jnp.zeros((8, LANE), F32)
                two = jnp.zeros((8, LANE), F32)
                for at, size in spans(TILE, 64):
                    span = slice(at, at + size)
                    index = base + at + lax.broadcasted_iota(jnp.int32, (size, LANE), 0)
                    value = jnp.where((index >= begin) & (index < end), agrad[span, cut], 0.0)
                    one = one + fold(value * xc_ref[span, cut].astype(F32))
                    two = two + fold(value)
                part_ref[KW + 1 + wanted, :, cut] += one
                part_ref[KW + 1 + NBW + wanted, :, cut] += two

    for c in range(lane_tiles):
        cut = slice(c * LANE, (c + 1) * LANE)
        sums = [part_ref[k, :, cut] for k in range(KW + 1)]
        for at, size in spans(TILE, 32):
            span = slice(at, at + size)
            reach, left = reaches[0, span, :], reaches[1, span, :]
            value = cg[c, span, :]
            for k in range(KW):
                offset = k - RIM
                moved = xs[c, EDGE + offset + at : EDGE + offset + at + size, :] * value
                sums[k] = sums[k] + fold(keep_within(moved, reach, left, offset))
            sums[KW] = sums[KW] + fold(value)
        for k in range(KW + 1):
            part_ref[k, :, cut] = sums[k]

    def edge(side, begin):
        for c in range(lane_tiles):
            edge_ref[side, :, c * LANE : (c + 1) * LANE] = cg[c, begin : begin + 8, :]

    @pl.when(tile == 0)
    def _():
        edge(0, 0)

    @pl.when(tile == tiles - 1)
    def _():
        edge(1, TILE - 8)

    if closing:
        _, other_edge, tail_ref, sums_ref, hsum_ref, bsum0, bsum1, order_ref = more
        vec_ref, quarter_refs = outs[-7], outs[3:7]
        core, plane = meta[0, 2 * utts + 2], meta[0, 2 * utts + 3]

        @pl.when(tile == tiles - 1)
        def _():
            vec_ref[0:8, :] = jnp.zeros((8, channels), F32)
            vec_ref[0:2, :] = tail_ref[0:2, :]
            for v in range(VROWS):
                at = v - (KW + 1 + 2 * NBW)
                rows_of = part_ref[v] if at < 0 else sums_ref[at]
                vec_ref[2 + v : 3 + v, :] = jnp.sum(rows_of, axis=0, keepdims=True)
            line = jnp.concatenate([bsum0[...], bsum1[...]], axis=1)
            for c in range(IN_ROWS):
                at = 2 + VROWS + c
                vec_ref[at : at + 1, :] = jnp.sum(
                    line[:, c * channels : (c + 1) * channels], axis=0, keepdims=True
                )

            parts = []
            for at in (0, BIN_PAD):
                value = jnp.sum(hsum_ref[:, at : at + BIN_PAD], axis=0, keepdims=True)
                value = jnp.broadcast_to(value, (8, BIN_PAD))
                for _ in range(3):
                    part = value.astype(BF16).astype(F32)
                    value = value - part
                    parts.append(part)
            moved = dot(jnp.concatenate(parts, axis=0).astype(BF16), order_ref[...], NT)
            halves = [moved[at : at + 8] + moved[at + 8 : at + 16] + moved[at + 16 : at + 24] for at in (0, 24)]
            flat = jnp.concatenate(halves, axis=1)
            column = lax.broadcasted_iota(jnp.int32, (8, 3 * channels), 1)
            moved = pltpu.roll(flat, 2 * BIN_PAD - (BIN_PAD - BINS), 1)
            joined = jnp.where(column < BINS, flat, moved)
            joined = jnp.where(column < NOUT, joined, 0.0)
            for c in range(HEAD_ROWS):
                at = 2 + VROWS + IN_ROWS + c
                vec_ref[at : at + 1, :] = joined[0:1, c * channels : (c + 1) * channels]
            vec_ref[28:32, :] = jnp.zeros((4, channels), F32)
            for ref, c, p in zip(
                quarter_refs,
                (core, 1 - core, core, 1 - core),
                (plane, plane, 1 - plane, 1 - plane),
            ):
                ref[0:8, :] = vec_ref[pl.ds(pl.multiple_of(c * HALF + p * QUART, QUART), QUART), :]
            for at, ref in ((8, other_edge), (16, edge_ref)):
                quarter_refs[1][at : at + 8, :] = jnp.where(core == 0, ref[1], ref[0])
                quarter_refs[3][at : at + 8, :] = jnp.where(core == 0, ref[0], ref[1])


def norm_backward(row, closing, meta, x, low, high, pre, table, xc, rc, utts):
    rows, frames, channels = x.shape
    tiles = frames // TILE
    block = lambda width: pl.BlockSpec((TILE, width), lambda i: (row * tiles + i, 0))
    sums = KW + 1 + 2 * NBW
    out_specs = [pl.BlockSpec((TILE, channels), lambda i: (i, 0)), WHOLE, WHOLE]
    out_shape = [
        shape_of((frames, channels), BF16),
        shape_of((2, 8, channels), F32),
        shape_of((sums, 8, channels), F32),
    ]
    if closing:
        out_specs += [WHOLE] * 4
        out_shape += [shape_of((8 * n, channels), F32) for n in (1, 3, 1, 3)]
    return pl.pallas_call(
        functools.partial(norm_body, row=row, tiles=tiles, utts=utts, closing=bool(closing)),
        grid=(tiles,),
        in_specs=[SCALARS]
        + [pl.BlockSpec((1, frames, channels), lambda i: (row, 0, 0))]
        + [pl.BlockSpec((1, EDGE, channels), lambda i: (row, 0, 0))] * 2
        + [block(FF)]
        + [
            pl.BlockSpec((FF, channels), lambda i: (0, 0)),
            pl.BlockSpec((BR, channels), lambda i: (NB - 1, 0)),
            block(channels),
            block(LANE),
        ]
        + [WHOLE] * len(closing),
        out_specs=out_specs,
        out_shape=out_shape,
        scratch_shapes=([pltpu.VMEM((BR, channels), F32)] if closing else [])
        + [
            pltpu.VMEM((channels // LANE, TILE + 2 * EDGE, LANE), F32),
            pltpu.VMEM((BR, channels), F32),
            pltpu.VMEM((2 * utts, channels), F32),
            pltpu.VMEM((TILE, channels), F32),
            pltpu.VMEM((channels // LANE, TILE, LANE), F32),
            pltpu.VMEM((2, TILE, LANE), jnp.int32),
        ],
        compiler_params=params(),
        cost_estimate=cost(2 * frames * 1536 * 512, 12 * MIB),
        name=f"norm_backward_{row}",
    )(meta, x, low, high, pre, table, table, xc, rc, *closing)


def conv_body(meta, cg_ref, before_ref, after_ref, near_ref, cross_ref, resg_ref, last_ref, *rest, row, tiles, utts):
    out_ref, cs, vecs = rest[-3:]
    tile = pl.program_id(0)
    channels = cg_ref.shape[1]
    core = meta[0, 2 * utts + 2]
    base = meta[row, 2 * utts + 1] + tile * TILE

    @pl.when(tile == 0)
    def _():
        vecs[...] = last_ref[...].astype(F32)

    for c in range(channels // LANE):
        cut = slice(c * LANE, (c + 1) * LANE)
        cs[c, EDGE : EDGE + TILE, :] = cg_ref[:, cut].astype(F32)
        near, cross = near_ref[8 + 8 * row : 16 + 8 * row, cut], cross_ref[8 + 8 * row : 16 + 8 * row, cut]
        before, after = before_ref[:, cut].astype(F32)[EDGE - 8 :], after_ref[:, cut].astype(F32)[:8]
        cs[c, EDGE - 8 : EDGE, :] = jnp.where(tile == 0, jnp.where(core == 0, cross, near), before)
        after = jnp.where(tile == tiles - 1, jnp.where(core == 0, near, cross), after)
        cs[c, EDGE + TILE : EDGE + TILE + 8, :] = after
    for at, size in spans(TILE, 32):
        span = slice(at, at + size)
        reach, left = frame_reach(meta, row, base + at, size, utts)
        for c in range(channels // LANE):
            cut = slice(c * LANE, (c + 1) * LANE)
            total = resg_ref[span, cut].astype(F32)
            for k in range(KW):
                offset = RIM - k
                moved = cs[c, EDGE + offset + at : EDGE + offset + at + size, :]
                total = total + keep_within(moved, reach, left, offset) * vecs[2 + k : 3 + k, cut]
            out_ref[0, span, cut] = total


def conv_backward(row, before, meta, cg, near, cross, resg, table, rows, utts):
    frames, channels = cg.shape
    tiles = frames // TILE
    per = TILE // EDGE
    more = [] if before is None else [before]
    return pl.pallas_call(
        functools.partial(conv_body, row=row, tiles=tiles, utts=utts),
        grid=(tiles,),
        in_specs=[
            SCALARS,
            pl.BlockSpec((TILE, channels), lambda i: (i, 0)),
            pl.BlockSpec((EDGE, channels), lambda i: (jnp.maximum(i * per - 1, 0), 0)),
            pl.BlockSpec((EDGE, channels), lambda i: (jnp.minimum((i + 1) * per, tiles * per - 1), 0)),
            WHOLE,
            WHOLE,
            pl.BlockSpec((TILE, channels), lambda i: (row * tiles + i, 0)),
            pl.BlockSpec((BR, channels), lambda i: (NB - 1, 0)),
        ]
        + [ANYWHERE] * len(more),
        out_specs=pl.BlockSpec((1, TILE, channels), lambda i: (row, i, 0)),
        out_shape=shape_of((rows, frames, channels), F32),
        input_output_aliases={8: 0} if more else {},
        scratch_shapes=[
            pltpu.VMEM((channels // LANE, TILE + 2 * EDGE, LANE), F32),
            pltpu.VMEM((BR, channels), F32),
        ],
        compiler_params=params(),
        cost_estimate=cost(16 * frames * 512, 6 * MIB),
        name=f"conv_backward_{row}",
    )(meta, cg, cg, cg, near, cross, resg, table, *more)


def wave_body(meta, spec_ref, prev_ref, halo_ref, synth_ref, win_ref, *rest, start, rows, utts):
    out_ref, spec_all, held_all, done_all = rest[-4:]
    tile = start + pl.program_id(0)
    lane = lax.broadcasted_iota(jnp.int32, (TILE // 2, LANE), 1)
    front = lane < LANE // 2
    for r in range(rows):
        spec, held, done = spec_all.at[r], held_all.at[r], done_all.at[r]
        base = meta[r, 2 * utts + 1] + tile * TILE
        spec[EDGE:, :] = spec_ref[r]
        spec[0:EDGE, :] = jnp.where(tile == 0, halo_ref[r], prev_ref[r])
        for parity in range(2):
            half = slice(parity * BIN_PAD, (parity + 1) * BIN_PAD)
            piece = dot(spec[:, half], synth_ref[parity], NN)
            for c in range(BIN_PAD // LANE):
                held[parity, c] = piece[:, c * LANE : (c + 1) * LANE]
        for at, size in spans(TILE, 32):
            reach, _ = frame_reach(meta, r, base + at, size, utts)
            for c in range(3):
                cut = slice(c * LANE, (c + 1) * LANE)
                total = None
                for j in range(LAPS):
                    rows_at = slice(EDGE + at - j, EDGE + at - j + size)
                    of = (j % 2) * 3 + c
                    one, two = held[0, of, rows_at, :], held[1, of, rows_at, :]
                    piece = (one + two if j < 2 else one - two) * win_ref[j : j + 1, cut]
                    total = piece if j == 0 else total + jnp.where(reach >= j, piece, 0.0)
                done[c, at : at + size, :] = total * over(win_ref, LAPS, reach, c)
        even = [done[c, pl.ds(0, TILE // 2, stride=2), :] for c in range(3)]
        odd = [pltpu.roll(done[c, pl.ds(1, TILE // 2, stride=2), :], LANE // 2, 1) for c in range(3)]
        part = (
            even[0],
            even[1],
            jnp.where(front, even[2], odd[0]),
            jnp.where(front, odd[0], odd[1]),
            jnp.where(front, odd[1], odd[2]),
        )
        for k in range(PAIR):
            out_ref[pl.ds(2 * k + r, TILE // 2, stride=2 * PAIR), :] = part[k]


def wave_forward(start, stop, before, meta, spec, halo, synth, win, utts):
    rows, frames, _ = spec.shape
    tiles = frames // TILE
    per = TILE // EDGE
    more = [] if before is None else [before]
    return pl.pallas_call(
        functools.partial(wave_body, start=start, rows=rows, utts=utts),
        grid=(stop - start,),
        in_specs=[
            SCALARS,
            pl.BlockSpec((rows, TILE, 2 * BIN_PAD), lambda i: (0, start + i, 0)),
            pl.BlockSpec((rows, EDGE, 2 * BIN_PAD), lambda i: (0, jnp.maximum((start + i) * per - 1, 0), 0)),
            WHOLE,
            WHOLE,
            WHOLE,
        ]
        + [ANYWHERE] * len(more),
        out_specs=pl.BlockSpec((PAIR * TILE, LANE), lambda i: (start + i, 0)),
        out_shape=shape_of((PAIR * TILE * tiles, LANE), F32),
        input_output_aliases={6: 0} if more else {},
        scratch_shapes=[
            pltpu.VMEM((rows, TILE + EDGE, 2 * BIN_PAD), BF16),
            pltpu.VMEM((rows, 2, BIN_PAD // LANE, TILE + EDGE, LANE), F32),
            pltpu.VMEM((rows, LAP_PAD // LANE, TILE, LANE), F32),
        ],
        compiler_params=params(),
        cost_estimate=cost(4 * rows * (stop - start) * TILE * 768 * 768, 10 * MIB),
        name=f"wave_forward_{start}",
    )(meta, spec, spec, halo, synth, win, *more)


def slot_body(slot_of, *refs, groups, lasts, copies, slots):
    count = max(g[0] for g in groups) + 1
    keeps, cames, last_refs = refs[:count], refs[count : 2 * count], refs[2 * count : 2 * count + lasts]
    out, *more = refs[2 * count + lasts :]
    for index, offset, start, stop in groups:

        def one(b, carry, keep=keeps[index], came=cames[index], offset=offset, start=start):
            value = keep[offset + b].astype(F32) + came[offset + b].astype(F32)
            out[slot_of[0, start + b]] = value.astype(BF16)
            return carry

        lax.fori_loop(0, stop - start, one, 0, unroll=8)
    total = last_refs[0][0:QUART, :]
    for ref in last_refs[1:]:
        total = total + ref[0:QUART, :]
    out[slot_of[0, NB - 1]] = total.astype(BF16)
    for ref, at in zip(more, copies):
        ref[...] = out[at * slots : (at + 1) * slots]


def to_slots(slot_of, keeps, cames, lasts, groups, owners, slots, copies):
    channels = keeps[0].shape[2]
    return pl.pallas_call(
        functools.partial(slot_body, groups=groups, lasts=len(lasts), copies=copies, slots=slots),
        in_specs=[SCALARS] + [WHOLE] * (2 * len(keeps) + len(lasts)),
        out_specs=[WHOLE] * (1 + len(copies)),
        out_shape=[shape_of((owners * slots, QUART, channels), BF16)]
        + [shape_of((slots, QUART, channels), BF16)] * len(copies),
        compiler_params=params(),
        cost_estimate=cost(0, 6 * MIB),
        name="to_slots",
    )(slot_of, *keeps, *cames, *lasts)


def adam_body(places, meta, mine_ref, other_ref, master, first, second, *rest, block):
    out_master, out_first, out_second = rest[-3:]
    one_fix = 1.0 / (1.0 - BETA_ONE**STEP_COUNT)
    two_fix = 1.0 / (1.0 - BETA_TWO**STEP_COUNT)
    core = meta[0, meta.shape[1] - 2]
    for s in range(block):
        bucket = places[0, pl.program_id(0) * block + s]
        mine, other = mine_ref[s].astype(F32), other_ref[s].astype(F32)
        for half in range(2):
            grad = jnp.where(bucket < NB, jnp.where(core == half, mine, other), 0.0)
            old = master[s, half, 0]
            one = BETA_ONE * first[s, half, 0] + (1.0 - BETA_ONE) * grad
            two = BETA_TWO * second[s, half, 0] + (1.0 - BETA_TWO) * grad * grad
            out_first[s, half, 0] = one
            out_second[s, half, 0] = two
            step = one * one_fix / (jnp.sqrt(two * two_fix) + ADAM_EPS)
            out_master[s, half, 0] = old - LEARN_RATE * (step + WEIGHT_DECAY * old)


def adam(places, meta, mine, other, master, first, second, before):
    slots, depth, channels = master.shape
    block = max(b for b in range(1, ADAM_BLOCK + 1) if slots % b == 0)
    plane_at = meta.shape[1] - 1
    cut = lambda v: v.reshape(slots, 2, 2, QUART, channels)
    def at_plane(i, places, meta):
        plane = meta[0, plane_at]
        return i, 0, 1 - plane if before else plane, 0, 0

    full = pl.BlockSpec((block, 2, 1, QUART, channels), at_plane)
    part = pl.BlockSpec((block, QUART, channels), lambda i, places, meta: (i, 0, 0))
    more = [cut(v) for v in before]
    outs = pl.pallas_call(
        functools.partial(adam_body, block=block),
        grid_spec=pltpu.PrefetchScalarGridSpec(
            num_scalar_prefetch=2,
            grid=(slots // block,),
            in_specs=[part] * 2 + [full] * 3 + [ANYWHERE] * len(more),
            out_specs=[full] * 3,
        ),
        out_shape=[shape_of((slots, 2, 2, QUART, channels), F32)] * 3,
        input_output_aliases={7 + v: v for v in range(len(more))},
        compiler_params=params(),
        cost_estimate=cost(0, 6 * MIB),
        name="adam_second" if more else "adam_first",
    )(places, meta, mine, other, cut(master), cut(first), cut(second), *more)
    return [v.reshape(slots, depth, channels) for v in outs]


def tie(*values):
    return lax.optimization_barrier(values)


def plus(*values):
    return sum([v.astype(F32) for v in values]).astype(BF16)


def local(frames_in, lengths, bw_ids, owner_list, master, moment1, moment2, wave_grad):
    rows, frames, channels = frames_in.shape
    slots = master.shape[0]
    utts = lengths.shape[1]
    owners = lax.axis_size("rows")
    seqs = lax.axis_size("seq")
    row_at = lax.axis_index("rows")
    seq_at = lax.axis_index("seq")
    core, plane = seq_at % 2, seq_at // 2
    ring = ring_of(owners)
    half_ring = owners // 2

    mine = lax.dynamic_slice_in_dim(master, core * HALF, HALF, axis=1).astype(BF16)

    lines = wave_grad.reshape(rows, frames * HOP // LANE, LANE).transpose(1, 0, 2).reshape(-1, LANE)
    order = jnp.asarray(order_table())
    synth = jnp.asarray(synthesis_table())
    win = jnp.asarray(window_tables())

    low = shifted(frames_in[:, frames - EDGE :], 1)
    high = shifted(frames_in[:, :EDGE], -1)
    later = shifted(lines[: PAIR * EDGE], -1)
    offsets = [0]
    for hop in range(1, half_ring):
        offsets += [-hop, hop]
    offsets.append(-half_ring)
    names = np.arange(owners, dtype=np.int32)
    ids = jnp.stack([row_at, seq_at]).astype(jnp.int32)
    meta, places, held, slot_of, counts = plan(
        ids,
        lengths,
        bw_ids,
        owner_list,
        jnp.asarray(ring if ring else names, jnp.int32),
        jnp.asarray(offsets if ring else names, jnp.int32),
        slots,
        frames,
        bool(ring),
    )

    cot = None
    tiles = frames // TILE
    if ring:
        ahead = back = mine
        arrived = [mine, seq_swap(mine, 1)]
        for hop in range(half_ring):
            source = (ahead, back)
            ahead = lax.ppermute(ahead, AXES, ring_step(ring, 1, seqs))
            if hop < half_ring - 1:
                back = lax.ppermute(back, AXES, ring_step(ring, -1, seqs))
            if hop == 0:
                ahead, back, low, high, later, meta = tie(ahead, back, low, high, later, meta)
            if hop in (1, 2):
                feed = tie(lines, *source)[0]
                begin, end = ((0, tiles // 2), (tiles // 2, tiles))[hop - 1]
                cot = spectrum_cotangent(begin, end, cot, meta, feed, later, synth, win, rows, utts)
                ahead, back, cot = tie(ahead, back, cot)
            if hop == half_ring - 1:
                fed = tie(places, *source)[0]
                partial_table = assemble(tuple(range(owners - 1)), meta, fed, counts, arrived, slots)
                ahead, partial_table = tie(ahead, partial_table)
            else:
                arrived += [ahead, seq_swap(ahead, 1), back, seq_swap(back, 1)]
        arrived = [ahead, seq_swap(ahead, 1)]
        owned = (owners - 1,)
        part_places, part_counts, part_slots = places, counts, slots
    else:
        gathered = lax.all_gather(mine, "rows", axis=0, tiled=True)
        arrived = [gathered, seq_swap(gathered, 1)]
        owned = (0,)
        arrived = [take_slots(slot_of, a) for a in arrived]
        part_places = jnp.arange(NB, dtype=jnp.int32)[None, :]
        part_counts, part_slots = jnp.full((1, 1), NB, jnp.int32), NB
        partial_table = jnp.zeros((NB * BR, channels), BF16)
        cot = spectrum_cotangent(0, tiles, cot, meta, lines, later, synth, win, rows, utts)

    (table, spec, act, der, ada, low_grad, resg, xc, rc, send, keep, tail, sums, hsum) = forward(
        owned, part_slots, meta, part_places, part_counts, frames_in, low, high, order, cot, arrived, partial_table, utts
    )
    halo = shifted(spec[:, frames - EDGE :], 1)

    keeps, cames, groups = [], [], []

    def split(keep, came):
        both = plus(keep, came)
        stay = lax.dynamic_slice_in_dim(both, plane * QUART, QUART, axis=1)
        leave = lax.dynamic_slice_in_dim(both, (1 - plane) * QUART, QUART, axis=1)
        return stay, leave

    def record(stay, came, begins, per):
        for at, begin in enumerate(begins):
            groups.append((len(keeps), at * per, begin, begin + per))
        keeps.append(stay)
        cames.append(came)

    per = CHUNK // BR
    pre, bsums = None, []
    begins, count = (2 * FF // BR,), 40
    waiting = []
    for chunk in range(FF // CHUNK):
        near = seq_swap(send, 1)
        pre, next_send, next_keep, bsum = mlp_backward(chunk, pre, meta, low_grad, act, der, ada, table, utts)
        near, pre, next_send, next_keep = tie(near, pre, next_send, next_keep)
        bsums.append(bsum)
        stay, leave = split(keep, near)
        waiting.append((stay, seq_swap(leave, 2), begins, count))
        send, keep = next_send, next_keep
        begins, count = (chunk * per, FF // BR + chunk * per), per

    near = seq_swap(send, 1)
    for stay, came, *where_from in waiting[:-1]:
        pre, came = tie(pre, came)
        record(stay, came, *where_from)
    cg0, edge0, parts = norm_backward(0, (), meta, frames_in, low, high, pre, table, xc, rc, utts)
    kept, came, *where_from = waiting[-1]
    near, cg0, edge0, parts, pre, came = tie(near, cg0, edge0, parts, pre, came)
    record(kept, came, *where_from)
    stay, leave = split(keep, near)
    came = seq_swap(leave, 2)
    closing = (parts, edge0, tail, sums, hsum, *bsums, order)
    cg1, _, _, own, to_near, to_far, to_cross = norm_backward(
        1, closing, meta, frames_in, low, high, pre, table, xc, rc, utts
    )
    lasts = (own, seq_swap(to_near, 1), seq_swap(to_far, 2), seq_swap(to_cross, 3))
    came, spec, *lasts = tie(came, spec, *lasts)
    record(stay, came, begins, count)
    first_sent = (owners - 1, owners - 3) if ring else ()
    chunks, *sent = to_slots(slot_of, keeps, cames, lasts, tuple(groups), owners, slots, first_sent)

    state = {}

    def work(stage, *ready):
        if stage in (0, 2):
            feed = tie(spec, *ready)[0]
            begin, end, before = ((0, tiles // 2, None), (tiles // 2, tiles, state.get("wave")))[stage // 2]
            state["wave"] = wave_forward(begin, end, before, meta, feed, halo, synth, win, utts)
            return "wave"
        if stage in (1, 3):
            row = stage // 2
            feed = tie((cg0, cg1)[row], *ready)[0]
            state["grad"] = conv_backward(
                row, state.get("grad"), meta, feed, lasts[1], lasts[3], resg, table, rows, utts
            )
            return "grad"

    if ring:
        cut = {o: chunks[i * slots : (i + 1) * slots] for i, o in enumerate(offsets)}
        up, down = sent
        for hop in range(half_ring):
            left_over = half_ring - 1 - hop
            source = (up, down)
            up = lax.ppermute(up, AXES, ring_step(ring, 1, seqs))
            if hop < half_ring - 1:
                down = lax.ppermute(down, AXES, ring_step(ring, -1, seqs))
            done = work(hop, *source)
            up, down, state[done] = tie(up, down, state[done])
            if left_over:
                up = plus(up, cut[left_over])
                if hop < half_ring - 2:
                    down = plus(down, cut[1 - left_over])
        own = plus(cut[0], up, down)
    else:
        own = lax.psum_scatter(chunks, "rows", scatter_dimension=0, tiled=True)
        for hop in range(4):
            work(hop, own)
    near, far = seq_swap(own, 1), seq_swap(own, 2)
    cross = seq_swap(far, 1)
    waveform = state["wave"].reshape(-1, rows, LANE).transpose(1, 0, 2).reshape(rows, frames * HOP)

    first = adam(held, meta, own, near, master, moment1, moment2, ())
    cross, *first = tie(cross, *first)
    new_master, new_first, new_second = adam(held, meta, far, cross, master, moment1, moment2, first)
    return waveform, state["grad"], new_master, new_first, new_second


def solution(mesh):
    in_specs = (
        P("rows", "seq", None),
        P("rows", None),
        P("rows", None),
        P(),
        P("rows", None, None),
        P("rows", None, None),
        P("rows", None, None),
        P("rows", "seq"),
    )
    out_specs = (
        P("rows", "seq"),
        P("rows", "seq", None),
        P("rows", None, None),
        P("rows", None, None),
        P("rows", None, None),
    )
    return jax.shard_map(local, mesh=mesh, in_specs=in_specs, out_specs=out_specs, check_vma=False)
```

```python
import functools
import math

import jax
import jax.numpy as jnp
import numpy as np
from jax import lax
from jax.experimental import pallas as pl
from jax.experimental.pallas import tpu as pltpu
from jax.sharding import PartitionSpec as P

FF = 1536
NFFT = 1280
HOP = 320
NBW = 4
KW = 7
UTT = 4
BR = 32
STEP_COUNT = 6
BINS = 641
NOUT = 1282
VROWS = 20
IN_ROWS = 3
HEAD_ROWS = 3
NB = 137

NORM_EPS = 1e-06
ENV_FLOOR = 0.5
BETA_ONE = 0.8
BETA_TWO = 0.9
LEARN_RATE = 0.04
WEIGHT_DECAY = 0.01
ADAM_EPS = 1e-08

LAPS = NFFT // HOP
RIM = (KW - 1) // 2
LAP_PAD = 384
BIN_PAD = 768
HALF = BR // 2
QUART = BR // 4
EDGE = 16
TILE = 256
CHUNK = 768
HALF_BIN = 384
PAIR = 5
ADAM_BLOCK = 27
LANE = 128
AXES = ("rows", "seq")

F32 = jnp.float32
BF16 = jnp.bfloat16
MIB = 1 << 20
VMEM_BYTES = 60 * MIB


def bin_order():
    order = np.full(BIN_PAD, -1)
    order[: (BINS + 1) // 2] = np.arange(0, BINS, 2)
    order[HALF_BIN : HALF_BIN + BINS // 2] = np.arange(1, BINS, 2)
    return order


def order_table():
    return (np.arange(BIN_PAD)[:, None] == bin_order()[None, :]).astype(jnp.bfloat16)


def synthesis_table():
    n = np.arange(2 * HOP)[None, :]
    order = bin_order()
    out = np.zeros((2, 2, HALF_BIN, 2, LAP_PAD), np.float32)
    for parity in range(2):
        k = order[parity * HALF_BIN : (parity + 1) * HALF_BIN]
        k = k[k >= 0][:, None]
        angle = (k * n % NFFT) * (2.0 * math.pi / NFFT)
        factor = np.where((k == 0) | (k == NFFT // 2), 1.0, 2.0) / NFFT
        out[parity, 0, : len(k), :, :HOP] = (factor * np.cos(angle)).reshape(-1, 2, HOP)
        out[parity, 1, : len(k), :, :HOP] = (-factor * np.sin(angle)).reshape(-1, 2, HOP)
    return out.reshape(2, BIN_PAD, 2 * LAP_PAD).astype(jnp.bfloat16)


def window_tables():
    window = 0.5 - 0.5 * np.cos(np.arange(NFFT) * (2.0 * math.pi / NFFT))
    rows = np.zeros((LAPS, LAP_PAD), np.float64)
    rows[:, :HOP] = window.reshape(LAPS, HOP)
    envelope = np.cumsum(rows**2, axis=0)
    return np.concatenate([rows, 1.0 / np.maximum(envelope, ENV_FLOOR)], axis=0).astype(np.float32)


def ring_of(count):
    if count != 8:
        return None
    return [0, 2, 4, 6, 7, 5, 3, 1]


def ring_step(ring, shift, seq_count):
    where = {r: i for i, r in enumerate(ring)}
    pairs = []
    for r in ring:
        target = ring[(where[r] + shift) % len(ring)]
        pairs += [(r * seq_count + s, target * seq_count + s) for s in range(seq_count)]
    return pairs


def seq_swap(value, bit):
    count = lax.axis_size("seq")
    return lax.ppermute(value, "seq", [(s, s ^ bit) for s in range(count)])


def rows_swap(value, bit):
    count = lax.axis_size("rows")
    return lax.ppermute(value, "rows", [(r, r ^ bit) for r in range(count)])


def shifted(value, distance):
    devices = range(lax.axis_size("seq"))
    return lax.ppermute(
        value, "seq", [(i - distance, i) for i in devices if i - distance in devices]
    )


def dot(a, b, dims):
    return lax.dot_general(a, b, (dims, ((), ())), preferred_element_type=F32)


NN = ((1,), (0,))
NT = ((1,), (1,))
TN = ((0,), (0,))


def frame_reach(meta, row, first, count, utts):
    index = first + lax.broadcasted_iota(jnp.int32, (count, 128), 0)
    start = jnp.zeros_like(index)
    end = jnp.zeros_like(index) + meta[row, 1]
    for u in range(1, utts):
        inside = index >= meta[row, u]
        start = jnp.where(inside, meta[row, u], start)
        end = jnp.where(inside, meta[row, u + 1], end)
    return index - start, end - 1 - index


def spans(count, size):
    return [(at, min(size, count - at)) for at in range(0, count, size)]


def over(table, base, reach, lane_tile, width=LANE):
    cut = slice(lane_tile * LANE, lane_tile * LANE + width)
    picked = jnp.broadcast_to(table[base + LAPS - 1 : base + LAPS, cut], (reach.shape[0], width))
    for j in range(LAPS - 2, -1, -1):
        picked = jnp.where(reach[:, :width] == j, table[base + j : base + j + 1, cut], picked)
    return picked


def keep_within(values, reach, left, offset):
    if offset < 0:
        return jnp.where(reach >= -offset, values, 0.0)
    if offset > 0:
        return jnp.where(left >= offset, values, 0.0)
    return values


def row_mean(values):
    return jnp.mean(values, axis=1, keepdims=True)


def fold(values):
    rows, columns = values.shape
    return jnp.sum(values.reshape(rows // 8, 8, columns), axis=0)


def sincos(angle):
    turns = jnp.round(angle * (0.5 / math.pi))
    rest = angle * 0.5 - turns * 3.1416015625
    rest = rest + turns * 8.908910206761537e-06
    sq = rest * rest
    sine = 1.0 + sq * (
        -0.16666656732559204
        + sq * (0.008333033882081509 + sq * (-0.00019807791977655143 + sq * 2.6022808015113696e-06))
    )
    cosine = 1.0 + sq * (
        -0.4999992549419403
        + sq * (0.04166382923722267 + sq * (-0.001385461655445397 + sq * 2.3163083824329078e-05))
    )
    sine = rest * sine
    double = sine + sine
    return double * cosine, 1.0 - double * sine


ANGLE_LIMIT = 1024.0


def params():
    return pltpu.CompilerParams(vmem_limit_bytes=VMEM_BYTES)


def cost(flops, bytes_accessed, transcendentals=0):
    return pl.CostEstimate(
        flops=int(flops), bytes_accessed=int(bytes_accessed), transcendentals=int(transcendentals)
    )


WHOLE = pl.BlockSpec(memory_space=pltpu.VMEM)
SCALARS = pl.BlockSpec(memory_space=pltpu.SMEM)
ANYWHERE = pl.BlockSpec(memory_space=pl.ANY)
shape_of = jax.ShapeDtypeStruct


def plan_body(ids, lengths, bw_ids, owner_list, order, offsets, meta, places, held, slot_of, counts, rel, *, frames, ring):
    rows, utts = lengths.shape
    owners, slots = order.shape[0], held.shape[1]
    row_at, seq_at = ids[0], ids[1]
    for r in range(rows):
        start = jnp.int32(0)
        meta[r, 0] = start
        for u in range(utts):
            start = start + lengths[r, u]
            meta[r, u + 1] = start
            meta[r, utts + 1 + u] = bw_ids[r, u]
        meta[r, 2 * utts + 1] = seq_at * frames
        meta[r, 2 * utts + 2] = lax.rem(seq_at, 2)
        meta[r, 2 * utts + 3] = lax.div(seq_at, 2)
    where = jnp.int32(0)
    if ring:
        for i in range(owners):
            where = jnp.where(order[i] == row_at, i, where)

    def name(i, carry):
        rel[order[lax.rem(where + offsets[i] + owners, owners)]] = i
        counts[0, i] = 0
        return carry

    def clear(i, carry):
        places[0, i] = NB
        return carry

    def place(b, carry):
        i = rel[owner_list[b]]
        n = counts[0, i]
        counts[0, i] = n + 1
        places[0, i * slots + n] = b
        slot_of[0, b] = i * slots + n
        return carry

    lax.fori_loop(0, owners, name, 0)
    lax.fori_loop(0, owners * slots, clear, 0, unroll=8)
    lax.fori_loop(0, NB, place, 0)
    own = rel[row_at]

    def keep(n, carry):
        held[0, n] = places[0, own * slots + n]
        return carry

    lax.fori_loop(0, slots, keep, 0)


def plan(ids, lengths, bw_ids, owner_list, order, offsets, slots, frames, ring):
    rows, utts = lengths.shape
    owners = order.shape[0]
    shapes = ((rows, 2 * utts + 4), (1, owners * slots), (1, slots), (1, NB), (1, owners))
    return pl.pallas_call(
        functools.partial(plan_body, frames=frames, ring=ring),
        in_specs=[SCALARS] * 6,
        out_specs=[SCALARS] * 5,
        out_shape=[shape_of(shape, jnp.int32) for shape in shapes],
        scratch_shapes=[pltpu.SMEM((owners,), jnp.int32)],
        compiler_params=params(),
        cost_estimate=cost(8000, 8 * 1024),
        name="plan",
    )(ids, lengths, bw_ids, owner_list, order, offsets)


def pre_body(meta, wave_ref, halo_ref, synth_ref, win_ref, *rest, start, tiles, rows, utts):
    out_ref, flat, scaled_all, even_all, odd_all = rest[-5:]
    step = pl.program_id(0)
    tile = start + step
    lines = PAIR * TILE
    extra = PAIR * EDGE
    count = TILE + EDGE
    lane = lax.broadcasted_iota(jnp.int32, (count // 2, LANE), 1)
    for at, size in spans(lines, 320):
        rows_at = pl.ds(pl.multiple_of(tile * lines + at, 16), size)
        flat[at : at + size, :] = wave_ref[rows_at, :].astype(F32)
    after = jnp.minimum((tile + 1) * lines, tiles * lines - extra)
    following = wave_ref[pl.ds(pl.multiple_of(after, 16), extra), :]
    flat[lines:, :] = jnp.where(tile == tiles - 1, halo_ref[...], following).astype(F32)
    for r in range(rows):
        scaled, even, odd = scaled_all.at[r], even_all.at[r], odd_all.at[r]
        base = meta[r, 2 * utts + 1] + tile * TILE
        part = [flat[pl.ds(2 * k + r, count // 2, stride=2 * PAIR), :] for k in range(PAIR)]
        turned = [pltpu.roll(v, LANE // 2, 1) for v in part[2:]]
        front = lane < LANE // 2
        frame = (
            part[0],
            part[1],
            jnp.where(front, part[2], 0.0),
            jnp.where(front, turned[0], turned[1]),
            jnp.where(front, turned[1], turned[2]),
            jnp.where(front, turned[2], 0.0),
        )
        for c in range(3):
            scaled[c, pl.ds(0, count // 2, stride=2), :] = frame[c]
            scaled[c, pl.ds(1, count // 2, stride=2), :] = frame[3 + c]
        for at, size in spans(count, 32):
            reach, _ = frame_reach(meta, r, base + at, size, utts)
            for c in range(3):
                scaled[c, at : at + size, :] = scaled[c, at : at + size, :] * over(win_ref, LAPS, reach, c)
        for at, size in spans(TILE, 32):
            _, left = frame_reach(meta, r, base + at, size, utts)
            for j in range(2):
                for c in range(3):
                    span = slice(c * LANE, (c + 1) * LANE)

                    def lap(i):
                        value = scaled[c, at + i : at + i + size, :] * win_ref[i : i + 1, span]
                        return keep_within(value, None, left, i).astype(BF16).astype(F32)

                    one, two = lap(j), lap(j + 2)
                    column = slice(j * LAP_PAD + c * LANE, j * LAP_PAD + (c + 1) * LANE)
                    even[at : at + size, column] = (one + two).astype(BF16)
                    odd[at : at + size, column] = (one - two).astype(BF16)
        out_ref[r, :, 0:BIN_PAD] = dot(even[...], synth_ref[0], NT).astype(BF16)
        out_ref[r, :, BIN_PAD:] = dot(odd[...], synth_ref[1], NT).astype(BF16)


def spectrum_cotangent(start, stop, before, meta, wave, halo, synth, win, rows, utts):
    tiles = wave.shape[0] // (PAIR * TILE)
    frames = tiles * TILE
    more = [] if before is None else [before]
    steps = stop - start
    return pl.pallas_call(
        functools.partial(pre_body, start=start, tiles=tiles, rows=rows, utts=utts),
        grid=(steps,),
        in_specs=[SCALARS, WHOLE, WHOLE, WHOLE, WHOLE] + [ANYWHERE] * len(more),
        out_specs=pl.BlockSpec((rows, TILE, 2 * BIN_PAD), lambda i: (0, start + i, 0)),
        out_shape=shape_of((rows, frames, 2 * BIN_PAD), BF16),
        input_output_aliases={5: 0} if more else {},
        scratch_shapes=[
            pltpu.VMEM((PAIR * (TILE + EDGE), LANE), F32),
            pltpu.VMEM((rows, LAP_PAD // LANE, TILE + EDGE, LANE), F32),
            pltpu.VMEM((rows, TILE, BIN_PAD), BF16),
            pltpu.VMEM((rows, TILE, BIN_PAD), BF16),
        ],
        compiler_params=params(),
        cost_estimate=cost(4 * rows * steps * TILE * 768 * 768, rows * steps * TILE * 3072 + 4 * MIB),
        name=f"spectrum_cotangent_{start}",
    )(meta, wave, halo, synth, win, *more)


def place_parts(places, counts, core, pieces, table, sem, slots, owners, start):
    done = {}
    for index, ref in enumerate(pieces):
        side = core if index % 2 == 0 else 1 - core
        owner = owners[index // 2]
        first = done.get((owner, index % 2), 0)
        done[owner, index % 2] = first + ref.shape[0]

        def one(s, carry, ref=ref, side=side, owner=owner, first=first):
            bucket = places[0, owner * slots + first + s]
            at = pl.multiple_of(bucket * BR + side * HALF, HALF)
            copy = pltpu.make_async_copy(ref.at[s], table.at[pl.ds(at, HALF), :], sem)
            if start:
                copy.start()
            else:
                copy.wait()
            return carry

        held = jnp.clip(counts[0, owner] - first, 0, ref.shape[0])
        lax.fori_loop(0, held, one, 0)


def assemble_body(meta, places, counts, *refs, slots, owners):
    pieces, table, sem = refs[: 2 * len(owners)], refs[-2], refs[-1]
    core = meta[0, meta.shape[1] - 2]
    place_parts(places, counts, core, pieces, table, sem, slots, owners, True)
    place_parts(places, counts, core, pieces, table, sem, slots, owners, False)


def assemble(owners, meta, places, counts, pieces, slots):
    channels = pieces[0].shape[2]
    return pl.pallas_call(
        functools.partial(assemble_body, slots=slots, owners=owners),
        in_specs=[SCALARS, SCALARS, SCALARS] + [ANYWHERE] * len(pieces),
        out_specs=WHOLE,
        out_shape=shape_of((NB * BR, channels), BF16),
        scratch_shapes=[pltpu.SemaphoreType.DMA],
        compiler_params=params(),
        cost_estimate=cost(0, 12 * MIB),
        name="assemble",
    )(meta, places, counts, *pieces)


def take_body(slot_of, ref, out, sem):
    def copy(b):
        return pltpu.make_async_copy(ref.at[slot_of[0, b]], out.at[b], sem)

    def start(b, carry):
        copy(b).start()
        return carry

    def wait(b, carry):
        copy(b).wait()
        return carry

    lax.fori_loop(0, NB, start, 0)
    lax.fori_loop(0, NB, wait, 0)


def take_slots(slot_of, gathered):
    return pl.pallas_call(
        take_body,
        in_specs=[SCALARS, ANYWHERE],
        out_specs=WHOLE,
        out_shape=shape_of((NB, *gathered.shape[1:]), BF16),
        scratch_shapes=[pltpu.SemaphoreType.DMA],
        compiler_params=params(),
        cost_estimate=cost(0, 6 * MIB),
        name="take_slots",
    )(slot_of, gathered)


def fill_frames(xs, x_ref, low_ref, high_ref, row, tile, tiles, channels):
    first = pl.multiple_of(tile * TILE, TILE)

    def put(at, block):
        block = block.astype(F32)
        for c in range(channels // LANE):
            xs[c, at : at + block.shape[0], :] = block[:, c * LANE : (c + 1) * LANE]

    for at, size in spans(TILE, 64):
        put(EDGE + at, x_ref[row, pl.ds(pl.multiple_of(first + at, 64), size), :])

    before = x_ref[row, pl.ds(pl.multiple_of(jnp.maximum(first - EDGE, 0), EDGE), EDGE), :]
    put(0, jnp.where(tile == 0, low_ref[row], before))
    end = jnp.minimum(first + TILE, (tiles - 1) * TILE)
    after = x_ref[row, pl.ds(pl.multiple_of(end, EDGE), EDGE), :]
    put(EDGE + TILE, jnp.where(tile == tiles - 1, high_ref[row], after))


def by_utterance(meta, row, utts, index, rows_of):
    value = jnp.broadcast_to(rows_of(0), (index.shape[0], LANE))
    for u in range(1, utts):
        value = jnp.where(index >= meta[row, u], rows_of(u), value)
    return value


def pick_rows(meta, row, utts, vec, out, channels):
    for u in range(utts):
        wanted = meta[row, utts + 1 + u]
        for at, offset in ((u, KW + 1), (utts + u, KW + 1 + NBW)):
            value = vec(offset)
            for b in range(1, NBW):
                value = jnp.where(wanted == b, vec(offset + b), value)
            out[at : at + 1, :] = value


def interleave(ones, others):
    at = 0
    for i, one in enumerate(ones):
        one()
        until = (i + 1) * len(others) // len(ones)
        for other in others[at:until]:
            other()
        at = until
    for other in others[at:]:
        other()


def forward_body(meta, places, counts, x_ref, low_ref, high_ref, order_ref, cot_ref, *rest, owners, slots, tiles, count, utts):
    pieces = rest[: 2 * len(owners)]
    table_in = rest[2 * len(owners)]
    (
        table_out,
        spec_ref,
        act_ref,
        der_ref,
        ada_ref,
        lowg_ref,
        resg_ref,
        xc_ref,
        rc_ref,
        send_ref,
        keep_ref,
        tail_ref,
        sums_ref,
        bsum_ref,
        table,
        xs,
        w_head,
        b_head,
        vecs,
        picks,
        grad,
        lines,
        hg,
        hg_old,
        pre_ref,
        logs_ref,
        angle_ref,
        ngrad_ref,
        slim,
        xn_ref,
        normed,
        normed_old,
        branch_ref,
        rn_ref,
        slow,
        sem,
        sems,
    ) = rest[2 * len(owners) + 1 :]
    step = pl.program_id(0)
    core = meta[0, 2 * utts + 2]
    channels = x_ref.shape[2]
    lane_tiles = channels // LANE
    now = jnp.minimum(step, count - 1)
    row, tile = now // tiles, now % tiles
    vec = lambda v: vecs[2 + v : 3 + v, :]
    vec_at = KW + 1 + 2 * NBW
    head_at = 2 * FF

    def store():
        return pltpu.make_async_copy(table, table_out, sems.at[1])

    @pl.when(step == 0)
    def _():
        whole = pltpu.make_async_copy(table_in, table, sems.at[0])
        whole.start()
        normed[...] = jnp.zeros_like(normed)
        w_head[...] = jnp.zeros_like(w_head)
        b_head[...] = jnp.zeros_like(b_head)
        whole.wait()
        place_parts(places, counts, core, pieces, table, sem, slots, owners, True)
        place_parts(places, counts, core, pieces, table, sem, slots, owners, False)
        store().start()
        vecs[...] = table[head_at + 1280 : head_at + 1280 + BR, :].astype(F32)

    @pl.when(step == 1)
    def _():
        sums_ref[...] = jnp.zeros_like(sums_ref)
        bsum_ref[...] = jnp.zeros_like(bsum_ref)

    @pl.when(step == 2)
    def _():
        grad[...] = jnp.zeros_like(grad)

    @pl.when(tile == 0)
    def _():
        pick_rows(meta, row, utts, vec, picks, channels)

    base = meta[row, 2 * utts + 1] + tile * TILE
    fill_frames(xs, x_ref, low_ref, high_ref, row, tile, tiles, channels)

    def convolve(at, size):
        reach, left = frame_reach(meta, row, base + at, size, utts)
        index = base + at + lax.broadcasted_iota(jnp.int32, (size, LANE), 0)
        conv = []
        for c in range(lane_tiles):
            cut = slice(c * LANE, (c + 1) * LANE)
            total = vecs[2 + KW : 3 + KW, cut]
            for k in range(KW):
                offset = k - RIM
                moved = xs[c, EDGE + offset + at : EDGE + offset + at + size, :]
                total = total + keep_within(moved, reach, left, offset) * vecs[2 + k : 3 + k, cut]
            conv.append(total)
        mean = jnp.sum(sum(conv), axis=1, keepdims=True) * (1.0 / channels)
        conv = [v - mean for v in conv]
        square = jnp.sum(sum([v * v for v in conv]), axis=1, keepdims=True) * (1.0 / channels)
        rc = jnp.broadcast_to(lax.rsqrt(square + NORM_EPS), (size, LANE))
        rc_ref[at : at + size, :] = rc
        for c in range(lane_tiles):
            cut = slice(c * LANE, (c + 1) * LANE)
            xc = conv[c] * rc
            xc_ref[at : at + size, cut] = xc.astype(BF16)
            scale = by_utterance(meta, row, utts, index, lambda u: picks[u : u + 1, cut])
            shift = by_utterance(meta, row, utts, index, lambda u: picks[utts + u : utts + u + 1, cut])
            ada_ref[at : at + size, cut] = (xc * scale + shift).astype(BF16)

    def head(at, size, turn):
        span = slice(at, at + size)
        for c in range(0, BIN_PAD, LANE):
            bins, angles = slice(c, c + LANE), slice(BIN_PAD + c, BIN_PAD + c + LANE)
            parity, inner = c // HALF_BIN, c % HALF_BIN
            reals = slice(parity * BIN_PAD + inner, parity * BIN_PAD + inner + LANE)
            imags = slice(reals.start + HALF_BIN, reals.stop + HALF_BIN)
            angle = angle_ref[span, bins] + b_head[0:1, angles]
            scale = jnp.exp(logs_ref[span, bins] + b_head[0:1, bins])
            sine, cosine = turn(angle)
            real, imag = scale * cosine, scale * sine
            spec_ref[span, reals] = real.astype(BF16)
            spec_ref[span, imags] = imag.astype(BF16)
            dre = cot_ref[span, reals].astype(F32)
            dim = cot_ref[span, imags].astype(F32)
            hg[span, bins] = (dre * real + dim * imag).astype(BF16)
            hg[span, angles] = (dim * real - dre * imag).astype(BF16)

    def gelu(at, size, c):
        for d in range(c * 512, (c + 1) * 512, 256):
            cut = slice(d, d + 256)
            bias = vecs[2 + VROWS + c : 3 + VROWS + c, d - c * 512 : d - c * 512 + 256]
            pre = pre_ref[at : at + size, cut] + bias
            phi = 0.5 + 0.5 * lax.erf(pre * math.sqrt(0.5))
            bell = jnp.exp(-0.5 * pre * pre) * (1.0 / math.sqrt(2.0 * math.pi))
            act_ref[at : at + size, cut] = (pre * phi).astype(BF16)
            der_ref[at : at + size, cut] = (phi + pre * bell).astype(BF16)

    def second_norm(at, size):
        span = slice(at, at + size)
        branch = slim[span, :] + vec(vec_at)
        branch_ref[span, :] = branch
        x = jnp.concatenate([xs[c, EDGE + at : EDGE + at + size, :] for c in range(lane_tiles)], axis=1)
        residual = x + vec(vec_at + 1) * branch
        residual = residual - row_mean(residual)
        rn = lax.rsqrt(row_mean(residual * residual) + NORM_EPS)
        rn_ref[span, :] = jnp.broadcast_to(rn, (size, LANE))
        xn = residual * rn
        xn_ref[span, :] = xn
        normed[span, :] = (xn * vec(vec_at + 2) + vec(vec_at + 3)).astype(BF16)

    def second_norm_back(at, size, sums):
        span = slice(at, at + size)
        ngrad = ngrad_ref[span, :]
        xn = xn_ref[span, :]
        e = ngrad * vec(vec_at + 2)
        resg = rn_ref[span, 0:1] * (e - row_mean(e) - xn * row_mean(e * xn))
        resg_ref[span, :] = resg.astype(BF16)
        low = (vec(vec_at + 1) * resg).astype(BF16)
        lowg_ref[span, :] = low
        return (
            sums[0] + fold(low.astype(F32)),
            sums[1] + fold(resg * branch_ref[span, :]),
            sums[2] + fold(ngrad * xn),
            sums[3] + fold(ngrad),
        )

    def head_dots(ref, begin):
        def one(c):
            ref[:, c : c + 256] = dot(normed[...], w_head[begin + c : begin + c + 256, :], NT)

        return [functools.partial(one, c) for c in range(0, BIN_PAD, 256)]

    def hidden_dot(c):
        pre_ref[:, c : c + 256] = dot(ada_ref[...], table[c : c + 256, :], NT)

    def grad_dot(c):
        grad[c : c + 256, :] += dot(hg_old[:, c : c + 256], normed_old[...], TN)

    def ngrad_dot(c):
        ngrad_ref[:, c : c + 256] = dot(hg[...], w_head[:, c : c + 256], NN)

    def branch_dot(c):
        slim[:, c : c + 256] = dot(act_ref[...], table[FF : 2 * FF, c : c + 256], NN)

    def head_again():
        def again(i, carry):
            rows = pl.ds(pl.multiple_of(i * 32, 32), 32)
            for c in range(0, BIN_PAD, LANE):
                bins, angles = slice(c, c + LANE), slice(BIN_PAD + c, BIN_PAD + c + LANE)
                parity, inner = c // HALF_BIN, c % HALF_BIN
                reals = slice(parity * BIN_PAD + inner, parity * BIN_PAD + inner + LANE)
                imags = slice(reals.start + HALF_BIN, reals.stop + HALF_BIN)
                angle = angle_ref[rows, bins] + b_head[0:1, angles]
                scale = jnp.exp(logs_ref[rows, bins] + b_head[0:1, bins])
                real, imag = scale * jnp.cos(angle), scale * jnp.sin(angle)
                spec_ref[rows, reals] = real.astype(BF16)
                spec_ref[rows, imags] = imag.astype(BF16)
                dre = cot_ref[rows, reals].astype(F32)
                dim = cot_ref[rows, imags].astype(F32)
                hg[rows, bins] = (dre * real + dim * imag).astype(BF16)
                hg[rows, angles] = (dim * real - dre * imag).astype(BF16)
            return carry

        lax.fori_loop(0, TILE // 32, again, 0)

    def build_head():
        last = vecs[...]
        line = jnp.concatenate([last[25:26], last[26:27], last[27:28]], axis=1)
        line = jnp.broadcast_to(line, (16, 3 * channels))
        moved = pltpu.roll(line, 3 * channels - BINS, 1)
        both = jnp.concatenate([line[0:8, 0:BIN_PAD], moved[0:8, 0:BIN_PAD]], axis=0)
        picked = dot(both.astype(BF16), order_ref[...], NN)
        b_head[:, 0:BIN_PAD] = picked[0:8]
        b_head[:, BIN_PAD:] = picked[8:16]
        inside = lax.broadcasted_iota(jnp.int32, (336, LANE), 0)
        for c in range(lane_tiles):
            cut = slice(c * LANE, (c + 1) * LANE)
            lines[c, 0:1312, :] = table[head_at : head_at + 1312, cut].astype(F32)
            lines[c, 1312:, :] = jnp.zeros((lines.shape[1] - 1312, LANE), F32)
            for part, start in ((0, 0), (BIN_PAD, BINS)):
                evens = lines[c, pl.ds(start, 336, stride=2), :]
                w_head[part : part + 336, cut] = jnp.where(inside < (BINS + 1) // 2, evens, 0.0).astype(BF16)
                odds = lines[c, pl.ds(start + 1, 320, stride=2), :]
                w_head[part + HALF_BIN : part + HALF_BIN + 320, cut] = odds.astype(BF16)
        longest = jnp.zeros((8, 1), F32)
        for at, size in spans(BIN_PAD, 64):
            weights = w_head[BIN_PAD + at : BIN_PAD + at + size, :].astype(F32)
            length = jnp.sum(weights * weights, axis=1, keepdims=True)
            longest = jnp.maximum(longest, jnp.max(length.reshape(size // 8, 8, 1), axis=0))
        gain, shift = jnp.abs(vec(vec_at + 2)), vec(vec_at + 3)
        normed_length = math.sqrt(channels) * jnp.max(gain) + jnp.sqrt(jnp.sum(shift * shift, keepdims=True))[0, 0]
        bound = 1.05 * normed_length * jnp.max(jnp.sqrt(longest)) + jnp.max(jnp.abs(b_head[:, BIN_PAD:]))
        slow[0] = jnp.where(bound < ANGLE_LIMIT, 0, 1)

    def over_all(call, values):
        return [functools.partial(call, v) for v in values]

    def in_spans(call, size, *more):
        return [functools.partial(call, at, length, *more) for at, length in spans(TILE, size)]

    def work(first, second):
        interleave(
            head_dots(logs_ref, 0) + head_dots(angle_ref, BIN_PAD) if second else [],
            in_spans(convolve, 32) if first else [],
        )
        interleave(
            (over_all(hidden_dot, range(0, FF, 256)) if first else [])
            + (over_all(grad_dot, range(0, 2 * BIN_PAD, 256)) if second else []),
            in_spans(head, 16, sincos) if second else [],
        )
        if second:
            pl.when(slow[0] > 0)(head_again)
        interleave(
            over_all(ngrad_dot, range(0, channels, 256)) if second else [],
            [call for c in range(IN_ROWS) for call in in_spans(gelu, 32, c)] if first else [],
        )
        sums = [sums_ref[v] for v in range(4)]

        def back(at, size):
            sums[:] = second_norm_back(at, size, sums)

        interleave(
            over_all(branch_dot, range(0, channels, 256)) if first else [],
            in_spans(back, 16) if second else [],
        )
        if second:
            for v in range(4):
                sums_ref[v] = sums[v]
            for c in range(0, 2 * BIN_PAD, 512):
                total = bsum_ref[:, c : c + 512]
                for at, size in spans(TILE, 32):
                    total = total + fold(hg[at : at + size, c : c + 512].astype(F32))
                bsum_ref[:, c : c + 512] = total
            hg_old[...] = hg[...]
            normed_old[...] = normed[...]
        if first:
            interleave([], in_spans(second_norm, 16))

    @pl.when(step == 0)
    def _():
        work(True, False)
        build_head()

    @pl.when((step > 0) & (step < count))
    def _():
        work(True, True)

    @pl.when(step == count)
    def _():
        work(False, True)

    @pl.when(step == count)
    def _():
        for c in range(0, 2 * BIN_PAD, 256):
            grad_dot(c)
        for c in range(lane_tiles):
            cut = slice(c * LANE, (c + 1) * LANE)
            for part, start in ((0, 0), (BIN_PAD, BINS)):
                lines[c, pl.ds(start + 1, 320, stride=2), :] = grad[part + HALF_BIN : part + HALF_BIN + 320, cut]
                lines[c, pl.ds(start, 320, stride=2), :] = grad[part : part + 320, cut]
                lines[c, start + 640 : start + 641, :] = grad[part + 320 : part + 321, cut]
            for b in range(40):
                low_half = lines[c, b * BR : b * BR + HALF, :].astype(BF16)
                high_half = lines[c, b * BR + HALF : b * BR + BR, :].astype(BF16)
                keep_ref[b, :, cut] = jnp.where(core == 0, low_half, high_half)
                send_ref[b, :, cut] = jnp.where(core == 0, high_half, low_half)
            tail_ref[:, cut] = lines[c, 1280:1288, :]
        store().wait()


def forward(owners, slots, meta, places, counts, x, low, high, order, cot, pieces, table, utts):
    rows, frames, channels = x.shape
    tiles = frames // TILE
    steps = rows * tiles
    count = rows * frames
    ahead = lambda i: jnp.minimum(i, steps - 1)
    behind = lambda i: jnp.maximum(i - 1, 0)
    wide = pl.BlockSpec((TILE, FF), lambda i: (ahead(i), 0))
    wide_late = pl.BlockSpec((None, TILE, FF), lambda i: (behind(i) // tiles, behind(i) % tiles, 0))
    slim = pl.BlockSpec((TILE, channels), lambda i: (ahead(i), 0))
    slim_late = pl.BlockSpec((TILE, channels), lambda i: (behind(i), 0))
    return pl.pallas_call(
        functools.partial(forward_body, owners=owners, slots=slots, tiles=tiles, count=steps, utts=utts),
        grid=(steps + 1,),
        in_specs=[SCALARS, SCALARS, SCALARS, WHOLE, WHOLE, WHOLE, WHOLE, wide_late]
        + [ANYWHERE] * (len(pieces) + 1),
        out_specs=[ANYWHERE, wide_late, wide, wide, slim, slim_late, slim_late, slim]
        + [pl.BlockSpec((TILE, LANE), lambda i: (ahead(i), 0))]
        + [WHOLE] * 5,
        out_shape=[
            shape_of((NB * BR, channels), BF16),
            shape_of((rows, frames, 2 * BIN_PAD), BF16),
            shape_of((count, FF), BF16),
            shape_of((count, FF), BF16),
            shape_of((count, channels), BF16),
            shape_of((count, channels), BF16),
            shape_of((count, channels), BF16),
            shape_of((count, channels), BF16),
            shape_of((count, LANE), F32),
            shape_of((40, HALF, channels), BF16),
            shape_of((40, HALF, channels), BF16),
            shape_of((8, channels), F32),
            shape_of((4, 8, channels), F32),
            shape_of((8, 2 * BIN_PAD), F32),
        ],
        scratch_shapes=[
            pltpu.VMEM((NB * BR, channels), BF16),
            pltpu.VMEM((channels // LANE, TILE + 2 * EDGE, LANE), F32),
            pltpu.VMEM((2 * BIN_PAD, channels), BF16),
            pltpu.VMEM((8, 2 * BIN_PAD), F32),
            pltpu.VMEM((BR, channels), F32),
            pltpu.VMEM((2 * utts, channels), F32),
            pltpu.VMEM((2 * BIN_PAD, channels), F32),
            pltpu.VMEM((channels // LANE, 1344, LANE), F32),
            pltpu.VMEM((TILE, 2 * BIN_PAD), BF16),
            pltpu.VMEM((TILE, 2 * BIN_PAD), BF16),
            pltpu.VMEM((TILE, FF), F32),
            pltpu.VMEM((TILE, BIN_PAD), F32),
            pltpu.VMEM((TILE, BIN_PAD), F32),
            pltpu.VMEM((TILE, channels), F32),
            pltpu.VMEM((TILE, channels), F32),
            pltpu.VMEM((TILE, channels), F32),
            pltpu.VMEM((TILE, channels), BF16),
            pltpu.VMEM((TILE, channels), BF16),
            pltpu.VMEM((TILE, channels), F32),
            pltpu.VMEM((TILE, LANE), F32),
            pltpu.SMEM((1,), jnp.int32),
            pltpu.SemaphoreType.DMA,
            pltpu.SemaphoreType.DMA((2,)),
        ],
        compiler_params=params(),
        cost_estimate=cost(10 * count * 1536 * 512, 40 * MIB, count * 4096),
        name="forward",
    )(meta, places, counts, x, low, high, order, cot, *pieces, table)


def mlp_body(meta, low_ref, act_ref, der_ref, ada_ref, wout_ref, *rest, utts):
    pre_ref, send_ref, keep_ref, bsum_ref, gout, gin, agrad = rest[-7:]
    step = pl.program_id(0)
    core = meta[0, 2 * utts + 2]
    tile = low_ref.shape[0]

    @pl.when(step == 0)
    def _():
        gout[...] = jnp.zeros_like(gout)
        gin[...] = jnp.zeros_like(gin)
        bsum_ref[...] = jnp.zeros_like(bsum_ref)

    def agrad_dot(c):
        agrad[:, c : c + 256] = dot(low_ref[...], wout_ref[c : c + 256, :], NT)

    def gout_dot(c):
        gout[c : c + 256, :] += dot(act_ref[:, c : c + 256], low_ref[...], TN)

    def gin_dot(c):
        gin[c : c + 256, :] += dot(pre_ref[:, c : c + 256], ada_ref[...], TN)

    def slope(c):
        cut = slice(c, c + 256)
        total = bsum_ref[:, cut]
        for at, size in spans(tile, 32):
            span = slice(at, at + size)
            pre = (agrad[span, cut] * der_ref[span, cut].astype(F32)).astype(BF16)
            pre_ref[span, cut] = pre
            total = total + fold(pre.astype(F32))
        bsum_ref[:, cut] = total

    cuts = range(0, CHUNK, 256)
    for c in cuts:
        agrad_dot(c)
    interleave([functools.partial(gout_dot, c) for c in cuts], [functools.partial(slope, c) for c in cuts])
    for c in cuts:
        gin_dot(c)

    @pl.when(step == pl.num_programs(0) - 1)
    def _():
        buckets = CHUNK // BR
        for at, ref in ((0, gin), (buckets, gout)):
            for b in range(buckets):
                low_half = ref[b * BR : b * BR + HALF, :].astype(BF16)
                high_half = ref[b * BR + HALF : b * BR + BR, :].astype(BF16)
                keep_ref[at + b] = jnp.where(core == 0, low_half, high_half)
                send_ref[at + b] = jnp.where(core == 0, high_half, low_half)


def mlp_backward(chunk, before, meta, low, act, der, ada, table, utts):
    count, channels = low.shape
    tile = 512
    slim = pl.BlockSpec((tile, channels), lambda i: (i, 0))
    part = pl.BlockSpec((tile, CHUNK), lambda i: (i, chunk))
    buckets = 2 * CHUNK // BR
    more = [] if before is None else [before]
    return pl.pallas_call(
        functools.partial(mlp_body, utts=utts),
        grid=(count // tile,),
        in_specs=[
            SCALARS,
            slim,
            part,
            part,
            slim,
            pl.BlockSpec((CHUNK, channels), lambda i: (FF // CHUNK + chunk, 0)),
        ]
        + [ANYWHERE] * len(more),
        out_specs=[part, WHOLE, WHOLE, WHOLE],
        out_shape=[
            shape_of((count, FF), BF16),
            shape_of((buckets, HALF, channels), BF16),
            shape_of((buckets, HALF, channels), BF16),
            shape_of((8, CHUNK), F32),
        ],
        input_output_aliases={6: 0} if more else {},
        scratch_shapes=[
            pltpu.VMEM((CHUNK, channels), F32),
            pltpu.VMEM((CHUNK, channels), F32),
            pltpu.VMEM((tile, CHUNK), F32),
        ],
        compiler_params=params(),
        cost_estimate=cost(6 * count * CHUNK * 512, 16 * MIB),
        name=f"mlp_backward_{chunk}",
    )(meta, low, act, der, ada, table, *more)


def norm_body(
    meta, x_ref, low_ref, high_ref, pre_ref, w_in, last_ref, xc_ref, rc_ref, *rest, row, tiles, utts, closing
):
    more = rest[: 8 if closing else 0]
    outs = rest[len(more) :]
    cg_ref, edge_ref, part_ref = outs[:3]
    xs, vecs, picks, agrad, cg, reaches = outs[-6:]
    tile = pl.program_id(0)
    channels = x_ref.shape[2]
    lane_tiles = channels // LANE
    base = meta[row, 2 * utts + 1] + tile * TILE
    vec = lambda v: vecs[2 + v : 3 + v, :]

    @pl.when(tile == 0)
    def _():
        vecs[...] = last_ref[...].astype(F32)
        part_ref[...] = more[0][...] if closing else jnp.zeros_like(part_ref)
        pick_rows(meta, row, utts, vec, picks, channels)

    agrad[...] = dot(pre_ref[...], w_in[...], NN)
    fill_frames(xs, x_ref, low_ref, high_ref, 0, tile, tiles, channels)
    for at, size in spans(TILE, 32):
        span = slice(at, at + size)
        reach, left = frame_reach(meta, row, base + at, size, utts)
        reaches[0, span, :] = reach
        reaches[1, span, :] = left
        index = base + at + lax.broadcasted_iota(jnp.int32, (size, LANE), 0)
        ecs, xcs = [], []
        for c in range(lane_tiles):
            cut = slice(c * LANE, (c + 1) * LANE)
            scale = by_utterance(meta, row, utts, index, lambda u: picks[u : u + 1, cut])
            ecs.append(agrad[span, cut] * scale)
            xcs.append(xc_ref[span, cut].astype(F32))
        m_one = jnp.sum(sum(ecs), axis=1, keepdims=True) * (1.0 / channels)
        m_two = jnp.sum(sum([e * v for e, v in zip(ecs, xcs)]), axis=1, keepdims=True) * (1.0 / channels)
        rc = rc_ref[span, :]
        for c in range(lane_tiles):
            cut = slice(c * LANE, (c + 1) * LANE)
            value = rc * (ecs[c] - m_one - xcs[c] * m_two)
            cg[c, span, :] = value
            cg_ref[span, cut] = value.astype(BF16)
    for u in range(utts):
        begin, end = meta[row, u], meta[row, u + 1]

        @pl.when((begin < base + TILE) & (end > base))
        def _(u=u, begin=begin, end=end):
            wanted = meta[row, utts + 1 + u]
            for c in range(lane_tiles):
                cut = slice(c * LANE, (c + 1) * LANE)
                one = jnp.zeros((8, LANE), F32)
                two = jnp.zeros((8, LANE), F32)
                for at, size in spans(TILE, 64):
                    span = slice(at, at + size)
                    index = base + at + lax.broadcasted_iota(jnp.int32, (size, LANE), 0)
                    value = jnp.where((index >= begin) & (index < end), agrad[span, cut], 0.0)
                    one = one + fold(value * xc_ref[span, cut].astype(F32))
                    two = two + fold(value)
                part_ref[KW + 1 + wanted, :, cut] += one
                part_ref[KW + 1 + NBW + wanted, :, cut] += two

    for c in range(lane_tiles):
        cut = slice(c * LANE, (c + 1) * LANE)
        sums = [part_ref[k, :, cut] for k in range(KW + 1)]
        for at, size in spans(TILE, 32):
            span = slice(at, at + size)
            reach, left = reaches[0, span, :], reaches[1, span, :]
            value = cg[c, span, :]
            for k in range(KW):
                offset = k - RIM
                moved = xs[c, EDGE + offset + at : EDGE + offset + at + size, :] * value
                sums[k] = sums[k] + fold(keep_within(moved, reach, left, offset))
            sums[KW] = sums[KW] + fold(value)
        for k in range(KW + 1):
            part_ref[k, :, cut] = sums[k]

    def edge(side, begin):
        for c in range(lane_tiles):
            edge_ref[side, :, c * LANE : (c + 1) * LANE] = cg[c, begin : begin + 8, :]

    @pl.when(tile == 0)
    def _():
        edge(0, 0)

    @pl.when(tile == tiles - 1)
    def _():
        edge(1, TILE - 8)

    if closing:
        _, other_edge, tail_ref, sums_ref, hsum_ref, bsum0, bsum1, order_ref = more
        vec_ref, quarter_refs = outs[-7], outs[3:7]
        core, plane = meta[0, 2 * utts + 2], meta[0, 2 * utts + 3]

        @pl.when(tile == tiles - 1)
        def _():
            vec_ref[0:8, :] = jnp.zeros((8, channels), F32)
            vec_ref[0:2, :] = tail_ref[0:2, :]
            for v in range(VROWS):
                at = v - (KW + 1 + 2 * NBW)
                rows_of = part_ref[v] if at < 0 else sums_ref[at]
                vec_ref[2 + v : 3 + v, :] = jnp.sum(rows_of, axis=0, keepdims=True)
            line = jnp.concatenate([bsum0[...], bsum1[...]], axis=1)
            for c in range(IN_ROWS):
                at = 2 + VROWS + c
                vec_ref[at : at + 1, :] = jnp.sum(
                    line[:, c * channels : (c + 1) * channels], axis=0, keepdims=True
                )

            parts = []
            for at in (0, BIN_PAD):
                value = jnp.sum(hsum_ref[:, at : at + BIN_PAD], axis=0, keepdims=True)
                value = jnp.broadcast_to(value, (8, BIN_PAD))
                for _ in range(3):
                    part = value.astype(BF16).astype(F32)
                    value = value - part
                    parts.append(part)
            moved = dot(jnp.concatenate(parts, axis=0).astype(BF16), order_ref[...], NT)
            halves = [moved[at : at + 8] + moved[at + 8 : at + 16] + moved[at + 16 : at + 24] for at in (0, 24)]
            flat = jnp.concatenate(halves, axis=1)
            column = lax.broadcasted_iota(jnp.int32, (8, 3 * channels), 1)
            moved = pltpu.roll(flat, 2 * BIN_PAD - (BIN_PAD - BINS), 1)
            joined = jnp.where(column < BINS, flat, moved)
            joined = jnp.where(column < NOUT, joined, 0.0)
            for c in range(HEAD_ROWS):
                at = 2 + VROWS + IN_ROWS + c
                vec_ref[at : at + 1, :] = joined[0:1, c * channels : (c + 1) * channels]
            vec_ref[28:32, :] = jnp.zeros((4, channels), F32)
            for ref, c, p in zip(
                quarter_refs,
                (core, 1 - core, core, 1 - core),
                (plane, plane, 1 - plane, 1 - plane),
            ):
                ref[0:8, :] = vec_ref[pl.ds(pl.multiple_of(c * HALF + p * QUART, QUART), QUART), :]
            for at, ref in ((8, other_edge), (16, edge_ref)):
                quarter_refs[1][at : at + 8, :] = jnp.where(core == 0, ref[1], ref[0])
                quarter_refs[3][at : at + 8, :] = jnp.where(core == 0, ref[0], ref[1])


def norm_backward(row, closing, meta, x, low, high, pre, table, xc, rc, utts):
    rows, frames, channels = x.shape
    tiles = frames // TILE
    block = lambda width: pl.BlockSpec((TILE, width), lambda i: (row * tiles + i, 0))
    sums = KW + 1 + 2 * NBW
    out_specs = [pl.BlockSpec((TILE, channels), lambda i: (i, 0)), WHOLE, WHOLE]
    out_shape = [
        shape_of((frames, channels), BF16),
        shape_of((2, 8, channels), F32),
        shape_of((sums, 8, channels), F32),
    ]
    if closing:
        out_specs += [WHOLE] * 4
        out_shape += [shape_of((8 * n, channels), F32) for n in (1, 3, 1, 3)]
    return pl.pallas_call(
        functools.partial(norm_body, row=row, tiles=tiles, utts=utts, closing=bool(closing)),
        grid=(tiles,),
        in_specs=[SCALARS]
        + [pl.BlockSpec((1, frames, channels), lambda i: (row, 0, 0))]
        + [pl.BlockSpec((1, EDGE, channels), lambda i: (row, 0, 0))] * 2
        + [block(FF)]
        + [
            pl.BlockSpec((FF, channels), lambda i: (0, 0)),
            pl.BlockSpec((BR, channels), lambda i: (NB - 1, 0)),
            block(channels),
            block(LANE),
        ]
        + [WHOLE] * len(closing),
        out_specs=out_specs,
        out_shape=out_shape,
        scratch_shapes=([pltpu.VMEM((BR, channels), F32)] if closing else [])
        + [
            pltpu.VMEM((channels // LANE, TILE + 2 * EDGE, LANE), F32),
            pltpu.VMEM((BR, channels), F32),
            pltpu.VMEM((2 * utts, channels), F32),
            pltpu.VMEM((TILE, channels), F32),
            pltpu.VMEM((channels // LANE, TILE, LANE), F32),
            pltpu.VMEM((2, TILE, LANE), jnp.int32),
        ],
        compiler_params=params(),
        cost_estimate=cost(2 * frames * 1536 * 512, 12 * MIB),
        name=f"norm_backward_{row}",
    )(meta, x, low, high, pre, table, table, xc, rc, *closing)


def conv_body(meta, cg_ref, before_ref, after_ref, near_ref, cross_ref, resg_ref, last_ref, *rest, row, tiles, utts):
    out_ref, cs, vecs = rest[-3:]
    tile = pl.program_id(0)
    channels = cg_ref.shape[1]
    core = meta[0, 2 * utts + 2]
    base = meta[row, 2 * utts + 1] + tile * TILE

    @pl.when(tile == 0)
    def _():
        vecs[...] = last_ref[...].astype(F32)

    for c in range(channels // LANE):
        cut = slice(c * LANE, (c + 1) * LANE)
        cs[c, EDGE : EDGE + TILE, :] = cg_ref[:, cut].astype(F32)
        near, cross = near_ref[8 + 8 * row : 16 + 8 * row, cut], cross_ref[8 + 8 * row : 16 + 8 * row, cut]
        before, after = before_ref[:, cut].astype(F32)[EDGE - 8 :], after_ref[:, cut].astype(F32)[:8]
        cs[c, EDGE - 8 : EDGE, :] = jnp.where(tile == 0, jnp.where(core == 0, cross, near), before)
        after = jnp.where(tile == tiles - 1, jnp.where(core == 0, near, cross), after)
        cs[c, EDGE + TILE : EDGE + TILE + 8, :] = after
    for at, size in spans(TILE, 32):
        span = slice(at, at + size)
        reach, left = frame_reach(meta, row, base + at, size, utts)
        for c in range(channels // LANE):
            cut = slice(c * LANE, (c + 1) * LANE)
            total = resg_ref[span, cut].astype(F32)
            for k in range(KW):
                offset = RIM - k
                moved = cs[c, EDGE + offset + at : EDGE + offset + at + size, :]
                total = total + keep_within(moved, reach, left, offset) * vecs[2 + k : 3 + k, cut]
            out_ref[0, span, cut] = total


def conv_backward(row, before, meta, cg, near, cross, resg, table, rows, utts):
    frames, channels = cg.shape
    tiles = frames // TILE
    per = TILE // EDGE
    more = [] if before is None else [before]
    return pl.pallas_call(
        functools.partial(conv_body, row=row, tiles=tiles, utts=utts),
        grid=(tiles,),
        in_specs=[
            SCALARS,
            pl.BlockSpec((TILE, channels), lambda i: (i, 0)),
            pl.BlockSpec((EDGE, channels), lambda i: (jnp.maximum(i * per - 1, 0), 0)),
            pl.BlockSpec((EDGE, channels), lambda i: (jnp.minimum((i + 1) * per, tiles * per - 1), 0)),
            WHOLE,
            WHOLE,
            pl.BlockSpec((TILE, channels), lambda i: (row * tiles + i, 0)),
            pl.BlockSpec((BR, channels), lambda i: (NB - 1, 0)),
        ]
        + [ANYWHERE] * len(more),
        out_specs=pl.BlockSpec((1, TILE, channels), lambda i: (row, i, 0)),
        out_shape=shape_of((rows, frames, channels), F32),
        input_output_aliases={8: 0} if more else {},
        scratch_shapes=[
            pltpu.VMEM((channels // LANE, TILE + 2 * EDGE, LANE), F32),
            pltpu.VMEM((BR, channels), F32),
        ],
        compiler_params=params(),
        cost_estimate=cost(16 * frames * 512, 6 * MIB),
        name=f"conv_backward_{row}",
    )(meta, cg, cg, cg, near, cross, resg, table, *more)


def wave_body(meta, spec_ref, prev_ref, halo_ref, synth_ref, win_ref, *rest, start, rows, utts):
    out_ref, spec_all, held_all, done_all = rest[-4:]
    tile = start + pl.program_id(0)
    lane = lax.broadcasted_iota(jnp.int32, (TILE // 2, LANE), 1)
    front = lane < LANE // 2
    for r in range(rows):
        spec, held, done = spec_all.at[r], held_all.at[r], done_all.at[r]
        base = meta[r, 2 * utts + 1] + tile * TILE
        spec[EDGE:, :] = spec_ref[r]
        spec[0:EDGE, :] = jnp.where(tile == 0, halo_ref[r], prev_ref[r])
        for parity in range(2):
            half = slice(parity * BIN_PAD, (parity + 1) * BIN_PAD)
            piece = dot(spec[:, half], synth_ref[parity], NN)
            for c in range(BIN_PAD // LANE):
                held[parity, c] = piece[:, c * LANE : (c + 1) * LANE]
        for at, size in spans(TILE, 32):
            reach, _ = frame_reach(meta, r, base + at, size, utts)
            for c in range(3):
                cut = slice(c * LANE, (c + 1) * LANE)
                total = None
                for j in range(LAPS):
                    rows_at = slice(EDGE + at - j, EDGE + at - j + size)
                    of = (j % 2) * 3 + c
                    one, two = held[0, of, rows_at, :], held[1, of, rows_at, :]
                    piece = (one + two if j < 2 else one - two) * win_ref[j : j + 1, cut]
                    total = piece if j == 0 else total + jnp.where(reach >= j, piece, 0.0)
                done[c, at : at + size, :] = total * over(win_ref, LAPS, reach, c)
        even = [done[c, pl.ds(0, TILE // 2, stride=2), :] for c in range(3)]
        odd = [pltpu.roll(done[c, pl.ds(1, TILE // 2, stride=2), :], LANE // 2, 1) for c in range(3)]
        part = (
            even[0],
            even[1],
            jnp.where(front, even[2], odd[0]),
            jnp.where(front, odd[0], odd[1]),
            jnp.where(front, odd[1], odd[2]),
        )
        for k in range(PAIR):
            out_ref[pl.ds(2 * k + r, TILE // 2, stride=2 * PAIR), :] = part[k]


def wave_forward(start, stop, before, meta, spec, halo, synth, win, utts):
    rows, frames, _ = spec.shape
    tiles = frames // TILE
    per = TILE // EDGE
    more = [] if before is None else [before]
    return pl.pallas_call(
        functools.partial(wave_body, start=start, rows=rows, utts=utts),
        grid=(stop - start,),
        in_specs=[
            SCALARS,
            pl.BlockSpec((rows, TILE, 2 * BIN_PAD), lambda i: (0, start + i, 0)),
            pl.BlockSpec((rows, EDGE, 2 * BIN_PAD), lambda i: (0, jnp.maximum((start + i) * per - 1, 0), 0)),
            WHOLE,
            WHOLE,
            WHOLE,
        ]
        + [ANYWHERE] * len(more),
        out_specs=pl.BlockSpec((PAIR * TILE, LANE), lambda i: (start + i, 0)),
        out_shape=shape_of((PAIR * TILE * tiles, LANE), F32),
        input_output_aliases={6: 0} if more else {},
        scratch_shapes=[
            pltpu.VMEM((rows, TILE + EDGE, 2 * BIN_PAD), BF16),
            pltpu.VMEM((rows, 2, BIN_PAD // LANE, TILE + EDGE, LANE), F32),
            pltpu.VMEM((rows, LAP_PAD // LANE, TILE, LANE), F32),
        ],
        compiler_params=params(),
        cost_estimate=cost(4 * rows * (stop - start) * TILE * 768 * 768, 10 * MIB),
        name=f"wave_forward_{start}",
    )(meta, spec, spec, halo, synth, win, *more)


def slot_body(slot_of, *refs, groups, lasts, copies, slots):
    count = max(g[0] for g in groups) + 1
    keeps, cames, last_refs = refs[:count], refs[count : 2 * count], refs[2 * count : 2 * count + lasts]
    out, *more = refs[2 * count + lasts :]
    for index, offset, start, stop in groups:

        def one(b, carry, keep=keeps[index], came=cames[index], offset=offset, start=start):
            value = keep[offset + b].astype(F32) + came[offset + b].astype(F32)
            out[slot_of[0, start + b]] = value.astype(BF16)
            return carry

        lax.fori_loop(0, stop - start, one, 0, unroll=True)
    total = last_refs[0][0:QUART, :]
    for ref in last_refs[1:]:
        total = total + ref[0:QUART, :]
    out[slot_of[0, NB - 1]] = total.astype(BF16)
    for ref, at in zip(more, copies):
        ref[...] = out[at * slots : (at + 1) * slots]


def to_slots(slot_of, keeps, cames, lasts, groups, owners, slots, copies):
    channels = keeps[0].shape[2]
    return pl.pallas_call(
        functools.partial(slot_body, groups=groups, lasts=len(lasts), copies=copies, slots=slots),
        in_specs=[SCALARS] + [WHOLE] * (2 * len(keeps) + len(lasts)),
        out_specs=[WHOLE] * (1 + len(copies)),
        out_shape=[shape_of((owners * slots, QUART, channels), BF16)]
        + [shape_of((slots, QUART, channels), BF16)] * len(copies),
        compiler_params=params(),
        cost_estimate=cost(0, 6 * MIB),
        name="to_slots",
    )(slot_of, *keeps, *cames, *lasts)


def adam_body(places, meta, mine_ref, other_ref, master, first, second, *rest, block):
    out_master, out_first, out_second = rest[-3:]
    one_fix = 1.0 / (1.0 - BETA_ONE**STEP_COUNT)
    two_fix = 1.0 / (1.0 - BETA_TWO**STEP_COUNT)
    core = meta[0, meta.shape[1] - 2]
    for s in range(block):
        bucket = places[0, pl.program_id(0) * block + s]
        mine, other = mine_ref[s].astype(F32), other_ref[s].astype(F32)
        for half in range(2):
            grad = jnp.where(bucket < NB, jnp.where(core == half, mine, other), 0.0)
            old = master[s, half, 0]
            one = BETA_ONE * first[s, half, 0] + (1.0 - BETA_ONE) * grad
            two = BETA_TWO * second[s, half, 0] + (1.0 - BETA_TWO) * grad * grad
            out_first[s, half, 0] = one
            out_second[s, half, 0] = two
            step = one * one_fix / (jnp.sqrt(two * two_fix) + ADAM_EPS)
            out_master[s, half, 0] = old - LEARN_RATE * (step + WEIGHT_DECAY * old)


def adam(places, meta, mine, other, master, first, second, before):
    slots, depth, channels = master.shape
    block = max(b for b in range(1, ADAM_BLOCK + 1) if slots % b == 0)
    plane_at = meta.shape[1] - 1
    cut = lambda v: v.reshape(slots, 2, 2, QUART, channels)
    def at_plane(i, places, meta):
        plane = meta[0, plane_at]
        return i, 0, 1 - plane if before else plane, 0, 0

    full = pl.BlockSpec((block, 2, 1, QUART, channels), at_plane)
    part = pl.BlockSpec((block, QUART, channels), lambda i, places, meta: (i, 0, 0))
    more = [cut(v) for v in before]
    outs = pl.pallas_call(
        functools.partial(adam_body, block=block),
        grid_spec=pltpu.PrefetchScalarGridSpec(
            num_scalar_prefetch=2,
            grid=(slots // block,),
            in_specs=[part] * 2 + [full] * 3 + [ANYWHERE] * len(more),
            out_specs=[full] * 3,
        ),
        out_shape=[shape_of((slots, 2, 2, QUART, channels), F32)] * 3,
        input_output_aliases={7 + v: v for v in range(len(more))},
        compiler_params=params(),
        cost_estimate=cost(0, 6 * MIB),
        name="adam_second" if more else "adam_first",
    )(places, meta, mine, other, cut(master), cut(first), cut(second), *more)
    return [v.reshape(slots, depth, channels) for v in outs]


def tie(*values):
    return lax.optimization_barrier(values)


def plus(*values):
    return sum([v.astype(F32) for v in values]).astype(BF16)


def local(frames_in, lengths, bw_ids, owner_list, master, moment1, moment2, wave_grad):
    rows, frames, channels = frames_in.shape
    slots = master.shape[0]
    utts = lengths.shape[1]
    owners = lax.axis_size("rows")
    seqs = lax.axis_size("seq")
    row_at = lax.axis_index("rows")
    seq_at = lax.axis_index("seq")
    core, plane = seq_at % 2, seq_at // 2
    ring = ring_of(owners)
    half_ring = owners // 2

    mine = lax.dynamic_slice_in_dim(master, core * HALF, HALF, axis=1).astype(BF16)

    lines = wave_grad.reshape(rows, frames * HOP // LANE, LANE).transpose(1, 0, 2).reshape(-1, LANE)
    order = jnp.asarray(order_table())
    synth = jnp.asarray(synthesis_table())
    win = jnp.asarray(window_tables())

    low = shifted(frames_in[:, frames - EDGE :], 1)
    high = shifted(frames_in[:, :EDGE], -1)
    later = shifted(lines[: PAIR * EDGE], -1)
    offsets = [0]
    for hop in range(1, half_ring):
        offsets += [-hop, hop]
    offsets.append(-half_ring)
    names = np.arange(owners, dtype=np.int32)
    ids = jnp.stack([row_at, seq_at]).astype(jnp.int32)
    meta, places, held, slot_of, counts = plan(
        ids,
        lengths,
        bw_ids,
        owner_list,
        jnp.asarray(ring if ring else names, jnp.int32),
        jnp.asarray(offsets if ring else names, jnp.int32),
        slots,
        frames,
        bool(ring),
    )

    cot = None
    tiles = frames // TILE
    if ring:
        ahead = back = mine
        arrived = [mine, seq_swap(mine, 1)]
        for hop in range(half_ring):
            source = (ahead, back)
            ahead = lax.ppermute(ahead, AXES, ring_step(ring, 1, seqs))
            if hop < half_ring - 1:
                back = lax.ppermute(back, AXES, ring_step(ring, -1, seqs))
            if hop == 0:
                ahead, back, low, high, later, meta = tie(ahead, back, low, high, later, meta)
            if hop in (1, 2):
                feed = tie(lines, *source)[0]
                begin, end = ((0, tiles // 2), (tiles // 2, tiles))[hop - 1]
                cot = spectrum_cotangent(begin, end, cot, meta, feed, later, synth, win, rows, utts)
                ahead, back, cot = tie(ahead, back, cot)
            if hop == half_ring - 1:
                fed = tie(places, *source)[0]
                partial_table = assemble(tuple(range(owners - 1)), meta, fed, counts, arrived, slots)
                ahead, partial_table = tie(ahead, partial_table)
            else:
                arrived += [ahead, seq_swap(ahead, 1), back, seq_swap(back, 1)]
        arrived = [ahead, seq_swap(ahead, 1)]
        owned = (owners - 1,)
        part_places, part_counts, part_slots = places, counts, slots
    else:
        gathered = lax.all_gather(mine, "rows", axis=0, tiled=True)
        arrived = [gathered, seq_swap(gathered, 1)]
        owned = (0,)
        arrived = [take_slots(slot_of, a) for a in arrived]
        part_places = jnp.arange(NB, dtype=jnp.int32)[None, :]
        part_counts, part_slots = jnp.full((1, 1), NB, jnp.int32), NB
        partial_table = jnp.zeros((NB * BR, channels), BF16)
        cot = spectrum_cotangent(0, tiles, cot, meta, lines, later, synth, win, rows, utts)

    (table, spec, act, der, ada, low_grad, resg, xc, rc, send, keep, tail, sums, hsum) = forward(
        owned, part_slots, meta, part_places, part_counts, frames_in, low, high, order, cot, arrived, partial_table, utts
    )
    halo = shifted(spec[:, frames - EDGE :], 1)

    keeps, cames, groups = [], [], []

    def split(keep, came):
        both = plus(keep, came)
        stay = lax.dynamic_slice_in_dim(both, plane * QUART, QUART, axis=1)
        leave = lax.dynamic_slice_in_dim(both, (1 - plane) * QUART, QUART, axis=1)
        return stay, leave

    def record(stay, came, begins, per):
        for at, begin in enumerate(begins):
            groups.append((len(keeps), at * per, begin, begin + per))
        keeps.append(stay)
        cames.append(came)

    per = CHUNK // BR
    pre, bsums = None, []
    begins, count = (2 * FF // BR,), 40
    waiting = []
    for chunk in range(FF // CHUNK):
        near = seq_swap(send, 1)
        pre, next_send, next_keep, bsum = mlp_backward(chunk, pre, meta, low_grad, act, der, ada, table, utts)
        near, pre, next_send, next_keep = tie(near, pre, next_send, next_keep)
        bsums.append(bsum)
        stay, leave = split(keep, near)
        waiting.append((stay, seq_swap(leave, 2), begins, count))
        send, keep = next_send, next_keep
        begins, count = (chunk * per, FF // BR + chunk * per), per

    near = seq_swap(send, 1)
    for stay, came, *where_from in waiting[:-1]:
        pre, came = tie(pre, came)
        record(stay, came, *where_from)
    cg0, edge0, parts = norm_backward(0, (), meta, frames_in, low, high, pre, table, xc, rc, utts)
    kept, came, *where_from = waiting[-1]
    near, cg0, edge0, parts, pre, came = tie(near, cg0, edge0, parts, pre, came)
    record(kept, came, *where_from)
    stay, leave = split(keep, near)
    came = seq_swap(leave, 2)
    closing = (parts, edge0, tail, sums, hsum, *bsums, order)
    cg1, _, _, own, to_near, to_far, to_cross = norm_backward(
        1, closing, meta, frames_in, low, high, pre, table, xc, rc, utts
    )
    lasts = (own, seq_swap(to_near, 1), seq_swap(to_far, 2), seq_swap(to_cross, 3))
    came, spec, *lasts = tie(came, spec, *lasts)
    record(stay, came, begins, count)
    first_sent = (owners - 1, owners - 3) if ring else ()
    chunks, *sent = to_slots(slot_of, keeps, cames, lasts, tuple(groups), owners, slots, first_sent)

    state = {}

    def work(stage, *ready):
        if stage in (0, 2):
            feed = tie(spec, *ready)[0]
            begin, end, before = ((0, tiles // 2, None), (tiles // 2, tiles, state.get("wave")))[stage // 2]
            state["wave"] = wave_forward(begin, end, before, meta, feed, halo, synth, win, utts)
            return "wave"
        if stage in (1, 3):
            row = stage // 2
            feed = tie((cg0, cg1)[row], *ready)[0]
            state["grad"] = conv_backward(
                row, state.get("grad"), meta, feed, lasts[1], lasts[3], resg, table, rows, utts
            )
            return "grad"

    if ring:
        cut = {o: chunks[i * slots : (i + 1) * slots] for i, o in enumerate(offsets)}
        up, down = sent
        for hop in range(half_ring):
            left_over = half_ring - 1 - hop
            source = (up, down)
            up = lax.ppermute(up, AXES, ring_step(ring, 1, seqs))
            if hop < half_ring - 1:
                down = lax.ppermute(down, AXES, ring_step(ring, -1, seqs))
            done = work(hop, *source)
            up, down, state[done] = tie(up, down, state[done])
            if left_over:
                up = plus(up, cut[left_over])
                if hop < half_ring - 2:
                    down = plus(down, cut[1 - left_over])
        own = plus(cut[0], up, down)
    else:
        own = lax.psum_scatter(chunks, "rows", scatter_dimension=0, tiled=True)
        for hop in range(4):
            work(hop, own)
    near, far = seq_swap(own, 1), seq_swap(own, 2)
    cross = seq_swap(far, 1)
    waveform = state["wave"].reshape(-1, rows, LANE).transpose(1, 0, 2).reshape(rows, frames * HOP)

    first = adam(held, meta, own, near, master, moment1, moment2, ())
    cross, *first = tie(cross, *first)
    new_master, new_first, new_second = adam(held, meta, far, cross, master, moment1, moment2, first)
    return waveform, state["grad"], new_master, new_first, new_second


def solution(mesh):
    in_specs = (
        P("rows", "seq", None),
        P("rows", None),
        P("rows", None),
        P(),
        P("rows", None, None),
        P("rows", None, None),
        P("rows", None, None),
        P("rows", "seq"),
    )
    out_specs = (
        P("rows", "seq"),
        P("rows", "seq", None),
        P("rows", None, None),
        P("rows", None, None),
        P("rows", None, None),
    )
    return jax.shard_map(local, mesh=mesh, in_specs=in_specs, out_specs=out_specs, check_vma=False)
```
